32 devices in a mesh: groups: 2 (over y), space: 4 (over z), tm: 2 (over x), freq: 2 (over core).
Axes of the slice: x: 2, y: 2, z: 4, core: 2. Of those that a mesh axis runs over, the one named last changes fastest.
Arguments:
- snapshots: float32 [16, 64, 16384], P(None, 'space', ('groups', 'tm')), parts along dimension 2, may hold values from -28 to 28, as said below
- weights: float32 [16384], P(('groups', 'tm', 'space')), parts along dimension 0, may hold values from 0.3 to 3
Outputs:
- modes: float32 [16, 2, 16, 16384], P('freq', None, None, ('groups', 'tm', 'space')), parts along dimension 3
- r_factor: float32 [4, 16, 16, 16], P('groups', 'freq'), parts along dimension 0
The draws below stay inside these ranges and needn't reach their ends.
There are 2 independent parts, one for each index of `groups`. The reference program is written for one: setup_inputs(seed, part) draws one part's arguments, and reference() takes and returns one part's arrays. A program takes and returns all parts, laid end to end along the dimension named above; each array names one. Nothing has to cross between parts.
Inputs may be any that keep to these rules, and one draw needn't show every extreme that they name: `snapshots`: velocity fluctuations of the jet.
All inputs are finite; a program needn't handle non-finite values.
Results may differ from the reference program's by a relative error of at most 0.00009.
Values sent between devices are 32-bit elements; how exact they have to be, the bound alone decides.
No kernel may reach another device: no remote copies, remote signals or barrier semaphores. Data moves between devices by JAX's collectives and lax.ppermute only.
A program may use at most 64 MiB of HBM per device.

```python
import math
import jax
import jax.numpy as jnp
from jax import lax

NB = 16
SEGMENT_FRAMES = 64
NF = 16
M = 8192


def draw_snapshots(key, part):
    first_key = jax.random.fold_in(jax.random.fold_in(key, 11), 0)
    place = jnp.arange(M, dtype=jnp.float32) / M
    envelope = 3.0 ** place
    field = jnp.clip(jax.random.normal(first_key, (NB, SEGMENT_FRAMES, M), jnp.float32), -6.0, 6.0)
    return field * envelope[None, None, :]


def levels(rng, extent, cuts, smallest, largest):
    factor_of, own = 1.0, jax.random.fold_in(rng, 6)
    for dim, blocks in cuts:
        heights = jnp.exp(jax.random.uniform(jax.random.fold_in(own, dim), (blocks,), jnp.float32, smallest / len(cuts), largest / len(cuts)))
        factor_of = factor_of * jnp.repeat(heights, extent[dim] // blocks).reshape([-1 if axis == dim else 1 for axis in range(len(extent))])
    return factor_of


def setup_inputs(seed: int = 0, part: int = 0) -> dict:
    seeds = jax.random.split(jax.random.key(seed), 3)
    part_splits = jax.random.split(jax.random.fold_in(seeds[2], part), 3)
    return {
        "snapshots": draw_snapshots(jax.random.fold_in(jax.random.fold_in(seeds[2], part), 71), part),
        "weights": jnp.clip(jnp.exp(math.log(3.0) - 2.3025851 * jax.random.uniform(part_splits[1], (M,), jnp.float32) ** levels(part_splits[1], (M,), ((0, 8),), -0.2, 0.2)), 0.3, 3.0),
    }


epsilon = 1e-05

def dft_table(first_freq, how_many, initial_moment, elapsed_timespan):
    recorded_moments = initial_moment + jnp.arange(elapsed_timespan, dtype=jnp.int32)
    fourier_cycle_rate = first_freq + 1 + jnp.arange(how_many, dtype=jnp.int32)
    every_time = jnp.arange(SEGMENT_FRAMES, dtype=jnp.float32)
    tapers = 0.5 - 0.5 * jnp.cos(2.0 * jnp.pi * every_time / SEGMENT_FRAMES)
    norm_taper = jnp.sqrt(jnp.sum(tapers * tapers))
    segment_hann_weighting = 0.5 - 0.5 * jnp.cos(2.0 * jnp.pi * recorded_moments.astype(jnp.float32) / SEGMENT_FRAMES)
    weighted = segment_hann_weighting / norm_taper
    twiddle_angle_list = fourier_cycle_rate[:, None] * recorded_moments[None, :] % SEGMENT_FRAMES
    phases = 2.0 * jnp.pi * twiddle_angle_list.astype(jnp.float32) / SEGMENT_FRAMES
    paired = jnp.stack([jnp.cos(phases) * weighted[None, :], -jnp.sin(phases) * weighted[None, :]], axis=1)
    return paired.reshape(2 * how_many, elapsed_timespan)

def contract(left, right):
    return jnp.einsum('fbm,fcm->fbc', left, right, precision=lax.Precision.HIGHEST)

def gram_terms(spectra, weights):
    real_part = spectra[:, 0]
    imag_part = spectra[:, 1]
    weighted_re = real_part * weights
    weighted_im = imag_part * weights
    gram_re = contract(weighted_re, real_part) + contract(weighted_im, imag_part)
    gram_im = contract(weighted_re, imag_part) - contract(weighted_im, real_part)
    return jnp.stack([gram_re, gram_im])

def factor(gram):
    positions = jnp.arange(NB, dtype=jnp.int32)
    rows_re = []
    rows_im = []
    for i in range(NB):
        accum_re = gram[0][:, i, :]
        accum_im = gram[1][:, i, :]
        for p in range(i):
            left_re = rows_re[p][:, i][:, None]
            left_im = rows_im[p][:, i][:, None]
            accum_re = accum_re - (left_re * rows_re[p] + left_im * rows_im[p])
            accum_im = accum_im - (left_re * rows_im[p] - left_im * rows_re[p])
        pivot = jnp.sqrt(accum_re[:, i] + epsilon)
        beyond = (positions > i)[None, :]
        at_diag = (positions == i)[None, :]
        rows_re.append(jnp.where(beyond, accum_re / pivot[:, None], 0.0) + jnp.where(at_diag, pivot[:, None], 0.0))
        rows_im.append(jnp.where(beyond, accum_im / pivot[:, None], 0.0))
    upper_re = jnp.stack(rows_re, axis=1)
    upper_im = jnp.stack(rows_im, axis=1)
    inverse_re = [None] * NB
    inverse_im = [None] * NB
    for i in range(NB - 1, -1, -1):
        accum_re = jnp.broadcast_to(jnp.where(positions == i, 1.0, 0.0).astype(jnp.float32)[None, :], upper_re[:, 0, :].shape)
        accum_im = jnp.zeros_like(accum_re)
        for p in range(i + 1, NB):
            coef_re = upper_re[:, i, p][:, None]
            coef_im = upper_im[:, i, p][:, None]
            accum_re = accum_re - (coef_re * inverse_re[p] - coef_im * inverse_im[p])
            accum_im = accum_im - (coef_re * inverse_im[p] + coef_im * inverse_re[p])
        pivot = upper_re[:, i, i][:, None]
        inverse_re[i] = accum_re / pivot
        inverse_im[i] = accum_im / pivot
    return (upper_re, upper_im, jnp.stack(inverse_re, axis=1), jnp.stack(inverse_im, axis=1))

def apply_inverse(left, inverse):
    return jnp.einsum('fbm,fbc->fcm', left, inverse, precision=lax.Precision.HIGHEST)

def build_modes(spectra, inverse_re, inverse_im):
    real_part = spectra[:, 0]
    imag_part = spectra[:, 1]
    modes_re = apply_inverse(real_part, inverse_re) - apply_inverse(imag_part, inverse_im)
    modes_im = apply_inverse(real_part, inverse_im) + apply_inverse(imag_part, inverse_re)
    return jnp.stack([modes_re, modes_im], axis=1)

def reference(snapshots, weights):
    table = dft_table(0, NF, 0, SEGMENT_FRAMES)
    spectra = jnp.einsum('ft,btm->fbm', table, snapshots, precision=lax.Precision.HIGHEST)
    spectra = spectra.reshape(NF, 2, NB, M)
    gram = gram_terms(spectra, weights) / M
    upper_re, upper_im, inverse_re, inverse_im = factor(gram)
    modes = build_modes(spectra, inverse_re, inverse_im)
    return (modes, jnp.stack([upper_re, upper_im]))
```

```python
import functools

import numpy as np
import jax
import jax.numpy as jnp
from jax import lax
from jax.experimental import pallas as pl
from jax.experimental.pallas import tpu as pltpu
from jax.sharding import PartitionSpec as P

NB = 16
SEGMENT_FRAMES = 64
NF = 16
HALF = NB // 2
STEP = 16
epsilon = 1e-05
VMEM_BYTES = 48 * 1024 * 1024


def dft_blocks(freq_count):
    times = np.arange(SEGMENT_FRAMES)
    taper = 0.5 - 0.5 * np.cos(2.0 * np.pi * times / SEGMENT_FRAMES)
    taper = taper / np.sqrt(np.sum(taper * taper))
    bins = 1 + np.arange(NF)
    angles = 2.0 * np.pi * (bins[:, None] * times[None, :] % SEGMENT_FRAMES) / SEGMENT_FRAMES
    table = np.stack([np.cos(angles) * taper, -np.sin(angles) * taper])
    local = NF // freq_count
    table = table.reshape(2, freq_count, local, SEGMENT_FRAMES // STEP, STEP)
    eye = np.eye(HALF)
    spread = np.einsum("rhfgt,bc->hrfbgct", table, eye)
    return spread.reshape(freq_count, 2 * local * HALF, SEGMENT_FRAMES * HALF).astype(np.float32)


def dot(a, b):
    return jnp.dot(a, b, precision=lax.Precision.HIGHEST, preferred_element_type=jnp.float32)


def cut_kernel(n, rows, share, x_ref, o_ref, sem):
    first = lax.axis_index("freq") * share
    copies = []
    for s in range(n):
        start = pl.multiple_of(s * rows + first, 128)
        copies.append(
            pltpu.make_async_copy(x_ref.at[:, :, pl.ds(start, share)], o_ref.at[s], sem.at[s])
        )
    for copy in copies:
        copy.start()
    for copy in copies:
        copy.wait()


def cut(snapshots, n, rows, share):
    blocks, local_times, _ = snapshots.shape
    if local_times % 8 == 0:
        return pl.pallas_call(
            functools.partial(cut_kernel, n, rows, share),
            out_shape=jax.ShapeDtypeStruct((n, blocks, local_times, share), jnp.float32),
            in_specs=[pl.BlockSpec(memory_space=pl.ANY)],
            out_specs=pl.BlockSpec(memory_space=pl.ANY),
            scratch_shapes=[pltpu.SemaphoreType.DMA((n,))],
        )(snapshots)
    shaped = snapshots.reshape(blocks, local_times, n, rows // share, share)
    own = lax.dynamic_index_in_dim(shaped, lax.axis_index("freq"), 3, keepdims=False)
    return own.transpose(2, 0, 1, 3)


def spectra_kernel(local, targets, freq_count, x_ref, t_ref, w_ref, own_ref, other_ref, gram_ref):
    share = x_ref.shape[3]
    half_rows = 2 * local * HALF
    for h, out_ref in ((0, own_ref), (1, other_ref)):
        for g in range(NB // HALF):
            data = x_ref[:, g * HALF : (g + 1) * HALF].reshape(SEGMENT_FRAMES * HALF, share)
            part = dot(t_ref[h], data)
            out_ref[:, g] = part.reshape(2 * local, HALF, share)
    width = local * NB
    line = lax.broadcasted_iota(jnp.int32, (width, width), 0) // NB
    lane = lax.broadcasted_iota(jnp.int32, (width, width), 1) // NB
    row = lax.broadcasted_iota(jnp.int32, (NB, width), 0)
    col = lax.broadcasted_iota(jnp.int32, (NB, width), 1) % NB
    packed = []
    for out_ref in (own_ref, other_ref):
        z = out_ref[...].reshape(2 * width, share)
        zw = z * w_ref[...]
        full = lax.dot_general(
            zw,
            z,
            (((1,), (1,)), ((), ())),
            precision=lax.Precision.HIGHEST,
            preferred_element_type=jnp.float32,
        )
        gram_re = full[:width, :width] + full[width:, width:]
        gram_im = full[:width, width:] - full[width:, :width]
        both = []
        for part in (gram_re, gram_im):
            kept = jnp.where(line == lane, part, 0.0)
            both.append(jnp.sum(kept.reshape(local, NB, width), axis=0))
        packed.append(jnp.where(row >= col, both[0], both[1]))
    me = lax.axis_index("freq")
    for d in range(targets):
        gram_ref[d] = jnp.where(me == d % freq_count, packed[0], packed[1])


def spectra_and_gram(pieces, tables, weights, local, targets, freq_count):
    share = pieces.shape[3]
    shape = jax.ShapeDtypeStruct((2 * local, NB // HALF, HALF, share), jnp.float32)
    return pl.pallas_call(
        functools.partial(spectra_kernel, local, targets, freq_count),
        out_shape=(
            shape,
            shape,
            jax.ShapeDtypeStruct((targets, NB, local * NB), jnp.float32),
        ),
        compiler_params=pltpu.CompilerParams(vmem_limit_bytes=VMEM_BYTES),
    )(pieces, tables, weights)


def inv_sqrt(x):
    y = lax.rsqrt(x)
    return y * (1.5 - 0.5 * x * (y * y))


def finish_kernel(local, total, gram_ref, own_ref, other_ref, modes_ref, factor_ref):
    width = local * NB
    share = own_ref.shape[3]
    gram = jnp.sum(gram_ref[...], axis=0) / total
    row = lax.broadcasted_iota(jnp.int32, (NB, width), 0)
    col = lax.broadcasted_iota(jnp.int32, (NB, width), 1) % NB
    stacked = [jnp.where(col == j, gram, 0.0) for j in range(NB)]
    for j in range(NB):
        line = jnp.broadcast_to(gram[j : j + 1, :], (NB, width))
        stacked.append(jnp.where((col == row) & (row > j), -line, 0.0))
    stacked = jnp.concatenate(stacked, axis=0)
    group_r = lax.broadcasted_iota(jnp.int32, (width, width), 0) // NB
    group_c = lax.broadcasted_iota(jnp.int32, (width, width), 1) // NB
    same = group_r == group_c
    ones = jnp.where(same, 1.0, 0.0).astype(jnp.bfloat16)
    spread = jnp.zeros(stacked.shape, jnp.float32)
    rest = stacked
    for _ in range(3):
        piece = rest.astype(jnp.bfloat16)
        rest = rest - piece.astype(jnp.float32)
        spread = spread + jnp.dot(piece, ones, preferred_element_type=jnp.float32)
    col_re = [[spread[j * NB + 8 * h : j * NB + 8 * h + 8] for h in (0, 1)] for j in range(NB)]
    base = NB * NB
    col_im = [
        [spread[base + j * NB + 8 * h : base + j * NB + 8 * h + 8] for h in (0, 1)]
        for j in range(NB)
    ]
    rows = [lax.broadcasted_iota(jnp.int32, (8, width), 0) + 8 * h for h in (0, 1)]
    lanes = lax.broadcasted_iota(jnp.int32, (8, width), 1) % NB
    inv_re = [jnp.where(rows[h] == lanes, 1.0, 0.0) for h in (0, 1)]
    inv_im = [jnp.zeros((8, width), jnp.float32) for h in (0, 1)]
    low_re = [jnp.zeros((8, width), jnp.float32) for h in (0, 1)]
    low_im = [jnp.zeros((8, width), jnp.float32) for h in (0, 1)]

    def pick(halves, i):
        return jnp.broadcast_to(halves[i // 8][i % 8 : i % 8 + 1, :], (8, width))

    for p in range(NB):
        pivot = pick(col_re[p], p) + epsilon
        scale = inv_sqrt(pivot)
        coef_re, coef_im = [None, None], [None, None]
        for h in range(p // 8, 2):
            below = rows[h] > p
            coef_re[h] = jnp.where(below, col_re[p][h] * scale, 0.0)
            coef_im[h] = jnp.where(below, col_im[p][h] * scale, 0.0)
            here = lanes == p
            diag = jnp.where(rows[h] == p, pivot * scale, coef_re[h])
            low_re[h] = jnp.where(here, diag, low_re[h])
            low_im[h] = jnp.where(here, coef_im[h], low_im[h])
        for j in range(p + 1, NB):
            a_re, a_im = pick(coef_re, j), pick(coef_im, j)
            for h in range(j // 8, 2):
                col_re[j][h] = col_re[j][h] - (coef_re[h] * a_re + coef_im[h] * a_im)
                col_im[j][h] = col_im[j][h] - (coef_im[h] * a_re - coef_re[h] * a_im)
        line_re = pick(inv_re, p) * scale
        line_im = pick(inv_im, p) * scale
        for h in range(p // 8, 2):
            at = rows[h] == p
            new_re = inv_re[h] - (coef_re[h] * line_re - coef_im[h] * line_im)
            new_im = inv_im[h] - (coef_re[h] * line_im + coef_im[h] * line_re)
            inv_re[h] = jnp.where(at, line_re, new_re)
            inv_im[h] = jnp.where(at, line_im, new_im)

    block_re = jnp.where(same, jnp.concatenate(inv_re * local, axis=0), 0.0)
    block_im = jnp.where(same, jnp.concatenate(inv_im * local, axis=0), 0.0)
    mixing = jnp.concatenate(
        [
            jnp.concatenate([block_re, block_im], axis=1),
            jnp.concatenate([-block_im, block_re], axis=1),
        ],
        axis=0,
    )
    me = lax.axis_index("freq")
    for k, ref in ((0, own_ref), (1, other_ref)):
        start = pl.multiple_of(((me + k) % 2) * share, 128)
        out = dot(mixing, ref[...].reshape(2 * width, share))
        for part in range(2):
            for f in range(local):
                at = part * width + f * NB
                modes_ref[f, part, :, pl.ds(start, share)] = out[at : at + NB]
    pad = jnp.zeros((width - NB, width), jnp.float32)
    turned_re = jnp.transpose(jnp.concatenate(low_re + [pad], axis=0))
    turned_im = jnp.transpose(jnp.concatenate(low_im + [pad], axis=0))
    for f in range(local):
        factor_ref[0, f] = turned_re[f * NB : (f + 1) * NB, :NB]
        factor_ref[1, f] = -turned_im[f * NB : (f + 1) * NB, :NB]


def finish(grams, own, other, local, total):
    share = own.shape[3]
    return pl.pallas_call(
        functools.partial(finish_kernel, local, total),
        out_shape=(
            jax.ShapeDtypeStruct((local, 2, NB, 2 * share), jnp.float32),
            jax.ShapeDtypeStruct((2, local, NB, NB), jnp.float32),
        ),
        compiler_params=pltpu.CompilerParams(vmem_limit_bytes=VMEM_BYTES),
    )(grams, own, other)


def on_device(snapshots, weights):
    n = lax.axis_size("space")
    tm_count = lax.axis_size("tm")
    freq_count = lax.axis_size("freq")
    local = NF // freq_count
    blocks, local_times, columns = snapshots.shape
    rows = columns // n
    share = rows // freq_count
    me = lax.axis_index("freq")

    tables = jnp.asarray(dft_blocks(freq_count))
    tables = jnp.where(me == 0, tables, tables[::-1])
    own_weights = lax.dynamic_index_in_dim(weights.reshape(freq_count, 1, share), me, 0, False)

    sent = cut(snapshots, n, rows, share)
    pieces = lax.all_to_all(sent, "space", split_axis=0, concat_axis=0, tiled=True)
    if local_times != STEP:
        pieces = pieces.transpose(1, 0, 2, 3).reshape(blocks, SEGMENT_FRAMES // STEP, STEP, share)
        pieces = pieces.transpose(1, 0, 2, 3)

    targets = n * tm_count * freq_count
    own, other, gram = spectra_and_gram(pieces, tables, own_weights, local, targets, freq_count)
    swap = [(i, freq_count - 1 - i) for i in range(freq_count)]
    other = lax.ppermute(other, "freq", swap)
    grams = lax.all_to_all(gram, ("space", "tm", "freq"), split_axis=0, concat_axis=0, tiled=True)
    total = rows * n * tm_count
    return finish(grams, own, other, local, total)


def solution(mesh):
    return jax.shard_map(
        on_device,
        mesh=mesh,
        in_specs=(P(None, "space", ("groups", "tm")), P(("groups", "tm", "space"))),
        out_specs=(
            P("freq", None, None, ("groups", "tm", "space")),
            P("groups", "freq", None, None),
        ),
        check_vma=False,
    )
```

```python
import functools

import numpy as np
import jax
import jax.numpy as jnp
from jax import lax
from jax.experimental import pallas as pl
from jax.experimental.pallas import tpu as pltpu
from jax.sharding import PartitionSpec as P

NB = 16
SEGMENT_FRAMES = 64
NF = 16
CUTS = 4
epsilon = 1e-05
VMEM_BYTES = 48 * 1024 * 1024


def dft_blocks(groups):
    times = np.arange(SEGMENT_FRAMES)
    taper = 0.5 - 0.5 * np.cos(2.0 * np.pi * times / SEGMENT_FRAMES)
    taper = taper / np.sqrt(np.sum(taper * taper))
    bins = 1 + np.arange(NF)
    angles = 2.0 * np.pi * (bins[:, None] * times[None, :] % SEGMENT_FRAMES) / SEGMENT_FRAMES
    table = np.stack([np.cos(angles) * taper, -np.sin(angles) * taper])
    step = SEGMENT_FRAMES // groups
    table = table.reshape(2, 2, NF // 2, groups, step)
    spread = np.einsum("rhfgt,bc->ghrfbct", table, np.eye(NB))
    return spread.reshape(groups, 2 * NF * NB, NB * step).astype(np.float32)


def dot(a, b):
    return jnp.dot(a, b, precision=lax.Precision.HIGHEST, preferred_element_type=jnp.float32)


def cut_kernel(n, k, rows, share, x_ref, o_ref, sem):
    to = lax.rem(lax.axis_index("space") + k, n)
    start = pl.multiple_of(to * rows + lax.axis_index("freq") * share, 128)
    part = NB // CUTS
    copies = []
    for i in range(CUTS):
        blocks = pl.ds(i * part, part)
        copies.append(
            pltpu.make_async_copy(
                x_ref.at[blocks, :, pl.ds(start, share)], o_ref.at[blocks], sem.at[i]
            )
        )
    for copy in copies:
        copy.start()
    for copy in copies:
        copy.wait()


def cut(snapshots, n, k, rows, share):
    blocks, local_times, _ = snapshots.shape
    if local_times % 8 == 0:
        piece = pl.pallas_call(
            functools.partial(cut_kernel, n, k, rows, share),
            out_shape=jax.ShapeDtypeStruct((blocks, local_times, share), jnp.float32),
            in_specs=[pl.BlockSpec(memory_space=pl.ANY)],
            out_specs=pl.BlockSpec(memory_space=pltpu.VMEM),
            scratch_shapes=[pltpu.SemaphoreType.DMA((CUTS,))],
        )(snapshots)
    else:
        to = lax.rem(lax.axis_index("space") + k, n)
        start = to * rows + lax.axis_index("freq") * share
        piece = lax.dynamic_slice_in_dim(snapshots, start, share, axis=2)
    return piece.reshape(blocks * local_times, share)


def early_kernel(n, offsets, t_ref, *refs):
    out_ref = refs[-1]
    me = lax.axis_index("space")
    total = None
    for k, ref in zip(offsets, refs):
        part = dot(t_ref[lax.rem(me - k + n, n)], ref[...])
        total = part if total is None else total + part
    out_ref[...] = total


def early(tables, n, offsets, pieces):
    share = pieces[0].shape[1]
    return pl.pallas_call(
        functools.partial(early_kernel, n, offsets),
        out_shape=jax.ShapeDtypeStruct((tables.shape[1], share), jnp.float32),
        compiler_params=pltpu.CompilerParams(vmem_limit_bytes=VMEM_BYTES),
    )(tables, *pieces)


def late_kernel(n, k, targets, t_ref, sum_ref, x_ref, w_ref, own_ref, other_ref, gram_ref):
    src = lax.rem(lax.axis_index("space") - k + n, n)
    spectra = sum_ref[...] + dot(t_ref[src], x_ref[...])
    half = spectra.shape[0] // 2
    width = half // 2
    local = width // NB
    line = lax.broadcasted_iota(jnp.int32, (width, width), 0) // NB
    lane = lax.broadcasted_iota(jnp.int32, (width, width), 1) // NB
    row = lax.broadcasted_iota(jnp.int32, (NB, width), 0)
    col = lax.broadcasted_iota(jnp.int32, (NB, width), 1) % NB
    first = lax.axis_index("freq") == 0
    halves = [spectra[:half], spectra[half:]]
    own_ref[...] = jnp.where(first, halves[0], halves[1])
    other_ref[...] = jnp.where(first, halves[1], halves[0])
    packed = []
    for z in halves:
        full = lax.dot_general(
            z * w_ref[...],
            z,
            (((1,), (1,)), ((), ())),
            precision=lax.Precision.HIGHEST,
            preferred_element_type=jnp.float32,
        )
        gram_re = full[:width, :width] + full[width:, width:]
        gram_im = full[:width, width:] - full[width:, :width]
        both = []
        for part in (gram_re, gram_im):
            kept = jnp.where(line == lane, part, 0.0)
            both.append(jnp.sum(kept.reshape(local, NB, width), axis=0))
        packed.append(jnp.where(row >= col, both[0], both[1]))
    for d in range(targets):
        gram_ref[d] = packed[d % 2]


def late(tables, n, k, partial_sum, piece, weights, targets):
    share = piece.shape[1]
    half = tables.shape[1] // 2
    shape = jax.ShapeDtypeStruct((half, share), jnp.float32)
    return pl.pallas_call(
        functools.partial(late_kernel, n, k, targets),
        out_shape=(
            shape,
            shape,
            jax.ShapeDtypeStruct((targets, NB, half // 2), jnp.float32),
        ),
        compiler_params=pltpu.CompilerParams(vmem_limit_bytes=VMEM_BYTES),
    )(tables, partial_sum, piece, weights)


def inv_sqrt(x):
    y = lax.rsqrt(x)
    return y * (1.5 - 0.5 * x * (y * y))


def finish_kernel(local, total, gram_ref, own_ref, other_ref, modes_ref, factor_ref):
    width = local * NB
    share = own_ref.shape[1]
    gram = jnp.sum(gram_ref[...], axis=0) / total
    row = lax.broadcasted_iota(jnp.int32, (NB, width), 0)
    col = lax.broadcasted_iota(jnp.int32, (NB, width), 1) % NB
    stacked = [jnp.where(col == j, gram, 0.0) for j in range(NB)]
    for j in range(NB):
        line = jnp.broadcast_to(gram[j : j + 1, :], (NB, width))
        stacked.append(jnp.where((col == row) & (row > j), -line, 0.0))
    stacked = jnp.concatenate(stacked, axis=0)
    group_r = lax.broadcasted_iota(jnp.int32, (width, width), 0) // NB
    group_c = lax.broadcasted_iota(jnp.int32, (width, width), 1) // NB
    same = group_r == group_c
    ones = jnp.where(same, 1.0, 0.0).astype(jnp.bfloat16)
    spread = jnp.zeros(stacked.shape, jnp.float32)
    rest = stacked
    for _ in range(3):
        piece = rest.astype(jnp.bfloat16)
        rest = rest - piece.astype(jnp.float32)
        spread = spread + jnp.dot(piece, ones, preferred_element_type=jnp.float32)
    col_re = [[spread[j * NB + 8 * h : j * NB + 8 * h + 8] for h in (0, 1)] for j in range(NB)]
    base = NB * NB
    col_im = [
        [spread[base + j * NB + 8 * h : base + j * NB + 8 * h + 8] for h in (0, 1)]
        for j in range(NB)
    ]
    rows = [lax.broadcasted_iota(jnp.int32, (8, width), 0) + 8 * h for h in (0, 1)]
    lanes = lax.broadcasted_iota(jnp.int32, (8, width), 1) % NB
    inv_re = [jnp.where(rows[h] == lanes, 1.0, 0.0) for h in (0, 1)]
    inv_im = [jnp.zeros((8, width), jnp.float32) for h in (0, 1)]
    low_re = [jnp.zeros((8, width), jnp.float32) for h in (0, 1)]
    low_im = [jnp.zeros((8, width), jnp.float32) for h in (0, 1)]

    def pick(halves, i):
        return jnp.broadcast_to(halves[i // 8][i % 8 : i % 8 + 1, :], (8, width))

    for p in range(NB):
        pivot = pick(col_re[p], p) + epsilon
        scale = inv_sqrt(pivot)
        coef_re, coef_im = [None, None], [None, None]
        for h in range(p // 8, 2):
            below = rows[h] > p
            coef_re[h] = jnp.where(below, col_re[p][h] * scale, 0.0)
            coef_im[h] = jnp.where(below, col_im[p][h] * scale, 0.0)
            here = lanes == p
            diag = jnp.where(rows[h] == p, pivot * scale, coef_re[h])
            low_re[h] = jnp.where(here, diag, low_re[h])
            low_im[h] = jnp.where(here, coef_im[h], low_im[h])
        for j in range(p + 1, NB):
            a_re, a_im = pick(coef_re, j), pick(coef_im, j)
            for h in range(j // 8, 2):
                col_re[j][h] = col_re[j][h] - (coef_re[h] * a_re + coef_im[h] * a_im)
                col_im[j][h] = col_im[j][h] - (coef_im[h] * a_re - coef_re[h] * a_im)
        line_re = pick(inv_re, p) * scale
        line_im = pick(inv_im, p) * scale
        for h in range(p // 8, 2):
            at = rows[h] == p
            new_re = inv_re[h] - (coef_re[h] * line_re - coef_im[h] * line_im)
            new_im = inv_im[h] - (coef_re[h] * line_im + coef_im[h] * line_re)
            inv_re[h] = jnp.where(at, line_re, new_re)
            inv_im[h] = jnp.where(at, line_im, new_im)

    block_re = jnp.where(same, jnp.concatenate(inv_re * local, axis=0), 0.0)
    block_im = jnp.where(same, jnp.concatenate(inv_im * local, axis=0), 0.0)
    mixing = jnp.concatenate(
        [
            jnp.concatenate([block_re, block_im], axis=1),
            jnp.concatenate([-block_im, block_re], axis=1),
        ],
        axis=0,
    )
    me = lax.axis_index("freq")
    for k, ref in ((0, own_ref), (1, other_ref)):
        start = pl.multiple_of(((me + k) % 2) * share, 128)
        out = dot(mixing, ref[...])
        for part in range(2):
            for f in range(local):
                at = part * width + f * NB
                modes_ref[f, part, :, pl.ds(start, share)] = out[at : at + NB]
    pad = jnp.zeros((width - NB, width), jnp.float32)
    turned_re = jnp.transpose(jnp.concatenate(low_re + [pad], axis=0))
    turned_im = jnp.transpose(jnp.concatenate(low_im + [pad], axis=0))
    for f in range(local):
        factor_ref[0, f] = turned_re[f * NB : (f + 1) * NB, :NB]
        factor_ref[1, f] = -turned_im[f * NB : (f + 1) * NB, :NB]


def finish(grams, own, other, local, total):
    share = own.shape[1]
    return pl.pallas_call(
        functools.partial(finish_kernel, local, total),
        out_shape=(
            jax.ShapeDtypeStruct((local, 2, NB, 2 * share), jnp.float32),
            jax.ShapeDtypeStruct((2, local, NB, NB), jnp.float32),
        ),
        compiler_params=pltpu.CompilerParams(vmem_limit_bytes=VMEM_BYTES),
    )(grams, own, other)


def on_device(snapshots, weights):
    n = lax.axis_size("space")
    tm_count = lax.axis_size("tm")
    freq_count = lax.axis_size("freq")
    local = NF // freq_count
    blocks, local_times, columns = snapshots.shape
    rows = columns // n
    share = rows // freq_count
    me = lax.axis_index("freq")

    tables = jnp.asarray(dft_blocks(n))
    own_weights = lax.dynamic_index_in_dim(weights.reshape(freq_count, 1, share), me, 0, False)

    order = [n // 2] + [k for k in range(1, n) if k != n // 2]
    pieces = []
    for k in order:
        sent = cut(snapshots, n, k, rows, share)
        pieces.append(lax.ppermute(sent, "space", [(i, (i + k) % n) for i in range(n)]))
    pieces = [cut(snapshots, n, 0, rows, share)] + pieces
    order = [0] + order

    targets = n * tm_count * freq_count
    before = early(tables, n, order[:-1], pieces[:-1])
    own, other, gram = late(tables, n, order[-1], before, pieces[-1], own_weights, targets)
    other = lax.ppermute(other, "freq", [(0, 1), (1, 0)])
    grams = lax.all_to_all(gram, ("space", "tm", "freq"), split_axis=0, concat_axis=0, tiled=True)
    total = rows * n * tm_count
    return finish(grams, own, other, local, total)


def solution(mesh):
    return jax.shard_map(
        on_device,
        mesh=mesh,
        in_specs=(P(None, "space", ("groups", "tm")), P(("groups", "tm", "space"))),
        out_specs=(
            P("freq", None, None, ("groups", "tm", "space")),
            P("groups", "freq", None, None),
        ),
        check_vma=False,
    )
```

```python
import functools

import numpy as np
import jax
import jax.numpy as jnp
from jax import lax
from jax.experimental import pallas as pl
from jax.experimental.pallas import tpu as pltpu
from jax.sharding import PartitionSpec as P

NB = 16
SEGMENT_FRAMES = 64
NF = 16
CUTS = 16
epsilon = 1e-05
VMEM_BYTES = 48 * 1024 * 1024


def dft_blocks(groups):
    times = np.arange(SEGMENT_FRAMES)
    taper = 0.5 - 0.5 * np.cos(2.0 * np.pi * times / SEGMENT_FRAMES)
    taper = taper / np.sqrt(np.sum(taper * taper))
    bins = 1 + np.arange(NF)
    angles = 2.0 * np.pi * (bins[:, None] * times[None, :] % SEGMENT_FRAMES) / SEGMENT_FRAMES
    table = np.stack([np.cos(angles) * taper, -np.sin(angles) * taper])
    step = SEGMENT_FRAMES // groups
    table = table.reshape(2, 2, NF // 2, groups, step)
    spread = np.einsum("rhfgt,bc->ghrfbct", table, np.eye(NB))
    return spread.reshape(groups, 2 * NF * NB, NB * step).astype(np.float32)


def dot(a, b):
    return jnp.dot(a, b, precision=lax.Precision.HIGHEST, preferred_element_type=jnp.float32)


def cut_kernel(n, k, rows, share, x_ref, o_ref, sem):
    to = lax.rem(lax.axis_index("space") + k, n)
    start = pl.multiple_of(to * rows + lax.axis_index("freq") * share, 128)
    part = NB // CUTS
    copies = []
    for i in range(CUTS):
        blocks = pl.ds(i * part, part)
        copies.append(
            pltpu.make_async_copy(
                x_ref.at[blocks, :, pl.ds(start, share)], o_ref.at[blocks], sem.at[i]
            )
        )
    for copy in copies:
        copy.start()
    for copy in copies:
        copy.wait()


def cut(snapshots, n, k, rows, share):
    blocks, local_times, _ = snapshots.shape
    if local_times % 8 == 0:
        piece = pl.pallas_call(
            functools.partial(cut_kernel, n, k, rows, share),
            out_shape=jax.ShapeDtypeStruct((blocks, local_times, share), jnp.float32),
            in_specs=[pl.BlockSpec(memory_space=pl.ANY)],
            out_specs=pl.BlockSpec(memory_space=pltpu.VMEM),
            scratch_shapes=[pltpu.SemaphoreType.DMA((CUTS,))],
        )(snapshots)
    else:
        to = lax.rem(lax.axis_index("space") + k, n)
        start = to * rows + lax.axis_index("freq") * share
        piece = lax.dynamic_slice_in_dim(snapshots, start, share, axis=2)
    return piece.reshape(blocks * local_times, share)


def early_kernel(n, k, t_ref, x_ref, *refs):
    src = lax.rem(lax.axis_index("space") - k + n, n)
    part = dot(t_ref[src], x_ref[...])
    refs[-1][...] = part if len(refs) == 1 else refs[0][...] + part


def early(tables, n, k, piece, *before):
    share = piece.shape[1]
    return pl.pallas_call(
        functools.partial(early_kernel, n, k),
        out_shape=jax.ShapeDtypeStruct((tables.shape[1], share), jnp.float32),
        compiler_params=pltpu.CompilerParams(vmem_limit_bytes=VMEM_BYTES),
    )(tables, piece, *before)


def late_kernel(n, k, targets, t_ref, sum_ref, x_ref, w_ref, own_ref, other_ref, gram_ref):
    src = lax.rem(lax.axis_index("space") - k + n, n)
    spectra = sum_ref[...] + dot(t_ref[src], x_ref[...])
    half = spectra.shape[0] // 2
    width = half // 2
    local = width // NB
    line = lax.broadcasted_iota(jnp.int32, (width, width), 0) // NB
    lane = lax.broadcasted_iota(jnp.int32, (width, width), 1) // NB
    row = lax.broadcasted_iota(jnp.int32, (NB, width), 0)
    col = lax.broadcasted_iota(jnp.int32, (NB, width), 1) % NB
    first = lax.axis_index("freq") == 0
    halves = [spectra[:half], spectra[half:]]
    own_ref[...] = jnp.where(first, halves[0], halves[1])
    other_ref[...] = jnp.where(first, halves[1], halves[0])
    packed = []
    for z in halves:
        full = lax.dot_general(
            z * w_ref[...],
            z,
            (((1,), (1,)), ((), ())),
            precision=lax.Precision.HIGHEST,
            preferred_element_type=jnp.float32,
        )
        gram_re = full[:width, :width] + full[width:, width:]
        gram_im = full[:width, width:] - full[width:, :width]
        both = []
        for part in (gram_re, gram_im):
            kept = jnp.where(line == lane, part, 0.0)
            both.append(jnp.sum(kept.reshape(local, NB, width), axis=0))
        packed.append(jnp.where(row >= col, both[0], both[1]))
    for d in range(targets):
        gram_ref[d] = packed[d % 2]


def late(tables, n, k, partial_sum, piece, weights, targets):
    share = piece.shape[1]
    half = tables.shape[1] // 2
    shape = jax.ShapeDtypeStruct((half, share), jnp.float32)
    return pl.pallas_call(
        functools.partial(late_kernel, n, k, targets),
        out_shape=(
            shape,
            shape,
            jax.ShapeDtypeStruct((targets, NB, half // 2), jnp.float32),
        ),
        compiler_params=pltpu.CompilerParams(vmem_limit_bytes=VMEM_BYTES),
    )(tables, partial_sum, piece, weights)


def share_kernel(gram_ref, out_ref):
    total = jnp.sum(gram_ref[...], axis=0)
    for d in range(out_ref.shape[0]):
        out_ref[d] = total


def add_and_repeat(grams, times):
    return pl.pallas_call(
        share_kernel,
        out_shape=jax.ShapeDtypeStruct((times,) + grams.shape[1:], jnp.float32),
    )(grams)


def inv_sqrt(x):
    y = lax.rsqrt(x)
    return y * (1.5 - 0.5 * x * (y * y))


def finish_kernel(local, total, gram_ref, own_ref, other_ref, modes_ref, factor_ref):
    width = local * NB
    share = own_ref.shape[1]
    gram = jnp.sum(gram_ref[...], axis=0) / total
    row = lax.broadcasted_iota(jnp.int32, (NB, width), 0)
    col = lax.broadcasted_iota(jnp.int32, (NB, width), 1) % NB
    stacked = [jnp.where(col == j, gram, 0.0) for j in range(NB)]
    for j in range(NB):
        line = jnp.broadcast_to(gram[j : j + 1, :], (NB, width))
        stacked.append(jnp.where((col == row) & (row > j), -line, 0.0))
    stacked = jnp.concatenate(stacked, axis=0)
    group_r = lax.broadcasted_iota(jnp.int32, (width, width), 0) // NB
    group_c = lax.broadcasted_iota(jnp.int32, (width, width), 1) // NB
    same = group_r == group_c
    ones = jnp.where(same, 1.0, 0.0).astype(jnp.bfloat16)
    spread = jnp.zeros(stacked.shape, jnp.float32)
    rest = stacked
    for _ in range(3):
        piece = rest.astype(jnp.bfloat16)
        rest = rest - piece.astype(jnp.float32)
        spread = spread + jnp.dot(piece, ones, preferred_element_type=jnp.float32)
    col_re = [[spread[j * NB + 8 * h : j * NB + 8 * h + 8] for h in (0, 1)] for j in range(NB)]
    base = NB * NB
    col_im = [
        [spread[base + j * NB + 8 * h : base + j * NB + 8 * h + 8] for h in (0, 1)]
        for j in range(NB)
    ]
    rows = [lax.broadcasted_iota(jnp.int32, (8, width), 0) + 8 * h for h in (0, 1)]
    lanes = lax.broadcasted_iota(jnp.int32, (8, width), 1) % NB
    inv_re = [jnp.where(rows[h] == lanes, 1.0, 0.0) for h in (0, 1)]
    inv_im = [jnp.zeros((8, width), jnp.float32) for h in (0, 1)]
    low_re = [jnp.zeros((8, width), jnp.float32) for h in (0, 1)]
    low_im = [jnp.zeros((8, width), jnp.float32) for h in (0, 1)]

    def pick(halves, i):
        return jnp.broadcast_to(halves[i // 8][i % 8 : i % 8 + 1, :], (8, width))

    for p in range(NB):
        pivot = pick(col_re[p], p) + epsilon
        scale = inv_sqrt(pivot)
        coef_re, coef_im = [None, None], [None, None]
        for h in range(p // 8, 2):
            below = rows[h] > p
            coef_re[h] = jnp.where(below, col_re[p][h] * scale, 0.0)
            coef_im[h] = jnp.where(below, col_im[p][h] * scale, 0.0)
            here = lanes == p
            diag = jnp.where(rows[h] == p, pivot * scale, coef_re[h])
            low_re[h] = jnp.where(here, diag, low_re[h])
            low_im[h] = jnp.where(here, coef_im[h], low_im[h])
        for j in range(p + 1, NB):
            a_re, a_im = pick(coef_re, j), pick(coef_im, j)
            for h in range(j // 8, 2):
                col_re[j][h] = col_re[j][h] - (coef_re[h] * a_re + coef_im[h] * a_im)
                col_im[j][h] = col_im[j][h] - (coef_im[h] * a_re - coef_re[h] * a_im)
        line_re = pick(inv_re, p) * scale
        line_im = pick(inv_im, p) * scale
        for h in range(p // 8, 2):
            at = rows[h] == p
            new_re = inv_re[h] - (coef_re[h] * line_re - coef_im[h] * line_im)
            new_im = inv_im[h] - (coef_re[h] * line_im + coef_im[h] * line_re)
            inv_re[h] = jnp.where(at, line_re, new_re)
            inv_im[h] = jnp.where(at, line_im, new_im)

    block_re = jnp.where(same, jnp.concatenate(inv_re * local, axis=0), 0.0)
    block_im = jnp.where(same, jnp.concatenate(inv_im * local, axis=0), 0.0)
    mixing = jnp.concatenate(
        [
            jnp.concatenate([block_re, block_im], axis=1),
            jnp.concatenate([-block_im, block_re], axis=1),
        ],
        axis=0,
    )
    me = lax.axis_index("freq")
    for k, ref in ((0, own_ref), (1, other_ref)):
        start = pl.multiple_of(((me + k) % 2) * share, 128)
        out = dot(mixing, ref[...])
        for part in range(2):
            for f in range(local):
                at = part * width + f * NB
                modes_ref[f, part, :, pl.ds(start, share)] = out[at : at + NB]
    pad = jnp.zeros((width - NB, width), jnp.float32)
    turned_re = jnp.transpose(jnp.concatenate(low_re + [pad], axis=0))
    turned_im = jnp.transpose(jnp.concatenate(low_im + [pad], axis=0))
    for f in range(local):
        factor_ref[0, f] = turned_re[f * NB : (f + 1) * NB, :NB]
        factor_ref[1, f] = -turned_im[f * NB : (f + 1) * NB, :NB]


def finish(grams, own, other, local, total):
    share = own.shape[1]
    return pl.pallas_call(
        functools.partial(finish_kernel, local, total),
        out_shape=(
            jax.ShapeDtypeStruct((local, 2, NB, 2 * share), jnp.float32),
            jax.ShapeDtypeStruct((2, local, NB, NB), jnp.float32),
        ),
        compiler_params=pltpu.CompilerParams(vmem_limit_bytes=VMEM_BYTES),
    )(grams, own, other)


def on_device(snapshots, weights):
    n = lax.axis_size("space")
    tm_count = lax.axis_size("tm")
    freq_count = lax.axis_size("freq")
    local = NF // freq_count
    blocks, local_times, columns = snapshots.shape
    rows = columns // n
    share = rows // freq_count
    me = lax.axis_index("freq")

    tables = jnp.asarray(dft_blocks(n))
    own_weights = lax.dynamic_index_in_dim(weights.reshape(freq_count, 1, share), me, 0, False)

    offsets = [n // 2] + [k for k in range(1, n) if k != n // 2]
    pieces = {}
    for k in offsets:
        sent = cut(snapshots, n, k, rows, share)
        pieces[k] = lax.ppermute(sent, "space", [(i, (i + k) % n) for i in range(n)])
    pieces[0] = cut(snapshots, n, 0, rows, share)

    before = early(tables, n, 0, pieces[0])
    for k in [n // 2] + [k for k in range(n - 1, 1, -1) if k != n // 2]:
        before = early(tables, n, k, pieces[k], before)
    targets = tm_count * freq_count
    own, other, gram = late(tables, n, 1, before, pieces[1], own_weights, targets)
    other = lax.ppermute(other, "freq", [(0, 1), (1, 0)])
    grams = lax.all_to_all(gram, ("tm", "freq"), split_axis=0, concat_axis=0, tiled=True)
    grams = add_and_repeat(grams, n)
    grams = lax.all_to_all(grams, "space", split_axis=0, concat_axis=0, tiled=True)
    total = rows * n * tm_count
    return finish(grams, own, other, local, total)


def solution(mesh):
    return jax.shard_map(
        on_device,
        mesh=mesh,
        in_specs=(P(None, "space", ("groups", "tm")), P(("groups", "tm", "space"))),
        out_specs=(
            P("freq", None, None, ("groups", "tm", "space")),
            P("groups", "freq", None, None),
        ),
        check_vma=False,
    )
```

```python
import functools

import numpy as np
import jax
import jax.numpy as jnp
from jax import lax
from jax.experimental import pallas as pl
from jax.experimental.pallas import tpu as pltpu
from jax.sharding import PartitionSpec as P

NB = 16
SEGMENT_FRAMES = 64
NF = 16
CUTS = 16
epsilon = 1e-05
MIB = 1024 * 1024


def dft_blocks(groups):
    times = np.arange(SEGMENT_FRAMES)
    taper = 0.5 - 0.5 * np.cos(2.0 * np.pi * times / SEGMENT_FRAMES)
    taper = taper / np.sqrt(np.sum(taper * taper))
    bins = 1 + np.arange(NF)
    angles = 2.0 * np.pi * (bins[:, None] * times[None, :] % SEGMENT_FRAMES) / SEGMENT_FRAMES
    table = np.stack([np.cos(angles) * taper, -np.sin(angles) * taper])
    step = SEGMENT_FRAMES // groups
    table = table.reshape(2, 2, NF // 2, groups, step)
    spread = np.einsum("rhfgt,bc->ghrfbct", table, np.eye(NB))
    return spread.reshape(groups, 2 * NF * NB, NB * step).astype(np.float32)


def dot(a, b):
    return jnp.dot(a, b, precision=lax.Precision.HIGHEST, preferred_element_type=jnp.float32)


def cut_kernel(n, k, rows, share, x_ref, o_ref, sem):
    to = lax.rem(lax.axis_index("space") + k, n)
    start = pl.multiple_of(to * rows + lax.axis_index("freq") * share, 128)
    part = NB // CUTS
    copies = []
    for i in range(CUTS):
        blocks = pl.ds(i * part, part)
        copies.append(
            pltpu.make_async_copy(
                x_ref.at[blocks, :, pl.ds(start, share)], o_ref.at[blocks], sem.at[i]
            )
        )
    for copy in copies:
        copy.start()
    for copy in copies:
        copy.wait()


def cut(snapshots, n, k, rows, share):
    blocks, local_times, _ = snapshots.shape
    if local_times % 8 == 0:
        piece = pl.pallas_call(
            functools.partial(cut_kernel, n, k, rows, share),
            out_shape=jax.ShapeDtypeStruct((blocks, local_times, share), jnp.float32),
            in_specs=[pl.BlockSpec(memory_space=pltpu.HBM)],
            out_specs=pl.BlockSpec(memory_space=pltpu.VMEM),
            scratch_shapes=[pltpu.SemaphoreType.DMA((CUTS,))],
            compiler_params=pltpu.CompilerParams(vmem_limit_bytes=4 * MIB),
        )(snapshots)
    else:
        to = lax.rem(lax.axis_index("space") + k, n)
        start = to * rows + lax.axis_index("freq") * share
        piece = lax.dynamic_slice_in_dim(snapshots, start, share, axis=2)
    return piece.reshape(blocks * local_times, share)


def early_kernel(n, k, t_ref, x_ref, *refs):
    src = lax.rem(lax.axis_index("space") - k + n, n)
    part = dot(t_ref[src], x_ref[...])
    refs[-1][...] = part if len(refs) == 1 else refs[0][...] + part


def early(tables, n, k, piece, *before):
    share = piece.shape[1]
    return pl.pallas_call(
        functools.partial(early_kernel, n, k),
        out_shape=jax.ShapeDtypeStruct((tables.shape[1], share), jnp.float32),
        compiler_params=pltpu.CompilerParams(vmem_limit_bytes=16 * MIB),
    )(tables, piece, *before)


def late_kernel(n, k, t_ref, sum_ref, x_ref, w_ref, own_ref, other_ref, gram_ref, lent_ref):
    src = lax.rem(lax.axis_index("space") - k + n, n)
    spectra = sum_ref[...] + dot(t_ref[src], x_ref[...])
    half = spectra.shape[0] // 2
    width = half // 2
    local = width // NB
    line = lax.broadcasted_iota(jnp.int32, (width, width), 0) // NB
    lane = lax.broadcasted_iota(jnp.int32, (width, width), 1) // NB
    row = lax.broadcasted_iota(jnp.int32, (NB, width), 0)
    col = lax.broadcasted_iota(jnp.int32, (NB, width), 1) % NB
    first = lax.axis_index("freq") == 0
    halves = [spectra[:half], spectra[half:]]
    own_ref[...] = jnp.where(first, halves[0], halves[1])
    other_ref[...] = jnp.where(first, halves[1], halves[0])
    packed = []
    for z in halves:
        full = lax.dot_general(
            z * w_ref[...],
            z,
            (((1,), (1,)), ((), ())),
            precision=lax.Precision.HIGHEST,
            preferred_element_type=jnp.float32,
        )
        gram_re = full[:width, :width] + full[width:, width:]
        gram_im = full[:width, width:] - full[width:, :width]
        both = []
        for part in (gram_re, gram_im):
            kept = jnp.where(line == lane, part, 0.0)
            both.append(jnp.sum(kept.reshape(local, NB, width), axis=0))
        packed.append(jnp.where(row >= col, both[0], both[1]))
    gram_ref[...] = jnp.where(first, packed[0], packed[1])
    lent_ref[...] = jnp.where(first, packed[1], packed[0])


def late(tables, n, k, partial_sum, piece, weights):
    share = piece.shape[1]
    half = tables.shape[1] // 2
    shape = jax.ShapeDtypeStruct((half, share), jnp.float32)
    gram_shape = jax.ShapeDtypeStruct((NB, half // 2), jnp.float32)
    return pl.pallas_call(
        functools.partial(late_kernel, n, k),
        out_shape=(shape, shape, gram_shape, gram_shape),
        compiler_params=pltpu.CompilerParams(vmem_limit_bytes=16 * MIB),
    )(tables, partial_sum, piece, weights)


def inv_sqrt(x):
    y = lax.rsqrt(x)
    return y * (1.5 - 0.5 * x * (y * y))


def finish_kernel(local, total, own_ref, other_ref, *refs):
    gram_refs, (modes_ref, factor_ref) = refs[:-2], refs[-2:]
    width = local * NB
    share = own_ref.shape[1]
    gram = sum(ref[...] for ref in gram_refs) / total
    row = lax.broadcasted_iota(jnp.int32, (NB, width), 0)
    col = lax.broadcasted_iota(jnp.int32, (NB, width), 1) % NB
    stacked = [jnp.where(col == j, gram, 0.0) for j in range(NB)]
    for j in range(NB):
        line = jnp.broadcast_to(gram[j : j + 1, :], (NB, width))
        stacked.append(jnp.where((col == row) & (row > j), -line, 0.0))
    stacked = jnp.concatenate(stacked, axis=0)
    group_r = lax.broadcasted_iota(jnp.int32, (width, width), 0) // NB
    group_c = lax.broadcasted_iota(jnp.int32, (width, width), 1) // NB
    same = group_r == group_c
    ones = jnp.where(same, 1.0, 0.0).astype(jnp.bfloat16)
    spread = jnp.zeros(stacked.shape, jnp.float32)
    rest = stacked
    for _ in range(3):
        piece = rest.astype(jnp.bfloat16)
        rest = rest - piece.astype(jnp.float32)
        spread = spread + jnp.dot(piece, ones, preferred_element_type=jnp.float32)
    col_re = [[spread[j * NB + 8 * h : j * NB + 8 * h + 8] for h in (0, 1)] for j in range(NB)]
    base = NB * NB
    col_im = [
        [spread[base + j * NB + 8 * h : base + j * NB + 8 * h + 8] for h in (0, 1)]
        for j in range(NB)
    ]
    rows = [lax.broadcasted_iota(jnp.int32, (8, width), 0) + 8 * h for h in (0, 1)]
    lanes = lax.broadcasted_iota(jnp.int32, (8, width), 1) % NB
    inv_re = [jnp.where(rows[h] == lanes, 1.0, 0.0) for h in (0, 1)]
    inv_im = [jnp.zeros((8, width), jnp.float32) for h in (0, 1)]
    low_re = [jnp.zeros((8, width), jnp.float32) for h in (0, 1)]
    low_im = [jnp.zeros((8, width), jnp.float32) for h in (0, 1)]

    def pick(halves, i):
        return jnp.broadcast_to(halves[i // 8][i % 8 : i % 8 + 1, :], (8, width))

    for p in range(NB):
        pivot = pick(col_re[p], p) + epsilon
        scale = inv_sqrt(pivot)
        coef_re, coef_im = [None, None], [None, None]
        for h in range(p // 8, 2):
            below = rows[h] > p
            coef_re[h] = jnp.where(below, col_re[p][h] * scale, 0.0)
            coef_im[h] = jnp.where(below, col_im[p][h] * scale, 0.0)
            here = lanes == p
            diag = jnp.where(rows[h] == p, pivot * scale, coef_re[h])
            low_re[h] = jnp.where(here, diag, low_re[h])
            low_im[h] = jnp.where(here, coef_im[h], low_im[h])
        for j in range(p + 1, NB):
            a_re, a_im = pick(coef_re, j), pick(coef_im, j)
            for h in range(j // 8, 2):
                col_re[j][h] = col_re[j][h] - (coef_re[h] * a_re + coef_im[h] * a_im)
                col_im[j][h] = col_im[j][h] - (coef_im[h] * a_re - coef_re[h] * a_im)
        line_re = pick(inv_re, p) * scale
        line_im = pick(inv_im, p) * scale
        for h in range(p // 8, 2):
            at = rows[h] == p
            new_re = inv_re[h] - (coef_re[h] * line_re - coef_im[h] * line_im)
            new_im = inv_im[h] - (coef_re[h] * line_im + coef_im[h] * line_re)
            inv_re[h] = jnp.where(at, line_re, new_re)
            inv_im[h] = jnp.where(at, line_im, new_im)

    block_re = jnp.where(same, jnp.concatenate(inv_re * local, axis=0), 0.0)
    block_im = jnp.where(same, jnp.concatenate(inv_im * local, axis=0), 0.0)
    mixing = jnp.concatenate(
        [
            jnp.concatenate([block_re, block_im], axis=1),
            jnp.concatenate([-block_im, block_re], axis=1),
        ],
        axis=0,
    )
    me = lax.axis_index("freq")
    for k, ref in ((0, own_ref), (1, other_ref)):
        start = pl.multiple_of(((me + k) % 2) * share, 128)
        out = dot(mixing, ref[...])
        for part in range(2):
            for f in range(local):
                at = part * width + f * NB
                modes_ref[f, part, :, pl.ds(start, share)] = out[at : at + NB]
    pad = jnp.zeros((width - NB, width), jnp.float32)
    turned_re = jnp.transpose(jnp.concatenate(low_re + [pad], axis=0))
    turned_im = jnp.transpose(jnp.concatenate(low_im + [pad], axis=0))
    for f in range(local):
        factor_ref[0, f] = turned_re[f * NB : (f + 1) * NB, :NB]
        factor_ref[1, f] = -turned_im[f * NB : (f + 1) * NB, :NB]


def finish(grams, own, other, local, total):
    share = own.shape[1]
    return pl.pallas_call(
        functools.partial(finish_kernel, local, total),
        out_shape=(
            jax.ShapeDtypeStruct((local, 2, NB, 2 * share), jnp.float32),
            jax.ShapeDtypeStruct((2, local, NB, NB), jnp.float32),
        ),
        compiler_params=pltpu.CompilerParams(vmem_limit_bytes=16 * MIB),
    )(own, other, *grams)


def copies(value, axis, size):
    return [value] + [
        lax.ppermute(value, axis, [(i, (i + k) % size) for i in range(size)])
        for k in range(1, size)
    ]


def on_device(snapshots, weights):
    n = lax.axis_size("space")
    tm_count = lax.axis_size("tm")
    freq_count = lax.axis_size("freq")
    local = NF // freq_count
    blocks, local_times, columns = snapshots.shape
    rows = columns // n
    share = rows // freq_count
    me = lax.axis_index("freq")

    tables = jnp.asarray(dft_blocks(n))
    own_weights = lax.dynamic_index_in_dim(weights.reshape(freq_count, 1, share), me, 0, False)

    offsets = [n // 2] + [k for k in range(1, n) if k != n // 2]
    pieces = {}
    for k in offsets:
        sent = cut(snapshots, n, k, rows, share)
        pieces[k] = lax.ppermute(sent, "space", [(i, (i + k) % n) for i in range(n)])
    pieces[0] = cut(snapshots, n, 0, rows, share)

    before = early(tables, n, 0, pieces[0])
    for k in [n // 2] + [k for k in range(n - 1, 1, -1) if k != n // 2]:
        before = early(tables, n, k, pieces[k], before)
    own, other, gram, lent = late(tables, n, 1, before, pieces[1], own_weights)
    swap = [(0, 1), (1, 0)]
    gram = gram + lax.ppermute(lent, "freq", swap)
    gram, other = lax.optimization_barrier((gram, other))
    other = lax.ppermute(other, "freq", swap)
    gram = sum(copies(gram, "tm", tm_count))
    grams = copies(gram, "space", n)
    total = rows * n * tm_count
    return finish(grams, own, other, local, total)


def solution(mesh):
    return jax.shard_map(
        on_device,
        mesh=mesh,
        in_specs=(P(None, "space", ("groups", "tm")), P(("groups", "tm", "space"))),
        out_specs=(
            P("freq", None, None, ("groups", "tm", "space")),
            P("groups", "freq", None, None),
        ),
        check_vma=False,
    )
```

```python
import functools

import numpy as np
import jax
import jax.numpy as jnp
from jax import lax
from jax.experimental import pallas as pl
from jax.experimental.pallas import tpu as pltpu
from jax.sharding import PartitionSpec as P

NB = 16
SEGMENT_FRAMES = 64
NF = 16
CUTS = 16
epsilon = 1e-05
MIB = 1024 * 1024


def dft_blocks(groups):
    times = np.arange(SEGMENT_FRAMES)
    taper = 0.5 - 0.5 * np.cos(2.0 * np.pi * times / SEGMENT_FRAMES)
    taper = taper / np.sqrt(np.sum(taper * taper))
    bins = 1 + np.arange(NF)
    angles = 2.0 * np.pi * (bins[:, None] * times[None, :] % SEGMENT_FRAMES) / SEGMENT_FRAMES
    table = np.stack([np.cos(angles) * taper, -np.sin(angles) * taper])
    step = SEGMENT_FRAMES // groups
    table = table.reshape(2, 2, NF // 2, groups, step)
    spread = np.einsum("rhfgt,bc->ghrfbct", table, np.eye(NB))
    return spread.reshape(groups, 2 * NF * NB, NB * step).astype(np.float32)


def dot(a, b):
    return jnp.dot(a, b, precision=lax.Precision.HIGHEST, preferred_element_type=jnp.float32)


def cut_kernel(n, k, rows, skip, x_ref, o_ref, sem):
    size = o_ref.shape[2]
    to = lax.rem(lax.axis_index("space") + k, n)
    share = rows // 2
    start = pl.multiple_of(to * rows + lax.axis_index("freq") * share + skip, 128)
    part = NB // CUTS
    copies = []
    for i in range(CUTS):
        blocks = pl.ds(i * part, part)
        copies.append(
            pltpu.make_async_copy(
                x_ref.at[blocks, :, pl.ds(start, size)], o_ref.at[blocks], sem.at[i]
            )
        )
    for copy in copies:
        copy.start()
    for copy in copies:
        copy.wait()


def cut(snapshots, n, k, rows, skip, size):
    blocks, local_times, _ = snapshots.shape
    if local_times % 8 == 0:
        piece = pl.pallas_call(
            functools.partial(cut_kernel, n, k, rows, skip),
            out_shape=pltpu.VMEM((blocks, local_times, size), jnp.float32),
            in_specs=[pl.BlockSpec(memory_space=pltpu.HBM)],
            out_specs=pl.BlockSpec(memory_space=pltpu.VMEM),
            scratch_shapes=[pltpu.SemaphoreType.DMA((CUTS,))],
            compiler_params=pltpu.CompilerParams(vmem_limit_bytes=4 * MIB),
        )(pltpu.with_memory_space_constraint(snapshots, pltpu.HBM))
    else:
        to = lax.rem(lax.axis_index("space") + k, n)
        start = to * rows + lax.axis_index("freq") * (rows // 2) + skip
        piece = lax.dynamic_slice_in_dim(snapshots, start, size, axis=2)
    return piece.reshape(blocks * local_times, size)


def early_kernel(n, k, t_ref, x_ref, *refs):
    src = lax.rem(lax.axis_index("space") - k + n, n)
    part = dot(t_ref[src], x_ref[...])
    refs[-1][...] = part if len(refs) == 1 else refs[0][...] + part


def early(tables, n, k, piece, *before):
    share = piece.shape[1]
    return pl.pallas_call(
        functools.partial(early_kernel, n, k),
        out_shape=jax.ShapeDtypeStruct((tables.shape[1], share), jnp.float32),
        compiler_params=pltpu.CompilerParams(vmem_limit_bytes=16 * MIB),
    )(tables, piece, *before)


def late_kernel(n, k, skip, t_ref, sum_ref, x_ref, w_ref, *refs):
    *before, own_ref, other_ref, gram_ref, lent_ref = refs
    cols = pl.ds(skip, x_ref.shape[1])
    src = lax.rem(lax.axis_index("space") - k + n, n)
    spectra = sum_ref[:, cols] + dot(t_ref[src], x_ref[...])
    half = spectra.shape[0] // 2
    width = half // 2
    local = width // NB
    line = lax.broadcasted_iota(jnp.int32, (width, width), 0) // NB
    lane = lax.broadcasted_iota(jnp.int32, (width, width), 1) // NB
    row = lax.broadcasted_iota(jnp.int32, (NB, width), 0)
    col = lax.broadcasted_iota(jnp.int32, (NB, width), 1) % NB
    first = lax.axis_index("freq") == 0
    halves = [spectra[:half], spectra[half:]]
    own_ref[...] = jnp.where(first, halves[0], halves[1])
    other_ref[...] = jnp.where(first, halves[1], halves[0])
    packed = []
    for z in halves:
        full = lax.dot_general(
            z * w_ref[:, cols],
            z,
            (((1,), (1,)), ((), ())),
            precision=lax.Precision.HIGHEST,
            preferred_element_type=jnp.float32,
        )
        gram_re = full[:width, :width] + full[width:, width:]
        gram_im = full[:width, width:] - full[width:, :width]
        both = []
        for part in (gram_re, gram_im):
            kept = jnp.where(line == lane, part, 0.0)
            both.append(jnp.sum(kept.reshape(local, NB, width), axis=0))
        packed.append(jnp.where(row >= col, both[0], both[1]))
    gram = jnp.where(first, packed[0], packed[1])
    lent = jnp.where(first, packed[1], packed[0])
    gram_ref[...] = gram + before[0][...] if before else gram
    lent_ref[...] = lent + before[1][...] if before else lent


def late(tables, n, k, skip, partial_sum, piece, weights, *before):
    share = piece.shape[1]
    half = tables.shape[1] // 2
    shape = jax.ShapeDtypeStruct((half, share), jnp.float32)
    gram_shape = jax.ShapeDtypeStruct((NB, half // 2), jnp.float32)
    return pl.pallas_call(
        functools.partial(late_kernel, n, k, skip),
        out_shape=(shape, shape, gram_shape, gram_shape),
        compiler_params=pltpu.CompilerParams(vmem_limit_bytes=16 * MIB),
    )(tables, partial_sum, piece, weights, *before)


def inv_sqrt(x):
    y = lax.rsqrt(x)
    return y * (1.5 - 0.5 * x * (y * y))


def finish_kernel(local, total, parts, *refs):
    own_refs, other_refs = refs[:parts], refs[parts : 2 * parts]
    *gram_refs, modes_ref, factor_ref = refs[2 * parts :]
    width = local * NB
    share = modes_ref.shape[3] // 2
    gram = sum(ref[...] for ref in gram_refs) / total
    row = lax.broadcasted_iota(jnp.int32, (NB, width), 0)
    col = lax.broadcasted_iota(jnp.int32, (NB, width), 1) % NB
    stacked = [jnp.where(col == j, gram, 0.0) for j in range(NB)]
    for j in range(NB):
        line = jnp.broadcast_to(gram[j : j + 1, :], (NB, width))
        stacked.append(jnp.where((col == row) & (row > j), -line, 0.0))
    stacked = jnp.concatenate(stacked, axis=0)
    group_r = lax.broadcasted_iota(jnp.int32, (width, width), 0) // NB
    group_c = lax.broadcasted_iota(jnp.int32, (width, width), 1) // NB
    same = group_r == group_c
    ones = jnp.where(same, 1.0, 0.0).astype(jnp.bfloat16)
    spread = jnp.zeros(stacked.shape, jnp.float32)
    rest = stacked
    for _ in range(3):
        piece = rest.astype(jnp.bfloat16)
        rest = rest - piece.astype(jnp.float32)
        spread = spread + jnp.dot(piece, ones, preferred_element_type=jnp.float32)
    col_re = [[spread[j * NB + 8 * h : j * NB + 8 * h + 8] for h in (0, 1)] for j in range(NB)]
    base = NB * NB
    col_im = [
        [spread[base + j * NB + 8 * h : base + j * NB + 8 * h + 8] for h in (0, 1)]
        for j in range(NB)
    ]
    rows = [lax.broadcasted_iota(jnp.int32, (8, width), 0) + 8 * h for h in (0, 1)]
    lanes = lax.broadcasted_iota(jnp.int32, (8, width), 1) % NB
    inv_re = [jnp.where(rows[h] == lanes, 1.0, 0.0) for h in (0, 1)]
    inv_im = [jnp.zeros((8, width), jnp.float32) for h in (0, 1)]
    low_re = [jnp.zeros((8, width), jnp.float32) for h in (0, 1)]
    low_im = [jnp.zeros((8, width), jnp.float32) for h in (0, 1)]

    def pick(halves, i):
        return jnp.broadcast_to(halves[i // 8][i % 8 : i % 8 + 1, :], (8, width))

    for p in range(NB):
        pivot = pick(col_re[p], p) + epsilon
        scale = inv_sqrt(pivot)
        coef_re, coef_im = [None, None], [None, None]
        for h in range(p // 8, 2):
            below = rows[h] > p
            coef_re[h] = jnp.where(below, col_re[p][h] * scale, 0.0)
            coef_im[h] = jnp.where(below, col_im[p][h] * scale, 0.0)
            here = lanes == p
            diag = jnp.where(rows[h] == p, pivot * scale, coef_re[h])
            low_re[h] = jnp.where(here, diag, low_re[h])
            low_im[h] = jnp.where(here, coef_im[h], low_im[h])
        for j in range(p + 1, NB):
            a_re, a_im = pick(coef_re, j), pick(coef_im, j)
            for h in range(j // 8, 2):
                col_re[j][h] = col_re[j][h] - (coef_re[h] * a_re + coef_im[h] * a_im)
                col_im[j][h] = col_im[j][h] - (coef_im[h] * a_re - coef_re[h] * a_im)
        line_re = pick(inv_re, p) * scale
        line_im = pick(inv_im, p) * scale
        for h in range(p // 8, 2):
            at = rows[h] == p
            new_re = inv_re[h] - (coef_re[h] * line_re - coef_im[h] * line_im)
            new_im = inv_im[h] - (coef_re[h] * line_im + coef_im[h] * line_re)
            inv_re[h] = jnp.where(at, line_re, new_re)
            inv_im[h] = jnp.where(at, line_im, new_im)

    block_re = jnp.where(same, jnp.concatenate(inv_re * local, axis=0), 0.0)
    block_im = jnp.where(same, jnp.concatenate(inv_im * local, axis=0), 0.0)
    mixing = jnp.concatenate(
        [
            jnp.concatenate([block_re, block_im], axis=1),
            jnp.concatenate([-block_im, block_re], axis=1),
        ],
        axis=0,
    )
    me = lax.axis_index("freq")
    size = share // parts
    for k, refs_of in ((0, own_refs), (1, other_refs)):
        for i, ref in enumerate(refs_of):
            start = pl.multiple_of(((me + k) % 2) * share + i * size, 128)
            out = dot(mixing, ref[...])
            for part in range(2):
                for f in range(local):
                    at = part * width + f * NB
                    modes_ref[f, part, :, pl.ds(start, size)] = out[at : at + NB]
    pad = jnp.zeros((width - NB, width), jnp.float32)
    turned_re = jnp.transpose(jnp.concatenate(low_re + [pad], axis=0))
    turned_im = jnp.transpose(jnp.concatenate(low_im + [pad], axis=0))
    for f in range(local):
        factor_ref[0, f] = turned_re[f * NB : (f + 1) * NB, :NB]
        factor_ref[1, f] = -turned_im[f * NB : (f + 1) * NB, :NB]


def finish(grams, own, other, local, total):
    share = sum(part.shape[1] for part in own)
    return pl.pallas_call(
        functools.partial(finish_kernel, local, total, len(own)),
        out_shape=(
            jax.ShapeDtypeStruct((local, 2, NB, 2 * share), jnp.float32),
            jax.ShapeDtypeStruct((2, local, NB, NB), jnp.float32),
        ),
        compiler_params=pltpu.CompilerParams(vmem_limit_bytes=16 * MIB),
    )(*own, *other, *grams)


def partner(value, axis, size, step):
    return lax.ppermute(value, axis, [(i, i ^ step) for i in range(size)])


def steps(size):
    return [1 << b for b in range(size.bit_length() - 1)]


def on_device(snapshots, weights):
    n = lax.axis_size("space")
    tm_count = lax.axis_size("tm")
    freq_count = lax.axis_size("freq")
    local = NF // freq_count
    blocks, local_times, columns = snapshots.shape
    rows = columns // n
    share = rows // freq_count
    me = lax.axis_index("freq")

    tables = jnp.asarray(dft_blocks(n))
    own_weights = lax.dynamic_index_in_dim(weights.reshape(freq_count, 1, share), me, 0, False)

    last = n // 2
    halves = (0, share // 2)

    def send(k, skip, size):
        sent = cut(snapshots, n, k, rows, skip, size)
        return lax.ppermute(sent, "space", [(i, (i + k) % n) for i in range(n)])

    offsets = [k for k in range(1, n) if k != last]
    pieces = [send(k, 0, share) for k in offsets]
    last_pieces = [send(last, skip, share // 2) for skip in halves]
    before = early(tables, n, 0, cut(snapshots, n, 0, rows, 0, share))
    for k, piece in zip(offsets, pieces):
        before = early(tables, n, k, piece, before)
    own, other, grams = [], [], []
    for skip, piece in zip(halves, last_pieces):
        if other:
            other[-1] = partner(other[-1], "freq", freq_count, 1)
            piece, other[-1] = lax.optimization_barrier((piece, other[-1]))
        mine, traded, *grams = late(tables, n, last, skip, before, piece, own_weights, *grams)
        own.append(mine)
        other.append(traded)
    gram, lent = grams
    gram = gram + partner(lent, "freq", freq_count, 1)
    for step in steps(tm_count):
        gram = gram + partner(gram, "tm", tm_count, step)
    for step in steps(n)[:-1]:
        gram = gram + partner(gram, "space", n, step)
    gram, traded = lax.optimization_barrier((gram, other[1]))
    other[1] = partner(traded, "freq", freq_count, 1)
    grams = [gram, partner(gram, "space", n, steps(n)[-1])]
    total = rows * n * tm_count
    return finish(grams, own, other, local, total)


def solution(mesh):
    return jax.shard_map(
        on_device,
        mesh=mesh,
        in_specs=(P(None, "space", ("groups", "tm")), P(("groups", "tm", "space"))),
        out_specs=(
            P("freq", None, None, ("groups", "tm", "space")),
            P("groups", "freq", None, None),
        ),
        check_vma=False,
    )
```

```python
import functools

import numpy as np
import jax
import jax.numpy as jnp
from jax import lax
from jax.experimental import pallas as pl
from jax.experimental.pallas import tpu as pltpu
from jax.sharding import PartitionSpec as P

NB = 16
SEGMENT_FRAMES = 64
NF = 16
CUTS = 16
epsilon = 1e-05
MIB = 1024 * 1024


def dft_blocks(groups):
    times = np.arange(SEGMENT_FRAMES)
    taper = 0.5 - 0.5 * np.cos(2.0 * np.pi * times / SEGMENT_FRAMES)
    taper = taper / np.sqrt(np.sum(taper * taper))
    bins = 1 + np.arange(NF)
    angles = 2.0 * np.pi * (bins[:, None] * times[None, :] % SEGMENT_FRAMES) / SEGMENT_FRAMES
    table = np.stack([np.cos(angles) * taper, -np.sin(angles) * taper])
    step = SEGMENT_FRAMES // groups
    table = table.reshape(2, 2, NF // 2, groups, step)
    spread = np.einsum("rhfgt,bc->ghrfbct", table, np.eye(NB))
    return spread.reshape(groups, 2 * NF * NB, NB * step).astype(np.float32)


def dot(a, b):
    return jnp.dot(a, b, precision=lax.Precision.HIGHEST, preferred_element_type=jnp.float32)


def cut_kernel(n, k, rows, skip, x_ref, o_ref, sem):
    size = o_ref.shape[2]
    to = lax.rem(lax.axis_index("space") + k, n)
    share = rows // 2
    start = pl.multiple_of(to * rows + lax.axis_index("freq") * share + skip, 128)
    part = NB // CUTS
    copies = []
    for i in range(CUTS):
        blocks = pl.ds(i * part, part)
        copies.append(
            pltpu.make_async_copy(
                x_ref.at[blocks, :, pl.ds(start, size)], o_ref.at[blocks], sem.at[i]
            )
        )
    for copy in copies:
        copy.start()
    for copy in copies:
        copy.wait()


def cut(snapshots, n, k, rows, skip, size):
    blocks, local_times, _ = snapshots.shape
    if local_times % 8 == 0:
        piece = pl.pallas_call(
            functools.partial(cut_kernel, n, k, rows, skip),
            out_shape=pltpu.VMEM((blocks, local_times, size), jnp.float32),
            in_specs=[pl.BlockSpec(memory_space=pltpu.HBM)],
            out_specs=pl.BlockSpec(memory_space=pltpu.VMEM),
            scratch_shapes=[pltpu.SemaphoreType.DMA((CUTS,))],
            compiler_params=pltpu.CompilerParams(vmem_limit_bytes=4 * MIB),
        )(pltpu.with_memory_space_constraint(snapshots, pltpu.HBM))
    else:
        to = lax.rem(lax.axis_index("space") + k, n)
        start = to * rows + lax.axis_index("freq") * (rows // 2) + skip
        piece = lax.dynamic_slice_in_dim(snapshots, start, size, axis=2)
    return piece.reshape(blocks * local_times, size)


def early_kernel(n, k, t_ref, x_ref, *refs):
    src = lax.rem(lax.axis_index("space") - k + n, n)
    part = dot(t_ref[src], x_ref[...])
    refs[-1][...] = part if len(refs) == 1 else refs[0][...] + part


def early(tables, n, k, piece, *before):
    share = piece.shape[1]
    return pl.pallas_call(
        functools.partial(early_kernel, n, k),
        out_shape=jax.ShapeDtypeStruct((tables.shape[1], share), jnp.float32),
        compiler_params=pltpu.CompilerParams(vmem_limit_bytes=16 * MIB),
    )(tables, piece, *before)


def late_kernel(n, k, skip, t_ref, sum_ref, x_ref, w_ref, *refs):
    *before, own_ref, other_ref, gram_ref, lent_ref = refs
    size = x_ref.shape[1]
    cols = pl.ds(skip, size)
    at = lax.axis_index("freq") * sum_ref.shape[1] + skip
    weights = w_ref[:, pl.ds(pl.multiple_of(at, 128), size)]
    src = lax.rem(lax.axis_index("space") - k + n, n)
    spectra = sum_ref[:, cols] + dot(t_ref[src], x_ref[...])
    half = spectra.shape[0] // 2
    width = half // 2
    local = width // NB
    line = lax.broadcasted_iota(jnp.int32, (width, width), 0) // NB
    lane = lax.broadcasted_iota(jnp.int32, (width, width), 1) // NB
    row = lax.broadcasted_iota(jnp.int32, (NB, width), 0)
    col = lax.broadcasted_iota(jnp.int32, (NB, width), 1) % NB
    first = lax.axis_index("freq") == 0
    halves = [spectra[:half], spectra[half:]]
    own_ref[...] = jnp.where(first, halves[0], halves[1])
    other_ref[...] = jnp.where(first, halves[1], halves[0])
    packed = []
    for z in halves:
        full = lax.dot_general(
            z * weights,
            z,
            (((1,), (1,)), ((), ())),
            precision=lax.Precision.HIGHEST,
            preferred_element_type=jnp.float32,
        )
        gram_re = full[:width, :width] + full[width:, width:]
        gram_im = full[:width, width:] - full[width:, :width]
        both = []
        for part in (gram_re, gram_im):
            kept = jnp.where(line == lane, part, 0.0)
            both.append(jnp.sum(kept.reshape(local, NB, width), axis=0))
        packed.append(jnp.where(row >= col, both[0], both[1]))
    gram = jnp.where(first, packed[0], packed[1])
    lent = jnp.where(first, packed[1], packed[0])
    gram_ref[...] = gram + before[0][...] if before else gram
    lent_ref[...] = lent + before[1][...] if before else lent


def late(tables, n, k, skip, partial_sum, piece, weights, *before):
    share = piece.shape[1]
    half = tables.shape[1] // 2
    shape = jax.ShapeDtypeStruct((half, share), jnp.float32)
    gram_shape = jax.ShapeDtypeStruct((NB, half // 2), jnp.float32)
    return pl.pallas_call(
        functools.partial(late_kernel, n, k, skip),
        out_shape=(shape, shape, gram_shape, gram_shape),
        compiler_params=pltpu.CompilerParams(vmem_limit_bytes=16 * MIB),
    )(tables, partial_sum, piece, weights, *before)


def inv_sqrt(x):
    y = lax.rsqrt(x)
    return y * (1.5 - 0.5 * x * (y * y))


def finish_kernel(local, total, parts, *refs):
    own_refs, other_refs = refs[:parts], refs[parts : 2 * parts]
    grams_ref, modes_ref, factor_ref = refs[2 * parts :]
    width = local * NB
    share = modes_ref.shape[3] // 2
    gram = jnp.sum(grams_ref[...].reshape(-1, NB, width), axis=0) / total
    row = lax.broadcasted_iota(jnp.int32, (NB, width), 0)
    col = lax.broadcasted_iota(jnp.int32, (NB, width), 1) % NB
    stacked = [jnp.where(col == j, gram, 0.0) for j in range(NB)]
    for j in range(NB):
        line = jnp.broadcast_to(gram[j : j + 1, :], (NB, width))
        stacked.append(jnp.where((col == row) & (row > j), -line, 0.0))
    stacked = jnp.concatenate(stacked, axis=0)
    group_r = lax.broadcasted_iota(jnp.int32, (width, width), 0) // NB
    group_c = lax.broadcasted_iota(jnp.int32, (width, width), 1) // NB
    same = group_r == group_c
    ones = jnp.where(same, 1.0, 0.0).astype(jnp.bfloat16)
    spread = jnp.zeros(stacked.shape, jnp.float32)
    rest = stacked
    for _ in range(3):
        piece = rest.astype(jnp.bfloat16)
        rest = rest - piece.astype(jnp.float32)
        spread = spread + jnp.dot(piece, ones, preferred_element_type=jnp.float32)
    col_re = [[spread[j * NB + 8 * h : j * NB + 8 * h + 8] for h in (0, 1)] for j in range(NB)]
    base = NB * NB
    col_im = [
        [spread[base + j * NB + 8 * h : base + j * NB + 8 * h + 8] for h in (0, 1)]
        for j in range(NB)
    ]
    rows = [lax.broadcasted_iota(jnp.int32, (8, width), 0) + 8 * h for h in (0, 1)]
    lanes = lax.broadcasted_iota(jnp.int32, (8, width), 1) % NB
    inv_re = [jnp.where(rows[h] == lanes, 1.0, 0.0) for h in (0, 1)]
    inv_im = [jnp.zeros((8, width), jnp.float32) for h in (0, 1)]
    low_re = [jnp.zeros((8, width), jnp.float32) for h in (0, 1)]
    low_im = [jnp.zeros((8, width), jnp.float32) for h in (0, 1)]

    def pick(halves, i):
        return jnp.broadcast_to(halves[i // 8][i % 8 : i % 8 + 1, :], (8, width))

    for p in range(NB):
        pivot = pick(col_re[p], p) + epsilon
        scale = inv_sqrt(pivot)
        coef_re, coef_im = [None, None], [None, None]
        for h in range(p // 8, 2):
            below = rows[h] > p
            coef_re[h] = jnp.where(below, col_re[p][h] * scale, 0.0)
            coef_im[h] = jnp.where(below, col_im[p][h] * scale, 0.0)
            here = lanes == p
            diag = jnp.where(rows[h] == p, pivot * scale, coef_re[h])
            low_re[h] = jnp.where(here, diag, low_re[h])
            low_im[h] = jnp.where(here, coef_im[h], low_im[h])
        for j in range(p + 1, NB):
            a_re, a_im = pick(coef_re, j), pick(coef_im, j)
            for h in range(j // 8, 2):
                col_re[j][h] = col_re[j][h] - (coef_re[h] * a_re + coef_im[h] * a_im)
                col_im[j][h] = col_im[j][h] - (coef_im[h] * a_re - coef_re[h] * a_im)
        line_re = pick(inv_re, p) * scale
        line_im = pick(inv_im, p) * scale
        for h in range(p // 8, 2):
            at = rows[h] == p
            new_re = inv_re[h] - (coef_re[h] * line_re - coef_im[h] * line_im)
            new_im = inv_im[h] - (coef_re[h] * line_im + coef_im[h] * line_re)
            inv_re[h] = jnp.where(at, line_re, new_re)
            inv_im[h] = jnp.where(at, line_im, new_im)

    block_re = jnp.where(same, jnp.concatenate(inv_re * local, axis=0), 0.0)
    block_im = jnp.where(same, jnp.concatenate(inv_im * local, axis=0), 0.0)
    mixing = jnp.concatenate(
        [
            jnp.concatenate([block_re, block_im], axis=1),
            jnp.concatenate([-block_im, block_re], axis=1),
        ],
        axis=0,
    )
    me = lax.axis_index("freq")
    size = share // parts
    for k, refs_of in ((0, own_refs), (1, other_refs)):
        for i, ref in enumerate(refs_of):
            start = pl.multiple_of(((me + k) % 2) * share + i * size, 128)
            out = dot(mixing, ref[...])
            for part in range(2):
                for f in range(local):
                    at = part * width + f * NB
                    modes_ref[f, part, :, pl.ds(start, size)] = out[at : at + NB]
    pad = jnp.zeros((width - NB, width), jnp.float32)
    turned_re = jnp.transpose(jnp.concatenate(low_re + [pad], axis=0))
    turned_im = jnp.transpose(jnp.concatenate(low_im + [pad], axis=0))
    for f in range(local):
        factor_ref[0, f] = turned_re[f * NB : (f + 1) * NB, :NB]
        factor_ref[1, f] = -turned_im[f * NB : (f + 1) * NB, :NB]


def finish(grams, own, other, local, total):
    share = sum(part.shape[1] for part in own)
    return pl.pallas_call(
        functools.partial(finish_kernel, local, total, len(own)),
        out_shape=(
            jax.ShapeDtypeStruct((local, 2, NB, 2 * share), jnp.float32),
            jax.ShapeDtypeStruct((2, local, NB, NB), jnp.float32),
        ),
        compiler_params=pltpu.CompilerParams(vmem_limit_bytes=16 * MIB),
    )(*own, *other, grams)


def partner(value, axis, size, step):
    return lax.ppermute(value, axis, [(i, i ^ step) for i in range(size)])


def steps(size):
    return [1 << b for b in range(size.bit_length() - 1)]


def on_device(snapshots, weights):
    n = lax.axis_size("space")
    tm_count = lax.axis_size("tm")
    freq_count = lax.axis_size("freq")
    local = NF // freq_count
    blocks, local_times, columns = snapshots.shape
    rows = columns // n
    share = rows // freq_count

    tables = jnp.asarray(dft_blocks(n))

    last = n // 2
    halves = (0, share // 2)

    def send(k, skip, size):
        sent = cut(snapshots, n, k, rows, skip, size)
        return lax.ppermute(sent, "space", [(i, (i + k) % n) for i in range(n)])

    offsets = [k for k in range(1, n) if k != last]
    pieces = [send(k, 0, share) for k in offsets]
    last_pieces = [send(last, skip, share // 2) for skip in halves]
    before = early(tables, n, 0, cut(snapshots, n, 0, rows, 0, share))
    for k, piece in zip(offsets, pieces):
        before = early(tables, n, k, piece, before)
    own, other, grams = [], [], []
    for skip, piece in zip(halves, last_pieces):
        if other:
            other[-1] = partner(other[-1], "freq", freq_count, 1)
            piece, other[-1] = lax.optimization_barrier((piece, other[-1]))
        mine, traded, *grams = late(tables, n, last, skip, before, piece, weights.reshape(1, rows), *grams)
        own.append(mine)
        other.append(traded)
    gram, lent = grams
    gram = gram + partner(lent, "freq", freq_count, 1)
    gram, traded = lax.optimization_barrier((gram, other[1]))
    other[1] = partner(traded, "freq", freq_count, 1)
    grams = lax.all_gather(gram, ("space", "tm"), tiled=True)
    total = rows * n * tm_count
    return finish(grams, own, other, local, total)


def solution(mesh):
    return jax.shard_map(
        on_device,
        mesh=mesh,
        in_specs=(P(None, "space", ("groups", "tm")), P(("groups", "tm", "space"))),
        out_specs=(
            P("freq", None, None, ("groups", "tm", "space")),
            P("groups", "freq", None, None),
        ),
        check_vma=False,
    )
```

```python
import functools

import numpy as np
import jax
import jax.numpy as jnp
from jax import lax
from jax.experimental import pallas as pl
from jax.experimental.pallas import tpu as pltpu
from jax.sharding import PartitionSpec as P

NB = 16
SEGMENT_FRAMES = 64
NF = 16
CUTS = 16
epsilon = 1e-05
MIB = 1024 * 1024


def dft_blocks(groups):
    times = np.arange(SEGMENT_FRAMES)
    taper = 0.5 - 0.5 * np.cos(2.0 * np.pi * times / SEGMENT_FRAMES)
    taper = taper / np.sqrt(np.sum(taper * taper))
    bins = 1 + np.arange(NF)
    angles = 2.0 * np.pi * (bins[:, None] * times[None, :] % SEGMENT_FRAMES) / SEGMENT_FRAMES
    table = np.stack([np.cos(angles) * taper, -np.sin(angles) * taper])
    step = SEGMENT_FRAMES // groups
    table = table.reshape(2, 2, NF // 2, groups, step)
    spread = np.einsum("rhfgt,bc->ghrfbct", table, np.eye(NB))
    return spread.reshape(groups, 2 * NF * NB, NB * step).astype(np.float32)


def dot(a, b):
    return jnp.dot(a, b, precision=lax.Precision.HIGHEST, preferred_element_type=jnp.float32)


def cut_kernel(n, k, rows, skip, x_ref, o_ref, sem):
    size = o_ref.shape[2]
    to = lax.rem(lax.axis_index("space") + k, n)
    share = rows // 2
    start = pl.multiple_of(to * rows + lax.axis_index("freq") * share + skip, 128)
    part = NB // CUTS
    copies = []
    for i in range(CUTS):
        blocks = pl.ds(i * part, part)
        copies.append(
            pltpu.make_async_copy(
                x_ref.at[blocks, :, pl.ds(start, size)], o_ref.at[blocks], sem.at[i]
            )
        )
    for copy in copies:
        copy.start()
    for copy in copies:
        copy.wait()


def cut(snapshots, n, k, rows, skip, size):
    blocks, local_times, _ = snapshots.shape
    if local_times % 8 == 0:
        piece = pl.pallas_call(
            functools.partial(cut_kernel, n, k, rows, skip),
            out_shape=pltpu.VMEM((blocks, local_times, size), jnp.float32),
            in_specs=[pl.BlockSpec(memory_space=pltpu.HBM)],
            out_specs=pl.BlockSpec(memory_space=pltpu.VMEM),
            scratch_shapes=[pltpu.SemaphoreType.DMA((CUTS,))],
            compiler_params=pltpu.CompilerParams(vmem_limit_bytes=4 * MIB),
        )(pltpu.with_memory_space_constraint(snapshots, pltpu.HBM))
    else:
        to = lax.rem(lax.axis_index("space") + k, n)
        start = to * rows + lax.axis_index("freq") * (rows // 2) + skip
        piece = lax.dynamic_slice_in_dim(snapshots, start, size, axis=2)
    return piece.reshape(blocks * local_times, size)


def early_kernel(n, k, t_ref, x_ref, *refs):
    src = lax.rem(lax.axis_index("space") - k + n, n)
    part = dot(t_ref[src], x_ref[...])
    refs[-1][...] = part if len(refs) == 1 else refs[0][...] + part


def early(tables, n, k, piece, *before):
    share = piece.shape[1]
    return pl.pallas_call(
        functools.partial(early_kernel, n, k),
        out_shape=jax.ShapeDtypeStruct((tables.shape[1], share), jnp.float32),
        compiler_params=pltpu.CompilerParams(vmem_limit_bytes=16 * MIB),
    )(tables, piece, *before)


def late_kernel(n, k, skip, t_ref, sum_ref, x_ref, w_ref, *refs):
    *before, own_ref, other_ref, gram_ref, lent_ref = refs
    size = x_ref.shape[1]
    cols = pl.ds(skip, size)
    at = lax.axis_index("freq") * sum_ref.shape[1] + skip
    weights = w_ref[:, pl.ds(pl.multiple_of(at, 128), size)]
    src = lax.rem(lax.axis_index("space") - k + n, n)
    spectra = sum_ref[:, cols] + dot(t_ref[src], x_ref[...])
    half = spectra.shape[0] // 2
    width = half // 2
    local = width // NB
    line = lax.broadcasted_iota(jnp.int32, (width, width), 0) // NB
    lane = lax.broadcasted_iota(jnp.int32, (width, width), 1) // NB
    row = lax.broadcasted_iota(jnp.int32, (NB, width), 0)
    col = lax.broadcasted_iota(jnp.int32, (NB, width), 1) % NB
    first = lax.axis_index("freq") == 0
    halves = [spectra[:half], spectra[half:]]
    own_ref[...] = jnp.where(first, halves[0], halves[1])
    other_ref[...] = jnp.where(first, halves[1], halves[0])
    packed = []
    for z in halves:
        full = lax.dot_general(
            z * weights,
            z,
            (((1,), (1,)), ((), ())),
            precision=lax.Precision.HIGHEST,
            preferred_element_type=jnp.float32,
        )
        gram_re = full[:width, :width] + full[width:, width:]
        gram_im = full[:width, width:] - full[width:, :width]
        both = []
        for part in (gram_re, gram_im):
            kept = jnp.where(line == lane, part, 0.0)
            both.append(jnp.sum(kept.reshape(local, NB, width), axis=0))
        packed.append(jnp.where(row >= col, both[0], both[1]))
    gram = jnp.where(first, packed[0], packed[1])
    lent = jnp.where(first, packed[1], packed[0])
    gram_ref[...] = gram + before[0][...] if before else gram
    lent_ref[...] = lent + before[1][...] if before else lent


def late(tables, n, k, skip, partial_sum, piece, weights, *before):
    share = piece.shape[1]
    half = tables.shape[1] // 2
    shape = jax.ShapeDtypeStruct((half, share), jnp.float32)
    gram_shape = jax.ShapeDtypeStruct((NB, half // 2), jnp.float32)
    return pl.pallas_call(
        functools.partial(late_kernel, n, k, skip),
        out_shape=(shape, shape, gram_shape, gram_shape),
        compiler_params=pltpu.CompilerParams(vmem_limit_bytes=16 * MIB),
    )(tables, partial_sum, piece, weights, *before)


def inv_sqrt(x):
    y = lax.rsqrt(x)
    return y * (1.5 - 0.5 * x * (y * y))


def finish_kernel(local, total, parts, *refs):
    own_refs, other_refs = refs[:parts], refs[parts : 2 * parts]
    grams_ref, modes_ref, factor_ref = refs[2 * parts :]
    width = local * NB
    share = modes_ref.shape[3] // 2
    gram = jnp.sum(grams_ref[...], axis=0) / total
    row = lax.broadcasted_iota(jnp.int32, (NB, width), 0)
    col = lax.broadcasted_iota(jnp.int32, (NB, width), 1) % NB
    stacked = [jnp.where(col == j, gram, 0.0) for j in range(NB)]
    for j in range(NB):
        line = jnp.broadcast_to(gram[j : j + 1, :], (NB, width))
        stacked.append(jnp.where((col == row) & (row > j), -line, 0.0))
    stacked = jnp.concatenate(stacked, axis=0)
    group_r = lax.broadcasted_iota(jnp.int32, (width, width), 0) // NB
    group_c = lax.broadcasted_iota(jnp.int32, (width, width), 1) // NB
    same = group_r == group_c
    ones = jnp.where(same, 1.0, 0.0).astype(jnp.bfloat16)
    spread = jnp.zeros(stacked.shape, jnp.float32)
    rest = stacked
    for _ in range(3):
        piece = rest.astype(jnp.bfloat16)
        rest = rest - piece.astype(jnp.float32)
        spread = spread + jnp.dot(piece, ones, preferred_element_type=jnp.float32)
    col_re = [[spread[j * NB + 8 * h : j * NB + 8 * h + 8] for h in (0, 1)] for j in range(NB)]
    base = NB * NB
    col_im = [
        [spread[base + j * NB + 8 * h : base + j * NB + 8 * h + 8] for h in (0, 1)]
        for j in range(NB)
    ]
    rows = [lax.broadcasted_iota(jnp.int32, (8, width), 0) + 8 * h for h in (0, 1)]
    lanes = lax.broadcasted_iota(jnp.int32, (8, width), 1) % NB
    inv_re = [jnp.where(rows[h] == lanes, 1.0, 0.0) for h in (0, 1)]
    inv_im = [jnp.zeros((8, width), jnp.float32) for h in (0, 1)]
    low_re = [jnp.zeros((8, width), jnp.float32) for h in (0, 1)]
    low_im = [jnp.zeros((8, width), jnp.float32) for h in (0, 1)]

    def pick(halves, i):
        return jnp.broadcast_to(halves[i // 8][i % 8 : i % 8 + 1, :], (8, width))

    for p in range(NB):
        pivot = pick(col_re[p], p) + epsilon
        scale = inv_sqrt(pivot)
        coef_re, coef_im = [None, None], [None, None]
        for h in range(p // 8, 2):
            below = rows[h] > p
            coef_re[h] = jnp.where(below, col_re[p][h] * scale, 0.0)
            coef_im[h] = jnp.where(below, col_im[p][h] * scale, 0.0)
            here = lanes == p
            diag = jnp.where(rows[h] == p, pivot * scale, coef_re[h])
            low_re[h] = jnp.where(here, diag, low_re[h])
            low_im[h] = jnp.where(here, coef_im[h], low_im[h])
        for j in range(p + 1, NB):
            a_re, a_im = pick(coef_re, j), pick(coef_im, j)
            for h in range(j // 8, 2):
                col_re[j][h] = col_re[j][h] - (coef_re[h] * a_re + coef_im[h] * a_im)
                col_im[j][h] = col_im[j][h] - (coef_im[h] * a_re - coef_re[h] * a_im)
        line_re = pick(inv_re, p) * scale
        line_im = pick(inv_im, p) * scale
        for h in range(p // 8, 2):
            at = rows[h] == p
            new_re = inv_re[h] - (coef_re[h] * line_re - coef_im[h] * line_im)
            new_im = inv_im[h] - (coef_re[h] * line_im + coef_im[h] * line_re)
            inv_re[h] = jnp.where(at, line_re, new_re)
            inv_im[h] = jnp.where(at, line_im, new_im)

    block_re = jnp.where(same, jnp.concatenate(inv_re * local, axis=0), 0.0)
    block_im = jnp.where(same, jnp.concatenate(inv_im * local, axis=0), 0.0)
    mixing = jnp.concatenate(
        [
            jnp.concatenate([block_re, block_im], axis=1),
            jnp.concatenate([-block_im, block_re], axis=1),
        ],
        axis=0,
    )
    me = lax.axis_index("freq")
    size = share // parts
    for k, refs_of in ((0, own_refs), (1, other_refs)):
        for i, ref in enumerate(refs_of):
            start = pl.multiple_of(((me + k) % 2) * share + i * size, 128)
            out = dot(mixing, ref[...])
            for part in range(2):
                for f in range(local):
                    at = part * width + f * NB
                    modes_ref[f, part, :, pl.ds(start, size)] = out[at : at + NB]
    pad = jnp.zeros((width - NB, width), jnp.float32)
    turned_re = jnp.transpose(jnp.concatenate(low_re + [pad], axis=0))
    turned_im = jnp.transpose(jnp.concatenate(low_im + [pad], axis=0))
    for f in range(local):
        factor_ref[0, f] = turned_re[f * NB : (f + 1) * NB, :NB]
        factor_ref[1, f] = -turned_im[f * NB : (f + 1) * NB, :NB]


def finish(grams, own, other, local, total):
    share = sum(part.shape[1] for part in own)
    return pl.pallas_call(
        functools.partial(finish_kernel, local, total, len(own)),
        out_shape=(
            jax.ShapeDtypeStruct((local, 2, NB, 2 * share), jnp.float32),
            jax.ShapeDtypeStruct((2, local, NB, NB), jnp.float32),
        ),
        compiler_params=pltpu.CompilerParams(vmem_limit_bytes=16 * MIB),
    )(*own, *other, grams)


def partner(value, axis, size, step):
    return lax.ppermute(value, axis, [(i, i ^ step) for i in range(size)])


def steps(size):
    return [1 << b for b in range(size.bit_length() - 1)]


def on_device(snapshots, weights):
    n = lax.axis_size("space")
    tm_count = lax.axis_size("tm")
    freq_count = lax.axis_size("freq")
    local = NF // freq_count
    blocks, local_times, columns = snapshots.shape
    rows = columns // n
    share = rows // freq_count

    tables = jnp.asarray(dft_blocks(n))

    last = n // 2
    halves = (0, share // 2)

    def send(k, skip, size):
        sent = cut(snapshots, n, k, rows, skip, size)
        return lax.ppermute(sent, "space", [(i, (i + k) % n) for i in range(n)])

    offsets = [k for k in range(1, n) if k != last]
    pieces = [send(k, 0, share) for k in offsets]
    last_pieces = [send(last, skip, share // 2) for skip in halves]
    before = early(tables, n, 0, cut(snapshots, n, 0, rows, 0, share))
    for k, piece in zip(offsets, pieces):
        before = early(tables, n, k, piece, before)
    own, other, grams = [], [], []
    for skip, piece in zip(halves, last_pieces):
        if other:
            other[-1] = partner(other[-1], "freq", freq_count, 1)
            piece, other[-1] = lax.optimization_barrier((piece, other[-1]))
        mine, traded, *grams = late(tables, n, last, skip, before, piece, weights.reshape(1, rows), *grams)
        own.append(mine)
        other.append(traded)
    gram, lent = grams
    gram = gram + partner(lent, "freq", freq_count, 1)
    gram, traded = lax.optimization_barrier((gram, other[1]))
    other[1] = partner(traded, "freq", freq_count, 1)
    grams = jnp.broadcast_to(gram, (n * tm_count,) + gram.shape)
    grams = lax.all_to_all(grams, ("space", "tm"), split_axis=0, concat_axis=0, tiled=True)
    total = rows * n * tm_count
    return finish(grams, own, other, local, total)


def solution(mesh):
    return jax.shard_map(
        on_device,
        mesh=mesh,
        in_specs=(P(None, "space", ("groups", "tm")), P(("groups", "tm", "space"))),
        out_specs=(
            P("freq", None, None, ("groups", "tm", "space")),
            P("groups", "freq", None, None),
        ),
        check_vma=False,
    )
```

```python
import functools

import numpy as np
import jax
import jax.numpy as jnp
from jax import lax
from jax.experimental import pallas as pl
from jax.experimental.pallas import tpu as pltpu
from jax.sharding import PartitionSpec as P

NB = 16
SEGMENT_FRAMES = 64
NF = 16
CUTS = 16
epsilon = 1e-05
MIB = 1024 * 1024


def dft_blocks(groups):
    times = np.arange(SEGMENT_FRAMES)
    taper = 0.5 - 0.5 * np.cos(2.0 * np.pi * times / SEGMENT_FRAMES)
    taper = taper / np.sqrt(np.sum(taper * taper))
    bins = 1 + np.arange(NF)
    angles = 2.0 * np.pi * (bins[:, None] * times[None, :] % SEGMENT_FRAMES) / SEGMENT_FRAMES
    table = np.stack([np.cos(angles) * taper, -np.sin(angles) * taper])
    step = SEGMENT_FRAMES // groups
    table = table.reshape(2, 2, NF // 2, groups, step)
    spread = np.einsum("rhfgt,bc->ghrfbct", table, np.eye(NB))
    spread = spread.reshape(groups, 2 * NF * NB, NB * step).astype(np.float32)
    high = spread.astype(jnp.bfloat16)
    low = (spread - high.astype(np.float32)).astype(jnp.bfloat16)
    return np.concatenate([high, high, low], axis=2)


def split(x):
    high = x.astype(jnp.bfloat16)
    return high, (x - high.astype(jnp.float32)).astype(jnp.bfloat16)


def times_split(left, x):
    high, low = split(x)
    right = jnp.concatenate([high, low, high], axis=0)
    return jnp.dot(left, right, preferred_element_type=jnp.float32)


def rows_product(a, b):
    a_high, a_low = split(a)
    b_high, b_low = split(b)
    total = 0.0
    for x, y in ((a_high, b_high), (a_high, b_low), (a_low, b_high)):
        total = total + lax.dot_general(
            x, y, (((1,), (1,)), ((), ())), preferred_element_type=jnp.float32
        )
    return total


def cut_kernel(n, k, rows, skip, x_ref, o_ref, sem):
    size = o_ref.shape[2]
    to = lax.rem(lax.axis_index("space") + k, n)
    share = rows // 2
    start = pl.multiple_of(to * rows + lax.axis_index("freq") * share + skip, 128)
    part = NB // CUTS
    copies = []
    for i in range(CUTS):
        blocks = pl.ds(i * part, part)
        copies.append(
            pltpu.make_async_copy(
                x_ref.at[blocks, :, pl.ds(start, size)], o_ref.at[blocks], sem.at[i]
            )
        )
    for copy in copies:
        copy.start()
    for copy in copies:
        copy.wait()


def cut(snapshots, n, k, rows, skip, size):
    blocks, local_times, _ = snapshots.shape
    if local_times % 8 == 0:
        piece = pl.pallas_call(
            functools.partial(cut_kernel, n, k, rows, skip),
            out_shape=pltpu.VMEM((blocks, local_times, size), jnp.float32),
            in_specs=[pl.BlockSpec(memory_space=pltpu.HBM)],
            out_specs=pl.BlockSpec(memory_space=pltpu.VMEM),
            scratch_shapes=[pltpu.SemaphoreType.DMA((CUTS,))],
            compiler_params=pltpu.CompilerParams(vmem_limit_bytes=4 * MIB),
        )(pltpu.with_memory_space_constraint(snapshots, pltpu.HBM))
    else:
        to = lax.rem(lax.axis_index("space") + k, n)
        start = to * rows + lax.axis_index("freq") * (rows // 2) + skip
        piece = lax.dynamic_slice_in_dim(snapshots, start, size, axis=2)
    return piece.reshape(blocks * local_times, size)


def early_kernel(n, k, t_ref, x_ref, *refs):
    src = lax.rem(lax.axis_index("space") - k + n, n)
    part = times_split(t_ref[src], x_ref[...])
    refs[-1][...] = part if len(refs) == 1 else refs[0][...] + part


def early(tables, n, k, piece, *before):
    share = piece.shape[1]
    return pl.pallas_call(
        functools.partial(early_kernel, n, k),
        out_shape=jax.ShapeDtypeStruct((tables.shape[1], share), jnp.float32),
        compiler_params=pltpu.CompilerParams(vmem_limit_bytes=16 * MIB),
    )(tables, piece, *before)


def late_kernel(n, k, skip, t_ref, sum_ref, x_ref, w_ref, *refs):
    *before, own_ref, other_ref, gram_ref = refs
    size = x_ref.shape[1]
    cols = pl.ds(skip, size)
    at = lax.axis_index("freq") * sum_ref.shape[1] + skip
    weights = w_ref[:, pl.ds(pl.multiple_of(at, 128), size)]
    src = lax.rem(lax.axis_index("space") - k + n, n)
    spectra = sum_ref[:, cols] + times_split(t_ref[src], x_ref[...])
    half = spectra.shape[0] // 2
    width = half // 2
    local = width // NB
    line = lax.broadcasted_iota(jnp.int32, (width, width), 0) // NB
    lane = lax.broadcasted_iota(jnp.int32, (width, width), 1) // NB
    row = lax.broadcasted_iota(jnp.int32, (NB, width), 0)
    col = lax.broadcasted_iota(jnp.int32, (NB, width), 1) % NB
    first = lax.axis_index("freq") == 0
    halves = [spectra[:half], spectra[half:]]
    own_ref[...] = jnp.where(first, halves[0], halves[1])
    other_ref[...] = jnp.where(first, halves[1], halves[0])
    packed = []
    for z in halves:
        full = rows_product(z * weights, z)
        gram_re = full[:width, :width] + full[width:, width:]
        gram_im = full[:width, width:] - full[width:, :width]
        both = []
        for part in (gram_re, gram_im):
            kept = jnp.where(line == lane, part, 0.0)
            both.append(jnp.sum(kept.reshape(local, NB, width), axis=0))
        packed.append(jnp.where(row >= col, both[0], both[1]))
    if before:
        packed = [packed[h] + before[0][h] for h in range(2)]
    for d in range(gram_ref.shape[0]):
        gram_ref[d] = packed[d % 2]


def late(tables, n, k, skip, targets, partial_sum, piece, weights, *before):
    share = piece.shape[1]
    half = tables.shape[1] // 2
    shape = jax.ShapeDtypeStruct((half, share), jnp.float32)
    gram_shape = jax.ShapeDtypeStruct((targets, NB, half // 2), jnp.float32)
    return pl.pallas_call(
        functools.partial(late_kernel, n, k, skip),
        out_shape=(shape, shape, gram_shape),
        compiler_params=pltpu.CompilerParams(vmem_limit_bytes=16 * MIB),
    )(tables, partial_sum, piece, weights, *before)


def inv_sqrt(x):
    y = lax.rsqrt(x)
    return y * (1.5 - 0.5 * x * (y * y))


def finish_kernel(local, total, parts, *refs):
    own_refs, other_refs = refs[:parts], refs[parts : 2 * parts]
    grams_ref, modes_ref, factor_ref, *slots, sem = refs[2 * parts :]
    width = local * NB
    share = modes_ref.shape[3] // 2
    gram = jnp.sum(grams_ref[...], axis=0) / total
    row = lax.broadcasted_iota(jnp.int32, (NB, width), 0)
    col = lax.broadcasted_iota(jnp.int32, (NB, width), 1) % NB
    stacked = [jnp.where(col == j, gram, 0.0) for j in range(NB)]
    for j in range(NB):
        line = jnp.broadcast_to(gram[j : j + 1, :], (NB, width))
        stacked.append(jnp.where((col == row) & (row > j), -line, 0.0))
    stacked = jnp.concatenate(stacked, axis=0)
    group_r = lax.broadcasted_iota(jnp.int32, (width, width), 0) // NB
    group_c = lax.broadcasted_iota(jnp.int32, (width, width), 1) // NB
    same = group_r == group_c
    ones = jnp.where(same, 1.0, 0.0).astype(jnp.bfloat16)
    spread = jnp.zeros(stacked.shape, jnp.float32)
    rest = stacked
    for _ in range(3):
        piece = rest.astype(jnp.bfloat16)
        rest = rest - piece.astype(jnp.float32)
        spread = spread + jnp.dot(piece, ones, preferred_element_type=jnp.float32)
    col_re = [[spread[j * NB + 8 * h : j * NB + 8 * h + 8] for h in (0, 1)] for j in range(NB)]
    base = NB * NB
    col_im = [
        [spread[base + j * NB + 8 * h : base + j * NB + 8 * h + 8] for h in (0, 1)]
        for j in range(NB)
    ]
    rows = [lax.broadcasted_iota(jnp.int32, (8, width), 0) + 8 * h for h in (0, 1)]
    lanes = lax.broadcasted_iota(jnp.int32, (8, width), 1) % NB
    inv_re = [jnp.where(rows[h] == lanes, 1.0, 0.0) for h in (0, 1)]
    inv_im = [jnp.zeros((8, width), jnp.float32) for h in (0, 1)]
    low_re = [jnp.zeros((8, width), jnp.float32) for h in (0, 1)]
    low_im = [jnp.zeros((8, width), jnp.float32) for h in (0, 1)]

    def pick(halves, i):
        return jnp.broadcast_to(halves[i // 8][i % 8 : i % 8 + 1, :], (8, width))

    for p in range(NB):
        pivot = pick(col_re[p], p) + epsilon
        scale = inv_sqrt(pivot)
        coef_re, coef_im = [None, None], [None, None]
        for h in range(p // 8, 2):
            below = rows[h] > p
            coef_re[h] = jnp.where(below, col_re[p][h] * scale, 0.0)
            coef_im[h] = jnp.where(below, col_im[p][h] * scale, 0.0)
            here = lanes == p
            diag = jnp.where(rows[h] == p, pivot * scale, coef_re[h])
            low_re[h] = jnp.where(here, diag, low_re[h])
            low_im[h] = jnp.where(here, coef_im[h], low_im[h])
        for j in range(p + 1, NB):
            a_re, a_im = pick(coef_re, j), pick(coef_im, j)
            for h in range(j // 8, 2):
                col_re[j][h] = col_re[j][h] - (coef_re[h] * a_re + coef_im[h] * a_im)
                col_im[j][h] = col_im[j][h] - (coef_im[h] * a_re - coef_re[h] * a_im)
        line_re = pick(inv_re, p) * scale
        line_im = pick(inv_im, p) * scale
        for h in range(p // 8, 2):
            at = rows[h] == p
            new_re = inv_re[h] - (coef_re[h] * line_re - coef_im[h] * line_im)
            new_im = inv_im[h] - (coef_re[h] * line_im + coef_im[h] * line_re)
            inv_re[h] = jnp.where(at, line_re, new_re)
            inv_im[h] = jnp.where(at, line_im, new_im)

    block_re = jnp.where(same, jnp.concatenate(inv_re * local, axis=0), 0.0)
    block_im = jnp.where(same, jnp.concatenate(inv_im * local, axis=0), 0.0)
    mixing = jnp.concatenate(
        [
            jnp.concatenate([block_re, block_im], axis=1),
            jnp.concatenate([-block_im, block_re], axis=1),
        ],
        axis=0,
    )
    me = lax.axis_index("freq")
    high, low = split(mixing)
    mixing = jnp.concatenate([high, high, low], axis=1)
    moves = []
    for k, refs_of in ((0, own_refs), (1, other_refs)):
        skip = 0
        for ref in refs_of:
            size = ref.shape[1]
            out = times_split(mixing, ref[...])
            slot = slots[len(moves)]
            for part in range(2):
                for f in range(local):
                    at = part * width + f * NB
                    slot[f, part] = out[at : at + NB]
            start = pl.multiple_of(((me + k) % 2) * share + skip, 128)
            moves.append(
                pltpu.make_async_copy(
                    slot, modes_ref.at[:, :, :, pl.ds(start, size)], sem.at[len(moves)]
                )
            )
            moves[-1].start()
            skip += size
    pad = jnp.zeros((width - NB, width), jnp.float32)
    turned_re = jnp.transpose(jnp.concatenate(low_re + [pad], axis=0))
    turned_im = jnp.transpose(jnp.concatenate(low_im + [pad], axis=0))
    for f in range(local):
        factor_ref[0, f] = turned_re[f * NB : (f + 1) * NB, :NB]
        factor_ref[1, f] = -turned_im[f * NB : (f + 1) * NB, :NB]
    for move in moves:
        move.wait()


def finish(grams, own, other, local, total):
    share = sum(part.shape[1] for part in own)
    return pl.pallas_call(
        functools.partial(finish_kernel, local, total, len(own)),
        out_shape=(
            jax.ShapeDtypeStruct((local, 2, NB, 2 * share), jnp.float32),
            jax.ShapeDtypeStruct((2, local, NB, NB), jnp.float32),
        ),
        out_specs=(
            pl.BlockSpec(memory_space=pltpu.HBM),
            pl.BlockSpec(memory_space=pltpu.VMEM),
        ),
        scratch_shapes=[
            *[pltpu.VMEM((local, 2, NB, part.shape[1]), jnp.float32) for part in own + other],
            pltpu.SemaphoreType.DMA((len(own + other),)),
        ],
        compiler_params=pltpu.CompilerParams(vmem_limit_bytes=16 * MIB),
    )(*own, *other, grams)


def partner(value, axis, size, step):
    return lax.ppermute(value, axis, [(i, i ^ step) for i in range(size)])


def on_device(snapshots, weights):
    n = lax.axis_size("space")
    tm_count = lax.axis_size("tm")
    freq_count = lax.axis_size("freq")
    local = NF // freq_count
    blocks, local_times, columns = snapshots.shape
    rows = columns // n
    share = rows // freq_count

    tables = jnp.asarray(dft_blocks(n))

    last = n // 2
    early_rows = share - share // 4
    parts = ((0, early_rows), (early_rows, share - early_rows))
    targets = n * tm_count * freq_count

    def send(k, skip, size):
        sent = cut(snapshots, n, k, rows, skip, size)
        return lax.ppermute(sent, "space", [(i, (i + k) % n) for i in range(n)])

    offsets = [k for k in range(1, n) if k != last]
    pieces = [send(k, 0, share) for k in offsets]
    last_pieces = [send(last, skip, size) for skip, size in parts]
    before = early(tables, n, 0, cut(snapshots, n, 0, rows, 0, share))
    for k, piece in zip(offsets, pieces):
        before = early(tables, n, k, piece, before)
    own, other, grams = [], [], []
    for (skip, _), piece in zip(parts, last_pieces):
        if other:
            other[-1] = partner(other[-1], "freq", freq_count, 1)
            piece, other[-1] = lax.optimization_barrier((piece, other[-1]))
        copies = targets if own else 2
        mine, traded, *grams = late(
            tables, n, last, skip, copies, before, piece, weights.reshape(1, rows), *grams
        )
        own.append(mine)
        other.append(traded)
    other[-1] = partner(other[-1], "freq", freq_count, 1)
    grams = lax.all_to_all(
        grams[0], ("space", "tm", "freq"), split_axis=0, concat_axis=0, tiled=True
    )
    total = rows * n * tm_count
    return finish(grams, own, other, local, total)


def solution(mesh):
    return jax.shard_map(
        on_device,
        mesh=mesh,
        in_specs=(P(None, "space", ("groups", "tm")), P(("groups", "tm", "space"))),
        out_specs=(
            P("freq", None, None, ("groups", "tm", "space")),
            P("groups", "freq", None, None),
        ),
        check_vma=False,
    )
```

```python
import functools

import numpy as np
import jax
import jax.numpy as jnp
from jax import lax
from jax.experimental import pallas as pl
from jax.experimental.pallas import tpu as pltpu
from jax.sharding import PartitionSpec as P

NB = 16
SEGMENT_FRAMES = 64
NF = 16
CUTS = 16
epsilon = 1e-05
MIB = 1024 * 1024
SMALL = pl.CostEstimate(flops=1, transcendentals=0, bytes_accessed=1)


def dft_blocks(groups):
    times = np.arange(SEGMENT_FRAMES)
    taper = 0.5 - 0.5 * np.cos(2.0 * np.pi * times / SEGMENT_FRAMES)
    taper = taper / np.sqrt(np.sum(taper * taper))
    bins = 1 + np.arange(NF)
    angles = 2.0 * np.pi * (bins[:, None] * times[None, :] % SEGMENT_FRAMES) / SEGMENT_FRAMES
    table = np.stack([np.cos(angles) * taper, -np.sin(angles) * taper])
    step = SEGMENT_FRAMES // groups
    table = table.reshape(2, 2, NF // 2, groups, step)
    spread = np.einsum("rhfgt,bc->ghrfbct", table, np.eye(NB))
    spread = spread.reshape(groups, 2 * NF * NB, NB * step).astype(np.float32)
    high = spread.astype(jnp.bfloat16)
    low = (spread - high.astype(np.float32)).astype(jnp.bfloat16)
    return np.concatenate([high, high, low], axis=2)


def split(x):
    high = x.astype(jnp.bfloat16)
    return high, (x - high.astype(jnp.float32)).astype(jnp.bfloat16)


def times_split(left, x):
    high, low = split(x)
    right = jnp.concatenate([high, low, high], axis=0)
    return jnp.dot(left, right, preferred_element_type=jnp.float32)


def rows_product(a, b):
    a_high, a_low = split(a)
    b_high, b_low = split(b)
    total = 0.0
    for x, y in ((a_high, b_high), (a_high, b_low), (a_low, b_high)):
        total = total + lax.dot_general(
            x, y, (((1,), (1,)), ((), ())), preferred_element_type=jnp.float32
        )
    return total


def cut_kernel(n, k, rows, skip, x_ref, o_ref, sem):
    size = o_ref.shape[2]
    to = lax.rem(lax.axis_index("space") + k, n)
    share = rows // 2
    start = pl.multiple_of(to * rows + lax.axis_index("freq") * share + skip, 128)
    part = NB // CUTS
    copies = []
    for i in range(CUTS):
        blocks = pl.ds(i * part, part)
        copies.append(
            pltpu.make_async_copy(
                x_ref.at[blocks, :, pl.ds(start, size)], o_ref.at[blocks], sem.at[i]
            )
        )
    for copy in copies:
        copy.start()
    for copy in copies:
        copy.wait()


def cut(snapshots, n, k, rows, skip, size):
    blocks, local_times, _ = snapshots.shape
    if local_times % 8 == 0:
        piece = pl.pallas_call(
            functools.partial(cut_kernel, n, k, rows, skip),
            out_shape=pltpu.VMEM((blocks, local_times, size), jnp.float32),
            in_specs=[pl.BlockSpec(memory_space=pltpu.HBM)],
            out_specs=pl.BlockSpec(memory_space=pltpu.VMEM),
            scratch_shapes=[pltpu.SemaphoreType.DMA((CUTS,))],
            compiler_params=pltpu.CompilerParams(vmem_limit_bytes=4 * MIB),
            cost_estimate=SMALL,
        )(pltpu.with_memory_space_constraint(snapshots, pltpu.HBM))
    else:
        to = lax.rem(lax.axis_index("space") + k, n)
        start = to * rows + lax.axis_index("freq") * (rows // 2) + skip
        piece = lax.dynamic_slice_in_dim(snapshots, start, size, axis=2)
    return piece.reshape(blocks * local_times, size)


def early_kernel(n, k, t_ref, x_ref, *refs):
    src = lax.rem(lax.axis_index("space") - k + n, n)
    part = times_split(t_ref[src], x_ref[...])
    refs[-1][...] = part if len(refs) == 1 else refs[0][...] + part


def early(tables, n, k, piece, *before):
    share = piece.shape[1]
    return pl.pallas_call(
        functools.partial(early_kernel, n, k),
        out_shape=jax.ShapeDtypeStruct((tables.shape[1], share), jnp.float32),
        compiler_params=pltpu.CompilerParams(vmem_limit_bytes=16 * MIB),
        cost_estimate=SMALL,
    )(tables, piece, *before)


def late_kernel(n, k, skip, t_ref, sum_ref, x_ref, w_ref, *refs):
    size = x_ref.shape[1]
    share = sum_ref.shape[1]
    cols = pl.ds(skip, size)
    at = lax.axis_index("freq") * share + skip
    weights = w_ref[:, pl.ds(pl.multiple_of(at, 128), size)]
    src = lax.rem(lax.axis_index("space") - k + n, n)
    spectra = sum_ref[:, cols] + times_split(t_ref[src], x_ref[...])
    half = spectra.shape[0] // 2
    width = half // 2
    local = width // NB
    line = lax.broadcasted_iota(jnp.int32, (width, width), 0) // NB
    lane = lax.broadcasted_iota(jnp.int32, (width, width), 1) // NB
    row = lax.broadcasted_iota(jnp.int32, (NB, width), 0)
    col = lax.broadcasted_iota(jnp.int32, (NB, width), 1) % NB
    first = lax.axis_index("freq") == 0
    halves = [spectra[:half], spectra[half:]]
    if skip:
        before_ref, own_ref, gram_ref = refs
    else:
        own_ref, gram_ref, other_ref, rest_ref = refs
        rest = sum_ref[:, size:]
        other_ref[...] = jnp.where(first, halves[1], halves[0])
        rest_ref[...] = jnp.where(first, rest[half:], rest[:half])
    own_ref[...] = jnp.where(first, halves[0], halves[1])
    packed = []
    for z in halves:
        full = rows_product(z * weights, z)
        gram_re = full[:width, :width] + full[width:, width:]
        gram_im = full[:width, width:] - full[width:, :width]
        both = []
        for part in (gram_re, gram_im):
            kept = jnp.where(line == lane, part, 0.0)
            both.append(jnp.sum(kept.reshape(local, NB, width), axis=0))
        packed.append(jnp.where(row >= col, both[0], both[1]))
    if skip:
        packed = [packed[h] + before_ref[h] for h in range(2)]
    for d in range(gram_ref.shape[0]):
        gram_ref[d] = packed[d % 2]


def late(tables, n, k, skip, targets, partial_sum, piece, weights, *before):
    share = partial_sum.shape[1]
    half = tables.shape[1] // 2
    shapes = [(half, piece.shape[1]), (targets, NB, half // 2)]
    if not skip:
        shapes += [(half, piece.shape[1]), (half, share - piece.shape[1])]
    return pl.pallas_call(
        functools.partial(late_kernel, n, k, skip),
        out_shape=[jax.ShapeDtypeStruct(shape, jnp.float32) for shape in shapes],
        compiler_params=pltpu.CompilerParams(vmem_limit_bytes=16 * MIB),
        cost_estimate=SMALL,
    )(tables, partial_sum, piece, weights, *before)


def inv_sqrt(x):
    y = lax.rsqrt(x)
    return y * (1.5 - 0.5 * x * (y * y))


def finish_kernel(
    n, k, total, t_ref, first_ref, second_ref, other_ref, rest_ref, raw_ref, grams_ref, modes_ref, factor_ref
):
    local = modes_ref.shape[0]
    width = local * NB
    share = modes_ref.shape[3] // 2
    gram = jnp.sum(grams_ref[...], axis=0) / total
    row = lax.broadcasted_iota(jnp.int32, (NB, width), 0)
    col = lax.broadcasted_iota(jnp.int32, (NB, width), 1) % NB
    stacked = [jnp.where(col == j, gram, 0.0) for j in range(NB)]
    for j in range(NB):
        line = jnp.broadcast_to(gram[j : j + 1, :], (NB, width))
        stacked.append(jnp.where((col == row) & (row > j), -line, 0.0))
    stacked = jnp.concatenate(stacked, axis=0)
    group_r = lax.broadcasted_iota(jnp.int32, (width, width), 0) // NB
    group_c = lax.broadcasted_iota(jnp.int32, (width, width), 1) // NB
    same = group_r == group_c
    ones = jnp.where(same, 1.0, 0.0).astype(jnp.bfloat16)
    spread = jnp.zeros(stacked.shape, jnp.float32)
    rest = stacked
    for _ in range(3):
        piece = rest.astype(jnp.bfloat16)
        rest = rest - piece.astype(jnp.float32)
        spread = spread + jnp.dot(piece, ones, preferred_element_type=jnp.float32)
    col_re = [[spread[j * NB + 8 * h : j * NB + 8 * h + 8] for h in (0, 1)] for j in range(NB)]
    base = NB * NB
    col_im = [
        [spread[base + j * NB + 8 * h : base + j * NB + 8 * h + 8] for h in (0, 1)]
        for j in range(NB)
    ]
    rows = [lax.broadcasted_iota(jnp.int32, (8, width), 0) + 8 * h for h in (0, 1)]
    lanes = lax.broadcasted_iota(jnp.int32, (8, width), 1) % NB
    inv_re = [jnp.where(rows[h] == lanes, 1.0, 0.0) for h in (0, 1)]
    inv_im = [jnp.zeros((8, width), jnp.float32) for h in (0, 1)]
    low_re = [jnp.zeros((8, width), jnp.float32) for h in (0, 1)]
    low_im = [jnp.zeros((8, width), jnp.float32) for h in (0, 1)]

    def pick(halves, i):
        return jnp.broadcast_to(halves[i // 8][i % 8 : i % 8 + 1, :], (8, width))

    for p in range(NB):
        pivot = pick(col_re[p], p) + epsilon
        scale = inv_sqrt(pivot)
        coef_re, coef_im = [None, None], [None, None]
        for h in range(p // 8, 2):
            below = rows[h] > p
            coef_re[h] = jnp.where(below, col_re[p][h] * scale, 0.0)
            coef_im[h] = jnp.where(below, col_im[p][h] * scale, 0.0)
            here = lanes == p
            diag = jnp.where(rows[h] == p, pivot * scale, coef_re[h])
            low_re[h] = jnp.where(here, diag, low_re[h])
            low_im[h] = jnp.where(here, coef_im[h], low_im[h])
        for j in range(p + 1, NB):
            a_re, a_im = pick(coef_re, j), pick(coef_im, j)
            for h in range(j // 8, 2):
                col_re[j][h] = col_re[j][h] - (coef_re[h] * a_re + coef_im[h] * a_im)
                col_im[j][h] = col_im[j][h] - (coef_im[h] * a_re - coef_re[h] * a_im)
        line_re = pick(inv_re, p) * scale
        line_im = pick(inv_im, p) * scale
        for h in range(p // 8, 2):
            at = rows[h] == p
            new_re = inv_re[h] - (coef_re[h] * line_re - coef_im[h] * line_im)
            new_im = inv_im[h] - (coef_re[h] * line_im + coef_im[h] * line_re)
            inv_re[h] = jnp.where(at, line_re, new_re)
            inv_im[h] = jnp.where(at, line_im, new_im)

    block_re = jnp.where(same, jnp.concatenate(inv_re * local, axis=0), 0.0)
    block_im = jnp.where(same, jnp.concatenate(inv_im * local, axis=0), 0.0)
    mixing = jnp.concatenate(
        [
            jnp.concatenate([block_re, block_im], axis=1),
            jnp.concatenate([-block_im, block_re], axis=1),
        ],
        axis=0,
    )
    me = lax.axis_index("freq")
    high, low = split(mixing)
    mixing = jnp.concatenate([high, high, low], axis=1)
    src = lax.rem(lax.axis_index("space") - k + n, n)
    lines = pl.ds(pl.multiple_of(me * 2 * width, 128), 2 * width)
    own = [first_ref[...], second_ref[...]]
    added = times_split(t_ref[src, lines], raw_ref[...])
    other = [other_ref[...], rest_ref[...] + added]
    for place, parts in ((me, own), (1 - me, other)):
        out = times_split(mixing, jnp.concatenate(parts, axis=1))
        cols = pl.ds(pl.multiple_of(place * share, 128), share)
        for part in range(2):
            for f in range(local):
                at = part * width + f * NB
                modes_ref[f, part, :, cols] = out[at : at + NB]
    pad = jnp.zeros((width - NB, width), jnp.float32)
    turned_re = jnp.transpose(jnp.concatenate(low_re + [pad], axis=0))
    turned_im = jnp.transpose(jnp.concatenate(low_im + [pad], axis=0))
    for f in range(local):
        factor_ref[0, f] = turned_re[f * NB : (f + 1) * NB, :NB]
        factor_ref[1, f] = -turned_im[f * NB : (f + 1) * NB, :NB]


def finish(tables, n, k, total, first, second, other, rest, raw, grams):
    local = tables.shape[1] // (4 * NB)
    share = other.shape[1] + rest.shape[1]
    return pl.pallas_call(
        functools.partial(finish_kernel, n, k, total),
        out_shape=(
            jax.ShapeDtypeStruct((local, 2, NB, 2 * share), jnp.float32),
            jax.ShapeDtypeStruct((2, local, NB, NB), jnp.float32),
        ),
        compiler_params=pltpu.CompilerParams(vmem_limit_bytes=16 * MIB),
    )(tables, first, second, other, rest, raw, grams)


def partner(value, axis, size, step):
    return lax.ppermute(value, axis, [(i, i ^ step) for i in range(size)])


def on_device(snapshots, weights):
    n = lax.axis_size("space")
    tm_count = lax.axis_size("tm")
    freq_count = lax.axis_size("freq")
    blocks, local_times, columns = snapshots.shape
    rows = columns // n
    share = rows // freq_count

    tables = jnp.asarray(dft_blocks(n))

    last = n // 2
    early_rows = share // 2
    parts = ((0, early_rows), (early_rows, share - early_rows))
    targets = n * tm_count * freq_count

    def send(k, skip, size):
        sent = cut(snapshots, n, k, rows, skip, size)
        return lax.ppermute(sent, "space", [(i, (i + k) % n) for i in range(n)])

    offsets = [k for k in range(1, n) if k != last]
    pieces = [send(k, 0, share) for k in offsets]
    last_pieces = [send(last, skip, size) for skip, size in parts]
    before = early(tables, n, 0, cut(snapshots, n, 0, rows, 0, share))
    for k, piece in zip(offsets, pieces):
        before = early(tables, n, k, piece, before)
    weights = weights.reshape(1, rows)
    first, gram, other, rest = late(tables, n, last, 0, 2, before, last_pieces[0], weights)
    other, rest = partner(other, "freq", freq_count, 1), partner(rest, "freq", freq_count, 1)
    raw, other, rest = lax.optimization_barrier((last_pieces[1], other, rest))
    second, gram = late(tables, n, last, early_rows, targets, before, raw, weights, gram)
    raw = partner(raw, "freq", freq_count, 1)
    gram, raw = lax.optimization_barrier((gram, raw))
    grams = lax.all_to_all(gram, ("space", "tm", "freq"), split_axis=0, concat_axis=0, tiled=True)
    total = rows * n * tm_count
    return finish(tables, n, last, total, first, second, other, rest, raw, grams)


def solution(mesh):
    return jax.shard_map(
        on_device,
        mesh=mesh,
        in_specs=(P(None, "space", ("groups", "tm")), P(("groups", "tm", "space"))),
        out_specs=(
            P("freq", None, None, ("groups", "tm", "space")),
            P("groups", "freq", None, None),
        ),
        check_vma=False,
    )
```

```python
import functools

import numpy as np
import jax
import jax.numpy as jnp
from jax import lax
from jax.experimental import pallas as pl
from jax.experimental.pallas import tpu as pltpu
from jax.sharding import PartitionSpec as P

NB = 16
SEGMENT_FRAMES = 64
NF = 16
CUTS = 16
TRADED = 128
epsilon = 1e-05
MIB = 1024 * 1024
SMALL = pl.CostEstimate(flops=1, transcendentals=0, bytes_accessed=1)


def dft_blocks(groups):
    times = np.arange(SEGMENT_FRAMES)
    taper = 0.5 - 0.5 * np.cos(2.0 * np.pi * times / SEGMENT_FRAMES)
    taper = taper / np.sqrt(np.sum(taper * taper))
    bins = 1 + np.arange(NF)
    angles = 2.0 * np.pi * (bins[:, None] * times[None, :] % SEGMENT_FRAMES) / SEGMENT_FRAMES
    table = np.stack([np.cos(angles) * taper, -np.sin(angles) * taper])
    step = SEGMENT_FRAMES // groups
    table = table.reshape(2, 2, NF // 2, groups, step)
    spread = np.einsum("rhfgt,bc->ghrfbct", table, np.eye(NB))
    spread = spread.reshape(groups, 2 * NF * NB, NB * step).astype(np.float32)
    high = spread.astype(jnp.bfloat16)
    low = (spread - high.astype(np.float32)).astype(jnp.bfloat16)
    return np.concatenate([high, high, low], axis=2)


def split(x):
    high = x.astype(jnp.bfloat16)
    return high, (x - high.astype(jnp.float32)).astype(jnp.bfloat16)


def times_split(left, x):
    high, low = split(x)
    right = jnp.concatenate([high, low, high], axis=0)
    return jnp.dot(left, right, preferred_element_type=jnp.float32)


def rows_product(a, b):
    a_high, a_low = split(a)
    b_high, b_low = split(b)
    total = 0.0
    for x, y in ((a_high, b_high), (a_high, b_low), (a_low, b_high)):
        total = total + lax.dot_general(
            x, y, (((1,), (1,)), ((), ())), preferred_element_type=jnp.float32
        )
    return total


def cut_kernel(n, k, rows, skip, x_ref, o_ref, sem):
    size = o_ref.shape[2]
    to = lax.bitwise_xor(lax.axis_index("space"), k)
    share = rows // 2
    start = pl.multiple_of(to * rows + lax.axis_index("freq") * share + skip, 128)
    part = NB // CUTS
    copies = []
    for i in range(CUTS):
        blocks = pl.ds(i * part, part)
        copies.append(
            pltpu.make_async_copy(
                x_ref.at[blocks, :, pl.ds(start, size)], o_ref.at[blocks], sem.at[i]
            )
        )
    for copy in copies:
        copy.start()
    for copy in copies:
        copy.wait()


def cut(snapshots, n, k, rows, skip, size):
    blocks, local_times, _ = snapshots.shape
    if local_times % 8 == 0:
        piece = pl.pallas_call(
            functools.partial(cut_kernel, n, k, rows, skip),
            out_shape=pltpu.VMEM((blocks, local_times, size), jnp.float32),
            in_specs=[pl.BlockSpec(memory_space=pltpu.HBM)],
            out_specs=pl.BlockSpec(memory_space=pltpu.VMEM),
            scratch_shapes=[pltpu.SemaphoreType.DMA((CUTS,))],
            compiler_params=pltpu.CompilerParams(vmem_limit_bytes=4 * MIB),
            cost_estimate=SMALL,
        )(pltpu.with_memory_space_constraint(snapshots, pltpu.HBM))
    else:
        to = lax.bitwise_xor(lax.axis_index("space"), k)
        start = to * rows + lax.axis_index("freq") * (rows // 2) + skip
        piece = lax.dynamic_slice_in_dim(snapshots, start, size, axis=2)
    return piece.reshape(blocks * local_times, size)


def early_kernel(n, k, t_ref, x_ref, *refs):
    src = lax.bitwise_xor(lax.axis_index("space"), k)
    part = times_split(t_ref[src], x_ref[...])
    refs[-1][...] = part if len(refs) == 1 else refs[0][...] + part


def early(tables, n, k, piece, *before):
    share = piece.shape[1]
    return pl.pallas_call(
        functools.partial(early_kernel, n, k),
        out_shape=jax.ShapeDtypeStruct((tables.shape[1], share), jnp.float32),
        compiler_params=pltpu.CompilerParams(vmem_limit_bytes=16 * MIB),
        cost_estimate=SMALL,
    )(tables, piece, *before)


def late_kernel(n, k, skip, t_ref, sum_ref, x_ref, w_ref, *refs):
    size = x_ref.shape[1]
    share = sum_ref.shape[1]
    cols = pl.ds(skip, size)
    at = lax.axis_index("freq") * share + skip
    weights = w_ref[:, pl.ds(pl.multiple_of(at, 128), size)]
    src = lax.bitwise_xor(lax.axis_index("space"), k)
    spectra = sum_ref[:, cols] + times_split(t_ref[src], x_ref[...])
    half = spectra.shape[0] // 2
    width = half // 2
    local = width // NB
    line = lax.broadcasted_iota(jnp.int32, (width, width), 0) // NB
    lane = lax.broadcasted_iota(jnp.int32, (width, width), 1) // NB
    row = lax.broadcasted_iota(jnp.int32, (NB, width), 0)
    col = lax.broadcasted_iota(jnp.int32, (NB, width), 1) % NB
    first = lax.axis_index("freq") == 0
    halves = [spectra[:half], spectra[half:]]
    if skip:
        before_ref, own_ref, gram_ref = refs
    else:
        own_ref, gram_ref, *other_refs = refs
        both = jnp.concatenate([spectra, sum_ref[:, size:]], axis=1)
        other = jnp.where(first, both[half:], both[:half])
        for i, ref in enumerate(other_refs):
            ref[...] = other[:, i * TRADED : (i + 1) * TRADED]
    own_ref[...] = jnp.where(first, halves[0], halves[1])
    packed = []
    for z in halves:
        full = rows_product(z * weights, z)
        gram_re = full[:width, :width] + full[width:, width:]
        gram_im = full[:width, width:] - full[width:, :width]
        both = []
        for part in (gram_re, gram_im):
            kept = jnp.where(line == lane, part, 0.0)
            both.append(jnp.sum(kept.reshape(local, NB, width), axis=0))
        packed.append(jnp.where(row >= col, both[0], both[1]))
    if skip:
        packed = [packed[h] + before_ref[h] for h in range(2)]
    for d in range(gram_ref.shape[0]):
        gram_ref[d] = packed[d % 2]


def late(tables, n, k, skip, targets, partial_sum, piece, weights, *before):
    share = partial_sum.shape[1]
    half = tables.shape[1] // 2
    shapes = [(half, piece.shape[1]), (targets, NB, half // 2)]
    if not skip:
        shapes += [(half, TRADED)] * (share // TRADED)
    return pl.pallas_call(
        functools.partial(late_kernel, n, k, skip),
        out_shape=[jax.ShapeDtypeStruct(shape, jnp.float32) for shape in shapes],
        compiler_params=pltpu.CompilerParams(vmem_limit_bytes=16 * MIB),
        cost_estimate=SMALL,
    )(tables, partial_sum, piece, weights, *before)


def inv_sqrt(x):
    y = lax.rsqrt(x)
    return y * (1.5 - 0.5 * x * (y * y))


def finish_kernel(
    n, k, total, t_ref, first_ref, second_ref, raw_ref, grams_ref, *refs
):
    *other_refs, modes_ref, factor_ref = refs
    local = modes_ref.shape[0]
    width = local * NB
    share = modes_ref.shape[3] // 2
    gram = jnp.sum(grams_ref[...], axis=0) / total
    row = lax.broadcasted_iota(jnp.int32, (NB, width), 0)
    col = lax.broadcasted_iota(jnp.int32, (NB, width), 1) % NB
    stacked = [jnp.where(col == j, gram, 0.0) for j in range(NB)]
    for j in range(NB):
        line = jnp.broadcast_to(gram[j : j + 1, :], (NB, width))
        stacked.append(jnp.where((col == row) & (row > j), -line, 0.0))
    stacked = jnp.concatenate(stacked, axis=0)
    group_r = lax.broadcasted_iota(jnp.int32, (width, width), 0) // NB
    group_c = lax.broadcasted_iota(jnp.int32, (width, width), 1) // NB
    same = group_r == group_c
    ones = jnp.where(same, 1.0, 0.0).astype(jnp.bfloat16)
    spread = jnp.zeros(stacked.shape, jnp.float32)
    rest = stacked
    for _ in range(3):
        piece = rest.astype(jnp.bfloat16)
        rest = rest - piece.astype(jnp.float32)
        spread = spread + jnp.dot(piece, ones, preferred_element_type=jnp.float32)
    col_re = [[spread[j * NB + 8 * h : j * NB + 8 * h + 8] for h in (0, 1)] for j in range(NB)]
    base = NB * NB
    col_im = [
        [spread[base + j * NB + 8 * h : base + j * NB + 8 * h + 8] for h in (0, 1)]
        for j in range(NB)
    ]
    rows = [lax.broadcasted_iota(jnp.int32, (8, width), 0) + 8 * h for h in (0, 1)]
    lanes = lax.broadcasted_iota(jnp.int32, (8, width), 1) % NB
    inv_re = [jnp.where(rows[h] == lanes, 1.0, 0.0) for h in (0, 1)]
    inv_im = [jnp.zeros((8, width), jnp.float32) for h in (0, 1)]
    low_re = [jnp.zeros((8, width), jnp.float32) for h in (0, 1)]
    low_im = [jnp.zeros((8, width), jnp.float32) for h in (0, 1)]

    def pick(halves, i):
        return jnp.broadcast_to(halves[i // 8][i % 8 : i % 8 + 1, :], (8, width))

    for p in range(NB):
        pivot = pick(col_re[p], p) + epsilon
        scale = inv_sqrt(pivot)
        coef_re, coef_im = [None, None], [None, None]
        for h in range(p // 8, 2):
            below = rows[h] > p
            coef_re[h] = jnp.where(below, col_re[p][h] * scale, 0.0)
            coef_im[h] = jnp.where(below, col_im[p][h] * scale, 0.0)
            here = lanes == p
            diag = jnp.where(rows[h] == p, pivot * scale, coef_re[h])
            low_re[h] = jnp.where(here, diag, low_re[h])
            low_im[h] = jnp.where(here, coef_im[h], low_im[h])
        for j in range(p + 1, NB):
            a_re, a_im = pick(coef_re, j), pick(coef_im, j)
            for h in range(j // 8, 2):
                col_re[j][h] = col_re[j][h] - (coef_re[h] * a_re + coef_im[h] * a_im)
                col_im[j][h] = col_im[j][h] - (coef_im[h] * a_re - coef_re[h] * a_im)
        line_re = pick(inv_re, p) * scale
        line_im = pick(inv_im, p) * scale
        for h in range(p // 8, 2):
            at = rows[h] == p
            new_re = inv_re[h] - (coef_re[h] * line_re - coef_im[h] * line_im)
            new_im = inv_im[h] - (coef_re[h] * line_im + coef_im[h] * line_re)
            inv_re[h] = jnp.where(at, line_re, new_re)
            inv_im[h] = jnp.where(at, line_im, new_im)

    block_re = jnp.where(same, jnp.concatenate(inv_re * local, axis=0), 0.0)
    block_im = jnp.where(same, jnp.concatenate(inv_im * local, axis=0), 0.0)
    mixing = jnp.concatenate(
        [
            jnp.concatenate([block_re, block_im], axis=1),
            jnp.concatenate([-block_im, block_re], axis=1),
        ],
        axis=0,
    )
    me = lax.axis_index("freq")
    high, low = split(mixing)
    mixing = jnp.concatenate([high, high, low], axis=1)
    src = lax.bitwise_xor(lax.axis_index("space"), k)
    lines = pl.ds(pl.multiple_of(me * 2 * width, 128), 2 * width)
    own = [first_ref[...], second_ref[...]]
    added = times_split(t_ref[src, lines], raw_ref[...])
    *other, rest = [ref[...] for ref in other_refs]
    other.append(rest + added)
    for place, parts in ((me, own), (1 - me, other)):
        out = times_split(mixing, jnp.concatenate(parts, axis=1))
        cols = pl.ds(pl.multiple_of(place * share, 128), share)
        for part in range(2):
            for f in range(local):
                at = part * width + f * NB
                modes_ref[f, part, :, cols] = out[at : at + NB]
    pad = jnp.zeros((width - NB, width), jnp.float32)
    turned_re = jnp.transpose(jnp.concatenate(low_re + [pad], axis=0))
    turned_im = jnp.transpose(jnp.concatenate(low_im + [pad], axis=0))
    for f in range(local):
        factor_ref[0, f] = turned_re[f * NB : (f + 1) * NB, :NB]
        factor_ref[1, f] = -turned_im[f * NB : (f + 1) * NB, :NB]


def finish(tables, n, k, total, first, second, raw, grams, others):
    local = tables.shape[1] // (4 * NB)
    share = first.shape[1] + second.shape[1]
    return pl.pallas_call(
        functools.partial(finish_kernel, n, k, total),
        out_shape=(
            jax.ShapeDtypeStruct((local, 2, NB, 2 * share), jnp.float32),
            jax.ShapeDtypeStruct((2, local, NB, NB), jnp.float32),
        ),
        compiler_params=pltpu.CompilerParams(vmem_limit_bytes=16 * MIB),
    )(tables, first, second, raw, grams, *others)


def partner(value, axis, size, step):
    return lax.ppermute(value, axis, [(i, i ^ step) for i in range(size)])


def on_device(snapshots, weights):
    n = lax.axis_size("space")
    tm_count = lax.axis_size("tm")
    freq_count = lax.axis_size("freq")
    blocks, local_times, columns = snapshots.shape
    rows = columns // n
    share = rows // freq_count

    tables = jnp.asarray(dft_blocks(n))

    last = n // 2
    early_rows = share - TRADED
    parts = ((0, early_rows), (early_rows, share - early_rows))
    targets = n * tm_count * freq_count

    def send(k, skip, size):
        sent = cut(snapshots, n, k, rows, skip, size)
        return partner(sent, "space", n, k)

    offsets = [k for k in range(n - 1, 0, -1) if k != last]
    pieces = [send(k, 0, share) for k in offsets]
    last_pieces = [send(last, skip, size) for skip, size in parts]
    before = early(tables, n, 0, cut(snapshots, n, 0, rows, 0, share))
    for k, piece in zip(offsets, pieces):
        before = early(tables, n, k, piece, before)
    weights = weights.reshape(1, rows)
    first, gram, *others = late(tables, n, last, 0, 2, before, last_pieces[0], weights)
    others = [partner(part, "freq", freq_count, 1) for part in others]
    raw, others = lax.optimization_barrier((last_pieces[1], others))
    second, gram = late(tables, n, last, early_rows, targets, before, raw, weights, gram)
    raw = partner(raw, "freq", freq_count, 1)
    gram, raw = lax.optimization_barrier((gram, raw))
    grams = lax.all_to_all(gram, ("space", "tm", "freq"), split_axis=0, concat_axis=0, tiled=True)
    total = rows * n * tm_count
    return finish(tables, n, last, total, first, second, raw, grams, others)


def solution(mesh):
    return jax.shard_map(
        on_device,
        mesh=mesh,
        in_specs=(P(None, "space", ("groups", "tm")), P(("groups", "tm", "space"))),
        out_specs=(
            P("freq", None, None, ("groups", "tm", "space")),
            P("groups", "freq", None, None),
        ),
        check_vma=False,
    )
```

```python
import functools

import numpy as np
import jax
import jax.numpy as jnp
from jax import lax
from jax.experimental import pallas as pl
from jax.experimental.pallas import tpu as pltpu
from jax.sharding import PartitionSpec as P

NB = 16
SEGMENT_FRAMES = 64
NF = 16
CUTS = 16
epsilon = 1e-05
MIB = 1024 * 1024
SMALL = pl.CostEstimate(flops=1, transcendentals=0, bytes_accessed=1)


def dft_blocks(groups):
    times = np.arange(SEGMENT_FRAMES)
    taper = 0.5 - 0.5 * np.cos(2.0 * np.pi * times / SEGMENT_FRAMES)
    taper = taper / np.sqrt(np.sum(taper * taper))
    bins = 1 + np.arange(NF)
    angles = 2.0 * np.pi * (bins[:, None] * times[None, :] % SEGMENT_FRAMES) / SEGMENT_FRAMES
    table = np.stack([np.cos(angles) * taper, -np.sin(angles) * taper])
    step = SEGMENT_FRAMES // groups
    table = table.reshape(2, 2, NF // 2, groups, step)
    spread = np.einsum("rhfgt,bc->ghrfbct", table, np.eye(NB))
    spread = spread.reshape(groups, 2 * NF * NB, NB * step).astype(np.float32)
    high = spread.astype(jnp.bfloat16)
    low = (spread - high.astype(np.float32)).astype(jnp.bfloat16)
    return np.concatenate([high, high, low], axis=2)


def split(x):
    high = x.astype(jnp.bfloat16)
    return high, (x - high.astype(jnp.float32)).astype(jnp.bfloat16)


def times_split(left, x):
    high, low = split(x)
    right = jnp.concatenate([high, low, high], axis=0)
    return jnp.dot(left, right, preferred_element_type=jnp.float32)


def rows_product(a, b):
    a_high, a_low = split(a)
    b_high, b_low = split(b)
    total = 0.0
    for x, y in ((a_high, b_high), (a_high, b_low), (a_low, b_high)):
        total = total + lax.dot_general(
            x, y, (((1,), (1,)), ((), ())), preferred_element_type=jnp.float32
        )
    return total


def cut_kernel(n, k, rows, skip, x_ref, o_ref, sem):
    size = o_ref.shape[2]
    to = lax.rem(lax.axis_index("space") + k, n)
    share = rows // 2
    start = pl.multiple_of(to * rows + lax.axis_index("freq") * share + skip, 128)
    part = NB // CUTS
    copies = []
    for i in range(CUTS):
        blocks = pl.ds(i * part, part)
        copies.append(
            pltpu.make_async_copy(
                x_ref.at[blocks, :, pl.ds(start, size)], o_ref.at[blocks], sem.at[i]
            )
        )
    for copy in copies:
        copy.start()
    for copy in copies:
        copy.wait()


def cut(snapshots, n, k, rows, skip, size):
    blocks, local_times, _ = snapshots.shape
    if local_times % 8 == 0:
        piece = pl.pallas_call(
            functools.partial(cut_kernel, n, k, rows, skip),
            out_shape=pltpu.VMEM((blocks, local_times, size), jnp.float32),
            in_specs=[pl.BlockSpec(memory_space=pltpu.HBM)],
            out_specs=pl.BlockSpec(memory_space=pltpu.VMEM),
            scratch_shapes=[pltpu.SemaphoreType.DMA((CUTS,))],
            compiler_params=pltpu.CompilerParams(vmem_limit_bytes=4 * MIB),
            cost_estimate=SMALL,
        )(pltpu.with_memory_space_constraint(snapshots, pltpu.HBM))
    else:
        to = lax.rem(lax.axis_index("space") + k, n)
        start = to * rows + lax.axis_index("freq") * (rows // 2) + skip
        piece = lax.dynamic_slice_in_dim(snapshots, start, size, axis=2)
    return piece.reshape(blocks * local_times, size)


def early_kernel(n, k, t_ref, x_ref, *refs):
    src = lax.rem(lax.axis_index("space") - k + n, n)
    part = times_split(t_ref[src], x_ref[...])
    refs[-1][...] = part if len(refs) == 1 else refs[0][...] + part


def early(tables, n, k, piece, *before):
    share = piece.shape[1]
    return pl.pallas_call(
        functools.partial(early_kernel, n, k),
        out_shape=jax.ShapeDtypeStruct((tables.shape[1], share), jnp.float32),
        compiler_params=pltpu.CompilerParams(vmem_limit_bytes=16 * MIB),
        cost_estimate=SMALL,
    )(tables, piece, *before)


def late_kernel(n, k, skip, t_ref, sum_ref, x_ref, w_ref, *refs):
    size = x_ref.shape[1]
    share = sum_ref.shape[1]
    cols = pl.ds(skip, size)
    at = lax.axis_index("freq") * share + skip
    weights = w_ref[:, pl.ds(pl.multiple_of(at, 128), size)]
    src = lax.rem(lax.axis_index("space") - k + n, n)
    spectra = sum_ref[:, cols] + times_split(t_ref[src], x_ref[...])
    half = spectra.shape[0] // 2
    width = half // 2
    local = width // NB
    line = lax.broadcasted_iota(jnp.int32, (width, width), 0) // NB
    lane = lax.broadcasted_iota(jnp.int32, (width, width), 1) // NB
    row = lax.broadcasted_iota(jnp.int32, (NB, width), 0)
    col = lax.broadcasted_iota(jnp.int32, (NB, width), 1) % NB
    first = lax.axis_index("freq") == 0
    halves = [spectra[:half], spectra[half:]]
    if skip:
        before_ref, own_ref, gram_ref = refs
    else:
        own_ref, gram_ref, other_ref, rest_ref = refs
        rest = sum_ref[:, size:]
        other_ref[...] = jnp.where(first, halves[1], halves[0])
        rest_ref[...] = jnp.where(first, rest[half:], rest[:half])
    own_ref[...] = jnp.where(first, halves[0], halves[1])
    packed = []
    for z in halves:
        full = rows_product(z * weights, z)
        gram_re = full[:width, :width] + full[width:, width:]
        gram_im = full[:width, width:] - full[width:, :width]
        both = []
        for part in (gram_re, gram_im):
            kept = jnp.where(line == lane, part, 0.0)
            both.append(jnp.sum(kept.reshape(local, NB, width), axis=0))
        packed.append(jnp.where(row >= col, both[0], both[1]))
    if skip:
        packed = [packed[h] + before_ref[h] for h in range(2)]
    for d in range(gram_ref.shape[0]):
        gram_ref[d] = packed[(d + 1) % 2 if skip else d]


def late(tables, n, k, skip, targets, partial_sum, piece, weights, *before):
    share = partial_sum.shape[1]
    half = tables.shape[1] // 2
    shapes = [(half, piece.shape[1]), (targets, NB, half // 2)]
    if not skip:
        shapes += [(half, piece.shape[1]), (half, share - piece.shape[1])]
    return pl.pallas_call(
        functools.partial(late_kernel, n, k, skip),
        out_shape=[jax.ShapeDtypeStruct(shape, jnp.float32) for shape in shapes],
        compiler_params=pltpu.CompilerParams(vmem_limit_bytes=16 * MIB),
        cost_estimate=SMALL,
    )(tables, partial_sum, piece, weights, *before)


def inv_sqrt(x):
    y = lax.rsqrt(x)
    return y * (1.5 - 0.5 * x * (y * y))


def finish_kernel(
    n, k, total, t_ref, first_ref, second_ref, other_ref, rest_ref, raw_ref, grams_ref, modes_ref, factor_ref
):
    local = modes_ref.shape[0]
    width = local * NB
    share = modes_ref.shape[3] // 2
    gram = jnp.sum(grams_ref[...], axis=0) / total
    row = lax.broadcasted_iota(jnp.int32, (NB, width), 0)
    col = lax.broadcasted_iota(jnp.int32, (NB, width), 1) % NB
    stacked = [jnp.where(col == j, gram, 0.0) for j in range(NB)]
    for j in range(NB):
        line = jnp.broadcast_to(gram[j : j + 1, :], (NB, width))
        stacked.append(jnp.where((col == row) & (row > j), -line, 0.0))
    stacked = jnp.concatenate(stacked, axis=0)
    group_r = lax.broadcasted_iota(jnp.int32, (width, width), 0) // NB
    group_c = lax.broadcasted_iota(jnp.int32, (width, width), 1) // NB
    same = group_r == group_c
    ones = jnp.where(same, 1.0, 0.0).astype(jnp.bfloat16)
    spread = jnp.zeros(stacked.shape, jnp.float32)
    rest = stacked
    for _ in range(3):
        piece = rest.astype(jnp.bfloat16)
        rest = rest - piece.astype(jnp.float32)
        spread = spread + jnp.dot(piece, ones, preferred_element_type=jnp.float32)
    col_re = [[spread[j * NB + 8 * h : j * NB + 8 * h + 8] for h in (0, 1)] for j in range(NB)]
    base = NB * NB
    col_im = [
        [spread[base + j * NB + 8 * h : base + j * NB + 8 * h + 8] for h in (0, 1)]
        for j in range(NB)
    ]
    rows = [lax.broadcasted_iota(jnp.int32, (8, width), 0) + 8 * h for h in (0, 1)]
    lanes = lax.broadcasted_iota(jnp.int32, (8, width), 1) % NB
    inv_re = [jnp.where(rows[h] == lanes, 1.0, 0.0) for h in (0, 1)]
    inv_im = [jnp.zeros((8, width), jnp.float32) for h in (0, 1)]
    low_re = [jnp.zeros((8, width), jnp.float32) for h in (0, 1)]
    low_im = [jnp.zeros((8, width), jnp.float32) for h in (0, 1)]

    def pick(halves, i):
        return jnp.broadcast_to(halves[i // 8][i % 8 : i % 8 + 1, :], (8, width))

    for p in range(NB):
        pivot = pick(col_re[p], p) + epsilon
        scale = inv_sqrt(pivot)
        coef_re, coef_im = [None, None], [None, None]
        for h in range(p // 8, 2):
            below = rows[h] > p
            coef_re[h] = jnp.where(below, col_re[p][h] * scale, 0.0)
            coef_im[h] = jnp.where(below, col_im[p][h] * scale, 0.0)
            here = lanes == p
            diag = jnp.where(rows[h] == p, pivot * scale, coef_re[h])
            low_re[h] = jnp.where(here, diag, low_re[h])
            low_im[h] = jnp.where(here, coef_im[h], low_im[h])
        for j in range(p + 1, NB):
            a_re, a_im = pick(coef_re, j), pick(coef_im, j)
            for h in range(j // 8, 2):
                col_re[j][h] = col_re[j][h] - (coef_re[h] * a_re + coef_im[h] * a_im)
                col_im[j][h] = col_im[j][h] - (coef_im[h] * a_re - coef_re[h] * a_im)
        line_re = pick(inv_re, p) * scale
        line_im = pick(inv_im, p) * scale
        for h in range(p // 8, 2):
            at = rows[h] == p
            new_re = inv_re[h] - (coef_re[h] * line_re - coef_im[h] * line_im)
            new_im = inv_im[h] - (coef_re[h] * line_im + coef_im[h] * line_re)
            inv_re[h] = jnp.where(at, line_re, new_re)
            inv_im[h] = jnp.where(at, line_im, new_im)

    block_re = jnp.where(same, jnp.concatenate(inv_re * local, axis=0), 0.0)
    block_im = jnp.where(same, jnp.concatenate(inv_im * local, axis=0), 0.0)
    mixing = jnp.concatenate(
        [
            jnp.concatenate([block_re, block_im], axis=1),
            jnp.concatenate([-block_im, block_re], axis=1),
        ],
        axis=0,
    )
    me = lax.axis_index("freq")
    high, low = split(mixing)
    mixing = jnp.concatenate([high, high, low], axis=1)
    src = lax.rem(lax.axis_index("space") - k + n, n)
    lines = pl.ds(pl.multiple_of(me * 2 * width, 128), 2 * width)
    own = [first_ref[...], second_ref[...]]
    added = times_split(t_ref[src, lines], raw_ref[...])
    other = [other_ref[...], rest_ref[...] + added]
    for place, parts in ((me, own), (1 - me, other)):
        out = times_split(mixing, jnp.concatenate(parts, axis=1))
        cols = pl.ds(pl.multiple_of(place * share, 128), share)
        for part in range(2):
            for f in range(local):
                at = part * width + f * NB
                modes_ref[f, part, :, cols] = out[at : at + NB]
    pad = jnp.zeros((width - NB, width), jnp.float32)
    turned_re = jnp.transpose(jnp.concatenate(low_re + [pad], axis=0))
    turned_im = jnp.transpose(jnp.concatenate(low_im + [pad], axis=0))
    for f in range(local):
        factor_ref[0, f] = turned_re[f * NB : (f + 1) * NB, :NB]
        factor_ref[1, f] = -turned_im[f * NB : (f + 1) * NB, :NB]


def finish(tables, n, k, total, first, second, other, rest, raw, grams):
    local = tables.shape[1] // (4 * NB)
    share = other.shape[1] + rest.shape[1]
    return pl.pallas_call(
        functools.partial(finish_kernel, n, k, total),
        out_shape=(
            jax.ShapeDtypeStruct((local, 2, NB, 2 * share), jnp.float32),
            jax.ShapeDtypeStruct((2, local, NB, NB), jnp.float32),
        ),
        compiler_params=pltpu.CompilerParams(vmem_limit_bytes=16 * MIB),
    )(tables, first, second, other, rest, raw, grams)


def partner(value, axis, size, step):
    return lax.ppermute(value, axis, [(i, i ^ step) for i in range(size)])


def on_device(snapshots, weights):
    n = lax.axis_size("space")
    tm_count = lax.axis_size("tm")
    freq_count = lax.axis_size("freq")
    blocks, local_times, columns = snapshots.shape
    rows = columns // n
    share = rows // freq_count

    tables = jnp.asarray(dft_blocks(n))

    last = n // 2
    early_rows = share // 2
    parts = ((0, early_rows), (early_rows, share - early_rows))
    targets = n * tm_count * freq_count

    def send(k, skip, size):
        sent = cut(snapshots, n, k, rows, skip, size)
        return lax.ppermute(sent, "space", [(i, (i + k) % n) for i in range(n)])

    offsets = [k for k in range(1, n) if k != last]
    pieces = [send(k, 0, share) for k in offsets]
    last_pieces = [send(last, skip, size) for skip, size in parts]
    before = early(tables, n, 0, cut(snapshots, n, 0, rows, 0, share))
    for k, piece in zip(offsets, pieces):
        before = early(tables, n, k, piece, before)
    weights = weights.reshape(1, rows)
    first, gram, other, rest = late(tables, n, last, 0, 2, before, last_pieces[0], weights)
    other, rest = partner(other, "freq", freq_count, 1), partner(rest, "freq", freq_count, 1)
    raw, other, rest = lax.optimization_barrier((last_pieces[1], other, rest))
    second, gram = late(tables, n, last, early_rows, targets, before, raw, weights, gram)
    raw = partner(raw, "freq", freq_count, 1)
    gram, raw = lax.optimization_barrier((gram, raw))
    grams = lax.all_to_all(
        gram,
        ("space", "tm", "freq"),
        split_axis=0,
        concat_axis=0,
        axis_index_groups=[list(range(targets - 1, -1, -1))],
        tiled=True,
    )
    total = rows * n * tm_count
    return finish(tables, n, last, total, first, second, other, rest, raw, grams)


def solution(mesh):
    return jax.shard_map(
        on_device,
        mesh=mesh,
        in_specs=(P(None, "space", ("groups", "tm")), P(("groups", "tm", "space"))),
        out_specs=(
            P("freq", None, None, ("groups", "tm", "space")),
            P("groups", "freq", None, None),
        ),
        check_vma=False,
    )
```

```python
import functools

import numpy as np
import jax
import jax.numpy as jnp
from jax import lax
from jax.experimental import pallas as pl
from jax.experimental.pallas import tpu as pltpu
from jax.sharding import PartitionSpec as P

NB = 16
SEGMENT_FRAMES = 64
NF = 16
CUTS = 16
epsilon = 1e-05
MIB = 1024 * 1024
SMALL = pl.CostEstimate(flops=1, transcendentals=0, bytes_accessed=1)


def dft_blocks(groups):
    times = np.arange(SEGMENT_FRAMES)
    taper = 0.5 - 0.5 * np.cos(2.0 * np.pi * times / SEGMENT_FRAMES)
    taper = taper / np.sqrt(np.sum(taper * taper))
    bins = 1 + np.arange(NF)
    angles = 2.0 * np.pi * (bins[:, None] * times[None, :] % SEGMENT_FRAMES) / SEGMENT_FRAMES
    table = np.stack([np.cos(angles) * taper, -np.sin(angles) * taper])
    step = SEGMENT_FRAMES // groups
    table = table.reshape(2, 2, NF // 2, groups, step)
    spread = np.einsum("rhfgt,bc->ghrfbct", table, np.eye(NB))
    spread = spread.reshape(groups, 2 * NF * NB, NB * step).astype(np.float32)
    high = spread.astype(jnp.bfloat16)
    low = (spread - high.astype(np.float32)).astype(jnp.bfloat16)
    return np.concatenate([high, high, low], axis=2)


def split(x):
    high = x.astype(jnp.bfloat16)
    return high, (x - high.astype(jnp.float32)).astype(jnp.bfloat16)


def times_split(left, x):
    high, low = split(x)
    right = jnp.concatenate([high, low, high], axis=0)
    return jnp.dot(left, right, preferred_element_type=jnp.float32)


def rows_product(a, b):
    a_high, a_low = split(a)
    b_high, b_low = split(b)
    total = 0.0
    for x, y in ((a_high, b_high), (a_high, b_low), (a_low, b_high)):
        total = total + lax.dot_general(
            x, y, (((1,), (1,)), ((), ())), preferred_element_type=jnp.float32
        )
    return total


def cut_kernel(n, k, rows, skip, x_ref, o_ref, sem):
    size = o_ref.shape[2]
    to = lax.bitwise_xor(lax.axis_index("space"), k)
    share = rows // 2
    start = pl.multiple_of(to * rows + lax.axis_index("freq") * share + skip, 128)
    part = NB // CUTS
    copies = []
    for i in range(CUTS):
        blocks = pl.ds(i * part, part)
        copies.append(
            pltpu.make_async_copy(
                x_ref.at[blocks, :, pl.ds(start, size)], o_ref.at[blocks], sem.at[i]
            )
        )
    for copy in copies:
        copy.start()
    for copy in copies:
        copy.wait()


def cut(snapshots, n, k, rows, skip, size):
    blocks, local_times, _ = snapshots.shape
    if local_times % 8 == 0:
        piece = pl.pallas_call(
            functools.partial(cut_kernel, n, k, rows, skip),
            out_shape=pltpu.VMEM((blocks, local_times, size), jnp.float32),
            in_specs=[pl.BlockSpec(memory_space=pltpu.HBM)],
            out_specs=pl.BlockSpec(memory_space=pltpu.VMEM),
            scratch_shapes=[pltpu.SemaphoreType.DMA((CUTS,))],
            compiler_params=pltpu.CompilerParams(vmem_limit_bytes=4 * MIB),
            cost_estimate=SMALL,
        )(pltpu.with_memory_space_constraint(snapshots, pltpu.HBM))
    else:
        to = lax.bitwise_xor(lax.axis_index("space"), k)
        start = to * rows + lax.axis_index("freq") * (rows // 2) + skip
        piece = lax.dynamic_slice_in_dim(snapshots, start, size, axis=2)
    return piece.reshape(blocks * local_times, size)


def early_kernel(n, k, t_ref, x_ref, *refs):
    src = lax.bitwise_xor(lax.axis_index("space"), k)
    part = times_split(t_ref[src], x_ref[...])
    refs[-1][...] = part if len(refs) == 1 else refs[0][...] + part


def early(tables, n, k, piece, *before):
    share = piece.shape[1]
    return pl.pallas_call(
        functools.partial(early_kernel, n, k),
        out_shape=jax.ShapeDtypeStruct((tables.shape[1], share), jnp.float32),
        compiler_params=pltpu.CompilerParams(vmem_limit_bytes=16 * MIB),
        cost_estimate=SMALL,
    )(tables, piece, *before)


def late_kernel(n, k, skip, t_ref, sum_ref, x_ref, w_ref, *refs):
    size = x_ref.shape[1]
    share = sum_ref.shape[1]
    cols = pl.ds(skip, size)
    at = lax.axis_index("freq") * share + skip
    weights = w_ref[:, pl.ds(pl.multiple_of(at, 128), size)]
    src = lax.bitwise_xor(lax.axis_index("space"), k)
    spectra = sum_ref[:, cols] + times_split(t_ref[src], x_ref[...])
    half = spectra.shape[0] // 2
    width = half // 2
    local = width // NB
    line = lax.broadcasted_iota(jnp.int32, (width, width), 0) // NB
    lane = lax.broadcasted_iota(jnp.int32, (width, width), 1) // NB
    row = lax.broadcasted_iota(jnp.int32, (NB, width), 0)
    col = lax.broadcasted_iota(jnp.int32, (NB, width), 1) % NB
    first = lax.axis_index("freq") == 0
    halves = [spectra[:half], spectra[half:]]
    if skip:
        before_ref, own_ref, gram_ref = refs
    else:
        own_ref, gram_ref, other_ref, rest_ref = refs
        rest = sum_ref[:, size:]
        other_ref[...] = jnp.where(first, halves[1], halves[0])
        rest_ref[...] = jnp.where(first, rest[half:], rest[:half])
    own_ref[...] = jnp.where(first, halves[0], halves[1])
    packed = []
    for z in halves:
        full = rows_product(z * weights, z)
        gram_re = full[:width, :width] + full[width:, width:]
        gram_im = full[:width, width:] - full[width:, :width]
        both = []
        for part in (gram_re, gram_im):
            kept = jnp.where(line == lane, part, 0.0)
            both.append(jnp.sum(kept.reshape(local, NB, width), axis=0))
        packed.append(jnp.where(row >= col, both[0], both[1]))
    if skip:
        packed = [packed[h] + before_ref[h] for h in range(2)]
    for d in range(gram_ref.shape[0]):
        gram_ref[d] = packed[(d + 1) % 2 if skip else d]


def late(tables, n, k, skip, targets, partial_sum, piece, weights, *before):
    share = partial_sum.shape[1]
    half = tables.shape[1] // 2
    shapes = [(half, piece.shape[1]), (targets, NB, half // 2)]
    if not skip:
        shapes += [(half, piece.shape[1]), (half, share - piece.shape[1])]
    return pl.pallas_call(
        functools.partial(late_kernel, n, k, skip),
        out_shape=[jax.ShapeDtypeStruct(shape, jnp.float32) for shape in shapes],
        compiler_params=pltpu.CompilerParams(vmem_limit_bytes=16 * MIB),
        cost_estimate=SMALL,
    )(tables, partial_sum, piece, weights, *before)


def inv_sqrt(x):
    y = lax.rsqrt(x)
    return y * (1.5 - 0.5 * x * (y * y))


def finish_kernel(
    n, k, total, t_ref, first_ref, second_ref, other_ref, rest_ref, raw_ref, grams_ref, modes_ref, factor_ref
):
    local = modes_ref.shape[0]
    width = local * NB
    share = modes_ref.shape[3] // 2
    gram = jnp.sum(grams_ref[...], axis=0) / total
    row = lax.broadcasted_iota(jnp.int32, (NB, width), 0)
    col = lax.broadcasted_iota(jnp.int32, (NB, width), 1) % NB
    stacked = [jnp.where(col == j, gram, 0.0) for j in range(NB)]
    for j in range(NB):
        line = jnp.broadcast_to(gram[j : j + 1, :], (NB, width))
        stacked.append(jnp.where((col == row) & (row > j), -line, 0.0))
    stacked = jnp.concatenate(stacked, axis=0)
    group_r = lax.broadcasted_iota(jnp.int32, (width, width), 0) // NB
    group_c = lax.broadcasted_iota(jnp.int32, (width, width), 1) // NB
    same = group_r == group_c
    ones = jnp.where(same, 1.0, 0.0).astype(jnp.bfloat16)
    spread = jnp.zeros(stacked.shape, jnp.float32)
    rest = stacked
    for _ in range(3):
        piece = rest.astype(jnp.bfloat16)
        rest = rest - piece.astype(jnp.float32)
        spread = spread + jnp.dot(piece, ones, preferred_element_type=jnp.float32)
    col_re = [[spread[j * NB + 8 * h : j * NB + 8 * h + 8] for h in (0, 1)] for j in range(NB)]
    base = NB * NB
    col_im = [
        [spread[base + j * NB + 8 * h : base + j * NB + 8 * h + 8] for h in (0, 1)]
        for j in range(NB)
    ]
    rows = [lax.broadcasted_iota(jnp.int32, (8, width), 0) + 8 * h for h in (0, 1)]
    lanes = lax.broadcasted_iota(jnp.int32, (8, width), 1) % NB
    inv_re = [jnp.where(rows[h] == lanes, 1.0, 0.0) for h in (0, 1)]
    inv_im = [jnp.zeros((8, width), jnp.float32) for h in (0, 1)]
    low_re = [jnp.zeros((8, width), jnp.float32) for h in (0, 1)]
    low_im = [jnp.zeros((8, width), jnp.float32) for h in (0, 1)]

    def pick(halves, i):
        return jnp.broadcast_to(halves[i // 8][i % 8 : i % 8 + 1, :], (8, width))

    for p in range(NB):
        pivot = pick(col_re[p], p) + epsilon
        scale = inv_sqrt(pivot)
        coef_re, coef_im = [None, None], [None, None]
        for h in range(p // 8, 2):
            below = rows[h] > p
            coef_re[h] = jnp.where(below, col_re[p][h] * scale, 0.0)
            coef_im[h] = jnp.where(below, col_im[p][h] * scale, 0.0)
            here = lanes == p
            diag = jnp.where(rows[h] == p, pivot * scale, coef_re[h])
            low_re[h] = jnp.where(here, diag, low_re[h])
            low_im[h] = jnp.where(here, coef_im[h], low_im[h])
        for j in range(p + 1, NB):
            a_re, a_im = pick(coef_re, j), pick(coef_im, j)
            for h in range(j // 8, 2):
                col_re[j][h] = col_re[j][h] - (coef_re[h] * a_re + coef_im[h] * a_im)
                col_im[j][h] = col_im[j][h] - (coef_im[h] * a_re - coef_re[h] * a_im)
        line_re = pick(inv_re, p) * scale
        line_im = pick(inv_im, p) * scale
        for h in range(p // 8, 2):
            at = rows[h] == p
            new_re = inv_re[h] - (coef_re[h] * line_re - coef_im[h] * line_im)
            new_im = inv_im[h] - (coef_re[h] * line_im + coef_im[h] * line_re)
            inv_re[h] = jnp.where(at, line_re, new_re)
            inv_im[h] = jnp.where(at, line_im, new_im)

    block_re = jnp.where(same, jnp.concatenate(inv_re * local, axis=0), 0.0)
    block_im = jnp.where(same, jnp.concatenate(inv_im * local, axis=0), 0.0)
    mixing = jnp.concatenate(
        [
            jnp.concatenate([block_re, block_im], axis=1),
            jnp.concatenate([-block_im, block_re], axis=1),
        ],
        axis=0,
    )
    me = lax.axis_index("freq")
    high, low = split(mixing)
    mixing = jnp.concatenate([high, high, low], axis=1)
    src = lax.bitwise_xor(lax.axis_index("space"), k)
    lines = pl.ds(pl.multiple_of(me * 2 * width, 128), 2 * width)
    own = [first_ref[...], second_ref[...]]
    added = times_split(t_ref[src, lines], raw_ref[...])
    other = [other_ref[...], rest_ref[...] + added]
    for place, parts in ((me, own), (1 - me, other)):
        out = times_split(mixing, jnp.concatenate(parts, axis=1))
        cols = pl.ds(pl.multiple_of(place * share, 128), share)
        for part in range(2):
            for f in range(local):
                at = part * width + f * NB
                modes_ref[f, part, :, cols] = out[at : at + NB]
    pad = jnp.zeros((width - NB, width), jnp.float32)
    turned_re = jnp.transpose(jnp.concatenate(low_re + [pad], axis=0))
    turned_im = jnp.transpose(jnp.concatenate(low_im + [pad], axis=0))
    for f in range(local):
        factor_ref[0, f] = turned_re[f * NB : (f + 1) * NB, :NB]
        factor_ref[1, f] = -turned_im[f * NB : (f + 1) * NB, :NB]


def finish(tables, n, k, total, first, second, other, rest, raw, grams):
    local = tables.shape[1] // (4 * NB)
    share = other.shape[1] + rest.shape[1]
    return pl.pallas_call(
        functools.partial(finish_kernel, n, k, total),
        out_shape=(
            jax.ShapeDtypeStruct((local, 2, NB, 2 * share), jnp.float32),
            jax.ShapeDtypeStruct((2, local, NB, NB), jnp.float32),
        ),
        compiler_params=pltpu.CompilerParams(vmem_limit_bytes=16 * MIB),
    )(tables, first, second, other, rest, raw, grams)


def partner(value, axis, size, step):
    return lax.ppermute(value, axis, [(i, i ^ step) for i in range(size)])


def on_device(snapshots, weights):
    n = lax.axis_size("space")
    tm_count = lax.axis_size("tm")
    freq_count = lax.axis_size("freq")
    blocks, local_times, columns = snapshots.shape
    rows = columns // n
    share = rows // freq_count

    tables = jnp.asarray(dft_blocks(n))

    last = n // 2
    early_rows = share // 2
    parts = ((0, early_rows), (early_rows, share - early_rows))
    targets = n * tm_count * freq_count

    def send(k, skip, size):
        sent = cut(snapshots, n, k, rows, skip, size)
        return partner(sent, "space", n, k)

    offsets = [k for k in range(n - 1, 0, -1) if k != last]
    pieces = [send(k, 0, share) for k in offsets]
    last_pieces = [send(last, skip, size) for skip, size in parts]
    before = early(tables, n, 0, cut(snapshots, n, 0, rows, 0, share))
    for k, piece in zip(offsets, pieces):
        before = early(tables, n, k, piece, before)
    weights = weights.reshape(1, rows)
    first, gram, other, rest = late(tables, n, last, 0, 2, before, last_pieces[0], weights)
    other, rest = partner(other, "freq", freq_count, 1), partner(rest, "freq", freq_count, 1)
    raw, other, rest = lax.optimization_barrier((last_pieces[1], other, rest))
    second, gram = late(tables, n, last, early_rows, targets, before, raw, weights, gram)
    raw = partner(raw, "freq", freq_count, 1)
    gram, raw = lax.optimization_barrier((gram, raw))
    grams = lax.all_to_all(
        gram,
        ("space", "tm", "freq"),
        split_axis=0,
        concat_axis=0,
        axis_index_groups=[list(range(targets - 1, -1, -1))],
        tiled=True,
    )
    total = rows * n * tm_count
    return finish(tables, n, last, total, first, second, other, rest, raw, grams)


def solution(mesh):
    return jax.shard_map(
        on_device,
        mesh=mesh,
        in_specs=(P(None, "space", ("groups", "tm")), P(("groups", "tm", "space"))),
        out_specs=(
            P("freq", None, None, ("groups", "tm", "space")),
            P("groups", "freq", None, None),
        ),
        check_vma=False,
    )
```

```python
import functools

import numpy as np
import jax
import jax.numpy as jnp
from jax import lax
from jax.experimental import pallas as pl
from jax.experimental.pallas import tpu as pltpu
from jax.sharding import PartitionSpec as P

NB = 16
SEGMENT_FRAMES = 64
NF = 16
CUTS = 4
epsilon = 1e-05
MIB = 1024 * 1024
SMALL = pl.CostEstimate(flops=1, transcendentals=0, bytes_accessed=1)


def dft_blocks(groups):
    times = np.arange(SEGMENT_FRAMES)
    taper = 0.5 - 0.5 * np.cos(2.0 * np.pi * times / SEGMENT_FRAMES)
    taper = taper / np.sqrt(np.sum(taper * taper))
    bins = 1 + np.arange(NF)
    angles = 2.0 * np.pi * (bins[:, None] * times[None, :] % SEGMENT_FRAMES) / SEGMENT_FRAMES
    table = np.stack([np.cos(angles) * taper, -np.sin(angles) * taper])
    step = SEGMENT_FRAMES // groups
    table = table.reshape(2, 2, NF // 2, groups, step)
    spread = np.einsum("rhfgt,bc->ghrfbct", table, np.eye(NB))
    spread = spread.reshape(groups, 2 * NF * NB, NB * step).astype(np.float32)
    high = spread.astype(jnp.bfloat16)
    low = (spread - high.astype(np.float32)).astype(jnp.bfloat16)
    return np.concatenate([high, high, low], axis=2)


def split(x):
    high = x.astype(jnp.bfloat16)
    return high, (x - high.astype(jnp.float32)).astype(jnp.bfloat16)


def times_split(left, x):
    high, low = split(x)
    right = jnp.concatenate([high, low, high], axis=0)
    return jnp.dot(left, right, preferred_element_type=jnp.float32)


def rows_product(a, b):
    a_high, a_low = split(a)
    b_high, b_low = split(b)
    total = 0.0
    for x, y in ((a_low, b_low), (a_low, b_high), (a_high, b_low), (a_high, b_high)):
        total = total + lax.dot_general(
            x, y, (((1,), (1,)), ((), ())), preferred_element_type=jnp.float32
        )
    return total


def cut_kernel(n, k, rows, skip, x_ref, o_ref, sem):
    size = o_ref.shape[2]
    to = lax.bitwise_xor(lax.axis_index("space"), k)
    share = rows // 2
    start = pl.multiple_of(to * rows + lax.axis_index("freq") * share + skip, 128)
    part = NB // CUTS
    copies = []
    for i in range(CUTS):
        blocks = pl.ds(i * part, part)
        copies.append(
            pltpu.make_async_copy(
                x_ref.at[blocks, :, pl.ds(start, size)], o_ref.at[blocks], sem.at[i]
            )
        )
    for copy in copies:
        copy.start()
    for copy in copies:
        copy.wait()


def cut(snapshots, n, k, rows, skip, size):
    blocks, local_times, _ = snapshots.shape
    if local_times % 8 == 0:
        piece = pl.pallas_call(
            functools.partial(cut_kernel, n, k, rows, skip),
            out_shape=pltpu.VMEM((blocks, local_times, size), jnp.float32),
            in_specs=[pl.BlockSpec(memory_space=pltpu.HBM)],
            out_specs=pl.BlockSpec(memory_space=pltpu.VMEM),
            scratch_shapes=[pltpu.SemaphoreType.DMA((CUTS,))],
            compiler_params=pltpu.CompilerParams(vmem_limit_bytes=4 * MIB),
            cost_estimate=SMALL,
        )(pltpu.with_memory_space_constraint(snapshots, pltpu.HBM))
    else:
        to = lax.bitwise_xor(lax.axis_index("space"), k)
        start = to * rows + lax.axis_index("freq") * (rows // 2) + skip
        piece = lax.dynamic_slice_in_dim(snapshots, start, size, axis=2)
    return piece.reshape(blocks * local_times, size)


def early_kernel(n, k, t_ref, x_ref, *refs):
    src = lax.bitwise_xor(lax.axis_index("space"), k)
    part = times_split(t_ref[src], x_ref[...])
    refs[-1][...] = part if len(refs) == 1 else refs[0][...] + part


def early(tables, n, k, piece, *before):
    share = piece.shape[1]
    return pl.pallas_call(
        functools.partial(early_kernel, n, k),
        out_shape=jax.ShapeDtypeStruct((tables.shape[1], share), jnp.float32),
        compiler_params=pltpu.CompilerParams(vmem_limit_bytes=16 * MIB),
        cost_estimate=SMALL,
    )(tables, piece, *before)


def late_kernel(n, k, skip, t_ref, sum_ref, x_ref, w_ref, *refs):
    size = x_ref.shape[1]
    share = sum_ref.shape[1]
    cols = pl.ds(skip, size)
    at = lax.axis_index("freq") * share + skip
    weights = w_ref[:, pl.ds(pl.multiple_of(at, 128), size)]
    src = lax.bitwise_xor(lax.axis_index("space"), k)
    spectra = sum_ref[:, cols] + times_split(t_ref[src], x_ref[...])
    half = spectra.shape[0] // 2
    width = half // 2
    local = width // NB
    line = lax.broadcasted_iota(jnp.int32, (width, width), 0) // NB
    lane = lax.broadcasted_iota(jnp.int32, (width, width), 1) // NB
    row = lax.broadcasted_iota(jnp.int32, (NB, width), 0)
    col = lax.broadcasted_iota(jnp.int32, (NB, width), 1) % NB
    first = lax.axis_index("freq") == 0
    halves = [spectra[:half], spectra[half:]]
    if skip:
        before_ref, own_ref, gram_ref, lent_ref = refs
    else:
        own_ref, gram_ref, other_ref, rest_ref = refs
        rest = sum_ref[:, size:]
        other_ref[...] = jnp.where(first, halves[1], halves[0])
        rest_ref[...] = jnp.where(first, rest[half:], rest[:half])
    own_ref[...] = jnp.where(first, halves[0], halves[1])
    packed = []
    for z in halves:
        full = rows_product(z * weights, z)
        gram_re = full[:width, :width] + full[width:, width:]
        gram_im = full[:width, width:] - full[width:, :width]
        both = []
        for part in (gram_re, gram_im):
            kept = jnp.where(line == lane, part, 0.0)
            both.append(jnp.sum(kept.reshape(local, NB, width), axis=0))
        packed.append(jnp.where(row >= col, both[0], both[1]))
    if skip:
        packed = [packed[h] + before_ref[h] for h in range(2)]
    if skip:
        gram_ref[...] = jnp.where(first, packed[0], packed[1])
        lent_ref[...] = jnp.where(first, packed[1], packed[0])
    else:
        for h in range(2):
            gram_ref[h] = packed[h]


def late(tables, n, k, skip, partial_sum, piece, weights, *before):
    share = partial_sum.shape[1]
    half = tables.shape[1] // 2
    gram = (NB, half // 2)
    shapes = [(half, piece.shape[1])]
    if skip:
        shapes += [gram, gram]
    else:
        shapes += [(2, *gram), (half, piece.shape[1]), (half, share - piece.shape[1])]
    return pl.pallas_call(
        functools.partial(late_kernel, n, k, skip),
        out_shape=[jax.ShapeDtypeStruct(shape, jnp.float32) for shape in shapes],
        compiler_params=pltpu.CompilerParams(vmem_limit_bytes=16 * MIB),
        cost_estimate=SMALL,
    )(tables, partial_sum, piece, weights, *before)


def inv_sqrt(x):
    y = lax.rsqrt(x)
    return y * (1.5 - 0.5 * x * (y * y))


def finish_kernel(
    n, k, total, t_ref, first_ref, second_ref, other_ref, rest_ref, raw_ref, grams_ref, modes_ref, factor_ref
):
    local = modes_ref.shape[0]
    width = local * NB
    share = modes_ref.shape[3] // 2
    gram = jnp.sum(grams_ref[...], axis=0) / total
    row = lax.broadcasted_iota(jnp.int32, (NB, width), 0)
    col = lax.broadcasted_iota(jnp.int32, (NB, width), 1) % NB
    stacked = [jnp.where(col == j, gram, 0.0) for j in range(NB)]
    for j in range(NB):
        line = jnp.broadcast_to(gram[j : j + 1, :], (NB, width))
        stacked.append(jnp.where((col == row) & (row > j), -line, 0.0))
    stacked = jnp.concatenate(stacked, axis=0)
    group_r = lax.broadcasted_iota(jnp.int32, (width, width), 0) // NB
    group_c = lax.broadcasted_iota(jnp.int32, (width, width), 1) // NB
    same = group_r == group_c
    ones = jnp.where(same, 1.0, 0.0).astype(jnp.bfloat16)
    spread = jnp.zeros(stacked.shape, jnp.float32)
    rest = stacked
    for _ in range(3):
        piece = rest.astype(jnp.bfloat16)
        rest = rest - piece.astype(jnp.float32)
        spread = spread + jnp.dot(piece, ones, preferred_element_type=jnp.float32)
    col_re = [[spread[j * NB + 8 * h : j * NB + 8 * h + 8] for h in (0, 1)] for j in range(NB)]
    base = NB * NB
    col_im = [
        [spread[base + j * NB + 8 * h : base + j * NB + 8 * h + 8] for h in (0, 1)]
        for j in range(NB)
    ]
    rows = [lax.broadcasted_iota(jnp.int32, (8, width), 0) + 8 * h for h in (0, 1)]
    lanes = lax.broadcasted_iota(jnp.int32, (8, width), 1) % NB
    inv_re = [jnp.where(rows[h] == lanes, 1.0, 0.0) for h in (0, 1)]
    inv_im = [jnp.zeros((8, width), jnp.float32) for h in (0, 1)]
    low_re = [jnp.zeros((8, width), jnp.float32) for h in (0, 1)]
    low_im = [jnp.zeros((8, width), jnp.float32) for h in (0, 1)]

    def pick(halves, i):
        return jnp.broadcast_to(halves[i // 8][i % 8 : i % 8 + 1, :], (8, width))

    for p in range(NB):
        pivot = pick(col_re[p], p) + epsilon
        scale = inv_sqrt(pivot)
        coef_re, coef_im = [None, None], [None, None]
        for h in range(p // 8, 2):
            below = rows[h] > p
            coef_re[h] = jnp.where(below, col_re[p][h] * scale, 0.0)
            coef_im[h] = jnp.where(below, col_im[p][h] * scale, 0.0)
            here = lanes == p
            diag = jnp.where(rows[h] == p, pivot * scale, coef_re[h])
            low_re[h] = jnp.where(here, diag, low_re[h])
            low_im[h] = jnp.where(here, coef_im[h], low_im[h])
        for j in range(p + 1, NB):
            a_re, a_im = pick(coef_re, j), pick(coef_im, j)
            for h in range(j // 8, 2):
                col_re[j][h] = col_re[j][h] - (coef_re[h] * a_re + coef_im[h] * a_im)
                col_im[j][h] = col_im[j][h] - (coef_im[h] * a_re - coef_re[h] * a_im)
        line_re = pick(inv_re, p) * scale
        line_im = pick(inv_im, p) * scale
        for h in range(p // 8, 2):
            at = rows[h] == p
            new_re = inv_re[h] - (coef_re[h] * line_re - coef_im[h] * line_im)
            new_im = inv_im[h] - (coef_re[h] * line_im + coef_im[h] * line_re)
            inv_re[h] = jnp.where(at, line_re, new_re)
            inv_im[h] = jnp.where(at, line_im, new_im)

    block_re = jnp.where(same, jnp.concatenate(inv_re * local, axis=0), 0.0)
    block_im = jnp.where(same, jnp.concatenate(inv_im * local, axis=0), 0.0)
    mixing = jnp.concatenate(
        [
            jnp.concatenate([block_re, block_im], axis=1),
            jnp.concatenate([-block_im, block_re], axis=1),
        ],
        axis=0,
    )
    me = lax.axis_index("freq")
    high, low = split(mixing)
    mixing = jnp.concatenate([high, high, low], axis=1)
    src = lax.bitwise_xor(lax.axis_index("space"), k)
    lines = pl.ds(pl.multiple_of(me * 2 * width, 128), 2 * width)
    own = [first_ref[...], second_ref[...]]
    added = times_split(t_ref[src, lines], raw_ref[...])
    other = [other_ref[...], rest_ref[...] + added]
    for place, parts in ((me, own), (1 - me, other)):
        out = times_split(mixing, jnp.concatenate(parts, axis=1))
        cols = pl.ds(pl.multiple_of(place * share, 128), share)
        for part in range(2):
            for f in range(local):
                at = part * width + f * NB
                modes_ref[f, part, :, cols] = out[at : at + NB]
    pad = jnp.zeros((width - NB, width), jnp.float32)
    turned_re = jnp.transpose(jnp.concatenate(low_re + [pad], axis=0))
    turned_im = jnp.transpose(jnp.concatenate(low_im + [pad], axis=0))
    for f in range(local):
        factor_ref[0, f] = turned_re[f * NB : (f + 1) * NB, :NB]
        factor_ref[1, f] = -turned_im[f * NB : (f + 1) * NB, :NB]


def finish(tables, n, k, total, first, second, other, rest, raw, grams):
    local = tables.shape[1] // (4 * NB)
    share = other.shape[1] + rest.shape[1]
    return pl.pallas_call(
        functools.partial(finish_kernel, n, k, total),
        out_shape=(
            jax.ShapeDtypeStruct((local, 2, NB, 2 * share), jnp.float32),
            jax.ShapeDtypeStruct((2, local, NB, NB), jnp.float32),
        ),
        compiler_params=pltpu.CompilerParams(vmem_limit_bytes=16 * MIB),
    )(tables, first, second, other, rest, raw, grams)


def partner(value, axis, size, step):
    return lax.ppermute(value, axis, [(i, i ^ step) for i in range(size)])


def on_device(snapshots, weights):
    n = lax.axis_size("space")
    tm_count = lax.axis_size("tm")
    freq_count = lax.axis_size("freq")
    blocks, local_times, columns = snapshots.shape
    rows = columns // n
    share = rows // freq_count

    tables = jnp.asarray(dft_blocks(n))

    last = n // 2
    early_rows = share // 2
    parts = ((0, early_rows), (early_rows, share - early_rows))
    targets = n * tm_count

    def send(k, skip, size):
        sent = cut(snapshots, n, k, rows, skip, size)
        return partner(sent, "space", n, k)

    offsets = [k for k in range(n - 1, 0, -1) if k != last]
    pieces = [send(k, 0, share) for k in offsets]
    last_pieces = [send(last, skip, size) for skip, size in parts]
    before = early(tables, n, 0, cut(snapshots, n, 0, rows, 0, share))
    for k, piece in zip(offsets, pieces):
        before = early(tables, n, k, piece, before)
    weights = weights.reshape(1, rows)
    first, gram, other, rest = late(tables, n, last, 0, before, last_pieces[0], weights)
    other, rest = partner(other, "freq", freq_count, 1), partner(rest, "freq", freq_count, 1)
    raw, other, rest = lax.optimization_barrier((last_pieces[1], other, rest))
    second, gram, lent = late(tables, n, last, early_rows, before, raw, weights, gram)
    raw = partner(raw, "freq", freq_count, 1)
    gram = gram + partner(lent, "freq", freq_count, 1)
    repeated = jnp.broadcast_to(gram, (targets,) + gram.shape)
    repeated, raw = lax.optimization_barrier((repeated, raw))
    grams = lax.all_to_all(
        repeated,
        ("space", "tm"),
        split_axis=0,
        concat_axis=0,
        axis_index_groups=[list(range(targets - 1, -1, -1))],
        tiled=True,
    )
    total = rows * targets
    return finish(tables, n, last, total, first, second, other, rest, raw, grams)


def solution(mesh):
    return jax.shard_map(
        on_device,
        mesh=mesh,
        in_specs=(P(None, "space", ("groups", "tm")), P(("groups", "tm", "space"))),
        out_specs=(
            P("freq", None, None, ("groups", "tm", "space")),
            P("groups", "freq", None, None),
        ),
        check_vma=False,
    )
```

```python
import functools

import numpy as np
import jax
import jax.numpy as jnp
from jax import lax
from jax.experimental import pallas as pl
from jax.experimental.pallas import tpu as pltpu
from jax.sharding import PartitionSpec as P

NB = 16
SEGMENT_FRAMES = 64
NF = 16
CUTS = 4
epsilon = 1e-05
MIB = 1024 * 1024
SMALL = pl.CostEstimate(flops=1, transcendentals=0, bytes_accessed=1)


def dft_blocks(groups):
    times = np.arange(SEGMENT_FRAMES)
    taper = 0.5 - 0.5 * np.cos(2.0 * np.pi * times / SEGMENT_FRAMES)
    taper = taper / np.sqrt(np.sum(taper * taper))
    bins = 1 + np.arange(NF)
    angles = 2.0 * np.pi * (bins[:, None] * times[None, :] % SEGMENT_FRAMES) / SEGMENT_FRAMES
    table = np.stack([np.cos(angles) * taper, -np.sin(angles) * taper])
    step = SEGMENT_FRAMES // groups
    table = table.reshape(2, 2, NF // 2, groups, step)
    spread = np.einsum("rhfgt,bc->ghrfbct", table, np.eye(NB))
    spread = spread.reshape(groups, 2 * NF * NB, NB * step).astype(np.float32)
    high = spread.astype(jnp.bfloat16)
    low = (spread - high.astype(np.float32)).astype(jnp.bfloat16)
    return np.concatenate([high, high, low], axis=2)


def split(x):
    high = x.astype(jnp.bfloat16)
    return high, (x - high.astype(jnp.float32)).astype(jnp.bfloat16)


def times_split(left, x):
    high, low = split(x)
    right = jnp.concatenate([high, low, high], axis=0)
    return jnp.dot(left, right, preferred_element_type=jnp.float32)


def rows_product(a, b):
    a_high, a_low = split(a)
    b_high, b_low = split(b)
    total = 0.0
    for x, y in ((a_low, b_low), (a_low, b_high), (a_high, b_low), (a_high, b_high)):
        total = total + lax.dot_general(
            x, y, (((1,), (1,)), ((), ())), preferred_element_type=jnp.float32
        )
    return total


def cut_kernel(n, k, rows, skip, x_ref, o_ref, sem):
    size = o_ref.shape[2]
    to = lax.bitwise_xor(lax.axis_index("space"), k)
    share = rows // 2
    start = pl.multiple_of(to * rows + lax.axis_index("freq") * share + skip, 128)
    part = NB // CUTS
    copies = []
    for i in range(CUTS):
        blocks = pl.ds(i * part, part)
        copies.append(
            pltpu.make_async_copy(
                x_ref.at[blocks, :, pl.ds(start, size)], o_ref.at[blocks], sem.at[i]
            )
        )
    for copy in copies:
        copy.start()
    for copy in copies:
        copy.wait()


def cut(snapshots, n, k, rows, skip, size):
    blocks, local_times, _ = snapshots.shape
    if local_times % 8 == 0:
        piece = pl.pallas_call(
            functools.partial(cut_kernel, n, k, rows, skip),
            out_shape=pltpu.VMEM((blocks, local_times, size), jnp.float32),
            in_specs=[pl.BlockSpec(memory_space=pltpu.HBM)],
            out_specs=pl.BlockSpec(memory_space=pltpu.VMEM),
            scratch_shapes=[pltpu.SemaphoreType.DMA((CUTS,))],
            compiler_params=pltpu.CompilerParams(vmem_limit_bytes=4 * MIB),
            cost_estimate=SMALL,
        )(pltpu.with_memory_space_constraint(snapshots, pltpu.HBM))
    else:
        to = lax.bitwise_xor(lax.axis_index("space"), k)
        start = to * rows + lax.axis_index("freq") * (rows // 2) + skip
        piece = lax.dynamic_slice_in_dim(snapshots, start, size, axis=2)
    return piece.reshape(blocks * local_times, size)


def early_kernel(n, k, t_ref, x_ref, *refs):
    src = lax.bitwise_xor(lax.axis_index("space"), k)
    part = times_split(t_ref[src], x_ref[...])
    refs[-1][...] = part if len(refs) == 1 else refs[0][...] + part


def early(tables, n, k, piece, *before):
    share = piece.shape[1]
    return pl.pallas_call(
        functools.partial(early_kernel, n, k),
        out_shape=jax.ShapeDtypeStruct((tables.shape[1], share), jnp.float32),
        compiler_params=pltpu.CompilerParams(vmem_limit_bytes=16 * MIB),
        cost_estimate=SMALL,
    )(tables, piece, *before)


def gram_of(z, weights):
    width = z.shape[0] // 2
    local = width // NB
    line = lax.broadcasted_iota(jnp.int32, (width, width), 0) // NB
    lane = lax.broadcasted_iota(jnp.int32, (width, width), 1) // NB
    row = lax.broadcasted_iota(jnp.int32, (NB, width), 0)
    col = lax.broadcasted_iota(jnp.int32, (NB, width), 1) % NB
    full = rows_product(z * weights, z)
    gram_re = full[:width, :width] + full[width:, width:]
    gram_im = full[:width, width:] - full[width:, :width]
    both = []
    for part in (gram_re, gram_im):
        kept = jnp.where(line == lane, part, 0.0)
        both.append(jnp.sum(kept.reshape(local, NB, width), axis=0))
    return jnp.where(row >= col, both[0], both[1])


def weights_at(w_ref, place, share, skip, size):
    return w_ref[:, pl.ds(pl.multiple_of(place * share + skip, 128), size)]


def first_part_kernel(
    n, k, t_ref, sum_ref, x_ref, w_ref, own_ref, rest_ref, other_ref, later_ref, gram_ref, lent_ref
):
    size = x_ref.shape[1]
    me = lax.axis_index("freq")
    src = lax.bitwise_xor(lax.axis_index("space"), k)
    spectra = sum_ref[:, :size] + times_split(t_ref[src], x_ref[...])
    weights = weights_at(w_ref, me, sum_ref.shape[1], 0, size)
    rest = sum_ref[:, size:]
    half = spectra.shape[0] // 2
    first = me == 0
    own_ref[...] = jnp.where(first, spectra[:half], spectra[half:])
    other_ref[...] = jnp.where(first, spectra[half:], spectra[:half])
    rest_ref[...] = jnp.where(first, rest[:half], rest[half:])
    later_ref[...] = jnp.where(first, rest[half:], rest[:half])
    grams = [gram_of(z, weights) for z in (spectra[:half], spectra[half:])]
    gram_ref[...] = jnp.where(first, grams[0], grams[1])
    lent_ref[...] = jnp.where(first, grams[1], grams[0])


def first_part(tables, n, k, partial_sum, piece, weights):
    share = partial_sum.shape[1]
    half = tables.shape[1] // 2
    size = piece.shape[1]
    gram = (NB, half // 2)
    shapes = [(half, size), (half, share - size), (half, size), (half, share - size), gram, gram]
    return pl.pallas_call(
        functools.partial(first_part_kernel, n, k),
        out_shape=[jax.ShapeDtypeStruct(shape, jnp.float32) for shape in shapes],
        compiler_params=pltpu.CompilerParams(vmem_limit_bytes=16 * MIB),
        cost_estimate=SMALL,
    )(tables, partial_sum, piece, weights)


def last_part_kernel(n, k, swapped, skip, t_ref, sum_ref, x_ref, w_ref, *refs):
    *before, own_ref, gram_ref = refs
    half, size = sum_ref.shape
    me = lax.axis_index("freq")
    src = lax.bitwise_xor(lax.axis_index("space"), k)
    lines = pl.ds(pl.multiple_of(me * half, 128), half)
    spectra = sum_ref[...] + times_split(t_ref[src, lines], x_ref[...])
    own_ref[...] = spectra
    place = 1 - me if swapped else me
    gram = gram_of(spectra, weights_at(w_ref, place, skip + size, skip, size))
    for ref in before:
        gram = gram + ref[...]
    if len(gram_ref.shape) == 2:
        gram_ref[...] = gram
    else:
        for d in range(gram_ref.shape[0]):
            gram_ref[d] = gram


def last_part(tables, n, k, swapped, skip, copies, partial_sum, piece, weights, *before):
    gram = (NB, partial_sum.shape[0] // 2)
    shapes = [partial_sum.shape, (copies, *gram) if copies else gram]
    return pl.pallas_call(
        functools.partial(last_part_kernel, n, k, swapped, skip),
        out_shape=[jax.ShapeDtypeStruct(shape, jnp.float32) for shape in shapes],
        compiler_params=pltpu.CompilerParams(vmem_limit_bytes=16 * MIB),
        cost_estimate=SMALL,
    )(tables, partial_sum, piece, weights, *before)


def inv_sqrt(x):
    y = lax.rsqrt(x)
    return y * (1.5 - 0.5 * x * (y * y))


def finish_kernel(
    total, own_ref, own_last_ref, other_ref, other_last_ref, grams_ref, modes_ref, factor_ref
):
    local = modes_ref.shape[0]
    width = local * NB
    share = modes_ref.shape[3] // 2
    gram = jnp.sum(grams_ref[...], axis=0) / total
    row = lax.broadcasted_iota(jnp.int32, (NB, width), 0)
    col = lax.broadcasted_iota(jnp.int32, (NB, width), 1) % NB
    stacked = [jnp.where(col == j, gram, 0.0) for j in range(NB)]
    for j in range(NB):
        line = jnp.broadcast_to(gram[j : j + 1, :], (NB, width))
        stacked.append(jnp.where((col == row) & (row > j), -line, 0.0))
    stacked = jnp.concatenate(stacked, axis=0)
    group_r = lax.broadcasted_iota(jnp.int32, (width, width), 0) // NB
    group_c = lax.broadcasted_iota(jnp.int32, (width, width), 1) // NB
    same = group_r == group_c
    ones = jnp.where(same, 1.0, 0.0).astype(jnp.bfloat16)
    spread = jnp.zeros(stacked.shape, jnp.float32)
    rest = stacked
    for _ in range(3):
        piece = rest.astype(jnp.bfloat16)
        rest = rest - piece.astype(jnp.float32)
        spread = spread + jnp.dot(piece, ones, preferred_element_type=jnp.float32)
    col_re = [[spread[j * NB + 8 * h : j * NB + 8 * h + 8] for h in (0, 1)] for j in range(NB)]
    base = NB * NB
    col_im = [
        [spread[base + j * NB + 8 * h : base + j * NB + 8 * h + 8] for h in (0, 1)]
        for j in range(NB)
    ]
    rows = [lax.broadcasted_iota(jnp.int32, (8, width), 0) + 8 * h for h in (0, 1)]
    lanes = lax.broadcasted_iota(jnp.int32, (8, width), 1) % NB
    inv_re = [jnp.where(rows[h] == lanes, 1.0, 0.0) for h in (0, 1)]
    inv_im = [jnp.zeros((8, width), jnp.float32) for h in (0, 1)]
    low_re = [jnp.zeros((8, width), jnp.float32) for h in (0, 1)]
    low_im = [jnp.zeros((8, width), jnp.float32) for h in (0, 1)]

    def pick(halves, i):
        return jnp.broadcast_to(halves[i // 8][i % 8 : i % 8 + 1, :], (8, width))

    pivots = [pick(col_re[j], j) + epsilon for j in range(NB)]
    scales = [jnp.zeros((8, width), jnp.float32) for h in (0, 1)]
    for p in range(NB):
        scale = inv_sqrt(pivots[p])
        inverse = scale * scale
        for h in range(p // 8, 2):
            below = rows[h] > p
            here = lanes == p
            scales[h] = jnp.where(rows[h] == p, scale, scales[h])
            col_re[p][h] = jnp.where(below, col_re[p][h], 0.0)
            col_im[p][h] = jnp.where(below, col_im[p][h], 0.0)
            diag = jnp.where(rows[h] == p, pivots[p], col_re[p][h])
            low_re[h] = jnp.where(here, diag * scale, low_re[h])
            low_im[h] = jnp.where(here, col_im[p][h] * scale, low_im[h])
        for j in range(p + 1, NB):
            a_re, a_im = pick(col_re[p], j), pick(col_im[p], j)
            u_re, u_im = a_re * inverse, a_im * inverse
            pivots[j] = pivots[j] - (a_re * u_re + a_im * u_im)
            for h in range(j // 8, 2):
                c_re, c_im = col_re[p][h], col_im[p][h]
                col_re[j][h] = col_re[j][h] - (c_re * u_re + c_im * u_im)
                col_im[j][h] = col_im[j][h] - (c_im * u_re - c_re * u_im)
        line_re = pick(inv_re, p) * inverse
        line_im = pick(inv_im, p) * inverse
        for h in range(p // 8, 2):
            c_re, c_im = col_re[p][h], col_im[p][h]
            inv_re[h] = inv_re[h] - (c_re * line_re - c_im * line_im)
            inv_im[h] = inv_im[h] - (c_re * line_im + c_im * line_re)
    inv_re = [inv_re[h] * scales[h] for h in (0, 1)]
    inv_im = [inv_im[h] * scales[h] for h in (0, 1)]

    block_re = jnp.where(same, jnp.concatenate(inv_re * local, axis=0), 0.0)
    block_im = jnp.where(same, jnp.concatenate(inv_im * local, axis=0), 0.0)
    mixing = jnp.concatenate(
        [
            jnp.concatenate([block_re, block_im], axis=1),
            jnp.concatenate([-block_im, block_re], axis=1),
        ],
        axis=0,
    )
    me = lax.axis_index("freq")
    high, low = split(mixing)
    mixing = jnp.concatenate([high, high, low], axis=1)
    own = [own_ref[...], own_last_ref[...]]
    other = [other_ref[...], other_last_ref[...]]
    for place, parts in ((me, own), (1 - me, other)):
        out = times_split(mixing, jnp.concatenate(parts, axis=1))
        cols = pl.ds(pl.multiple_of(place * share, 128), share)
        for part in range(2):
            for f in range(local):
                at = part * width + f * NB
                modes_ref[f, part, :, cols] = out[at : at + NB]
    pad = jnp.zeros((width - NB, width), jnp.float32)
    turned_re = jnp.transpose(jnp.concatenate(low_re + [pad], axis=0))
    turned_im = jnp.transpose(jnp.concatenate(low_im + [pad], axis=0))
    for f in range(local):
        factor_ref[0, f] = turned_re[f * NB : (f + 1) * NB, :NB]
        factor_ref[1, f] = -turned_im[f * NB : (f + 1) * NB, :NB]


def finish(total, own, own_last, other, other_last, grams):
    half, size = own.shape
    local = half // (2 * NB)
    share = size + own_last.shape[1]
    return pl.pallas_call(
        functools.partial(finish_kernel, total),
        out_shape=(
            jax.ShapeDtypeStruct((local, 2, NB, 2 * share), jnp.float32),
            jax.ShapeDtypeStruct((2, local, NB, NB), jnp.float32),
        ),
        compiler_params=pltpu.CompilerParams(vmem_limit_bytes=16 * MIB),
    )(own, own_last, other, other_last, grams)


def partner(value, axis, size, step):
    return lax.ppermute(value, axis, [(i, i ^ step) for i in range(size)])


def on_device(snapshots, weights):
    n = lax.axis_size("space")
    tm_count = lax.axis_size("tm")
    freq_count = lax.axis_size("freq")
    blocks, local_times, columns = snapshots.shape
    rows = columns // n
    share = rows // freq_count

    tables = jnp.asarray(dft_blocks(n))

    last = n // 2
    early_rows = share // 2
    parts = ((0, early_rows), (early_rows, share - early_rows))
    targets = n * tm_count

    def send(k, skip, size):
        sent = cut(snapshots, n, k, rows, skip, size)
        return partner(sent, "space", n, k)

    offsets = [k for k in range(n - 1, 0, -1) if k != last]
    pieces = [send(k, 0, share) for k in offsets]
    last_pieces = [send(last, skip, size) for skip, size in parts]
    before = early(tables, n, 0, cut(snapshots, n, 0, rows, 0, share))
    for k, piece in zip(offsets, pieces):
        before = early(tables, n, k, piece, before)
    weights = weights.reshape(1, rows)
    own, rest, other, later, gram, lent = first_part(
        tables, n, last, before, last_pieces[0], weights
    )
    traded = [partner(part, "freq", freq_count, 1) for part in (other, later, lent)]
    piece, (other, later, lent) = lax.optimization_barrier((last_pieces[1], traded))
    raw = partner(piece, "freq", freq_count, 1)
    own_last, gram = last_part(
        tables, n, last, False, early_rows, 0, rest, piece, weights, gram, lent
    )
    other_last, gram = last_part(
        tables, n, last, True, early_rows, targets, later, raw, weights, gram
    )
    grams = lax.all_to_all(
        gram,
        ("space", "tm"),
        split_axis=0,
        concat_axis=0,
        axis_index_groups=[list(range(targets - 1, -1, -1))],
        tiled=True,
    )
    total = rows * targets
    return finish(total, own, own_last, other, other_last, grams)


def solution(mesh):
    return jax.shard_map(
        on_device,
        mesh=mesh,
        in_specs=(P(None, "space", ("groups", "tm")), P(("groups", "tm", "space"))),
        out_specs=(
            P("freq", None, None, ("groups", "tm", "space")),
            P("groups", "freq", None, None),
        ),
        check_vma=False,
    )
```

```python
import functools

import numpy as np
import jax
import jax.numpy as jnp
from jax import lax
from jax.experimental import pallas as pl
from jax.experimental.pallas import tpu as pltpu
from jax.sharding import PartitionSpec as P

NB = 16
SEGMENT_FRAMES = 64
NF = 16
CUTS = 4
epsilon = 1e-05
MIB = 1024 * 1024
SMALL = pl.CostEstimate(flops=1, transcendentals=0, bytes_accessed=1)


def dft_blocks(groups):
    times = np.arange(SEGMENT_FRAMES)
    taper = 0.5 - 0.5 * np.cos(2.0 * np.pi * times / SEGMENT_FRAMES)
    taper = taper / np.sqrt(np.sum(taper * taper))
    bins = 1 + np.arange(NF)
    angles = 2.0 * np.pi * (bins[:, None] * times[None, :] % SEGMENT_FRAMES) / SEGMENT_FRAMES
    table = np.stack([np.cos(angles) * taper, -np.sin(angles) * taper])
    step = SEGMENT_FRAMES // groups
    table = table.reshape(2, 2, NF // 2, groups, step)
    spread = np.einsum("rhfgt,bc->ghrfbct", table, np.eye(NB))
    spread = spread.reshape(groups, 2 * NF * NB, NB * step).astype(np.float32)
    high = spread.astype(jnp.bfloat16)
    low = (spread - high.astype(np.float32)).astype(jnp.bfloat16)
    return np.concatenate([high, high, low], axis=2)


def split(x):
    high = x.astype(jnp.bfloat16)
    return high, (x - high.astype(jnp.float32)).astype(jnp.bfloat16)


def times_split(left, x):
    high, low = split(x)
    right = jnp.concatenate([high, low, high], axis=0)
    return jnp.dot(left, right, preferred_element_type=jnp.float32)


def rows_product(a, b):
    a_high, a_low = split(a)
    b_high, b_low = split(b)
    total = 0.0
    for x, y in ((a_low, b_low), (a_low, b_high), (a_high, b_low), (a_high, b_high)):
        total = total + lax.dot_general(
            x, y, (((1,), (1,)), ((), ())), preferred_element_type=jnp.float32
        )
    return total


def cut_kernel(n, k, rows, skip, x_ref, o_ref, sem):
    size = o_ref.shape[2]
    to = lax.bitwise_xor(lax.axis_index("space"), k)
    share = rows // 2
    start = pl.multiple_of(to * rows + lax.axis_index("freq") * share + skip, 128)
    part = NB // CUTS
    copies = []
    for i in range(CUTS):
        blocks = pl.ds(i * part, part)
        copies.append(
            pltpu.make_async_copy(
                x_ref.at[blocks, :, pl.ds(start, size)], o_ref.at[blocks], sem.at[i]
            )
        )
    for copy in copies:
        copy.start()
    for copy in copies:
        copy.wait()


def cut(snapshots, n, k, rows, skip, size):
    blocks, local_times, _ = snapshots.shape
    if local_times % 8 == 0:
        piece = pl.pallas_call(
            functools.partial(cut_kernel, n, k, rows, skip),
            out_shape=pltpu.VMEM((blocks, local_times, size), jnp.float32),
            in_specs=[pl.BlockSpec(memory_space=pltpu.HBM)],
            out_specs=pl.BlockSpec(memory_space=pltpu.VMEM),
            scratch_shapes=[pltpu.SemaphoreType.DMA((CUTS,))],
            compiler_params=pltpu.CompilerParams(vmem_limit_bytes=4 * MIB),
            cost_estimate=SMALL,
        )(pltpu.with_memory_space_constraint(snapshots, pltpu.HBM))
    else:
        to = lax.bitwise_xor(lax.axis_index("space"), k)
        start = to * rows + lax.axis_index("freq") * (rows // 2) + skip
        piece = lax.dynamic_slice_in_dim(snapshots, start, size, axis=2)
    return piece.reshape(blocks * local_times, size)


def early_kernel(n, k, t_ref, x_ref, *refs):
    src = lax.bitwise_xor(lax.axis_index("space"), k)
    part = times_split(t_ref[src], x_ref[...])
    refs[-1][...] = part if len(refs) == 1 else refs[0][...] + part


def early(tables, n, k, piece, *before):
    share = piece.shape[1]
    return pl.pallas_call(
        functools.partial(early_kernel, n, k),
        out_shape=jax.ShapeDtypeStruct((tables.shape[1], share), jnp.float32),
        compiler_params=pltpu.CompilerParams(vmem_limit_bytes=16 * MIB),
        cost_estimate=SMALL,
    )(tables, piece, *before)


def gram_of(z, weights):
    width = z.shape[0] // 2
    local = width // NB
    line = lax.broadcasted_iota(jnp.int32, (width, width), 0) // NB
    lane = lax.broadcasted_iota(jnp.int32, (width, width), 1) // NB
    row = lax.broadcasted_iota(jnp.int32, (NB, width), 0)
    col = lax.broadcasted_iota(jnp.int32, (NB, width), 1) % NB
    full = rows_product(z * weights, z)
    gram_re = full[:width, :width] + full[width:, width:]
    gram_im = full[:width, width:] - full[width:, :width]
    both = []
    for part in (gram_re, gram_im):
        kept = jnp.where(line == lane, part, 0.0)
        both.append(jnp.sum(kept.reshape(local, NB, width), axis=0))
    return jnp.where(row >= col, both[0], both[1])


def weights_at(w_ref, place, share, skip, size):
    return w_ref[:, pl.ds(pl.multiple_of(place * share + skip, 128), size)]


def first_part_kernel(
    n, k, t_ref, sum_ref, x_ref, w_ref, own_ref, rest_ref, other_ref, later_ref, gram_ref, lent_ref
):
    size = x_ref.shape[1]
    me = lax.axis_index("freq")
    src = lax.bitwise_xor(lax.axis_index("space"), k)
    spectra = sum_ref[:, :size] + times_split(t_ref[src], x_ref[...])
    weights = weights_at(w_ref, me, sum_ref.shape[1], 0, size)
    rest = sum_ref[:, size:]
    half = spectra.shape[0] // 2
    first = me == 0
    own_ref[...] = jnp.where(first, spectra[:half], spectra[half:])
    other_ref[...] = jnp.where(first, spectra[half:], spectra[:half])
    rest_ref[...] = jnp.where(first, rest[:half], rest[half:])
    later_ref[...] = jnp.where(first, rest[half:], rest[:half])
    grams = [gram_of(z, weights) for z in (spectra[:half], spectra[half:])]
    gram_ref[...] = jnp.where(first, grams[0], grams[1])
    lent_ref[...] = jnp.where(first, grams[1], grams[0])


def first_part(tables, n, k, partial_sum, piece, weights):
    share = partial_sum.shape[1]
    half = tables.shape[1] // 2
    size = piece.shape[1]
    gram = (NB, half // 2)
    shapes = [(half, size), (half, share - size), (half, size), (half, share - size), gram, gram]
    return pl.pallas_call(
        functools.partial(first_part_kernel, n, k),
        out_shape=[jax.ShapeDtypeStruct(shape, jnp.float32) for shape in shapes],
        compiler_params=pltpu.CompilerParams(vmem_limit_bytes=16 * MIB),
        cost_estimate=SMALL,
    )(tables, partial_sum, piece, weights)


def last_part_kernel(n, k, swapped, skip, t_ref, sum_ref, x_ref, w_ref, *refs):
    *before, own_ref, gram_ref = refs
    half, size = sum_ref.shape
    me = lax.axis_index("freq")
    src = lax.bitwise_xor(lax.axis_index("space"), k)
    lines = pl.ds(pl.multiple_of(me * half, 128), half)
    spectra = sum_ref[...] + times_split(t_ref[src, lines], x_ref[...])
    own_ref[...] = spectra
    place = 1 - me if swapped else me
    gram = gram_of(spectra, weights_at(w_ref, place, skip + size, skip, size))
    for ref in before:
        gram = gram + ref[...]
    if len(gram_ref.shape) == 2:
        gram_ref[...] = gram
    else:
        for d in range(gram_ref.shape[0]):
            gram_ref[d] = gram


def last_part(tables, n, k, swapped, skip, copies, partial_sum, piece, weights, *before):
    gram = (NB, partial_sum.shape[0] // 2)
    shapes = [partial_sum.shape, (copies, *gram) if copies else gram]
    return pl.pallas_call(
        functools.partial(last_part_kernel, n, k, swapped, skip),
        out_shape=[jax.ShapeDtypeStruct(shape, jnp.float32) for shape in shapes],
        compiler_params=pltpu.CompilerParams(vmem_limit_bytes=16 * MIB),
        cost_estimate=SMALL,
    )(tables, partial_sum, piece, weights, *before)


def inv_sqrt(x):
    y = lax.rsqrt(x)
    return y * (1.5 - 0.5 * x * (y * y))


def finish_kernel(
    total, own_ref, own_last_ref, other_ref, other_last_ref, grams_ref, modes_ref, factor_ref
):
    local = modes_ref.shape[0]
    width = local * NB
    share = modes_ref.shape[3] // 2
    gram = jnp.sum(grams_ref[...], axis=0) / total
    row = lax.broadcasted_iota(jnp.int32, (NB, width), 0)
    col = lax.broadcasted_iota(jnp.int32, (NB, width), 1) % NB
    stacked = [jnp.where(col == j, gram, 0.0) for j in range(NB)]
    for j in range(NB):
        line = jnp.broadcast_to(gram[j : j + 1, :], (NB, width))
        stacked.append(jnp.where((col == row) & (row > j), -line, 0.0))
    stacked = jnp.concatenate(stacked, axis=0)
    group_r = lax.broadcasted_iota(jnp.int32, (width, width), 0) // NB
    group_c = lax.broadcasted_iota(jnp.int32, (width, width), 1) // NB
    same = group_r == group_c
    ones = jnp.where(same, 1.0, 0.0).astype(jnp.bfloat16)
    spread = jnp.zeros(stacked.shape, jnp.float32)
    rest = stacked
    for _ in range(3):
        piece = rest.astype(jnp.bfloat16)
        rest = rest - piece.astype(jnp.float32)
        spread = spread + jnp.dot(piece, ones, preferred_element_type=jnp.float32)
    col_re = [[spread[j * NB + 8 * h : j * NB + 8 * h + 8] for h in (0, 1)] for j in range(NB)]
    base = NB * NB
    col_im = [
        [spread[base + j * NB + 8 * h : base + j * NB + 8 * h + 8] for h in (0, 1)]
        for j in range(NB)
    ]
    rows = [lax.broadcasted_iota(jnp.int32, (8, width), 0) + 8 * h for h in (0, 1)]
    lanes = lax.broadcasted_iota(jnp.int32, (8, width), 1) % NB
    inv_re = [jnp.where(rows[h] == lanes, 1.0, 0.0) for h in (0, 1)]
    inv_im = [jnp.zeros((8, width), jnp.float32) for h in (0, 1)]
    low_re = [jnp.zeros((8, width), jnp.float32) for h in (0, 1)]
    low_im = [jnp.zeros((8, width), jnp.float32) for h in (0, 1)]

    def pick(halves, i):
        return jnp.broadcast_to(halves[i // 8][i % 8 : i % 8 + 1, :], (8, width))

    pivots = [pick(col_re[j], j) + epsilon for j in range(NB)]
    scales = [jnp.zeros((8, width), jnp.float32) for h in (0, 1)]
    for p in range(NB):
        scale = inv_sqrt(pivots[p])
        inverse = scale * scale
        for h in range(p // 8, 2):
            below = rows[h] > p
            here = lanes == p
            scales[h] = jnp.where(rows[h] == p, scale, scales[h])
            col_re[p][h] = jnp.where(below, col_re[p][h], 0.0)
            col_im[p][h] = jnp.where(below, col_im[p][h], 0.0)
            diag = jnp.where(rows[h] == p, pivots[p], col_re[p][h])
            low_re[h] = jnp.where(here, diag * scale, low_re[h])
            low_im[h] = jnp.where(here, col_im[p][h] * scale, low_im[h])
        for j in range(p + 1, NB):
            a_re, a_im = pick(col_re[p], j), pick(col_im[p], j)
            u_re, u_im = a_re * inverse, a_im * inverse
            pivots[j] = pivots[j] - (a_re * u_re + a_im * u_im)
            for h in range(j // 8, 2):
                c_re, c_im = col_re[p][h], col_im[p][h]
                col_re[j][h] = col_re[j][h] - (c_re * u_re + c_im * u_im)
                col_im[j][h] = col_im[j][h] - (c_im * u_re - c_re * u_im)
        line_re = pick(inv_re, p) * inverse
        line_im = pick(inv_im, p) * inverse
        for h in range(p // 8, 2):
            c_re, c_im = col_re[p][h], col_im[p][h]
            inv_re[h] = inv_re[h] - (c_re * line_re - c_im * line_im)
            inv_im[h] = inv_im[h] - (c_re * line_im + c_im * line_re)
    inv_re = [inv_re[h] * scales[h] for h in (0, 1)]
    inv_im = [inv_im[h] * scales[h] for h in (0, 1)]

    block_re = jnp.where(same, jnp.concatenate(inv_re * local, axis=0), 0.0)
    block_im = jnp.where(same, jnp.concatenate(inv_im * local, axis=0), 0.0)
    mixing = jnp.concatenate(
        [
            jnp.concatenate([block_re, block_im], axis=1),
            jnp.concatenate([-block_im, block_re], axis=1),
        ],
        axis=0,
    )
    me = lax.axis_index("freq")
    high, low = split(mixing)
    mixing = jnp.concatenate([high, high, low], axis=1)
    own = [own_ref[...], own_last_ref[...]]
    other = [other_ref[...], other_last_ref[...]]
    for place, parts in ((me, own), (1 - me, other)):
        out = times_split(mixing, jnp.concatenate(parts, axis=1))
        cols = pl.ds(pl.multiple_of(place * share, 128), share)
        for part in range(2):
            for f in range(local):
                at = part * width + f * NB
                modes_ref[f, part, :, cols] = out[at : at + NB]
    pad = jnp.zeros((width - NB, width), jnp.float32)
    turned_re = jnp.transpose(jnp.concatenate(low_re + [pad], axis=0))
    turned_im = jnp.transpose(jnp.concatenate(low_im + [pad], axis=0))
    for f in range(local):
        factor_ref[0, f] = turned_re[f * NB : (f + 1) * NB, :NB]
        factor_ref[1, f] = -turned_im[f * NB : (f + 1) * NB, :NB]


def finish(total, own, own_last, other, other_last, grams):
    half, size = own.shape
    local = half // (2 * NB)
    share = size + own_last.shape[1]
    return pl.pallas_call(
        functools.partial(finish_kernel, total),
        out_shape=(
            jax.ShapeDtypeStruct((local, 2, NB, 2 * share), jnp.float32),
            jax.ShapeDtypeStruct((2, local, NB, NB), jnp.float32),
        ),
        compiler_params=pltpu.CompilerParams(vmem_limit_bytes=16 * MIB),
    )(own, own_last, other, other_last, grams)


def partner(value, axis, size, step):
    return lax.ppermute(value, axis, [(i, i ^ step) for i in range(size)])


def on_device(snapshots, weights):
    n = lax.axis_size("space")
    tm_count = lax.axis_size("tm")
    freq_count = lax.axis_size("freq")
    blocks, local_times, columns = snapshots.shape
    rows = columns // n
    share = rows // freq_count

    tables = jnp.asarray(dft_blocks(n))

    last = n - 1
    early_rows = share // 2
    parts = ((0, early_rows), (early_rows, share - early_rows))
    targets = n * tm_count

    def send(k, skip, size):
        sent = cut(snapshots, n, k, rows, skip, size)
        return partner(sent, "space", n, k)

    offsets = [k for k in range(n - 1, 0, -1) if k != last]
    pieces = [send(k, 0, share) for k in offsets]
    last_pieces = [send(last, skip, size) for skip, size in parts]
    before = early(tables, n, 0, cut(snapshots, n, 0, rows, 0, share))
    for k, piece in zip(offsets, pieces):
        before = early(tables, n, k, piece, before)
    weights = weights.reshape(1, rows)
    own, rest, other, later, gram, lent = first_part(
        tables, n, last, before, last_pieces[0], weights
    )
    traded = [partner(part, "freq", freq_count, 1) for part in (other, later, lent)]
    piece, (other, later, lent) = lax.optimization_barrier((last_pieces[1], traded))
    raw = partner(piece, "freq", freq_count, 1)
    own_last, gram = last_part(
        tables, n, last, False, early_rows, 0, rest, piece, weights, gram, lent
    )
    other_last, gram = last_part(
        tables, n, last, True, early_rows, targets, later, raw, weights, gram
    )
    grams = lax.all_to_all(
        gram,
        ("space", "tm"),
        split_axis=0,
        concat_axis=0,
        axis_index_groups=[list(range(targets - 1, -1, -1))],
        tiled=True,
    )
    total = rows * targets
    return finish(total, own, own_last, other, other_last, grams)


def solution(mesh):
    return jax.shard_map(
        on_device,
        mesh=mesh,
        in_specs=(P(None, "space", ("groups", "tm")), P(("groups", "tm", "space"))),
        out_specs=(
            P("freq", None, None, ("groups", "tm", "space")),
            P("groups", "freq", None, None),
        ),
        check_vma=False,
    )
```

```python
import functools

import numpy as np
import jax
import jax.numpy as jnp
from jax import lax
from jax.experimental import pallas as pl
from jax.experimental.pallas import tpu as pltpu
from jax.sharding import PartitionSpec as P

NB = 16
SEGMENT_FRAMES = 64
NF = 16
CUTS = 4
epsilon = 1e-05
MIB = 1024 * 1024
SMALL = pl.CostEstimate(flops=1, transcendentals=0, bytes_accessed=1)


def dft_blocks(groups):
    times = np.arange(SEGMENT_FRAMES)
    taper = 0.5 - 0.5 * np.cos(2.0 * np.pi * times / SEGMENT_FRAMES)
    taper = taper / np.sqrt(np.sum(taper * taper))
    bins = 1 + np.arange(NF)
    angles = 2.0 * np.pi * (bins[:, None] * times[None, :] % SEGMENT_FRAMES) / SEGMENT_FRAMES
    table = np.stack([np.cos(angles) * taper, -np.sin(angles) * taper])
    step = SEGMENT_FRAMES // groups
    table = table.reshape(2, 2, NF // 2, groups, step)
    spread = np.einsum("rhfgt,bc->ghrfbct", table, np.eye(NB))
    spread = spread.reshape(groups, 2 * NF * NB, NB * step).astype(np.float32)
    high = spread.astype(jnp.bfloat16)
    low = (spread - high.astype(np.float32)).astype(jnp.bfloat16)
    return np.concatenate([high, high, low], axis=2)


def split(x):
    high = x.astype(jnp.bfloat16)
    return high, (x - high.astype(jnp.float32)).astype(jnp.bfloat16)


def times_split(left, x):
    high, low = split(x)
    right = jnp.concatenate([high, low, high], axis=0)
    return jnp.dot(left, right, preferred_element_type=jnp.float32)


def rows_product(a, b):
    a_high, a_low = split(a)
    b_high, b_low = split(b)
    total = 0.0
    for x, y in ((a_low, b_low), (a_low, b_high), (a_high, b_low), (a_high, b_high)):
        total = total + lax.dot_general(
            x, y, (((1,), (1,)), ((), ())), preferred_element_type=jnp.float32
        )
    return total


def cut_kernel(n, k, rows, skip, x_ref, o_ref, sem):
    size = o_ref.shape[2]
    to = lax.bitwise_xor(lax.axis_index("space"), k)
    share = rows // 2
    start = pl.multiple_of(to * rows + lax.axis_index("freq") * share + skip, 128)
    part = NB // CUTS
    copies = []
    for i in range(CUTS):
        blocks = pl.ds(i * part, part)
        copies.append(
            pltpu.make_async_copy(
                x_ref.at[blocks, :, pl.ds(start, size)], o_ref.at[blocks], sem.at[i]
            )
        )
    for copy in copies:
        copy.start()
    for copy in copies:
        copy.wait()


def cut(snapshots, n, k, rows, skip, size):
    blocks, local_times, _ = snapshots.shape
    if local_times % 8 == 0:
        piece = pl.pallas_call(
            functools.partial(cut_kernel, n, k, rows, skip),
            out_shape=pltpu.VMEM((blocks, local_times, size), jnp.float32),
            in_specs=[pl.BlockSpec(memory_space=pltpu.HBM)],
            out_specs=pl.BlockSpec(memory_space=pltpu.VMEM),
            scratch_shapes=[pltpu.SemaphoreType.DMA((CUTS,))],
            compiler_params=pltpu.CompilerParams(vmem_limit_bytes=4 * MIB),
            cost_estimate=SMALL,
        )(pltpu.with_memory_space_constraint(snapshots, pltpu.HBM))
    else:
        to = lax.bitwise_xor(lax.axis_index("space"), k)
        start = to * rows + lax.axis_index("freq") * (rows // 2) + skip
        piece = lax.dynamic_slice_in_dim(snapshots, start, size, axis=2)
    return piece.reshape(blocks * local_times, size)


def early_kernel(n, k, t_ref, x_ref, *refs):
    src = lax.bitwise_xor(lax.axis_index("space"), k)
    part = times_split(t_ref[src], x_ref[...])
    refs[-1][...] = part if len(refs) == 1 else refs[0][...] + part


def early(tables, n, k, piece, *before):
    share = piece.shape[1]
    return pl.pallas_call(
        functools.partial(early_kernel, n, k),
        out_shape=jax.ShapeDtypeStruct((tables.shape[1], share), jnp.float32),
        compiler_params=pltpu.CompilerParams(vmem_limit_bytes=16 * MIB),
        cost_estimate=SMALL,
    )(tables, piece, *before)


def gram_of(z, weights):
    width = z.shape[0] // 2
    local = width // NB
    line = lax.broadcasted_iota(jnp.int32, (width, width), 0) // NB
    lane = lax.broadcasted_iota(jnp.int32, (width, width), 1) // NB
    row = lax.broadcasted_iota(jnp.int32, (NB, width), 0)
    col = lax.broadcasted_iota(jnp.int32, (NB, width), 1) % NB
    full = rows_product(z * weights, z)
    gram_re = full[:width, :width] + full[width:, width:]
    gram_im = full[:width, width:] - full[width:, :width]
    both = []
    for part in (gram_re, gram_im):
        kept = jnp.where(line == lane, part, 0.0)
        both.append(jnp.sum(kept.reshape(local, NB, width), axis=0))
    return jnp.where(row >= col, both[0], both[1])


def weights_at(w_ref, place, share, skip, size):
    return w_ref[:, pl.ds(pl.multiple_of(place * share + skip, 128), size)]


def first_part_kernel(
    n, k, t_ref, sum_ref, x_ref, w_ref, own_ref, rest_ref, other_ref, later_ref, gram_ref, lent_ref
):
    size = x_ref.shape[1]
    me = lax.axis_index("freq")
    src = lax.bitwise_xor(lax.axis_index("space"), k)
    spectra = sum_ref[:, :size] + times_split(t_ref[src], x_ref[...])
    weights = weights_at(w_ref, me, sum_ref.shape[1], 0, size)
    rest = sum_ref[:, size:]
    half = spectra.shape[0] // 2
    first = me == 0
    own_ref[...] = jnp.where(first, spectra[:half], spectra[half:])
    other_ref[...] = jnp.where(first, spectra[half:], spectra[:half])
    rest_ref[...] = jnp.where(first, rest[:half], rest[half:])
    later_ref[...] = jnp.where(first, rest[half:], rest[:half])
    grams = [gram_of(z, weights) for z in (spectra[:half], spectra[half:])]
    gram_ref[...] = jnp.where(first, grams[0], grams[1])
    lent_ref[...] = jnp.where(first, grams[1], grams[0])


def first_part(tables, n, k, partial_sum, piece, weights):
    share = partial_sum.shape[1]
    half = tables.shape[1] // 2
    size = piece.shape[1]
    gram = (NB, half // 2)
    shapes = [(half, size), (half, share - size), (half, size), (half, share - size), gram, gram]
    return pl.pallas_call(
        functools.partial(first_part_kernel, n, k),
        out_shape=[jax.ShapeDtypeStruct(shape, jnp.float32) for shape in shapes],
        compiler_params=pltpu.CompilerParams(vmem_limit_bytes=16 * MIB),
        cost_estimate=SMALL,
    )(tables, partial_sum, piece, weights)


def last_part_kernel(n, k, swapped, t_ref, sum_ref, x_ref, w_ref, *refs):
    half, size = sum_ref.shape
    me = lax.axis_index("freq")
    src = lax.bitwise_xor(lax.axis_index("space"), k)
    lines = pl.ds(pl.multiple_of(me * half, 128), half)
    spectra = sum_ref[...] + times_split(t_ref[src, lines], x_ref[...])
    share = w_ref.shape[1] // 2
    skip = share - size
    place = 1 - me if swapped else me
    gram = gram_of(spectra, weights_at(w_ref, place, share, skip, size))
    if swapped:
        before_ref, high_ref, low_ref, gram_ref = refs
        gram = gram + before_ref[...]
        high_ref[...], low_ref[...] = split(spectra)
        for d in range(gram_ref.shape[0]):
            gram_ref[d] = gram
        return
    gram_own_ref, gram_lent_ref, own_ref, other_ref, *refs = refs
    high_ref, low_ref, other_high_ref, other_low_ref, gram_ref = refs
    gram_ref[...] = gram + gram_own_ref[...] + gram_lent_ref[...]
    high_ref[:, :skip], low_ref[:, :skip] = split(own_ref[...])
    high_ref[:, skip:], low_ref[:, skip:] = split(spectra)
    other_high_ref[...], other_low_ref[...] = split(other_ref[...])


def last_part(tables, n, k, copies, partial_sum, piece, weights, *before):
    half, size = partial_sum.shape
    share = weights.shape[1] // 2
    gram = (NB, half // 2)
    widths = [size, size] if copies else [share, share, share - size, share - size]
    parts = [jax.ShapeDtypeStruct((half, width), jnp.bfloat16) for width in widths]
    gram = jax.ShapeDtypeStruct((copies, *gram) if copies else gram, jnp.float32)
    return pl.pallas_call(
        functools.partial(last_part_kernel, n, k, bool(copies)),
        out_shape=[*parts, gram],
        compiler_params=pltpu.CompilerParams(vmem_limit_bytes=16 * MIB),
        cost_estimate=SMALL,
    )(tables, partial_sum, piece, weights, *before)


def inv_sqrt(x):
    y = lax.rsqrt(x)
    return y * (1.5 - 0.5 * x * (y * y))


def finish_kernel(
    total,
    own_high_ref,
    own_low_ref,
    first_high_ref,
    first_low_ref,
    last_high_ref,
    last_low_ref,
    grams_ref,
    modes_ref,
    factor_ref,
    slots,
    sems,
):
    local = modes_ref.shape[0]
    width = local * NB
    share = modes_ref.shape[3] // 2
    gram = jnp.sum(grams_ref[...], axis=0) / total
    row = lax.broadcasted_iota(jnp.int32, (NB, width), 0)
    col = lax.broadcasted_iota(jnp.int32, (NB, width), 1) % NB
    stacked = [jnp.where(col == j, gram, 0.0) for j in range(NB)]
    for j in range(NB):
        line = jnp.broadcast_to(gram[j : j + 1, :], (NB, width))
        stacked.append(jnp.where((col == row) & (row > j), -line, 0.0))
    stacked = jnp.concatenate(stacked, axis=0)
    group_r = lax.broadcasted_iota(jnp.int32, (width, width), 0) // NB
    group_c = lax.broadcasted_iota(jnp.int32, (width, width), 1) // NB
    same = group_r == group_c
    ones = jnp.where(same, 1.0, 0.0).astype(jnp.bfloat16)
    spread = jnp.zeros(stacked.shape, jnp.float32)
    rest = stacked
    for _ in range(3):
        piece = rest.astype(jnp.bfloat16)
        rest = rest - piece.astype(jnp.float32)
        spread = spread + jnp.dot(piece, ones, preferred_element_type=jnp.float32)
    col_re = [[spread[j * NB + 8 * h : j * NB + 8 * h + 8] for h in (0, 1)] for j in range(NB)]
    base = NB * NB
    col_im = [
        [spread[base + j * NB + 8 * h : base + j * NB + 8 * h + 8] for h in (0, 1)]
        for j in range(NB)
    ]
    rows = [lax.broadcasted_iota(jnp.int32, (8, width), 0) + 8 * h for h in (0, 1)]
    lanes = lax.broadcasted_iota(jnp.int32, (8, width), 1) % NB
    inv_re = [jnp.where(rows[h] == lanes, 1.0, 0.0) for h in (0, 1)]
    inv_im = [jnp.zeros((8, width), jnp.float32) for h in (0, 1)]
    low_re = [jnp.zeros((8, width), jnp.float32) for h in (0, 1)]
    low_im = [jnp.zeros((8, width), jnp.float32) for h in (0, 1)]

    def pick(halves, i):
        return jnp.broadcast_to(halves[i // 8][i % 8 : i % 8 + 1, :], (8, width))

    pivots = [pick(col_re[j], j) + epsilon for j in range(NB)]
    scales = [jnp.zeros((8, width), jnp.float32) for h in (0, 1)]
    for p in range(NB):
        scale = inv_sqrt(pivots[p])
        inverse = scale * scale
        for h in range(p // 8, 2):
            below = rows[h] > p
            here = lanes == p
            scales[h] = jnp.where(rows[h] == p, scale, scales[h])
            col_re[p][h] = jnp.where(below, col_re[p][h], 0.0)
            col_im[p][h] = jnp.where(below, col_im[p][h], 0.0)
            diag = jnp.where(rows[h] == p, pivots[p], col_re[p][h])
            low_re[h] = jnp.where(here, diag * scale, low_re[h])
            low_im[h] = jnp.where(here, col_im[p][h] * scale, low_im[h])
        for j in range(p + 1, NB):
            a_re, a_im = pick(col_re[p], j), pick(col_im[p], j)
            u_re, u_im = a_re * inverse, a_im * inverse
            pivots[j] = pivots[j] - (a_re * u_re + a_im * u_im)
            for h in range(j // 8, 2):
                c_re, c_im = col_re[p][h], col_im[p][h]
                col_re[j][h] = col_re[j][h] - (c_re * u_re + c_im * u_im)
                col_im[j][h] = col_im[j][h] - (c_im * u_re - c_re * u_im)
        line_re = pick(inv_re, p) * inverse
        line_im = pick(inv_im, p) * inverse
        for h in range(p // 8, 2):
            c_re, c_im = col_re[p][h], col_im[p][h]
            inv_re[h] = inv_re[h] - (c_re * line_re - c_im * line_im)
            inv_im[h] = inv_im[h] - (c_re * line_im + c_im * line_re)
    inv_re = [inv_re[h] * scales[h] for h in (0, 1)]
    inv_im = [inv_im[h] * scales[h] for h in (0, 1)]

    me = lax.axis_index("freq")
    own = own_high_ref[...], own_low_ref[...]
    other = [
        jnp.concatenate([a[...], b[...]], axis=1)
        for a, b in ((first_high_ref, last_high_ref), (first_low_ref, last_low_ref))
    ]
    part = width // 2
    lane = lax.broadcasted_iota(jnp.int32, (NB, width), 1)
    left_half = lane < part
    line = lax.broadcasted_iota(jnp.int32, (width, width), 0) % part // NB
    block = lax.broadcasted_iota(jnp.int32, (width, width), 1) % part // NB
    inv_re, inv_im = jnp.concatenate(inv_re, axis=0), jnp.concatenate(inv_im, axis=0)
    turned_re, turned_im = pltpu.roll(inv_re, part, 1), pltpu.roll(inv_im, part, 1)
    moves = []
    for h in range(2):
        stay = left_half if h == 0 else jnp.logical_not(left_half)
        twice_re = jnp.where(stay, inv_re, turned_re)
        twice_im = jnp.where(stay, inv_im, turned_im)
        top = jnp.where(left_half, twice_re, twice_im)
        bottom = jnp.where(left_half, -twice_im, twice_re)
        count = part // NB
        mixing = jnp.concatenate([top] * count + [bottom] * count, axis=0)
        high, low = split(jnp.where(line == block, mixing, 0.0))
        left = jnp.concatenate([high, high, low], axis=1)
        lines = [slice(r * width + h * part, r * width + (h + 1) * part) for r in range(2)]
        for place, (x_high, x_low) in ((me, own), (1 - me, other)):
            right = [x[at] for x in (x_high, x_low, x_high) for at in lines]
            out = jnp.dot(
                left, jnp.concatenate(right, axis=0), preferred_element_type=jnp.float32
            )
            cols = pl.ds(pl.multiple_of(place * share, 128), share)
            for r in range(2):
                for f in range(count):
                    at = r * part + f * NB
                    slots[h, f, r, :, cols] = out[at : at + NB]
        moves.append(
            pltpu.make_async_copy(
                slots.at[h], modes_ref.at[pl.ds(h * count, count)], sems.at[h]
            )
        )
        moves[-1].start()
    pad = jnp.zeros((width - NB, width), jnp.float32)
    turned_re = jnp.transpose(jnp.concatenate(low_re + [pad], axis=0))
    turned_im = jnp.transpose(jnp.concatenate(low_im + [pad], axis=0))
    for f in range(local):
        factor_ref[0, f] = turned_re[f * NB : (f + 1) * NB, :NB]
        factor_ref[1, f] = -turned_im[f * NB : (f + 1) * NB, :NB]
    for move in moves:
        move.wait()


def finish(total, own, others, grams):
    half, share = own[0].shape
    local = half // (2 * NB)
    return pl.pallas_call(
        functools.partial(finish_kernel, total),
        out_shape=(
            jax.ShapeDtypeStruct((local, 2, NB, 2 * share), jnp.float32),
            jax.ShapeDtypeStruct((2, local, NB, NB), jnp.float32),
        ),
        out_specs=(
            pl.BlockSpec(memory_space=pltpu.HBM),
            pl.BlockSpec(memory_space=pltpu.VMEM),
        ),
        scratch_shapes=[
            pltpu.VMEM((2, local // 2, 2, NB, 2 * share), jnp.float32),
            pltpu.SemaphoreType.DMA((2,)),
        ],
        compiler_params=pltpu.CompilerParams(vmem_limit_bytes=16 * MIB),
    )(*own, *others, grams)


def partner(value, axis, size, step):
    return lax.ppermute(value, axis, [(i, i ^ step) for i in range(size)])


def on_device(snapshots, weights):
    n = lax.axis_size("space")
    tm_count = lax.axis_size("tm")
    freq_count = lax.axis_size("freq")
    blocks, local_times, columns = snapshots.shape
    rows = columns // n
    share = rows // freq_count

    tables = jnp.asarray(dft_blocks(n))

    last = n - 1
    early_rows = share // 2
    parts = ((0, early_rows), (early_rows, share - early_rows))
    targets = n * tm_count

    def send(k, skip, size):
        sent = cut(snapshots, n, k, rows, skip, size)
        return partner(sent, "space", n, k)

    offsets = [k for k in range(n - 1, 0, -1) if k != last]
    pieces = [send(k, 0, share) for k in offsets]
    last_pieces = [send(last, skip, size) for skip, size in parts]
    before = early(tables, n, 0, cut(snapshots, n, 0, rows, 0, share))
    for k, piece in zip(offsets, pieces):
        before = early(tables, n, k, piece, before)
    weights = weights.reshape(1, rows)
    own, rest, other, later, gram, lent = first_part(
        tables, n, last, before, last_pieces[0], weights
    )
    traded = [partner(part, "freq", freq_count, 1) for part in (other, later, lent)]
    piece, (other, later, lent) = lax.optimization_barrier((last_pieces[1], traded))
    raw = partner(piece, "freq", freq_count, 1)
    *parts, gram = last_part(
        tables, n, last, 0, rest, piece, weights, gram, lent, own, other
    )
    *last_parts, gram = last_part(tables, n, last, targets, later, raw, weights, gram)
    grams = lax.all_to_all(
        gram,
        ("space", "tm"),
        split_axis=0,
        concat_axis=0,
        axis_index_groups=[list(range(targets - 1, -1, -1))],
        tiled=True,
    )
    total = rows * targets
    return finish(total, parts[:2], [*parts[2:], *last_parts], grams)


def solution(mesh):
    return jax.shard_map(
        on_device,
        mesh=mesh,
        in_specs=(P(None, "space", ("groups", "tm")), P(("groups", "tm", "space"))),
        out_specs=(
            P("freq", None, None, ("groups", "tm", "space")),
            P("groups", "freq", None, None),
        ),
        check_vma=False,
    )
```

```python
import functools

import numpy as np
import jax
import jax.numpy as jnp
from jax import lax
from jax.experimental import pallas as pl
from jax.experimental.pallas import tpu as pltpu
from jax.sharding import PartitionSpec as P

NB = 16
SEGMENT_FRAMES = 64
NF = 16
CUTS = 4
epsilon = 1e-05
MIB = 1024 * 1024
SMALL = pl.CostEstimate(flops=1, transcendentals=0, bytes_accessed=1)


def dft_blocks(groups):
    times = np.arange(SEGMENT_FRAMES)
    taper = 0.5 - 0.5 * np.cos(2.0 * np.pi * times / SEGMENT_FRAMES)
    taper = taper / np.sqrt(np.sum(taper * taper))
    bins = 1 + np.arange(NF)
    angles = 2.0 * np.pi * (bins[:, None] * times[None, :] % SEGMENT_FRAMES) / SEGMENT_FRAMES
    table = np.stack([np.cos(angles) * taper, -np.sin(angles) * taper])
    step = SEGMENT_FRAMES // groups
    table = table.reshape(2, 2, NF // 2, groups, step)
    spread = np.einsum("rhfgt,bc->ghrfbct", table, np.eye(NB))
    spread = spread.reshape(groups, 2 * NF * NB, NB * step).astype(np.float32)
    high = spread.astype(jnp.bfloat16)
    low = (spread - high.astype(np.float32)).astype(jnp.bfloat16)
    return np.concatenate([high, high, low], axis=2)


def split(x):
    high = x.astype(jnp.bfloat16)
    return high, (x - high.astype(jnp.float32)).astype(jnp.bfloat16)


def times_split(left, x):
    high, low = split(x)
    right = jnp.concatenate([high, low, high], axis=0)
    return jnp.dot(left, right, preferred_element_type=jnp.float32)


def rows_product(a, b):
    a_high, a_low = split(a)
    b_high, b_low = split(b)
    total = 0.0
    for x, y in ((a_low, b_low), (a_low, b_high), (a_high, b_low), (a_high, b_high)):
        total = total + lax.dot_general(
            x, y, (((1,), (1,)), ((), ())), preferred_element_type=jnp.float32
        )
    return total


def cut_kernel(n, k, rows, skip, x_ref, o_ref, sem):
    size = o_ref.shape[2]
    to = lax.bitwise_xor(lax.axis_index("space"), k)
    share = rows // 2
    start = pl.multiple_of(to * rows + lax.axis_index("freq") * share + skip, 128)
    part = NB // CUTS
    copies = []
    for i in range(CUTS):
        blocks = pl.ds(i * part, part)
        copies.append(
            pltpu.make_async_copy(
                x_ref.at[blocks, :, pl.ds(start, size)], o_ref.at[blocks], sem.at[i]
            )
        )
    for copy in copies:
        copy.start()
    for copy in copies:
        copy.wait()


def cut(snapshots, n, k, rows, skip, size):
    blocks, local_times, _ = snapshots.shape
    if local_times % 8 == 0:
        piece = pl.pallas_call(
            functools.partial(cut_kernel, n, k, rows, skip),
            out_shape=pltpu.VMEM((blocks, local_times, size), jnp.float32),
            in_specs=[pl.BlockSpec(memory_space=pltpu.HBM)],
            out_specs=pl.BlockSpec(memory_space=pltpu.VMEM),
            scratch_shapes=[pltpu.SemaphoreType.DMA((CUTS,))],
            compiler_params=pltpu.CompilerParams(vmem_limit_bytes=4 * MIB),
            cost_estimate=SMALL,
        )(pltpu.with_memory_space_constraint(snapshots, pltpu.HBM))
    else:
        to = lax.bitwise_xor(lax.axis_index("space"), k)
        start = to * rows + lax.axis_index("freq") * (rows // 2) + skip
        piece = lax.dynamic_slice_in_dim(snapshots, start, size, axis=2)
    return piece.reshape(blocks * local_times, size)


def early_kernel(n, k, t_ref, x_ref, *refs):
    src = lax.bitwise_xor(lax.axis_index("space"), k)
    part = times_split(t_ref[src], x_ref[...])
    refs[-1][...] = part if len(refs) == 1 else refs[0][...] + part


def early(tables, n, k, piece, *before):
    share = piece.shape[1]
    return pl.pallas_call(
        functools.partial(early_kernel, n, k),
        out_shape=jax.ShapeDtypeStruct((tables.shape[1], share), jnp.float32),
        compiler_params=pltpu.CompilerParams(vmem_limit_bytes=16 * MIB),
        cost_estimate=SMALL,
    )(tables, piece, *before)


def gram_of(z, weights):
    width = z.shape[0] // 2
    local = width // NB
    line = lax.broadcasted_iota(jnp.int32, (width, width), 0) // NB
    lane = lax.broadcasted_iota(jnp.int32, (width, width), 1) // NB
    row = lax.broadcasted_iota(jnp.int32, (NB, width), 0)
    col = lax.broadcasted_iota(jnp.int32, (NB, width), 1) % NB
    full = rows_product(z * weights, z)
    gram_re = full[:width, :width] + full[width:, width:]
    gram_im = full[:width, width:] - full[width:, :width]
    both = []
    for part in (gram_re, gram_im):
        kept = jnp.where(line == lane, part, 0.0)
        both.append(jnp.sum(kept.reshape(local, NB, width), axis=0))
    return jnp.where(row >= col, both[0], both[1])


def weights_at(w_ref, place, share, skip, size):
    return w_ref[:, pl.ds(pl.multiple_of(place * share + skip, 128), size)]


def first_part_kernel(
    n, k, t_ref, sum_ref, x_ref, w_ref, own_ref, rest_ref, other_ref, later_ref, gram_ref, lent_ref
):
    size = x_ref.shape[1]
    me = lax.axis_index("freq")
    src = lax.bitwise_xor(lax.axis_index("space"), k)
    spectra = sum_ref[:, :size] + times_split(t_ref[src], x_ref[...])
    weights = weights_at(w_ref, me, sum_ref.shape[1], 0, size)
    rest = sum_ref[:, size:]
    half = spectra.shape[0] // 2
    first = me == 0
    own_ref[...] = jnp.where(first, spectra[:half], spectra[half:])
    other_ref[...] = jnp.where(first, spectra[half:], spectra[:half])
    rest_ref[...] = jnp.where(first, rest[:half], rest[half:])
    later_ref[...] = jnp.where(first, rest[half:], rest[:half])
    grams = [gram_of(z, weights) for z in (spectra[:half], spectra[half:])]
    gram_ref[...] = jnp.where(first, grams[0], grams[1])
    lent_ref[...] = jnp.where(first, grams[1], grams[0])


def first_part(tables, n, k, partial_sum, piece, weights):
    share = partial_sum.shape[1]
    half = tables.shape[1] // 2
    size = piece.shape[1]
    gram = (NB, half // 2)
    shapes = [(half, size), (half, share - size), (half, size), (half, share - size), gram, gram]
    return pl.pallas_call(
        functools.partial(first_part_kernel, n, k),
        out_shape=[jax.ShapeDtypeStruct(shape, jnp.float32) for shape in shapes],
        compiler_params=pltpu.CompilerParams(vmem_limit_bytes=16 * MIB),
        cost_estimate=SMALL,
    )(tables, partial_sum, piece, weights)


def last_part_kernel(n, k, swapped, t_ref, sum_ref, x_ref, w_ref, *refs):
    half, size = sum_ref.shape
    me = lax.axis_index("freq")
    src = lax.bitwise_xor(lax.axis_index("space"), k)
    lines = pl.ds(pl.multiple_of(me * half, 128), half)
    spectra = sum_ref[...] + times_split(t_ref[src, lines], x_ref[...])
    share = w_ref.shape[1] // 2
    skip = share - size
    place = 1 - me if swapped else me
    gram = gram_of(spectra, weights_at(w_ref, place, share, skip, size))
    if swapped:
        before_ref, high_ref, low_ref, gram_ref = refs
        gram = gram + before_ref[...]
        high_ref[...], low_ref[...] = split(spectra)
        for d in range(gram_ref.shape[0]):
            gram_ref[d] = gram
        return
    gram_own_ref, gram_lent_ref, own_ref, other_ref, *refs = refs
    high_ref, low_ref, other_high_ref, other_low_ref, gram_ref = refs
    gram_ref[...] = gram + gram_own_ref[...] + gram_lent_ref[...]
    high_ref[:, :skip], low_ref[:, :skip] = split(own_ref[...])
    high_ref[:, skip:], low_ref[:, skip:] = split(spectra)
    other_high_ref[...], other_low_ref[...] = split(other_ref[...])


def last_part(tables, n, k, copies, partial_sum, piece, weights, *before):
    half, size = partial_sum.shape
    share = weights.shape[1] // 2
    gram = (NB, half // 2)
    widths = [size, size] if copies else [share, share, share - size, share - size]
    parts = [jax.ShapeDtypeStruct((half, width), jnp.bfloat16) for width in widths]
    gram = jax.ShapeDtypeStruct((copies, *gram) if copies else gram, jnp.float32)
    return pl.pallas_call(
        functools.partial(last_part_kernel, n, k, bool(copies)),
        out_shape=[*parts, gram],
        compiler_params=pltpu.CompilerParams(vmem_limit_bytes=16 * MIB),
        cost_estimate=SMALL,
    )(tables, partial_sum, piece, weights, *before)


def inv_sqrt(x):
    y = lax.rsqrt(x)
    return y * (1.5 - 0.5 * x * (y * y))


def finish_kernel(
    total,
    own_high_ref,
    own_low_ref,
    first_high_ref,
    first_low_ref,
    last_high_ref,
    last_low_ref,
    grams_ref,
    modes_ref,
    factor_ref,
):
    local = modes_ref.shape[0]
    width = local * NB
    share = modes_ref.shape[3] // 2
    gram = jnp.sum(grams_ref[...], axis=0) / total
    row = lax.broadcasted_iota(jnp.int32, (NB, width), 0)
    col = lax.broadcasted_iota(jnp.int32, (NB, width), 1) % NB
    stacked = [jnp.where(col == j, gram, 0.0) for j in range(NB)]
    for j in range(NB):
        line = jnp.broadcast_to(gram[j : j + 1, :], (NB, width))
        stacked.append(jnp.where((col == row) & (row > j), -line, 0.0))
    stacked = jnp.concatenate(stacked, axis=0)
    group_r = lax.broadcasted_iota(jnp.int32, (width, width), 0) // NB
    group_c = lax.broadcasted_iota(jnp.int32, (width, width), 1) // NB
    same = group_r == group_c
    ones = jnp.where(same, 1.0, 0.0).astype(jnp.bfloat16)
    spread = jnp.zeros(stacked.shape, jnp.float32)
    rest = stacked
    for _ in range(3):
        piece = rest.astype(jnp.bfloat16)
        rest = rest - piece.astype(jnp.float32)
        spread = spread + jnp.dot(piece, ones, preferred_element_type=jnp.float32)
    col_re = [[spread[j * NB + 8 * h : j * NB + 8 * h + 8] for h in (0, 1)] for j in range(NB)]
    base = NB * NB
    col_im = [
        [spread[base + j * NB + 8 * h : base + j * NB + 8 * h + 8] for h in (0, 1)]
        for j in range(NB)
    ]
    rows = [lax.broadcasted_iota(jnp.int32, (8, width), 0) + 8 * h for h in (0, 1)]
    lanes = lax.broadcasted_iota(jnp.int32, (8, width), 1) % NB
    inv_re = [jnp.where(rows[h] == lanes, 1.0, 0.0) for h in (0, 1)]
    inv_im = [jnp.zeros((8, width), jnp.float32) for h in (0, 1)]
    low_re = [jnp.zeros((8, width), jnp.float32) for h in (0, 1)]
    low_im = [jnp.zeros((8, width), jnp.float32) for h in (0, 1)]

    def pick(halves, i):
        return jnp.broadcast_to(halves[i // 8][i % 8 : i % 8 + 1, :], (8, width))

    pivots = [pick(col_re[j], j) + epsilon for j in range(NB)]
    scales = [jnp.zeros((8, width), jnp.float32) for h in (0, 1)]
    for p in range(NB):
        scale = inv_sqrt(pivots[p])
        inverse = scale * scale
        for h in range(p // 8, 2):
            below = rows[h] > p
            here = lanes == p
            scales[h] = jnp.where(rows[h] == p, scale, scales[h])
            col_re[p][h] = jnp.where(below, col_re[p][h], 0.0)
            col_im[p][h] = jnp.where(below, col_im[p][h], 0.0)
            diag = jnp.where(rows[h] == p, pivots[p], col_re[p][h])
            low_re[h] = jnp.where(here, diag * scale, low_re[h])
            low_im[h] = jnp.where(here, col_im[p][h] * scale, low_im[h])
        for j in range(p + 1, NB):
            a_re, a_im = pick(col_re[p], j), pick(col_im[p], j)
            u_re, u_im = a_re * inverse, a_im * inverse
            pivots[j] = pivots[j] - (a_re * u_re + a_im * u_im)
            for h in range(j // 8, 2):
                c_re, c_im = col_re[p][h], col_im[p][h]
                col_re[j][h] = col_re[j][h] - (c_re * u_re + c_im * u_im)
                col_im[j][h] = col_im[j][h] - (c_im * u_re - c_re * u_im)
        line_re = pick(inv_re, p) * inverse
        line_im = pick(inv_im, p) * inverse
        for h in range(p // 8, 2):
            c_re, c_im = col_re[p][h], col_im[p][h]
            inv_re[h] = inv_re[h] - (c_re * line_re - c_im * line_im)
            inv_im[h] = inv_im[h] - (c_re * line_im + c_im * line_re)
    inv_re = [inv_re[h] * scales[h] for h in (0, 1)]
    inv_im = [inv_im[h] * scales[h] for h in (0, 1)]

    me = lax.axis_index("freq")
    own = own_high_ref[...], own_low_ref[...]
    other = [
        jnp.concatenate([a[...], b[...]], axis=1)
        for a, b in ((first_high_ref, last_high_ref), (first_low_ref, last_low_ref))
    ]
    part = width // 2
    lane = lax.broadcasted_iota(jnp.int32, (NB, width), 1)
    left_half = lane < part
    line = lax.broadcasted_iota(jnp.int32, (width, width), 0) % part // NB
    block = lax.broadcasted_iota(jnp.int32, (width, width), 1) % part // NB
    inv_re, inv_im = jnp.concatenate(inv_re, axis=0), jnp.concatenate(inv_im, axis=0)
    turned_re, turned_im = pltpu.roll(inv_re, part, 1), pltpu.roll(inv_im, part, 1)
    for h in range(2):
        stay = left_half if h == 0 else jnp.logical_not(left_half)
        twice_re = jnp.where(stay, inv_re, turned_re)
        twice_im = jnp.where(stay, inv_im, turned_im)
        top = jnp.where(left_half, twice_re, twice_im)
        bottom = jnp.where(left_half, -twice_im, twice_re)
        count = part // NB
        mixing = jnp.concatenate([top] * count + [bottom] * count, axis=0)
        high, low = split(jnp.where(line == block, mixing, 0.0))
        left = jnp.concatenate([high, high, low], axis=1)
        lines = [slice(r * width + h * part, r * width + (h + 1) * part) for r in range(2)]
        for place, (x_high, x_low) in ((me, own), (1 - me, other)):
            right = [x[at] for x in (x_high, x_low, x_high) for at in lines]
            out = jnp.dot(
                left, jnp.concatenate(right, axis=0), preferred_element_type=jnp.float32
            )
            cols = pl.ds(pl.multiple_of(place * share, 128), share)
            for r in range(2):
                for f in range(count):
                    at = r * part + f * NB
                    modes_ref[h * count + f, r, :, cols] = out[at : at + NB]
    pad = jnp.zeros((width - NB, width), jnp.float32)
    turned_re = jnp.transpose(jnp.concatenate(low_re + [pad], axis=0))
    turned_im = jnp.transpose(jnp.concatenate(low_im + [pad], axis=0))
    for f in range(local):
        factor_ref[0, f] = turned_re[f * NB : (f + 1) * NB, :NB]
        factor_ref[1, f] = -turned_im[f * NB : (f + 1) * NB, :NB]


def finish(total, own, others, grams):
    half, share = own[0].shape
    local = half // (2 * NB)
    return pl.pallas_call(
        functools.partial(finish_kernel, total),
        out_shape=(
            jax.ShapeDtypeStruct((local, 2, NB, 2 * share), jnp.float32),
            jax.ShapeDtypeStruct((2, local, NB, NB), jnp.float32),
        ),
        compiler_params=pltpu.CompilerParams(vmem_limit_bytes=16 * MIB),
    )(*own, *others, grams)


def partner(value, axis, size, step):
    return lax.ppermute(value, axis, [(i, i ^ step) for i in range(size)])


def on_device(snapshots, weights):
    n = lax.axis_size("space")
    tm_count = lax.axis_size("tm")
    freq_count = lax.axis_size("freq")
    blocks, local_times, columns = snapshots.shape
    rows = columns // n
    share = rows // freq_count

    tables = jnp.asarray(dft_blocks(n))

    last = n - 1
    early_rows = share // 2
    parts = ((0, early_rows), (early_rows, share - early_rows))
    targets = n * tm_count

    def send(k, skip, size):
        sent = cut(snapshots, n, k, rows, skip, size)
        return partner(sent, "space", n, k)

    offsets = [k for k in range(n - 1, 0, -1) if k != last]
    pieces = [send(k, 0, share) for k in offsets]
    last_pieces = [send(last, skip, size) for skip, size in parts]
    before = early(tables, n, 0, cut(snapshots, n, 0, rows, 0, share))
    for k, piece in zip(offsets, pieces):
        before = early(tables, n, k, piece, before)
    weights = weights.reshape(1, rows)
    own, rest, other, later, gram, lent = first_part(
        tables, n, last, before, last_pieces[0], weights
    )
    traded = [partner(part, "freq", freq_count, 1) for part in (other, later, lent)]
    piece, (other, later, lent) = lax.optimization_barrier((last_pieces[1], traded))
    raw = partner(piece, "freq", freq_count, 1)
    *parts, gram = last_part(
        tables, n, last, 0, rest, piece, weights, gram, lent, own, other
    )
    *last_parts, gram = last_part(tables, n, last, targets, later, raw, weights, gram)
    grams = lax.all_to_all(
        gram,
        ("space", "tm"),
        split_axis=0,
        concat_axis=0,
        axis_index_groups=[list(range(targets - 1, -1, -1))],
        tiled=True,
    )
    total = rows * targets
    return finish(total, parts[:2], [*parts[2:], *last_parts], grams)


def solution(mesh):
    return jax.shard_map(
        on_device,
        mesh=mesh,
        in_specs=(P(None, "space", ("groups", "tm")), P(("groups", "tm", "space"))),
        out_specs=(
            P("freq", None, None, ("groups", "tm", "space")),
            P("groups", "freq", None, None),
        ),
        check_vma=False,
    )
```

```python
import functools

import numpy as np
import jax
import jax.numpy as jnp
from jax import lax
from jax.experimental import pallas as pl
from jax.experimental.pallas import tpu as pltpu
from jax.sharding import PartitionSpec as P

NB = 16
SEGMENT_FRAMES = 64
NF = 16
CUTS = 4
epsilon = 1e-05
MIB = 1024 * 1024
SMALL = pl.CostEstimate(flops=1, transcendentals=0, bytes_accessed=1)


def dft_blocks(groups):
    times = np.arange(SEGMENT_FRAMES)
    taper = 0.5 - 0.5 * np.cos(2.0 * np.pi * times / SEGMENT_FRAMES)
    taper = taper / np.sqrt(np.sum(taper * taper))
    bins = 1 + np.arange(NF)
    angles = 2.0 * np.pi * (bins[:, None] * times[None, :] % SEGMENT_FRAMES) / SEGMENT_FRAMES
    table = np.stack([np.cos(angles) * taper, -np.sin(angles) * taper])
    step = SEGMENT_FRAMES // groups
    table = table.reshape(2, 2, NF // 2, groups, step)
    spread = np.einsum("rhfgt,bc->ghrfbct", table, np.eye(NB))
    spread = spread.reshape(groups, 2 * NF * NB, NB * step).astype(np.float32)
    high = spread.astype(jnp.bfloat16)
    low = (spread - high.astype(np.float32)).astype(jnp.bfloat16)
    return np.concatenate([high, high, low], axis=2)


def split(x):
    high = x.astype(jnp.bfloat16)
    return high, (x - high.astype(jnp.float32)).astype(jnp.bfloat16)


def times_split(left, x):
    high, low = split(x)
    right = jnp.concatenate([high, low, high], axis=0)
    return jnp.dot(left, right, preferred_element_type=jnp.float32)


def rows_product(a, b):
    a_high, a_low = split(a)
    b_high, b_low = split(b)
    total = 0.0
    for x, y in ((a_low, b_low), (a_low, b_high), (a_high, b_low), (a_high, b_high)):
        total = total + lax.dot_general(
            x, y, (((1,), (1,)), ((), ())), preferred_element_type=jnp.float32
        )
    return total


def cut_kernel(n, k, rows, skip, x_ref, o_ref, sem):
    size = o_ref.shape[2]
    to = lax.bitwise_xor(lax.axis_index("space"), k)
    share = rows // 2
    start = pl.multiple_of(to * rows + lax.axis_index("freq") * share + skip, 128)
    part = NB // CUTS
    copies = []
    for i in range(CUTS):
        blocks = pl.ds(i * part, part)
        copies.append(
            pltpu.make_async_copy(
                x_ref.at[blocks, :, pl.ds(start, size)], o_ref.at[blocks], sem.at[i]
            )
        )
    for copy in copies:
        copy.start()
    for copy in copies:
        copy.wait()


def cut(snapshots, n, k, rows, skip, size):
    blocks, local_times, _ = snapshots.shape
    if local_times % 8 == 0:
        piece = pl.pallas_call(
            functools.partial(cut_kernel, n, k, rows, skip),
            out_shape=pltpu.VMEM((blocks, local_times, size), jnp.float32),
            in_specs=[pl.BlockSpec(memory_space=pltpu.HBM)],
            out_specs=pl.BlockSpec(memory_space=pltpu.VMEM),
            scratch_shapes=[pltpu.SemaphoreType.DMA((CUTS,))],
            compiler_params=pltpu.CompilerParams(vmem_limit_bytes=4 * MIB),
            cost_estimate=SMALL,
        )(pltpu.with_memory_space_constraint(snapshots, pltpu.HBM))
    else:
        to = lax.bitwise_xor(lax.axis_index("space"), k)
        start = to * rows + lax.axis_index("freq") * (rows // 2) + skip
        piece = lax.dynamic_slice_in_dim(snapshots, start, size, axis=2)
    return piece.reshape(blocks * local_times, size)


def early_kernel(n, k, t_ref, x_ref, *refs):
    src = lax.bitwise_xor(lax.axis_index("space"), k)
    part = times_split(t_ref[src], x_ref[...])
    refs[-1][...] = part if len(refs) == 1 else refs[0][...] + part


def early(tables, n, k, piece, *before):
    share = piece.shape[1]
    return pl.pallas_call(
        functools.partial(early_kernel, n, k),
        out_shape=jax.ShapeDtypeStruct((tables.shape[1], share), jnp.float32),
        compiler_params=pltpu.CompilerParams(vmem_limit_bytes=16 * MIB),
        cost_estimate=SMALL,
    )(tables, piece, *before)


def gram_of(z, weights):
    width = z.shape[0] // 2
    local = width // NB
    line = lax.broadcasted_iota(jnp.int32, (width, width), 0) // NB
    lane = lax.broadcasted_iota(jnp.int32, (width, width), 1) // NB
    row = lax.broadcasted_iota(jnp.int32, (NB, width), 0)
    col = lax.broadcasted_iota(jnp.int32, (NB, width), 1) % NB
    full = rows_product(z * weights, z)
    gram_re = full[:width, :width] + full[width:, width:]
    gram_im = full[:width, width:] - full[width:, :width]
    both = []
    for part in (gram_re, gram_im):
        kept = jnp.where(line == lane, part, 0.0)
        both.append(jnp.sum(kept.reshape(local, NB, width), axis=0))
    return jnp.where(row >= col, both[0], both[1])


def weights_at(w_ref, place, share, skip, size):
    return w_ref[:, pl.ds(pl.multiple_of(place * share + skip, 128), size)]


def first_part_kernel(
    n, k, t_ref, sum_ref, x_ref, w_ref, own_ref, rest_ref, other_ref, later_ref, gram_ref, lent_ref
):
    size = x_ref.shape[1]
    me = lax.axis_index("freq")
    src = lax.bitwise_xor(lax.axis_index("space"), k)
    spectra = sum_ref[:, :size] + times_split(t_ref[src], x_ref[...])
    weights = weights_at(w_ref, me, sum_ref.shape[1], 0, size)
    rest = sum_ref[:, size:]
    half = spectra.shape[0] // 2
    first = me == 0
    own_ref[...] = jnp.where(first, spectra[:half], spectra[half:])
    other_ref[...] = jnp.where(first, spectra[half:], spectra[:half])
    rest_ref[...] = jnp.where(first, rest[:half], rest[half:])
    later_ref[...] = jnp.where(first, rest[half:], rest[:half])
    grams = [gram_of(z, weights) for z in (spectra[:half], spectra[half:])]
    gram_ref[...] = jnp.where(first, grams[0], grams[1])
    lent_ref[...] = jnp.where(first, grams[1], grams[0])


def first_part(tables, n, k, partial_sum, piece, weights):
    share = partial_sum.shape[1]
    half = tables.shape[1] // 2
    size = piece.shape[1]
    gram = (NB, half // 2)
    shapes = [(half, size), (half, share - size), (half, size), (half, share - size), gram, gram]
    return pl.pallas_call(
        functools.partial(first_part_kernel, n, k),
        out_shape=[jax.ShapeDtypeStruct(shape, jnp.float32) for shape in shapes],
        compiler_params=pltpu.CompilerParams(vmem_limit_bytes=16 * MIB),
        cost_estimate=SMALL,
    )(tables, partial_sum, piece, weights)


def last_part_kernel(n, k, swapped, t_ref, sum_ref, x_ref, w_ref, *refs):
    half, size = sum_ref.shape
    me = lax.axis_index("freq")
    src = lax.bitwise_xor(lax.axis_index("space"), k)
    lines = pl.ds(pl.multiple_of(me * half, 128), half)
    spectra = sum_ref[...] + times_split(t_ref[src, lines], x_ref[...])
    share = w_ref.shape[1] // 2
    skip = share - size
    place = 1 - me if swapped else me
    gram = gram_of(spectra, weights_at(w_ref, place, share, skip, size))
    if swapped:
        before_ref, high_ref, low_ref, gram_ref = refs
        gram = gram + before_ref[...]
        high_ref[...], low_ref[...] = split(spectra)
        for d in range(gram_ref.shape[0]):
            gram_ref[d] = gram
        return
    gram_own_ref, gram_lent_ref, own_ref, other_ref, *refs = refs
    high_ref, low_ref, other_high_ref, other_low_ref, gram_ref = refs
    gram_ref[...] = gram + gram_own_ref[...] + gram_lent_ref[...]
    high_ref[:, :skip], low_ref[:, :skip] = split(own_ref[...])
    high_ref[:, skip:], low_ref[:, skip:] = split(spectra)
    other_high_ref[...], other_low_ref[...] = split(other_ref[...])


def last_part(tables, n, k, copies, partial_sum, piece, weights, *before):
    half, size = partial_sum.shape
    share = weights.shape[1] // 2
    gram = (NB, half // 2)
    widths = [size, size] if copies else [share, share, share - size, share - size]
    parts = [jax.ShapeDtypeStruct((half, width), jnp.bfloat16) for width in widths]
    gram = jax.ShapeDtypeStruct((copies, *gram) if copies else gram, jnp.float32)
    return pl.pallas_call(
        functools.partial(last_part_kernel, n, k, bool(copies)),
        out_shape=[*parts, gram],
        compiler_params=pltpu.CompilerParams(vmem_limit_bytes=16 * MIB),
        cost_estimate=SMALL,
    )(tables, partial_sum, piece, weights, *before)


def inv_sqrt(x):
    y = lax.rsqrt(x)
    return y * (1.5 - 0.5 * x * (y * y))


def finish_kernel(
    total,
    own_high_ref,
    own_low_ref,
    first_high_ref,
    first_low_ref,
    last_high_ref,
    last_low_ref,
    grams_ref,
    modes_ref,
    factor_ref,
):
    local = modes_ref.shape[0]
    width = local * NB
    share = modes_ref.shape[3] // 2
    gram = jnp.sum(grams_ref[...], axis=0) / total
    row = lax.broadcasted_iota(jnp.int32, (NB, width), 0)
    col = lax.broadcasted_iota(jnp.int32, (NB, width), 1) % NB
    stacked = [jnp.where(col == j, gram, 0.0) for j in range(NB)]
    for j in range(NB):
        line = jnp.broadcast_to(gram[j : j + 1, :], (NB, width))
        stacked.append(jnp.where((col == row) & (row > j), -line, 0.0))
    stacked = jnp.concatenate(stacked, axis=0)
    group_r = lax.broadcasted_iota(jnp.int32, (width, width), 0) // NB
    group_c = lax.broadcasted_iota(jnp.int32, (width, width), 1) // NB
    same = group_r == group_c
    ones = jnp.where(same, 1.0, 0.0).astype(jnp.bfloat16)
    spread = jnp.zeros(stacked.shape, jnp.float32)
    rest = stacked
    for _ in range(3):
        piece = rest.astype(jnp.bfloat16)
        rest = rest - piece.astype(jnp.float32)
        spread = spread + jnp.dot(piece, ones, preferred_element_type=jnp.float32)
    col_re = [[spread[j * NB + 8 * h : j * NB + 8 * h + 8] for h in (0, 1)] for j in range(NB)]
    base = NB * NB
    col_im = [
        [spread[base + j * NB + 8 * h : base + j * NB + 8 * h + 8] for h in (0, 1)]
        for j in range(NB)
    ]
    rows = [lax.broadcasted_iota(jnp.int32, (8, width), 0) + 8 * h for h in (0, 1)]
    lanes = lax.broadcasted_iota(jnp.int32, (8, width), 1) % NB
    inv_re = [jnp.where(rows[h] == lanes, 1.0, 0.0) for h in (0, 1)]
    inv_im = [jnp.zeros((8, width), jnp.float32) for h in (0, 1)]
    low_re = [jnp.zeros((8, width), jnp.float32) for h in (0, 1)]
    low_im = [jnp.zeros((8, width), jnp.float32) for h in (0, 1)]

    def pick(halves, i):
        return jnp.broadcast_to(halves[i // 8][i % 8 : i % 8 + 1, :], (8, width))

    pivots = [pick(col_re[j], j) + epsilon for j in range(NB)]
    scales = [jnp.zeros((8, width), jnp.float32) for h in (0, 1)]
    for p in range(NB):
        scale = inv_sqrt(pivots[p])
        inverse = scale * scale
        for h in range(p // 8, 2):
            below = rows[h] > p
            here = lanes == p
            scales[h] = jnp.where(rows[h] == p, scale, scales[h])
            col_re[p][h] = jnp.where(below, col_re[p][h], 0.0)
            col_im[p][h] = jnp.where(below, col_im[p][h], 0.0)
            diag = jnp.where(rows[h] == p, pivots[p], col_re[p][h])
            low_re[h] = jnp.where(here, diag * scale, low_re[h])
            low_im[h] = jnp.where(here, col_im[p][h] * scale, low_im[h])
        for j in range(p + 1, NB):
            a_re, a_im = pick(col_re[p], j), pick(col_im[p], j)
            u_re, u_im = a_re * inverse, a_im * inverse
            pivots[j] = pivots[j] - (a_re * u_re + a_im * u_im)
            for h in range(j // 8, 2):
                c_re, c_im = col_re[p][h], col_im[p][h]
                col_re[j][h] = col_re[j][h] - (c_re * u_re + c_im * u_im)
                col_im[j][h] = col_im[j][h] - (c_im * u_re - c_re * u_im)
        line_re = pick(inv_re, p) * inverse
        line_im = pick(inv_im, p) * inverse
        for h in range(p // 8, 2):
            c_re, c_im = col_re[p][h], col_im[p][h]
            inv_re[h] = inv_re[h] - (c_re * line_re - c_im * line_im)
            inv_im[h] = inv_im[h] - (c_re * line_im + c_im * line_re)
    inv_re = [inv_re[h] * scales[h] for h in (0, 1)]
    inv_im = [inv_im[h] * scales[h] for h in (0, 1)]

    me = lax.axis_index("freq")
    own = own_high_ref[...], own_low_ref[...]
    other = [
        jnp.concatenate([a[...], b[...]], axis=1)
        for a, b in ((first_high_ref, last_high_ref), (first_low_ref, last_low_ref))
    ]
    part = width // 2
    lane = lax.broadcasted_iota(jnp.int32, (NB, width), 1)
    left_half = lane < part
    line = lax.broadcasted_iota(jnp.int32, (width, width), 0) % part // NB
    block = lax.broadcasted_iota(jnp.int32, (width, width), 1) % part // NB
    inv_re, inv_im = jnp.concatenate(inv_re, axis=0), jnp.concatenate(inv_im, axis=0)
    turned_re, turned_im = pltpu.roll(inv_re, part, 1), pltpu.roll(inv_im, part, 1)
    for h in range(2):
        stay = left_half if h == 0 else jnp.logical_not(left_half)
        twice_re = jnp.where(stay, inv_re, turned_re)
        twice_im = jnp.where(stay, inv_im, turned_im)
        top = jnp.where(left_half, twice_re, twice_im)
        bottom = jnp.where(left_half, -twice_im, twice_re)
        count = part // NB
        mixing = jnp.concatenate([top] * count + [bottom] * count, axis=0)
        high, low = split(jnp.where(line == block, mixing, 0.0))
        left = jnp.concatenate([high, high, low], axis=1)
        lines = [slice(r * width + h * part, r * width + (h + 1) * part) for r in range(2)]
        for place, (x_high, x_low) in ((me, own), (1 - me, other)):
            right = [x[at] for x in (x_high, x_low, x_high) for at in lines]
            out = jnp.dot(
                left, jnp.concatenate(right, axis=0), preferred_element_type=jnp.float32
            )
            cols = pl.ds(pl.multiple_of(place * share, 128), share)
            for r in range(2):
                for f in range(count):
                    at = r * part + f * NB
                    modes_ref[h * count + f, r, :, cols] = out[at : at + NB]
    pad = jnp.zeros((width - NB, width), jnp.float32)
    turned_re = jnp.transpose(jnp.concatenate(low_re + [pad], axis=0))
    turned_im = jnp.transpose(jnp.concatenate(low_im + [pad], axis=0))
    for f in range(local):
        factor_ref[0, f] = turned_re[f * NB : (f + 1) * NB, :NB]
        factor_ref[1, f] = -turned_im[f * NB : (f + 1) * NB, :NB]


def finish(total, own, others, grams):
    half, share = own[0].shape
    local = half // (2 * NB)
    return pl.pallas_call(
        functools.partial(finish_kernel, total),
        out_shape=(
            jax.ShapeDtypeStruct((local, 2, NB, 2 * share), jnp.float32),
            jax.ShapeDtypeStruct((2, local, NB, NB), jnp.float32),
        ),
        compiler_params=pltpu.CompilerParams(vmem_limit_bytes=16 * MIB),
    )(*own, *others, grams)


def partner(value, axis, size, step):
    return lax.ppermute(value, axis, [(i, i ^ step) for i in range(size)])


def on_device(snapshots, weights):
    n = lax.axis_size("space")
    tm_count = lax.axis_size("tm")
    freq_count = lax.axis_size("freq")
    blocks, local_times, columns = snapshots.shape
    rows = columns // n
    share = rows // freq_count

    tables = jnp.asarray(dft_blocks(n))

    last = n - 1
    early_rows = share // 2
    parts = ((0, early_rows), (early_rows, share - early_rows))
    targets = n * tm_count

    def send(k, skip, size):
        sent = cut(snapshots, n, k, rows, skip, size)
        return partner(sent, "space", n, k)

    offsets = [k for k in range(n - 1, 0, -1) if k != last]
    pieces = [send(k, 0, share) for k in offsets]
    last_pieces = [send(last, skip, size) for skip, size in parts]
    before = early(tables, n, 0, cut(snapshots, n, 0, rows, 0, share))
    for k, piece in zip(offsets, pieces):
        before = early(tables, n, k, piece, before)
    weights = weights.reshape(1, rows)
    own, rest, other, later, gram, lent = first_part(
        tables, n, last, before, last_pieces[0], weights
    )
    traded = [partner(part, "freq", freq_count, 1) for part in (other, later, lent)]
    piece, (other, later, lent) = lax.optimization_barrier((last_pieces[1], traded))
    raw = partner(piece, "freq", freq_count, 1)
    *parts, gram = last_part(
        tables, n, last, 0, rest, piece, weights, gram, lent, own, other
    )
    *last_parts, gram = last_part(tables, n, last, targets, later, raw, weights, gram)
    order = sorted(range(n), key=lambda z: abs(2 * z - n))
    order = [z * tm_count + x for z in order for x in range(tm_count - 1, -1, -1)]
    grams = lax.all_to_all(
        gram,
        ("space", "tm"),
        split_axis=0,
        concat_axis=0,
        axis_index_groups=[order],
        tiled=True,
    )
    total = rows * targets
    return finish(total, parts[:2], [*parts[2:], *last_parts], grams)


def solution(mesh):
    return jax.shard_map(
        on_device,
        mesh=mesh,
        in_specs=(P(None, "space", ("groups", "tm")), P(("groups", "tm", "space"))),
        out_specs=(
            P("freq", None, None, ("groups", "tm", "space")),
            P("groups", "freq", None, None),
        ),
        check_vma=False,
    )
```

```python
import functools

import numpy as np
import jax
import jax.numpy as jnp
from jax import lax
from jax.experimental import pallas as pl
from jax.experimental.pallas import tpu as pltpu
from jax.sharding import PartitionSpec as P

NB = 16
SEGMENT_FRAMES = 64
NF = 16
CUTS = 4
epsilon = 1e-05
MIB = 1024 * 1024
SMALL = pl.CostEstimate(flops=1, transcendentals=0, bytes_accessed=1)


def dft_blocks(groups):
    times = np.arange(SEGMENT_FRAMES)
    taper = 0.5 - 0.5 * np.cos(2.0 * np.pi * times / SEGMENT_FRAMES)
    taper = taper / np.sqrt(np.sum(taper * taper))
    bins = 1 + np.arange(NF)
    angles = 2.0 * np.pi * (bins[:, None] * times[None, :] % SEGMENT_FRAMES) / SEGMENT_FRAMES
    table = np.stack([np.cos(angles) * taper, -np.sin(angles) * taper])
    step = SEGMENT_FRAMES // groups
    table = table.reshape(2, 2, NF // 2, groups, step)
    spread = np.einsum("rhfgt,bc->ghrfbct", table, np.eye(NB))
    spread = spread.reshape(groups, 2 * NF * NB, NB * step).astype(np.float32)
    high = spread.astype(jnp.bfloat16)
    low = (spread - high.astype(np.float32)).astype(jnp.bfloat16)
    return np.concatenate([high, high, low], axis=2)


def split(x):
    high = x.astype(jnp.bfloat16)
    return high, (x - high.astype(jnp.float32)).astype(jnp.bfloat16)


def times_split(left, x):
    high, low = split(x)
    right = jnp.concatenate([high, low, high], axis=0)
    return jnp.dot(left, right, preferred_element_type=jnp.float32)


def rows_product(a, b):
    a_high, a_low = split(a)
    b_high, b_low = split(b)
    total = 0.0
    for x, y in ((a_low, b_low), (a_low, b_high), (a_high, b_low), (a_high, b_high)):
        total = total + lax.dot_general(
            x, y, (((1,), (1,)), ((), ())), preferred_element_type=jnp.float32
        )
    return total


def cut_kernel(n, k, rows, skip, x_ref, o_ref, sem):
    size = o_ref.shape[2]
    to = lax.bitwise_xor(lax.axis_index("space"), k)
    share = rows // 2
    start = pl.multiple_of(to * rows + lax.axis_index("freq") * share + skip, 128)
    part = NB // CUTS
    copies = []
    for i in range(CUTS):
        blocks = pl.ds(i * part, part)
        copies.append(
            pltpu.make_async_copy(
                x_ref.at[blocks, :, pl.ds(start, size)], o_ref.at[blocks], sem.at[i]
            )
        )
    for copy in copies:
        copy.start()
    for copy in copies:
        copy.wait()


def cut(snapshots, n, k, rows, skip, size):
    blocks, local_times, _ = snapshots.shape
    if local_times % 8 == 0:
        piece = pl.pallas_call(
            functools.partial(cut_kernel, n, k, rows, skip),
            out_shape=pltpu.VMEM((blocks, local_times, size), jnp.float32),
            in_specs=[pl.BlockSpec(memory_space=pltpu.HBM)],
            out_specs=pl.BlockSpec(memory_space=pltpu.VMEM),
            scratch_shapes=[pltpu.SemaphoreType.DMA((CUTS,))],
            compiler_params=pltpu.CompilerParams(vmem_limit_bytes=4 * MIB),
            cost_estimate=SMALL,
        )(pltpu.with_memory_space_constraint(snapshots, pltpu.HBM))
    else:
        to = lax.bitwise_xor(lax.axis_index("space"), k)
        start = to * rows + lax.axis_index("freq") * (rows // 2) + skip
        piece = lax.dynamic_slice_in_dim(snapshots, start, size, axis=2)
    return piece.reshape(blocks * local_times, size)


def early_kernel(n, k, skip, t_ref, x_ref, *refs):
    src = lax.bitwise_xor(lax.axis_index("space"), k)
    part = times_split(t_ref[src], x_ref[...])
    if len(refs) == 1:
        refs[0][...] = part
        return
    before_ref, out_ref = refs
    end = skip + x_ref.shape[1]
    out_ref[:, skip:end] = before_ref[:, skip:end] + part
    if skip:
        out_ref[:, :skip] = before_ref[:, :skip]
    if end < out_ref.shape[1]:
        out_ref[:, end:] = before_ref[:, end:]


def early(tables, n, k, skip, piece, *before):
    share = before[0].shape[1] if before else piece.shape[1]
    return pl.pallas_call(
        functools.partial(early_kernel, n, k, skip),
        out_shape=jax.ShapeDtypeStruct((tables.shape[1], share), jnp.float32),
        compiler_params=pltpu.CompilerParams(vmem_limit_bytes=16 * MIB),
        cost_estimate=SMALL,
    )(tables, piece, *before)


def gram_of(z, weights):
    width = z.shape[0] // 2
    local = width // NB
    line = lax.broadcasted_iota(jnp.int32, (width, width), 0) // NB
    lane = lax.broadcasted_iota(jnp.int32, (width, width), 1) // NB
    row = lax.broadcasted_iota(jnp.int32, (NB, width), 0)
    col = lax.broadcasted_iota(jnp.int32, (NB, width), 1) % NB
    full = rows_product(z * weights, z)
    gram_re = full[:width, :width] + full[width:, width:]
    gram_im = full[:width, width:] - full[width:, :width]
    both = []
    for part in (gram_re, gram_im):
        kept = jnp.where(line == lane, part, 0.0)
        both.append(jnp.sum(kept.reshape(local, NB, width), axis=0))
    return jnp.where(row >= col, both[0], both[1])


def weights_at(w_ref, place, share, skip, size):
    return w_ref[:, pl.ds(pl.multiple_of(place * share + skip, 128), size)]


def first_part_kernel(
    sum_ref, w_ref, own_ref, rest_ref, other_ref, later_ref, gram_ref, lent_ref
):
    size = own_ref.shape[1]
    me = lax.axis_index("freq")
    spectra = sum_ref[:, :size]
    weights = weights_at(w_ref, me, sum_ref.shape[1], 0, size)
    rest = sum_ref[:, size:]
    half = spectra.shape[0] // 2
    first = me == 0
    own_ref[...] = jnp.where(first, spectra[:half], spectra[half:])
    other_ref[...] = jnp.where(first, spectra[half:], spectra[:half])
    rest_ref[...] = jnp.where(first, rest[:half], rest[half:])
    later_ref[...] = jnp.where(first, rest[half:], rest[:half])
    grams = [gram_of(z, weights) for z in (spectra[:half], spectra[half:])]
    gram_ref[...] = jnp.where(first, grams[0], grams[1])
    lent_ref[...] = jnp.where(first, grams[1], grams[0])


def first_part(size, partial_sum, weights):
    share = partial_sum.shape[1]
    half = partial_sum.shape[0] // 2
    gram = (NB, half // 2)
    shapes = [(half, size), (half, share - size), (half, size), (half, share - size), gram, gram]
    return pl.pallas_call(
        first_part_kernel,
        out_shape=[jax.ShapeDtypeStruct(shape, jnp.float32) for shape in shapes],
        compiler_params=pltpu.CompilerParams(vmem_limit_bytes=16 * MIB),
        cost_estimate=SMALL,
    )(partial_sum, weights)


def last_part_kernel(n, k, swapped, t_ref, sum_ref, x_ref, w_ref, *refs):
    half, size = sum_ref.shape
    me = lax.axis_index("freq")
    src = lax.bitwise_xor(lax.axis_index("space"), k)
    lines = pl.ds(pl.multiple_of(me * half, 128), half)
    spectra = sum_ref[...] + times_split(t_ref[src, lines], x_ref[...])
    share = w_ref.shape[1] // 2
    skip = share - size
    place = 1 - me if swapped else me
    gram = gram_of(spectra, weights_at(w_ref, place, share, skip, size))
    if swapped:
        before_ref, high_ref, low_ref, gram_ref = refs
        gram = gram + before_ref[...]
        high_ref[...], low_ref[...] = split(spectra)
        for d in range(gram_ref.shape[0]):
            gram_ref[d] = gram
        return
    gram_own_ref, gram_lent_ref, own_ref, other_ref, *refs = refs
    high_ref, low_ref, other_high_ref, other_low_ref, gram_ref = refs
    gram_ref[...] = gram + gram_own_ref[...] + gram_lent_ref[...]
    high_ref[:, :skip], low_ref[:, :skip] = split(own_ref[...])
    high_ref[:, skip:], low_ref[:, skip:] = split(spectra)
    other_high_ref[...], other_low_ref[...] = split(other_ref[...])


def last_part(tables, n, k, copies, partial_sum, piece, weights, *before):
    half, size = partial_sum.shape
    share = weights.shape[1] // 2
    gram = (NB, half // 2)
    widths = [size, size] if copies else [share, share, share - size, share - size]
    parts = [jax.ShapeDtypeStruct((half, width), jnp.bfloat16) for width in widths]
    gram = jax.ShapeDtypeStruct((copies, *gram) if copies else gram, jnp.float32)
    return pl.pallas_call(
        functools.partial(last_part_kernel, n, k, bool(copies)),
        out_shape=[*parts, gram],
        compiler_params=pltpu.CompilerParams(vmem_limit_bytes=16 * MIB),
        cost_estimate=SMALL,
    )(tables, partial_sum, piece, weights, *before)


def inv_sqrt(x):
    y = lax.rsqrt(x)
    return y * (1.5 - 0.5 * x * (y * y))


def finish_kernel(
    total,
    own_high_ref,
    own_low_ref,
    first_high_ref,
    first_low_ref,
    last_high_ref,
    last_low_ref,
    grams_ref,
    modes_ref,
    factor_ref,
):
    local = modes_ref.shape[0]
    width = local * NB
    share = modes_ref.shape[3] // 2
    gram = jnp.sum(grams_ref[...], axis=0) / total
    row = lax.broadcasted_iota(jnp.int32, (NB, width), 0)
    col = lax.broadcasted_iota(jnp.int32, (NB, width), 1) % NB
    stacked = [jnp.where(col == j, gram, 0.0) for j in range(NB)]
    for j in range(NB):
        line = jnp.broadcast_to(gram[j : j + 1, :], (NB, width))
        stacked.append(jnp.where((col == row) & (row > j), -line, 0.0))
    stacked = jnp.concatenate(stacked, axis=0)
    group_r = lax.broadcasted_iota(jnp.int32, (width, width), 0) // NB
    group_c = lax.broadcasted_iota(jnp.int32, (width, width), 1) // NB
    same = group_r == group_c
    ones = jnp.where(same, 1.0, 0.0).astype(jnp.bfloat16)
    spread = jnp.zeros(stacked.shape, jnp.float32)
    rest = stacked
    for _ in range(3):
        piece = rest.astype(jnp.bfloat16)
        rest = rest - piece.astype(jnp.float32)
        spread = spread + jnp.dot(piece, ones, preferred_element_type=jnp.float32)
    col_re = [[spread[j * NB + 8 * h : j * NB + 8 * h + 8] for h in (0, 1)] for j in range(NB)]
    base = NB * NB
    col_im = [
        [spread[base + j * NB + 8 * h : base + j * NB + 8 * h + 8] for h in (0, 1)]
        for j in range(NB)
    ]
    rows = [lax.broadcasted_iota(jnp.int32, (8, width), 0) + 8 * h for h in (0, 1)]
    lanes = lax.broadcasted_iota(jnp.int32, (8, width), 1) % NB
    inv_re = [jnp.where(rows[h] == lanes, 1.0, 0.0) for h in (0, 1)]
    inv_im = [jnp.zeros((8, width), jnp.float32) for h in (0, 1)]
    low_re = [jnp.zeros((8, width), jnp.float32) for h in (0, 1)]
    low_im = [jnp.zeros((8, width), jnp.float32) for h in (0, 1)]

    def pick(halves, i):
        return jnp.broadcast_to(halves[i // 8][i % 8 : i % 8 + 1, :], (8, width))

    pivots = [pick(col_re[j], j) + epsilon for j in range(NB)]
    scales = [jnp.zeros((8, width), jnp.float32) for h in (0, 1)]
    for p in range(NB):
        scale = inv_sqrt(pivots[p])
        inverse = scale * scale
        for h in range(p // 8, 2):
            below = rows[h] > p
            here = lanes == p
            scales[h] = jnp.where(rows[h] == p, scale, scales[h])
            col_re[p][h] = jnp.where(below, col_re[p][h], 0.0)
            col_im[p][h] = jnp.where(below, col_im[p][h], 0.0)
            diag = jnp.where(rows[h] == p, pivots[p], col_re[p][h])
            low_re[h] = jnp.where(here, diag * scale, low_re[h])
            low_im[h] = jnp.where(here, col_im[p][h] * scale, low_im[h])
        for j in range(p + 1, NB):
            a_re, a_im = pick(col_re[p], j), pick(col_im[p], j)
            u_re, u_im = a_re * inverse, a_im * inverse
            pivots[j] = pivots[j] - (a_re * u_re + a_im * u_im)
            for h in range(j // 8, 2):
                c_re, c_im = col_re[p][h], col_im[p][h]
                col_re[j][h] = col_re[j][h] - (c_re * u_re + c_im * u_im)
                col_im[j][h] = col_im[j][h] - (c_im * u_re - c_re * u_im)
        line_re = pick(inv_re, p) * inverse
        line_im = pick(inv_im, p) * inverse
        for h in range(p // 8, 2):
            c_re, c_im = col_re[p][h], col_im[p][h]
            inv_re[h] = inv_re[h] - (c_re * line_re - c_im * line_im)
            inv_im[h] = inv_im[h] - (c_re * line_im + c_im * line_re)
    inv_re = [inv_re[h] * scales[h] for h in (0, 1)]
    inv_im = [inv_im[h] * scales[h] for h in (0, 1)]

    me = lax.axis_index("freq")
    own = own_high_ref[...], own_low_ref[...]
    other = [
        jnp.concatenate([a[...], b[...]], axis=1)
        for a, b in ((first_high_ref, last_high_ref), (first_low_ref, last_low_ref))
    ]
    part = width // 2
    lane = lax.broadcasted_iota(jnp.int32, (NB, width), 1)
    left_half = lane < part
    line = lax.broadcasted_iota(jnp.int32, (width, width), 0) % part // NB
    block = lax.broadcasted_iota(jnp.int32, (width, width), 1) % part // NB
    inv_re, inv_im = jnp.concatenate(inv_re, axis=0), jnp.concatenate(inv_im, axis=0)
    turned_re, turned_im = pltpu.roll(inv_re, part, 1), pltpu.roll(inv_im, part, 1)
    for h in range(2):
        stay = left_half if h == 0 else jnp.logical_not(left_half)
        twice_re = jnp.where(stay, inv_re, turned_re)
        twice_im = jnp.where(stay, inv_im, turned_im)
        top = jnp.where(left_half, twice_re, twice_im)
        bottom = jnp.where(left_half, -twice_im, twice_re)
        count = part // NB
        mixing = jnp.concatenate([top] * count + [bottom] * count, axis=0)
        high, low = split(jnp.where(line == block, mixing, 0.0))
        left = jnp.concatenate([high, high, low], axis=1)
        lines = [slice(r * width + h * part, r * width + (h + 1) * part) for r in range(2)]
        for place, (x_high, x_low) in ((me, own), (1 - me, other)):
            right = [x[at] for x in (x_high, x_low, x_high) for at in lines]
            out = jnp.dot(
                left, jnp.concatenate(right, axis=0), preferred_element_type=jnp.float32
            )
            cols = pl.ds(pl.multiple_of(place * share, 128), share)
            for r in range(2):
                for f in range(count):
                    at = r * part + f * NB
                    modes_ref[h * count + f, r, :, cols] = out[at : at + NB]
    pad = jnp.zeros((width - NB, width), jnp.float32)
    turned_re = jnp.transpose(jnp.concatenate(low_re + [pad], axis=0))
    turned_im = jnp.transpose(jnp.concatenate(low_im + [pad], axis=0))
    for f in range(local):
        factor_ref[0, f] = turned_re[f * NB : (f + 1) * NB, :NB]
        factor_ref[1, f] = -turned_im[f * NB : (f + 1) * NB, :NB]


def finish(total, own, others, grams):
    half, share = own[0].shape
    local = half // (2 * NB)
    return pl.pallas_call(
        functools.partial(finish_kernel, total),
        out_shape=(
            jax.ShapeDtypeStruct((local, 2, NB, 2 * share), jnp.float32),
            jax.ShapeDtypeStruct((2, local, NB, NB), jnp.float32),
        ),
        compiler_params=pltpu.CompilerParams(vmem_limit_bytes=16 * MIB),
    )(*own, *others, grams)


def partner(value, axis, size, step):
    return lax.ppermute(value, axis, [(i, i ^ step) for i in range(size)])


def on_device(snapshots, weights):
    n = lax.axis_size("space")
    tm_count = lax.axis_size("tm")
    freq_count = lax.axis_size("freq")
    blocks, local_times, columns = snapshots.shape
    rows = columns // n
    share = rows // freq_count

    tables = jnp.asarray(dft_blocks(n))

    last = n - 1
    early_rows = share // 2
    targets = n * tm_count

    def send(k, skip, size):
        sent = cut(snapshots, n, k, rows, skip, size)
        return partner(sent, "space", n, k)

    halves = ((0, early_rows), (early_rows, share - early_rows))
    sends = [(last, *halves[0])]
    sends += [(k, *half) for k in range(n - 2, 0, -1) for half in halves]
    pieces = [(k, skip, send(k, skip, size)) for k, skip, size in sends]
    last_piece = send(last, *halves[1])
    before = early(tables, n, 0, 0, cut(snapshots, n, 0, rows, 0, share))
    for k, skip, piece in pieces:
        before = early(tables, n, k, skip, piece, before)
    weights = weights.reshape(1, rows)
    own, rest, other, later, gram, lent = first_part(early_rows, before, weights)
    traded = [partner(part, "freq", freq_count, 1) for part in (other, later, lent)]
    piece, (other, later, lent) = lax.optimization_barrier((last_piece, traded))
    raw = partner(piece, "freq", freq_count, 1)
    *parts, gram = last_part(
        tables, n, last, 0, rest, piece, weights, gram, lent, own, other
    )
    *last_parts, gram = last_part(tables, n, last, targets, later, raw, weights, gram)
    order = sorted(range(n), key=lambda z: abs(4 * z - (2 * n - 3)))
    order = [z * tm_count + x for z in order for x in range(tm_count - 1, -1, -1)]
    grams = lax.all_to_all(
        gram,
        ("space", "tm"),
        split_axis=0,
        concat_axis=0,
        axis_index_groups=[order],
        tiled=True,
    )
    total = rows * targets
    return finish(total, parts[:2], [*parts[2:], *last_parts], grams)


def solution(mesh):
    return jax.shard_map(
        on_device,
        mesh=mesh,
        in_specs=(P(None, "space", ("groups", "tm")), P(("groups", "tm", "space"))),
        out_specs=(
            P("freq", None, None, ("groups", "tm", "space")),
            P("groups", "freq", None, None),
        ),
        check_vma=False,
    )
```

```python
import functools

import numpy as np
import jax
import jax.numpy as jnp
from jax import lax
from jax.experimental import pallas as pl
from jax.experimental.pallas import tpu as pltpu
from jax.sharding import PartitionSpec as P

NB = 16
SEGMENT_FRAMES = 64
NF = 16
CUTS = 4
TRADED = 128
epsilon = 1e-05
MIB = 1024 * 1024
SMALL = pl.CostEstimate(flops=1, transcendentals=0, bytes_accessed=1)


def dft_blocks(groups):
    times = np.arange(SEGMENT_FRAMES)
    taper = 0.5 - 0.5 * np.cos(2.0 * np.pi * times / SEGMENT_FRAMES)
    taper = taper / np.sqrt(np.sum(taper * taper))
    bins = 1 + np.arange(NF)
    angles = 2.0 * np.pi * (bins[:, None] * times[None, :] % SEGMENT_FRAMES) / SEGMENT_FRAMES
    table = np.stack([np.cos(angles) * taper, -np.sin(angles) * taper])
    step = SEGMENT_FRAMES // groups
    table = table.reshape(2, 2, NF // 2, groups, step)
    spread = np.einsum("rhfgt,bc->ghrfbct", table, np.eye(NB))
    spread = spread.reshape(groups, 2 * NF * NB, NB * step).astype(np.float32)
    high = spread.astype(jnp.bfloat16)
    low = (spread - high.astype(np.float32)).astype(jnp.bfloat16)
    return np.concatenate([high, high, low], axis=2)


def split(x):
    high = x.astype(jnp.bfloat16)
    return high, (x - high.astype(jnp.float32)).astype(jnp.bfloat16)


def times_split(left, x):
    high, low = split(x)
    right = jnp.concatenate([high, low, high], axis=0)
    return jnp.dot(left, right, preferred_element_type=jnp.float32)


def rows_product(a, b):
    a_high, a_low = split(a)
    b_high, b_low = split(b)
    total = 0.0
    for x, y in ((a_low, b_low), (a_low, b_high), (a_high, b_low), (a_high, b_high)):
        total = total + lax.dot_general(
            x, y, (((1,), (1,)), ((), ())), preferred_element_type=jnp.float32
        )
    return total


def cut_kernel(n, k, rows, skip, x_ref, o_ref, sem):
    size = o_ref.shape[2]
    to = lax.bitwise_xor(lax.axis_index("space"), k)
    share = rows // 2
    start = pl.multiple_of(to * rows + lax.axis_index("freq") * share + skip, 128)
    part = NB // CUTS
    copies = []
    for i in range(CUTS):
        blocks = pl.ds(i * part, part)
        copies.append(
            pltpu.make_async_copy(
                x_ref.at[blocks, :, pl.ds(start, size)], o_ref.at[blocks], sem.at[i]
            )
        )
    for copy in copies:
        copy.start()
    for copy in copies:
        copy.wait()


def cut(snapshots, n, k, rows, skip, size):
    blocks, local_times, _ = snapshots.shape
    if local_times % 8 == 0:
        piece = pl.pallas_call(
            functools.partial(cut_kernel, n, k, rows, skip),
            out_shape=pltpu.VMEM((blocks, local_times, size), jnp.float32),
            in_specs=[pl.BlockSpec(memory_space=pltpu.HBM)],
            out_specs=pl.BlockSpec(memory_space=pltpu.VMEM),
            scratch_shapes=[pltpu.SemaphoreType.DMA((CUTS,))],
            compiler_params=pltpu.CompilerParams(vmem_limit_bytes=4 * MIB),
            cost_estimate=SMALL,
        )(pltpu.with_memory_space_constraint(snapshots, pltpu.HBM))
    else:
        to = lax.bitwise_xor(lax.axis_index("space"), k)
        start = to * rows + lax.axis_index("freq") * (rows // 2) + skip
        piece = lax.dynamic_slice_in_dim(snapshots, start, size, axis=2)
    return piece.reshape(blocks * local_times, size)


def early_kernel(n, k, skip, t_ref, x_ref, *refs):
    src = lax.bitwise_xor(lax.axis_index("space"), k)
    part = times_split(t_ref[src], x_ref[...])
    if len(refs) == 1:
        refs[0][...] = part
        return
    before_ref, out_ref = refs
    end = skip + x_ref.shape[1]
    out_ref[:, skip:end] = before_ref[:, skip:end] + part
    if skip:
        out_ref[:, :skip] = before_ref[:, :skip]
    if end < out_ref.shape[1]:
        out_ref[:, end:] = before_ref[:, end:]


def early(tables, n, k, skip, piece, *before):
    share = before[0].shape[1] if before else piece.shape[1]
    return pl.pallas_call(
        functools.partial(early_kernel, n, k, skip),
        out_shape=jax.ShapeDtypeStruct((tables.shape[1], share), jnp.float32),
        compiler_params=pltpu.CompilerParams(vmem_limit_bytes=16 * MIB),
        cost_estimate=SMALL,
    )(tables, piece, *before)


def gram_of(z, weights):
    width = z.shape[0] // 2
    local = width // NB
    line = lax.broadcasted_iota(jnp.int32, (width, width), 0) // NB
    lane = lax.broadcasted_iota(jnp.int32, (width, width), 1) // NB
    row = lax.broadcasted_iota(jnp.int32, (NB, width), 0)
    col = lax.broadcasted_iota(jnp.int32, (NB, width), 1) % NB
    full = rows_product(z * weights, z)
    gram_re = full[:width, :width] + full[width:, width:]
    gram_im = full[:width, width:] - full[width:, :width]
    both = []
    for part in (gram_re, gram_im):
        kept = jnp.where(line == lane, part, 0.0)
        both.append(jnp.sum(kept.reshape(local, NB, width), axis=0))
    return jnp.where(row >= col, both[0], both[1])


def weights_at(w_ref, place, share, skip, size):
    return w_ref[:, pl.ds(pl.multiple_of(place * share + skip, 128), size)]


def first_part_kernel(sum_ref, w_ref, own_ref, rest_ref, gram_ref, lent_ref, *traded_refs):
    size = own_ref.shape[1]
    me = lax.axis_index("freq")
    total = sum_ref[...]
    spectra = total[:, :size]
    weights = weights_at(w_ref, me, sum_ref.shape[1], 0, size)
    half = total.shape[0] // 2
    first = me == 0
    mine = jnp.where(first, total[:half], total[half:])
    own_ref[...] = mine[:, :size]
    rest_ref[...] = mine[:, size:]
    other = jnp.where(first, total[half:], total[:half])
    for i, ref in enumerate(traded_refs):
        ref[...] = other[:, i * TRADED : (i + 1) * TRADED]
    grams = [gram_of(z, weights) for z in (spectra[:half], spectra[half:])]
    gram_ref[...] = jnp.where(first, grams[0], grams[1])
    lent_ref[...] = jnp.where(first, grams[1], grams[0])


def first_part(size, partial_sum, weights):
    share = partial_sum.shape[1]
    half = partial_sum.shape[0] // 2
    gram = (NB, half // 2)
    shapes = [(half, size), (half, share - size), gram, gram]
    shapes += [(half, TRADED)] * (share // TRADED)
    return pl.pallas_call(
        first_part_kernel,
        out_shape=[jax.ShapeDtypeStruct(shape, jnp.float32) for shape in shapes],
        compiler_params=pltpu.CompilerParams(vmem_limit_bytes=16 * MIB),
        cost_estimate=SMALL,
    )(partial_sum, weights)


def last_part_kernel(n, k, swapped, t_ref, sum_ref, x_ref, w_ref, *refs):
    half, size = sum_ref.shape
    me = lax.axis_index("freq")
    src = lax.bitwise_xor(lax.axis_index("space"), k)
    lines = pl.ds(pl.multiple_of(me * half, 128), half)
    spectra = sum_ref[...] + times_split(t_ref[src, lines], x_ref[...])
    share = w_ref.shape[1] // 2
    skip = share - size
    place = 1 - me if swapped else me
    gram = gram_of(spectra, weights_at(w_ref, place, share, skip, size))
    if swapped:
        before_ref, lent_ref, high_ref, low_ref, gram_ref = refs
        gram = gram + before_ref[...] + lent_ref[...]
        high_ref[...], low_ref[...] = split(spectra)
        for d in range(gram_ref.shape[0]):
            gram_ref[d] = gram
        return
    before_ref, own_ref, *other_refs = refs[:-5]
    high_ref, low_ref, other_high_ref, other_low_ref, gram_ref = refs[-5:]
    gram_ref[...] = gram + before_ref[...]
    high_ref[:, :skip], low_ref[:, :skip] = split(own_ref[...])
    high_ref[:, skip:], low_ref[:, skip:] = split(spectra)
    other = jnp.concatenate([ref[...] for ref in other_refs], axis=1)
    other_high_ref[...], other_low_ref[...] = split(other)


def last_part(tables, n, k, copies, partial_sum, piece, weights, *before):
    half, size = partial_sum.shape
    share = weights.shape[1] // 2
    gram = (NB, half // 2)
    widths = [size, size] if copies else [share, share, share - size, share - size]
    parts = [jax.ShapeDtypeStruct((half, width), jnp.bfloat16) for width in widths]
    gram = jax.ShapeDtypeStruct((copies, *gram) if copies else gram, jnp.float32)
    return pl.pallas_call(
        functools.partial(last_part_kernel, n, k, bool(copies)),
        out_shape=[*parts, gram],
        compiler_params=pltpu.CompilerParams(vmem_limit_bytes=16 * MIB),
        cost_estimate=SMALL,
    )(tables, partial_sum, piece, weights, *before)


def inv_sqrt(x):
    y = lax.rsqrt(x)
    return y * (1.5 - 0.5 * x * (y * y))


def finish_kernel(
    total,
    own_high_ref,
    own_low_ref,
    first_high_ref,
    first_low_ref,
    last_high_ref,
    last_low_ref,
    grams_ref,
    modes_ref,
    factor_ref,
):
    local = modes_ref.shape[0]
    width = local * NB
    share = modes_ref.shape[3] // 2
    gram = jnp.sum(grams_ref[...], axis=0) / total
    row = lax.broadcasted_iota(jnp.int32, (NB, width), 0)
    col = lax.broadcasted_iota(jnp.int32, (NB, width), 1) % NB
    stacked = [jnp.where(col == j, gram, 0.0) for j in range(NB)]
    for j in range(NB):
        line = jnp.broadcast_to(gram[j : j + 1, :], (NB, width))
        stacked.append(jnp.where((col == row) & (row > j), -line, 0.0))
    stacked = jnp.concatenate(stacked, axis=0)
    group_r = lax.broadcasted_iota(jnp.int32, (width, width), 0) // NB
    group_c = lax.broadcasted_iota(jnp.int32, (width, width), 1) // NB
    same = group_r == group_c
    ones = jnp.where(same, 1.0, 0.0).astype(jnp.bfloat16)
    spread = jnp.zeros(stacked.shape, jnp.float32)
    rest = stacked
    for _ in range(3):
        piece = rest.astype(jnp.bfloat16)
        rest = rest - piece.astype(jnp.float32)
        spread = spread + jnp.dot(piece, ones, preferred_element_type=jnp.float32)
    col_re = [[spread[j * NB + 8 * h : j * NB + 8 * h + 8] for h in (0, 1)] for j in range(NB)]
    base = NB * NB
    col_im = [
        [spread[base + j * NB + 8 * h : base + j * NB + 8 * h + 8] for h in (0, 1)]
        for j in range(NB)
    ]
    rows = [lax.broadcasted_iota(jnp.int32, (8, width), 0) + 8 * h for h in (0, 1)]
    lanes = lax.broadcasted_iota(jnp.int32, (8, width), 1) % NB
    inv_re = [jnp.where(rows[h] == lanes, 1.0, 0.0) for h in (0, 1)]
    inv_im = [jnp.zeros((8, width), jnp.float32) for h in (0, 1)]
    low_re = [jnp.zeros((8, width), jnp.float32) for h in (0, 1)]
    low_im = [jnp.zeros((8, width), jnp.float32) for h in (0, 1)]

    def pick(halves, i):
        return jnp.broadcast_to(halves[i // 8][i % 8 : i % 8 + 1, :], (8, width))

    pivots = [pick(col_re[j], j) + epsilon for j in range(NB)]
    scales = [jnp.zeros((8, width), jnp.float32) for h in (0, 1)]
    for p in range(NB):
        scale = inv_sqrt(pivots[p])
        inverse = scale * scale
        for h in range(p // 8, 2):
            below = rows[h] > p
            here = lanes == p
            scales[h] = jnp.where(rows[h] == p, scale, scales[h])
            col_re[p][h] = jnp.where(below, col_re[p][h], 0.0)
            col_im[p][h] = jnp.where(below, col_im[p][h], 0.0)
            diag = jnp.where(rows[h] == p, pivots[p], col_re[p][h])
            low_re[h] = jnp.where(here, diag * scale, low_re[h])
            low_im[h] = jnp.where(here, col_im[p][h] * scale, low_im[h])
        for j in range(p + 1, NB):
            a_re, a_im = pick(col_re[p], j), pick(col_im[p], j)
            u_re, u_im = a_re * inverse, a_im * inverse
            pivots[j] = pivots[j] - (a_re * u_re + a_im * u_im)
            for h in range(j // 8, 2):
                c_re, c_im = col_re[p][h], col_im[p][h]
                col_re[j][h] = col_re[j][h] - (c_re * u_re + c_im * u_im)
                col_im[j][h] = col_im[j][h] - (c_im * u_re - c_re * u_im)
        line_re = pick(inv_re, p) * inverse
        line_im = pick(inv_im, p) * inverse
        for h in range(p // 8, 2):
            c_re, c_im = col_re[p][h], col_im[p][h]
            inv_re[h] = inv_re[h] - (c_re * line_re - c_im * line_im)
            inv_im[h] = inv_im[h] - (c_re * line_im + c_im * line_re)
    inv_re = [inv_re[h] * scales[h] for h in (0, 1)]
    inv_im = [inv_im[h] * scales[h] for h in (0, 1)]

    me = lax.axis_index("freq")
    own = own_high_ref[...], own_low_ref[...]
    other = [
        jnp.concatenate([a[...], b[...]], axis=1)
        for a, b in ((first_high_ref, last_high_ref), (first_low_ref, last_low_ref))
    ]
    part = width // 2
    lane = lax.broadcasted_iota(jnp.int32, (NB, width), 1)
    left_half = lane < part
    line = lax.broadcasted_iota(jnp.int32, (width, width), 0) % part // NB
    block = lax.broadcasted_iota(jnp.int32, (width, width), 1) % part // NB
    inv_re, inv_im = jnp.concatenate(inv_re, axis=0), jnp.concatenate(inv_im, axis=0)
    turned_re, turned_im = pltpu.roll(inv_re, part, 1), pltpu.roll(inv_im, part, 1)
    for h in range(2):
        stay = left_half if h == 0 else jnp.logical_not(left_half)
        twice_re = jnp.where(stay, inv_re, turned_re)
        twice_im = jnp.where(stay, inv_im, turned_im)
        top = jnp.where(left_half, twice_re, twice_im)
        bottom = jnp.where(left_half, -twice_im, twice_re)
        count = part // NB
        mixing = jnp.concatenate([top] * count + [bottom] * count, axis=0)
        high, low = split(jnp.where(line == block, mixing, 0.0))
        left = jnp.concatenate([high, high, low], axis=1)
        lines = [slice(r * width + h * part, r * width + (h + 1) * part) for r in range(2)]
        for place, (x_high, x_low) in ((me, own), (1 - me, other)):
            right = [x[at] for x in (x_high, x_low, x_high) for at in lines]
            out = jnp.dot(
                left, jnp.concatenate(right, axis=0), preferred_element_type=jnp.float32
            )
            cols = pl.ds(pl.multiple_of(place * share, 128), share)
            for r in range(2):
                for f in range(count):
                    at = r * part + f * NB
                    modes_ref[h * count + f, r, :, cols] = out[at : at + NB]
    pad = jnp.zeros((width - NB, width), jnp.float32)
    turned_re = jnp.transpose(jnp.concatenate(low_re + [pad], axis=0))
    turned_im = jnp.transpose(jnp.concatenate(low_im + [pad], axis=0))
    for f in range(local):
        factor_ref[0, f] = turned_re[f * NB : (f + 1) * NB, :NB]
        factor_ref[1, f] = -turned_im[f * NB : (f + 1) * NB, :NB]


def finish(total, own, others, grams):
    half, share = own[0].shape
    local = half // (2 * NB)
    return pl.pallas_call(
        functools.partial(finish_kernel, total),
        out_shape=(
            jax.ShapeDtypeStruct((local, 2, NB, 2 * share), jnp.float32),
            jax.ShapeDtypeStruct((2, local, NB, NB), jnp.float32),
        ),
        compiler_params=pltpu.CompilerParams(vmem_limit_bytes=16 * MIB),
    )(*own, *others, grams)


def partner(value, axis, size, step):
    return lax.ppermute(value, axis, [(i, i ^ step) for i in range(size)])


def on_device(snapshots, weights):
    n = lax.axis_size("space")
    tm_count = lax.axis_size("tm")
    freq_count = lax.axis_size("freq")
    blocks, local_times, columns = snapshots.shape
    rows = columns // n
    share = rows // freq_count

    tables = jnp.asarray(dft_blocks(n))

    last = n - 1
    early_rows = share - TRADED
    targets = n * tm_count

    def send(k, skip, size):
        sent = cut(snapshots, n, k, rows, skip, size)
        return partner(sent, "space", n, k)

    half = share // 2
    sends = [(last, 0, early_rows)]
    sends += [(k, skip, half) for k in range(n - 2, 0, -1) for skip in (0, half)]
    pieces = [(k, skip, send(k, skip, size)) for k, skip, size in sends]
    last_piece = send(last, early_rows, share - early_rows)
    before = early(tables, n, 0, 0, cut(snapshots, n, 0, rows, 0, share))
    for k, skip, piece in pieces:
        before = early(tables, n, k, skip, piece, before)
    weights = weights.reshape(1, rows)
    own, rest, gram, lent, *traded = first_part(early_rows, before, weights)
    lent = partner(lent, "freq", freq_count, 1)
    traded = [partner(part, "freq", freq_count, 1) for part in traded]
    piece, (*others, later) = lax.optimization_barrier((last_piece, traded))
    raw = partner(piece, "freq", freq_count, 1)
    *parts, gram = last_part(tables, n, last, 0, rest, piece, weights, gram, own, *others)
    *last_parts, gram = last_part(tables, n, last, targets, later, raw, weights, gram, lent)
    order = sorted(range(n), key=lambda z: abs(4 * z - (2 * n - 3)))
    order = [z * tm_count + x for z in order for x in range(tm_count - 1, -1, -1)]
    grams = lax.all_to_all(
        gram,
        ("space", "tm"),
        split_axis=0,
        concat_axis=0,
        axis_index_groups=[order],
        tiled=True,
    )
    total = rows * targets
    return finish(total, parts[:2], [*parts[2:], *last_parts], grams)


def solution(mesh):
    return jax.shard_map(
        on_device,
        mesh=mesh,
        in_specs=(P(None, "space", ("groups", "tm")), P(("groups", "tm", "space"))),
        out_specs=(
            P("freq", None, None, ("groups", "tm", "space")),
            P("groups", "freq", None, None),
        ),
        check_vma=False,
    )
```

```python
import functools

import numpy as np
import jax
import jax.numpy as jnp
from jax import lax
from jax.experimental import pallas as pl
from jax.experimental.pallas import tpu as pltpu
from jax.sharding import PartitionSpec as P

NB = 16
SEGMENT_FRAMES = 64
NF = 16
CUTS = 4
epsilon = 1e-05
MIB = 1024 * 1024
SMALL = pl.CostEstimate(flops=1, transcendentals=0, bytes_accessed=1)


def dft_blocks(groups):
    times = np.arange(SEGMENT_FRAMES)
    taper = 0.5 - 0.5 * np.cos(2.0 * np.pi * times / SEGMENT_FRAMES)
    taper = taper / np.sqrt(np.sum(taper * taper))
    bins = 1 + np.arange(NF)
    angles = 2.0 * np.pi * (bins[:, None] * times[None, :] % SEGMENT_FRAMES) / SEGMENT_FRAMES
    table = np.stack([np.cos(angles) * taper, -np.sin(angles) * taper])
    step = SEGMENT_FRAMES // groups
    table = table.reshape(2, 2, NF // 2, groups, step)
    spread = np.einsum("rhfgt,bc->ghrfbct", table, np.eye(NB))
    spread = spread.reshape(groups, 2 * NF * NB, NB * step).astype(np.float32)
    high = spread.astype(jnp.bfloat16)
    low = (spread - high.astype(np.float32)).astype(jnp.bfloat16)
    return np.concatenate([high, high, low], axis=2)


def split(x):
    high = x.astype(jnp.bfloat16)
    return high, (x - high.astype(jnp.float32)).astype(jnp.bfloat16)


def times_split(left, x):
    high, low = split(x)
    right = jnp.concatenate([high, low, high], axis=0)
    return jnp.dot(left, right, preferred_element_type=jnp.float32)


def rows_product(a, b):
    a_high, a_low = split(a)
    b_high, b_low = split(b)
    total = 0.0
    for x, y in ((a_low, b_low), (a_low, b_high), (a_high, b_low), (a_high, b_high)):
        total = total + lax.dot_general(
            x, y, (((1,), (1,)), ((), ())), preferred_element_type=jnp.float32
        )
    return total


def cut_kernel(n, k, rows, skip, x_ref, o_ref, sem):
    size = o_ref.shape[2]
    to = lax.bitwise_xor(lax.axis_index("space"), k)
    share = rows // 2
    start = pl.multiple_of(to * rows + lax.axis_index("freq") * share + skip, 128)
    part = NB // CUTS
    copies = []
    for i in range(CUTS):
        blocks = pl.ds(i * part, part)
        copies.append(
            pltpu.make_async_copy(
                x_ref.at[blocks, :, pl.ds(start, size)], o_ref.at[blocks], sem.at[i]
            )
        )
    for copy in copies:
        copy.start()
    for copy in copies:
        copy.wait()


def cut(snapshots, n, k, rows, skip, size):
    blocks, local_times, _ = snapshots.shape
    if local_times % 8 == 0:
        piece = pl.pallas_call(
            functools.partial(cut_kernel, n, k, rows, skip),
            out_shape=pltpu.VMEM((blocks, local_times, size), jnp.float32),
            in_specs=[pl.BlockSpec(memory_space=pltpu.HBM)],
            out_specs=pl.BlockSpec(memory_space=pltpu.VMEM),
            scratch_shapes=[pltpu.SemaphoreType.DMA((CUTS,))],
            compiler_params=pltpu.CompilerParams(vmem_limit_bytes=4 * MIB),
            cost_estimate=SMALL,
        )(pltpu.with_memory_space_constraint(snapshots, pltpu.HBM))
    else:
        to = lax.bitwise_xor(lax.axis_index("space"), k)
        start = to * rows + lax.axis_index("freq") * (rows // 2) + skip
        piece = lax.dynamic_slice_in_dim(snapshots, start, size, axis=2)
    return piece.reshape(blocks * local_times, size)


def early_kernel(n, k, skip, t_ref, x_ref, *refs):
    src = lax.bitwise_xor(lax.axis_index("space"), k)
    part = times_split(t_ref[src], x_ref[...])
    if len(refs) == 1:
        refs[0][...] = part
        return
    before_ref, out_ref = refs
    end = skip + x_ref.shape[1]
    out_ref[:, skip:end] = before_ref[:, skip:end] + part
    if skip:
        out_ref[:, :skip] = before_ref[:, :skip]
    if end < out_ref.shape[1]:
        out_ref[:, end:] = before_ref[:, end:]


def early(tables, n, k, skip, piece, *before):
    share = before[0].shape[1] if before else piece.shape[1]
    return pl.pallas_call(
        functools.partial(early_kernel, n, k, skip),
        out_shape=jax.ShapeDtypeStruct((tables.shape[1], share), jnp.float32),
        compiler_params=pltpu.CompilerParams(vmem_limit_bytes=16 * MIB),
        cost_estimate=SMALL,
    )(tables, piece, *before)


def gram_of(z, weights):
    width = z.shape[0] // 2
    local = width // NB
    line = lax.broadcasted_iota(jnp.int32, (width, width), 0) // NB
    lane = lax.broadcasted_iota(jnp.int32, (width, width), 1) // NB
    row = lax.broadcasted_iota(jnp.int32, (NB, width), 0)
    col = lax.broadcasted_iota(jnp.int32, (NB, width), 1) % NB
    full = rows_product(z * weights, z)
    gram_re = full[:width, :width] + full[width:, width:]
    gram_im = full[:width, width:] - full[width:, :width]
    both = []
    for part in (gram_re, gram_im):
        kept = jnp.where(line == lane, part, 0.0)
        both.append(jnp.sum(kept.reshape(local, NB, width), axis=0))
    return jnp.where(row >= col, both[0], both[1])


def weights_at(w_ref, place, share, skip, size):
    return w_ref[:, pl.ds(pl.multiple_of(place * share + skip, 128), size)]


def first_part_kernel(
    sum_ref, w_ref, own_ref, rest_ref, other_ref, later_ref, gram_ref, lent_ref
):
    size = own_ref.shape[1]
    me = lax.axis_index("freq")
    spectra = sum_ref[:, :size]
    weights = weights_at(w_ref, me, sum_ref.shape[1], 0, size)
    rest = sum_ref[:, size:]
    half = spectra.shape[0] // 2
    first = me == 0
    own_ref[...] = jnp.where(first, spectra[:half], spectra[half:])
    other_ref[...] = jnp.where(first, spectra[half:], spectra[:half])
    rest_ref[...] = jnp.where(first, rest[:half], rest[half:])
    later_ref[...] = jnp.where(first, rest[half:], rest[:half])
    grams = [gram_of(z, weights) for z in (spectra[:half], spectra[half:])]
    gram_ref[...] = jnp.where(first, grams[0], grams[1])
    lent_ref[...] = jnp.where(first, grams[1], grams[0])


def first_part(size, partial_sum, weights):
    share = partial_sum.shape[1]
    half = partial_sum.shape[0] // 2
    gram = (NB, half // 2)
    shapes = [(half, size), (half, share - size), (half, size), (half, share - size), gram, gram]
    return pl.pallas_call(
        first_part_kernel,
        out_shape=[jax.ShapeDtypeStruct(shape, jnp.float32) for shape in shapes],
        compiler_params=pltpu.CompilerParams(vmem_limit_bytes=16 * MIB),
        cost_estimate=SMALL,
    )(partial_sum, weights)


def last_part_kernel(n, k, swapped, t_ref, sum_ref, x_ref, w_ref, *refs):
    half, size = sum_ref.shape
    me = lax.axis_index("freq")
    src = lax.bitwise_xor(lax.axis_index("space"), k)
    lines = pl.ds(pl.multiple_of(me * half, 128), half)
    spectra = sum_ref[...] + times_split(t_ref[src, lines], x_ref[...])
    share = w_ref.shape[1] // 2
    skip = share - size
    place = 1 - me if swapped else me
    gram = gram_of(spectra, weights_at(w_ref, place, share, skip, size))
    if swapped:
        before_ref, high_ref, low_ref, gram_ref = refs
        gram = gram + before_ref[...]
        high_ref[...], low_ref[...] = split(spectra)
        for d in range(gram_ref.shape[0]):
            gram_ref[d] = gram
        return
    gram_own_ref, gram_lent_ref, own_ref, other_ref, *refs = refs
    high_ref, low_ref, other_high_ref, other_low_ref, gram_ref = refs
    gram_ref[...] = gram + gram_own_ref[...] + gram_lent_ref[...]
    high_ref[:, :skip], low_ref[:, :skip] = split(own_ref[...])
    high_ref[:, skip:], low_ref[:, skip:] = split(spectra)
    other_high_ref[...], other_low_ref[...] = split(other_ref[...])


def last_part(tables, n, k, copies, partial_sum, piece, weights, *before):
    half, size = partial_sum.shape
    share = weights.shape[1] // 2
    gram = (NB, half // 2)
    widths = [size, size] if copies else [share, share, share - size, share - size]
    parts = [jax.ShapeDtypeStruct((half, width), jnp.bfloat16) for width in widths]
    gram = jax.ShapeDtypeStruct((copies, *gram) if copies else gram, jnp.float32)
    return pl.pallas_call(
        functools.partial(last_part_kernel, n, k, bool(copies)),
        out_shape=[*parts, gram],
        compiler_params=pltpu.CompilerParams(vmem_limit_bytes=16 * MIB),
        cost_estimate=SMALL,
    )(tables, partial_sum, piece, weights, *before)


def inv_sqrt(x):
    y = lax.rsqrt(x)
    return y * (1.5 - 0.5 * x * (y * y))


def finish_kernel(
    total,
    own_high_ref,
    own_low_ref,
    first_high_ref,
    first_low_ref,
    last_high_ref,
    last_low_ref,
    grams_ref,
    modes_ref,
    factor_ref,
):
    local = modes_ref.shape[0]
    width = local * NB
    share = modes_ref.shape[3] // 2
    gram = jnp.sum(grams_ref[...], axis=0) / total
    row = lax.broadcasted_iota(jnp.int32, (NB, width), 0)
    col = lax.broadcasted_iota(jnp.int32, (NB, width), 1) % NB
    stacked = [jnp.where(col == j, gram, 0.0) for j in range(NB)]
    for j in range(NB):
        line = jnp.broadcast_to(gram[j : j + 1, :], (NB, width))
        stacked.append(jnp.where((col == row) & (row > j), -line, 0.0))
    stacked = jnp.concatenate(stacked, axis=0)
    group_r = lax.broadcasted_iota(jnp.int32, (width, width), 0) // NB
    group_c = lax.broadcasted_iota(jnp.int32, (width, width), 1) // NB
    same = group_r == group_c
    ones = jnp.where(same, 1.0, 0.0).astype(jnp.bfloat16)
    spread = jnp.zeros(stacked.shape, jnp.float32)
    rest = stacked
    for _ in range(3):
        piece = rest.astype(jnp.bfloat16)
        rest = rest - piece.astype(jnp.float32)
        spread = spread + jnp.dot(piece, ones, preferred_element_type=jnp.float32)
    col_re = [[spread[j * NB + 8 * h : j * NB + 8 * h + 8] for h in (0, 1)] for j in range(NB)]
    base = NB * NB
    col_im = [
        [spread[base + j * NB + 8 * h : base + j * NB + 8 * h + 8] for h in (0, 1)]
        for j in range(NB)
    ]
    rows = [lax.broadcasted_iota(jnp.int32, (8, width), 0) + 8 * h for h in (0, 1)]
    lanes = lax.broadcasted_iota(jnp.int32, (8, width), 1) % NB
    inv_re = [jnp.where(rows[h] == lanes, 1.0, 0.0) for h in (0, 1)]
    inv_im = [jnp.zeros((8, width), jnp.float32) for h in (0, 1)]
    low_re = [jnp.zeros((8, width), jnp.float32) for h in (0, 1)]
    low_im = [jnp.zeros((8, width), jnp.float32) for h in (0, 1)]

    def pick(halves, i):
        return jnp.broadcast_to(halves[i // 8][i % 8 : i % 8 + 1, :], (8, width))

    pivots = [pick(col_re[j], j) + epsilon for j in range(NB)]
    scales = [jnp.zeros((8, width), jnp.float32) for h in (0, 1)]
    for p in range(NB):
        scale = inv_sqrt(pivots[p])
        inverse = scale * scale
        for h in range(p // 8, 2):
            below = rows[h] > p
            here = lanes == p
            scales[h] = jnp.where(rows[h] == p, scale, scales[h])
            col_re[p][h] = jnp.where(below, col_re[p][h], 0.0)
            col_im[p][h] = jnp.where(below, col_im[p][h], 0.0)
            diag = jnp.where(rows[h] == p, pivots[p], col_re[p][h])
            low_re[h] = jnp.where(here, diag * scale, low_re[h])
            low_im[h] = jnp.where(here, col_im[p][h] * scale, low_im[h])
        for j in range(p + 1, NB):
            a_re, a_im = pick(col_re[p], j), pick(col_im[p], j)
            u_re, u_im = a_re * inverse, a_im * inverse
            pivots[j] = pivots[j] - (a_re * u_re + a_im * u_im)
            for h in range(j // 8, 2):
                c_re, c_im = col_re[p][h], col_im[p][h]
                col_re[j][h] = col_re[j][h] - (c_re * u_re + c_im * u_im)
                col_im[j][h] = col_im[j][h] - (c_im * u_re - c_re * u_im)
        line_re = pick(inv_re, p) * inverse
        line_im = pick(inv_im, p) * inverse
        for h in range(p // 8, 2):
            c_re, c_im = col_re[p][h], col_im[p][h]
            inv_re[h] = inv_re[h] - (c_re * line_re - c_im * line_im)
            inv_im[h] = inv_im[h] - (c_re * line_im + c_im * line_re)
    inv_re = [inv_re[h] * scales[h] for h in (0, 1)]
    inv_im = [inv_im[h] * scales[h] for h in (0, 1)]

    pad = jnp.zeros((width - NB, width), jnp.float32)
    upper_re = jnp.transpose(jnp.concatenate(low_re + [pad], axis=0))
    upper_im = jnp.transpose(jnp.concatenate(low_im + [pad], axis=0))
    for f in range(local):
        factor_ref[0, f] = upper_re[f * NB : (f + 1) * NB, :NB]
        factor_ref[1, f] = -upper_im[f * NB : (f + 1) * NB, :NB]
    me = lax.axis_index("freq")
    own = own_high_ref[...], own_low_ref[...]
    other = [
        jnp.concatenate([a[...], b[...]], axis=1)
        for a, b in ((first_high_ref, last_high_ref), (first_low_ref, last_low_ref))
    ]
    part = width // 2
    lane = lax.broadcasted_iota(jnp.int32, (NB, width), 1)
    left_half = lane < part
    line = lax.broadcasted_iota(jnp.int32, (width, width), 0) % part // NB
    block = lax.broadcasted_iota(jnp.int32, (width, width), 1) % part // NB
    inv_re, inv_im = jnp.concatenate(inv_re, axis=0), jnp.concatenate(inv_im, axis=0)
    turned_re, turned_im = pltpu.roll(inv_re, part, 1), pltpu.roll(inv_im, part, 1)
    for h in range(2):
        stay = left_half if h == 0 else jnp.logical_not(left_half)
        twice_re = jnp.where(stay, inv_re, turned_re)
        twice_im = jnp.where(stay, inv_im, turned_im)
        top = jnp.where(left_half, twice_re, twice_im)
        bottom = jnp.where(left_half, -twice_im, twice_re)
        count = part // NB
        mixing = jnp.concatenate([top] * count + [bottom] * count, axis=0)
        high, low = split(jnp.where(line == block, mixing, 0.0))
        left = jnp.concatenate([high, high, low], axis=1)
        lines = [slice(r * width + h * part, r * width + (h + 1) * part) for r in range(2)]
        for place, (x_high, x_low) in ((me, own), (1 - me, other)):
            right = [x[at] for x in (x_high, x_low, x_high) for at in lines]
            out = jnp.dot(
                left, jnp.concatenate(right, axis=0), preferred_element_type=jnp.float32
            )
            cols = pl.ds(pl.multiple_of(place * share, 128), share)
            for r in range(2):
                for f in range(count):
                    at = r * part + f * NB
                    modes_ref[h * count + f, r, :, cols] = out[at : at + NB]


def finish(total, own, others, grams):
    half, share = own[0].shape
    local = half // (2 * NB)
    return pl.pallas_call(
        functools.partial(finish_kernel, total),
        out_shape=(
            jax.ShapeDtypeStruct((local, 2, NB, 2 * share), jnp.float32),
            jax.ShapeDtypeStruct((2, local, NB, NB), jnp.float32),
        ),
        compiler_params=pltpu.CompilerParams(vmem_limit_bytes=16 * MIB),
    )(*own, *others, grams)


def partner(value, axis, size, step):
    return lax.ppermute(value, axis, [(i, i ^ step) for i in range(size)])


def on_device(snapshots, weights):
    n = lax.axis_size("space")
    tm_count = lax.axis_size("tm")
    freq_count = lax.axis_size("freq")
    blocks, local_times, columns = snapshots.shape
    rows = columns // n
    share = rows // freq_count

    tables = jnp.asarray(dft_blocks(n))

    last = n - 1
    early_rows = share // 2
    targets = n * tm_count

    def send(k, skip, size):
        sent = cut(snapshots, n, k, rows, skip, size)
        return partner(sent, "space", n, k)

    halves = ((0, early_rows), (early_rows, share - early_rows))
    sends = [(last, *halves[0])]
    sends += [(k, *half) for k in range(n - 2, 0, -1) for half in halves]
    pieces = [(k, skip, send(k, skip, size)) for k, skip, size in sends]
    last_piece = send(last, *halves[1])
    before = early(tables, n, 0, 0, cut(snapshots, n, 0, rows, 0, share))
    for k, skip, piece in pieces:
        before = early(tables, n, k, skip, piece, before)
    weights = weights.reshape(1, rows)
    own, rest, other, later, gram, lent = first_part(early_rows, before, weights)
    traded = [partner(part, "freq", freq_count, 1) for part in (other, later, lent)]
    piece, (other, later, lent) = lax.optimization_barrier((last_piece, traded))
    raw = partner(piece, "freq", freq_count, 1)
    *parts, gram = last_part(
        tables, n, last, 0, rest, piece, weights, gram, lent, own, other
    )
    *last_parts, gram = last_part(tables, n, last, targets, later, raw, weights, gram)
    order = [(z + 1) % n * tm_count + x for z in range(n) for x in range(tm_count - 1, -1, -1)]
    grams = lax.all_to_all(
        gram,
        ("space", "tm"),
        split_axis=0,
        concat_axis=0,
        axis_index_groups=[order],
        tiled=True,
    )
    total = rows * targets
    return finish(total, parts[:2], [*parts[2:], *last_parts], grams)


def solution(mesh):
    return jax.shard_map(
        on_device,
        mesh=mesh,
        in_specs=(P(None, "space", ("groups", "tm")), P(("groups", "tm", "space"))),
        out_specs=(
            P("freq", None, None, ("groups", "tm", "space")),
            P("groups", "freq", None, None),
        ),
        check_vma=False,
    )
```

```python
import functools

import numpy as np
import jax
import jax.numpy as jnp
from jax import lax
from jax.experimental import pallas as pl
from jax.experimental.pallas import tpu as pltpu
from jax.sharding import PartitionSpec as P

NB = 16
SEGMENT_FRAMES = 64
NF = 16
CUTS = 4
epsilon = 1e-05
MIB = 1024 * 1024
SMALL = pl.CostEstimate(flops=1, transcendentals=0, bytes_accessed=1)


def dft_blocks(groups):
    times = np.arange(SEGMENT_FRAMES)
    taper = 0.5 - 0.5 * np.cos(2.0 * np.pi * times / SEGMENT_FRAMES)
    taper = taper / np.sqrt(np.sum(taper * taper))
    bins = 1 + np.arange(NF)
    angles = 2.0 * np.pi * (bins[:, None] * times[None, :] % SEGMENT_FRAMES) / SEGMENT_FRAMES
    table = np.stack([np.cos(angles) * taper, -np.sin(angles) * taper])
    step = SEGMENT_FRAMES // groups
    table = table.reshape(2, 2, NF // 2, groups, step)
    spread = np.einsum("rhfgt,bc->ghrfbct", table, np.eye(NB))
    spread = spread.reshape(groups, 2 * NF * NB, NB * step).astype(np.float32)
    high = spread.astype(jnp.bfloat16)
    low = (spread - high.astype(np.float32)).astype(jnp.bfloat16)
    return np.concatenate([high, high, low], axis=2)


def split(x):
    high = x.astype(jnp.bfloat16)
    return high, (x - high.astype(jnp.float32)).astype(jnp.bfloat16)


def times_split(left, x):
    high, low = split(x)
    right = jnp.concatenate([high, low, high], axis=0)
    return jnp.dot(left, right, preferred_element_type=jnp.float32)


def rows_product(a, b):
    a_high, a_low = split(a)
    b_high, b_low = split(b)
    total = 0.0
    for x, y in ((a_low, b_low), (a_low, b_high), (a_high, b_low), (a_high, b_high)):
        total = total + lax.dot_general(
            x, y, (((1,), (1,)), ((), ())), preferred_element_type=jnp.float32
        )
    return total


def cut_kernel(n, k, rows, skip, x_ref, o_ref, sem):
    size = o_ref.shape[2]
    to = lax.bitwise_xor(lax.axis_index("space"), k)
    share = rows // 2
    start = pl.multiple_of(to * rows + lax.axis_index("freq") * share + skip, 128)
    part = NB // CUTS
    copies = []
    for i in range(CUTS):
        blocks = pl.ds(i * part, part)
        copies.append(
            pltpu.make_async_copy(
                x_ref.at[blocks, :, pl.ds(start, size)], o_ref.at[blocks], sem.at[i]
            )
        )
    for copy in copies:
        copy.start()
    for copy in copies:
        copy.wait()


def cut(snapshots, n, k, rows, skip, size):
    blocks, local_times, _ = snapshots.shape
    if local_times % 8 == 0:
        piece = pl.pallas_call(
            functools.partial(cut_kernel, n, k, rows, skip),
            out_shape=pltpu.VMEM((blocks, local_times, size), jnp.float32),
            in_specs=[pl.BlockSpec(memory_space=pltpu.HBM)],
            out_specs=pl.BlockSpec(memory_space=pltpu.VMEM),
            scratch_shapes=[pltpu.SemaphoreType.DMA((CUTS,))],
            compiler_params=pltpu.CompilerParams(vmem_limit_bytes=4 * MIB),
            cost_estimate=SMALL,
        )(pltpu.with_memory_space_constraint(snapshots, pltpu.HBM))
    else:
        to = lax.bitwise_xor(lax.axis_index("space"), k)
        start = to * rows + lax.axis_index("freq") * (rows // 2) + skip
        piece = lax.dynamic_slice_in_dim(snapshots, start, size, axis=2)
    return piece.reshape(blocks * local_times, size)


def early_kernel(n, k, skip, t_ref, x_ref, *refs):
    src = lax.bitwise_xor(lax.axis_index("space"), k)
    part = times_split(t_ref[src], x_ref[...])
    if len(refs) == 1:
        refs[0][...] = part
        return
    before_ref, out_ref = refs
    end = skip + x_ref.shape[1]
    out_ref[:, skip:end] = before_ref[:, skip:end] + part
    if skip:
        out_ref[:, :skip] = before_ref[:, :skip]
    if end < out_ref.shape[1]:
        out_ref[:, end:] = before_ref[:, end:]


def early(tables, n, k, skip, piece, *before):
    share = before[0].shape[1] if before else piece.shape[1]
    return pl.pallas_call(
        functools.partial(early_kernel, n, k, skip),
        out_shape=jax.ShapeDtypeStruct((tables.shape[1], share), jnp.float32),
        compiler_params=pltpu.CompilerParams(vmem_limit_bytes=16 * MIB),
        cost_estimate=SMALL,
    )(tables, piece, *before)


def gram_of(z, weights):
    width = z.shape[0] // 2
    local = width // NB
    line = lax.broadcasted_iota(jnp.int32, (width, width), 0) // NB
    lane = lax.broadcasted_iota(jnp.int32, (width, width), 1) // NB
    row = lax.broadcasted_iota(jnp.int32, (NB, width), 0)
    col = lax.broadcasted_iota(jnp.int32, (NB, width), 1) % NB
    full = rows_product(z * weights, z)
    gram_re = full[:width, :width] + full[width:, width:]
    gram_im = full[:width, width:] - full[width:, :width]
    both = []
    for part in (gram_re, gram_im):
        kept = jnp.where(line == lane, part, 0.0)
        both.append(jnp.sum(kept.reshape(local, NB, width), axis=0))
    return jnp.where(row >= col, both[0], both[1])


def weights_at(w_ref, place, share, skip, size):
    return w_ref[:, pl.ds(pl.multiple_of(place * share + skip, 128), size)]


def first_part_kernel(
    sum_ref, w_ref, own_ref, rest_ref, other_ref, later_ref, gram_ref, lent_ref
):
    size = own_ref.shape[1]
    me = lax.axis_index("freq")
    spectra = sum_ref[:, :size]
    weights = weights_at(w_ref, me, sum_ref.shape[1], 0, size)
    rest = sum_ref[:, size:]
    half = spectra.shape[0] // 2
    first = me == 0
    own_ref[...] = jnp.where(first, spectra[:half], spectra[half:])
    other_ref[...] = jnp.where(first, spectra[half:], spectra[:half])
    rest_ref[...] = jnp.where(first, rest[:half], rest[half:])
    later_ref[...] = jnp.where(first, rest[half:], rest[:half])
    grams = [gram_of(z, weights) for z in (spectra[:half], spectra[half:])]
    gram_ref[...] = jnp.where(first, grams[0], grams[1])
    lent_ref[...] = jnp.where(first, grams[1], grams[0])


def first_part(size, partial_sum, weights):
    share = partial_sum.shape[1]
    half = partial_sum.shape[0] // 2
    gram = (NB, half // 2)
    shapes = [(half, size), (half, share - size), (half, size), (half, share - size), gram, gram]
    return pl.pallas_call(
        first_part_kernel,
        out_shape=[jax.ShapeDtypeStruct(shape, jnp.float32) for shape in shapes],
        compiler_params=pltpu.CompilerParams(vmem_limit_bytes=16 * MIB),
        cost_estimate=SMALL,
    )(partial_sum, weights)


def last_part_kernel(n, k, swapped, t_ref, sum_ref, x_ref, w_ref, *refs):
    half, size = sum_ref.shape
    me = lax.axis_index("freq")
    src = lax.bitwise_xor(lax.axis_index("space"), k)
    lines = pl.ds(pl.multiple_of(me * half, 128), half)
    spectra = sum_ref[...] + times_split(t_ref[src, lines], x_ref[...])
    share = w_ref.shape[1] // 2
    skip = share - size
    place = 1 - me if swapped else me
    gram = gram_of(spectra, weights_at(w_ref, place, share, skip, size))
    if swapped:
        before_ref, high_ref, low_ref, gram_ref = refs
        gram = gram + before_ref[...]
        high_ref[...], low_ref[...] = split(spectra)
        for d in range(gram_ref.shape[0]):
            gram_ref[d] = gram
        return
    gram_own_ref, gram_lent_ref, own_ref, other_ref, *refs = refs
    high_ref, low_ref, other_high_ref, other_low_ref, gram_ref = refs
    gram_ref[...] = gram + gram_own_ref[...] + gram_lent_ref[...]
    high_ref[:, :skip], low_ref[:, :skip] = split(own_ref[...])
    high_ref[:, skip:], low_ref[:, skip:] = split(spectra)
    other_high_ref[...], other_low_ref[...] = split(other_ref[...])


def last_part(tables, n, k, copies, partial_sum, piece, weights, *before):
    half, size = partial_sum.shape
    share = weights.shape[1] // 2
    gram = (NB, half // 2)
    widths = [size, size] if copies else [share, share, share - size, share - size]
    parts = [jax.ShapeDtypeStruct((half, width), jnp.bfloat16) for width in widths]
    gram = jax.ShapeDtypeStruct((copies, *gram) if copies else gram, jnp.float32)
    return pl.pallas_call(
        functools.partial(last_part_kernel, n, k, bool(copies)),
        out_shape=[*parts, gram],
        compiler_params=pltpu.CompilerParams(vmem_limit_bytes=16 * MIB),
        cost_estimate=SMALL,
    )(tables, partial_sum, piece, weights, *before)


def inv_sqrt(x):
    y = lax.rsqrt(x)
    return y * (1.5 - 0.5 * x * (y * y))


def finish_kernel(
    total,
    own_high_ref,
    own_low_ref,
    first_high_ref,
    first_low_ref,
    last_high_ref,
    last_low_ref,
    grams_ref,
    modes_ref,
    factor_ref,
):
    local = modes_ref.shape[0]
    width = local * NB
    share = modes_ref.shape[3] // 2
    gram = jnp.sum(grams_ref[...], axis=0) / total
    row = lax.broadcasted_iota(jnp.int32, (NB, width), 0)
    col = lax.broadcasted_iota(jnp.int32, (NB, width), 1) % NB
    stacked = [jnp.where(col == j, gram, 0.0) for j in range(NB)]
    for j in range(NB):
        line = jnp.broadcast_to(gram[j : j + 1, :], (NB, width))
        stacked.append(jnp.where((col == row) & (row > j), -line, 0.0))
    stacked = jnp.concatenate(stacked, axis=0)
    group_r = lax.broadcasted_iota(jnp.int32, (width, width), 0) // NB
    group_c = lax.broadcasted_iota(jnp.int32, (width, width), 1) // NB
    same = group_r == group_c
    ones = jnp.where(same, 1.0, 0.0).astype(jnp.bfloat16)
    spread = jnp.zeros(stacked.shape, jnp.float32)
    rest = stacked
    for _ in range(3):
        piece = rest.astype(jnp.bfloat16)
        rest = rest - piece.astype(jnp.float32)
        spread = spread + jnp.dot(piece, ones, preferred_element_type=jnp.float32)
    col_re = [[spread[j * NB + 8 * h : j * NB + 8 * h + 8] for h in (0, 1)] for j in range(NB)]
    base = NB * NB
    col_im = [
        [spread[base + j * NB + 8 * h : base + j * NB + 8 * h + 8] for h in (0, 1)]
        for j in range(NB)
    ]
    rows = [lax.broadcasted_iota(jnp.int32, (8, width), 0) + 8 * h for h in (0, 1)]
    lanes = lax.broadcasted_iota(jnp.int32, (8, width), 1) % NB
    inv_re = [jnp.where(rows[h] == lanes, 1.0, 0.0) for h in (0, 1)]
    inv_im = [jnp.zeros((8, width), jnp.float32) for h in (0, 1)]
    low_re = [jnp.zeros((8, width), jnp.float32) for h in (0, 1)]
    low_im = [jnp.zeros((8, width), jnp.float32) for h in (0, 1)]

    def pick(halves, i):
        return jnp.broadcast_to(halves[i // 8][i % 8 : i % 8 + 1, :], (8, width))

    pivots = [pick(col_re[j], j) + epsilon for j in range(NB)]
    scales = [jnp.zeros((8, width), jnp.float32) for h in (0, 1)]
    for p in range(NB):
        scale = inv_sqrt(pivots[p])
        inverse = scale * scale
        for h in range(p // 8, 2):
            below = rows[h] > p
            here = lanes == p
            scales[h] = jnp.where(rows[h] == p, scale, scales[h])
            col_re[p][h] = jnp.where(below, col_re[p][h], 0.0)
            col_im[p][h] = jnp.where(below, col_im[p][h], 0.0)
            diag = jnp.where(rows[h] == p, pivots[p], col_re[p][h])
            low_re[h] = jnp.where(here, diag * scale, low_re[h])
            low_im[h] = jnp.where(here, col_im[p][h] * scale, low_im[h])
        for j in range(p + 1, NB):
            a_re, a_im = pick(col_re[p], j), pick(col_im[p], j)
            u_re, u_im = a_re * inverse, a_im * inverse
            pivots[j] = pivots[j] - (a_re * u_re + a_im * u_im)
            for h in range(j // 8, 2):
                c_re, c_im = col_re[p][h], col_im[p][h]
                col_re[j][h] = col_re[j][h] - (c_re * u_re + c_im * u_im)
                col_im[j][h] = col_im[j][h] - (c_im * u_re - c_re * u_im)
        line_re = pick(inv_re, p) * inverse
        line_im = pick(inv_im, p) * inverse
        for h in range(p // 8, 2):
            c_re, c_im = col_re[p][h], col_im[p][h]
            inv_re[h] = inv_re[h] - (c_re * line_re - c_im * line_im)
            inv_im[h] = inv_im[h] - (c_re * line_im + c_im * line_re)
    inv_re = [inv_re[h] * scales[h] for h in (0, 1)]
    inv_im = [inv_im[h] * scales[h] for h in (0, 1)]

    pad = jnp.zeros((width - NB, width), jnp.float32)
    upper_re = jnp.transpose(jnp.concatenate(low_re + [pad], axis=0))
    upper_im = jnp.transpose(jnp.concatenate(low_im + [pad], axis=0))
    for f in range(local):
        factor_ref[0, f] = upper_re[f * NB : (f + 1) * NB, :NB]
        factor_ref[1, f] = -upper_im[f * NB : (f + 1) * NB, :NB]
    me = lax.axis_index("freq")
    own = own_high_ref[...], own_low_ref[...]
    other = [
        jnp.concatenate([a[...], b[...]], axis=1)
        for a, b in ((first_high_ref, last_high_ref), (first_low_ref, last_low_ref))
    ]
    part = width // 2
    lane = lax.broadcasted_iota(jnp.int32, (NB, width), 1)
    left_half = lane < part
    line = lax.broadcasted_iota(jnp.int32, (width, width), 0) % part // NB
    block = lax.broadcasted_iota(jnp.int32, (width, width), 1) % part // NB
    inv_re, inv_im = jnp.concatenate(inv_re, axis=0), jnp.concatenate(inv_im, axis=0)
    turned_re, turned_im = pltpu.roll(inv_re, part, 1), pltpu.roll(inv_im, part, 1)
    for h in range(2):
        stay = left_half if h == 0 else jnp.logical_not(left_half)
        twice_re = jnp.where(stay, inv_re, turned_re)
        twice_im = jnp.where(stay, inv_im, turned_im)
        top = jnp.where(left_half, twice_re, twice_im)
        bottom = jnp.where(left_half, -twice_im, twice_re)
        count = part // NB
        mixing = jnp.concatenate([top] * count + [bottom] * count, axis=0)
        high, low = split(jnp.where(line == block, mixing, 0.0))
        left = jnp.concatenate([high, high, low], axis=1)
        lines = [slice(r * width + h * part, r * width + (h + 1) * part) for r in range(2)]
        for place, (x_high, x_low) in ((me, own), (1 - me, other)):
            right = [x[at] for x in (x_high, x_low, x_high) for at in lines]
            out = jnp.dot(
                left, jnp.concatenate(right, axis=0), preferred_element_type=jnp.float32
            )
            cols = pl.ds(pl.multiple_of(place * share, 128), share)
            for r in range(2):
                for f in range(count):
                    at = r * part + f * NB
                    modes_ref[h * count + f, r, :, cols] = out[at : at + NB]


def finish(total, own, others, grams):
    half, share = own[0].shape
    local = half // (2 * NB)
    return pl.pallas_call(
        functools.partial(finish_kernel, total),
        out_shape=(
            jax.ShapeDtypeStruct((local, 2, NB, 2 * share), jnp.float32),
            jax.ShapeDtypeStruct((2, local, NB, NB), jnp.float32),
        ),
        compiler_params=pltpu.CompilerParams(vmem_limit_bytes=16 * MIB),
    )(*own, *others, grams)


def partner(value, axis, size, step):
    return lax.ppermute(value, axis, [(i, i ^ step) for i in range(size)])


def on_device(snapshots, weights):
    n = lax.axis_size("space")
    tm_count = lax.axis_size("tm")
    freq_count = lax.axis_size("freq")
    blocks, local_times, columns = snapshots.shape
    rows = columns // n
    share = rows // freq_count

    tables = jnp.asarray(dft_blocks(n))

    last = n - 1
    early_rows = share // 2
    targets = n * tm_count

    def send(k, skip, size):
        sent = cut(snapshots, n, k, rows, skip, size)
        return partner(sent, "space", n, k)

    halves = ((0, early_rows), (early_rows, share - early_rows))
    sends = [(last, *halves[0])]
    sends += [(k, *half) for k in range(n - 2, 0, -1) for half in halves]
    pieces = [(k, skip, send(k, skip, size)) for k, skip, size in sends]
    last_piece = send(last, *halves[1])
    before = early(tables, n, 0, 0, cut(snapshots, n, 0, rows, 0, share))
    for k, skip, piece in pieces:
        before = early(tables, n, k, skip, piece, before)
    weights = weights.reshape(1, rows)
    own, rest, other, later, gram, lent = first_part(early_rows, before, weights)
    traded = [partner(part, "freq", freq_count, 1) for part in (other, later, lent)]
    piece, (other, later, lent) = lax.optimization_barrier((last_piece, traded))
    raw = partner(piece, "freq", freq_count, 1)
    *parts, gram = last_part(
        tables, n, last, 0, rest, piece, weights, gram, lent, own, other
    )
    *last_parts, gram = last_part(tables, n, last, targets, later, raw, weights, gram)
    order = list(range(targets - 1, -1, -1))
    grams = lax.all_to_all(
        gram,
        ("space", "tm"),
        split_axis=0,
        concat_axis=0,
        axis_index_groups=[order],
        tiled=True,
    )
    total = rows * targets
    return finish(total, parts[:2], [*parts[2:], *last_parts], grams)


def solution(mesh):
    return jax.shard_map(
        on_device,
        mesh=mesh,
        in_specs=(P(None, "space", ("groups", "tm")), P(("groups", "tm", "space"))),
        out_specs=(
            P("freq", None, None, ("groups", "tm", "space")),
            P("groups", "freq", None, None),
        ),
        check_vma=False,
    )
```

```python
import functools

import numpy as np
import jax
import jax.numpy as jnp
from jax import lax
from jax.experimental import pallas as pl
from jax.experimental.pallas import tpu as pltpu
from jax.sharding import PartitionSpec as P

NB = 16
SEGMENT_FRAMES = 64
NF = 16
CUTS = 4
epsilon = 1e-05
MIB = 1024 * 1024
SMALL = pl.CostEstimate(flops=1, transcendentals=0, bytes_accessed=1)


def dft_blocks(groups):
    times = np.arange(SEGMENT_FRAMES)
    taper = 0.5 - 0.5 * np.cos(2.0 * np.pi * times / SEGMENT_FRAMES)
    taper = taper / np.sqrt(np.sum(taper * taper))
    bins = 1 + np.arange(NF)
    angles = 2.0 * np.pi * (bins[:, None] * times[None, :] % SEGMENT_FRAMES) / SEGMENT_FRAMES
    table = np.stack([np.cos(angles) * taper, -np.sin(angles) * taper])
    step = SEGMENT_FRAMES // groups
    table = table.reshape(2, 2, NF // 2, groups, step)
    spread = np.einsum("rhfgt,bc->ghrfbct", table, np.eye(NB))
    spread = spread.reshape(groups, 2 * NF * NB, NB * step).astype(np.float32)
    high = spread.astype(jnp.bfloat16)
    low = (spread - high.astype(np.float32)).astype(jnp.bfloat16)
    return np.concatenate([high, high, low], axis=2)


def split(x):
    high = x.astype(jnp.bfloat16)
    return high, (x - high.astype(jnp.float32)).astype(jnp.bfloat16)


def times_split(left, x):
    high, low = split(x)
    right = jnp.concatenate([high, low, high], axis=0)
    return jnp.dot(left, right, preferred_element_type=jnp.float32)


def rows_product(a, b):
    lines, columns = a.shape[0], b.shape[0]
    full = lax.dot_general(
        jnp.concatenate(split(a), axis=0),
        jnp.concatenate(split(b), axis=0),
        (((1,), (1,)), ((), ())),
        preferred_element_type=jnp.float32,
    )
    small = full[lines:, columns:] + full[lines:, :columns] + full[:lines, columns:]
    return small + full[:lines, :columns]


def cut_kernel(n, k, rows, skip, x_ref, o_ref, sem):
    size = o_ref.shape[2]
    to = lax.bitwise_xor(lax.axis_index("space"), k)
    share = rows // 2
    start = pl.multiple_of(to * rows + lax.axis_index("freq") * share + skip, 128)
    part = NB // CUTS
    copies = []
    for i in range(CUTS):
        blocks = pl.ds(i * part, part)
        copies.append(
            pltpu.make_async_copy(
                x_ref.at[blocks, :, pl.ds(start, size)], o_ref.at[blocks], sem.at[i]
            )
        )
    for copy in copies:
        copy.start()
    for copy in copies:
        copy.wait()


def cut(snapshots, n, k, rows, skip, size):
    blocks, local_times, _ = snapshots.shape
    if local_times % 8 == 0:
        piece = pl.pallas_call(
            functools.partial(cut_kernel, n, k, rows, skip),
            out_shape=pltpu.VMEM((blocks, local_times, size), jnp.float32),
            in_specs=[pl.BlockSpec(memory_space=pltpu.HBM)],
            out_specs=pl.BlockSpec(memory_space=pltpu.VMEM),
            scratch_shapes=[pltpu.SemaphoreType.DMA((CUTS,))],
            compiler_params=pltpu.CompilerParams(vmem_limit_bytes=4 * MIB),
            cost_estimate=SMALL,
        )(pltpu.with_memory_space_constraint(snapshots, pltpu.HBM))
    else:
        to = lax.bitwise_xor(lax.axis_index("space"), k)
        start = to * rows + lax.axis_index("freq") * (rows // 2) + skip
        piece = lax.dynamic_slice_in_dim(snapshots, start, size, axis=2)
    return piece.reshape(blocks * local_times, size)


def early_kernel(n, k, skip, t_ref, x_ref, *refs):
    src = lax.bitwise_xor(lax.axis_index("space"), k)
    part = times_split(t_ref[src], x_ref[...])
    if len(refs) == 1:
        refs[0][...] = part
        return
    before_ref, out_ref = refs
    end = skip + x_ref.shape[1]
    out_ref[:, skip:end] = before_ref[:, skip:end] + part
    if skip:
        out_ref[:, :skip] = before_ref[:, :skip]
    if end < out_ref.shape[1]:
        out_ref[:, end:] = before_ref[:, end:]


def early(tables, n, k, skip, piece, *before):
    share = before[0].shape[1] if before else piece.shape[1]
    return pl.pallas_call(
        functools.partial(early_kernel, n, k, skip),
        out_shape=jax.ShapeDtypeStruct((tables.shape[1], share), jnp.float32),
        compiler_params=pltpu.CompilerParams(vmem_limit_bytes=16 * MIB),
        cost_estimate=SMALL,
    )(tables, piece, *before)


def gram_of(z, weights):
    width = z.shape[0] // 2
    local = width // NB
    line = lax.broadcasted_iota(jnp.int32, (width, width), 0) // NB
    lane = lax.broadcasted_iota(jnp.int32, (width, width), 1) // NB
    row = lax.broadcasted_iota(jnp.int32, (NB, width), 0)
    col = lax.broadcasted_iota(jnp.int32, (NB, width), 1) % NB
    full = rows_product(z * weights, z)
    gram_re = full[:width, :width] + full[width:, width:]
    gram_im = full[:width, width:] - full[width:, :width]
    both = []
    for part in (gram_re, gram_im):
        kept = jnp.where(line == lane, part, 0.0)
        both.append(jnp.sum(kept.reshape(local, NB, width), axis=0))
    return jnp.where(row >= col, both[0], both[1])


def weights_at(w_ref, place, share, skip, size):
    return w_ref[:, pl.ds(pl.multiple_of(place * share + skip, 128), size)]


def first_part_kernel(
    sum_ref, w_ref, own_ref, rest_ref, other_ref, later_ref, gram_ref, lent_ref
):
    size = own_ref.shape[1]
    me = lax.axis_index("freq")
    spectra = sum_ref[:, :size]
    weights = weights_at(w_ref, me, sum_ref.shape[1], 0, size)
    rest = sum_ref[:, size:]
    half = spectra.shape[0] // 2
    first = me == 0
    own_ref[...] = jnp.where(first, spectra[:half], spectra[half:])
    other_ref[...] = jnp.where(first, spectra[half:], spectra[:half])
    rest_ref[...] = jnp.where(first, rest[:half], rest[half:])
    later_ref[...] = jnp.where(first, rest[half:], rest[:half])
    grams = [gram_of(z, weights) for z in (spectra[:half], spectra[half:])]
    gram_ref[...] = jnp.where(first, grams[0], grams[1])
    lent_ref[...] = jnp.where(first, grams[1], grams[0])


def first_part(size, partial_sum, weights):
    share = partial_sum.shape[1]
    half = partial_sum.shape[0] // 2
    gram = (NB, half // 2)
    shapes = [(half, size), (half, share - size), (half, size), (half, share - size), gram, gram]
    return pl.pallas_call(
        first_part_kernel,
        out_shape=[jax.ShapeDtypeStruct(shape, jnp.float32) for shape in shapes],
        compiler_params=pltpu.CompilerParams(vmem_limit_bytes=16 * MIB),
        cost_estimate=SMALL,
    )(partial_sum, weights)


def last_part_kernel(n, k, swapped, t_ref, sum_ref, x_ref, w_ref, *refs):
    half, size = sum_ref.shape
    me = lax.axis_index("freq")
    src = lax.bitwise_xor(lax.axis_index("space"), k)
    lines = pl.ds(pl.multiple_of(me * half, 128), half)
    spectra = sum_ref[...] + times_split(t_ref[src, lines], x_ref[...])
    share = w_ref.shape[1] // 2
    skip = share - size
    place = 1 - me if swapped else me
    gram = gram_of(spectra, weights_at(w_ref, place, share, skip, size))
    if swapped:
        before_ref, high_ref, low_ref, gram_ref = refs
        gram = gram + before_ref[...]
        high_ref[...], low_ref[...] = split(spectra)
        for d in range(gram_ref.shape[0]):
            gram_ref[d] = gram
        return
    gram_own_ref, gram_lent_ref, own_ref, other_ref, *refs = refs
    high_ref, low_ref, other_high_ref, other_low_ref, gram_ref = refs
    gram_ref[...] = gram + gram_own_ref[...] + gram_lent_ref[...]
    high_ref[:, :skip], low_ref[:, :skip] = split(own_ref[...])
    high_ref[:, skip:], low_ref[:, skip:] = split(spectra)
    other_high_ref[...], other_low_ref[...] = split(other_ref[...])


def last_part(tables, n, k, copies, partial_sum, piece, weights, *before):
    half, size = partial_sum.shape
    share = weights.shape[1] // 2
    gram = (NB, half // 2)
    widths = [size, size] if copies else [share, share, share - size, share - size]
    parts = [jax.ShapeDtypeStruct((half, width), jnp.bfloat16) for width in widths]
    gram = jax.ShapeDtypeStruct((copies, *gram) if copies else gram, jnp.float32)
    return pl.pallas_call(
        functools.partial(last_part_kernel, n, k, bool(copies)),
        out_shape=[*parts, gram],
        compiler_params=pltpu.CompilerParams(vmem_limit_bytes=16 * MIB),
        cost_estimate=SMALL,
    )(tables, partial_sum, piece, weights, *before)


def inv_sqrt(x):
    y = lax.rsqrt(x)
    return y * (1.5 - 0.5 * x * (y * y))


def finish_kernel(
    total,
    own_high_ref,
    own_low_ref,
    first_high_ref,
    first_low_ref,
    last_high_ref,
    last_low_ref,
    grams_ref,
    modes_ref,
    factor_ref,
):
    local = modes_ref.shape[0]
    width = local * NB
    share = modes_ref.shape[3] // 2
    gram = jnp.sum(grams_ref[...], axis=0) / total
    row = lax.broadcasted_iota(jnp.int32, (NB, width), 0)
    col = lax.broadcasted_iota(jnp.int32, (NB, width), 1) % NB
    stacked = [jnp.where(col == j, gram, 0.0) for j in range(NB)]
    for j in range(NB):
        line = jnp.broadcast_to(gram[j : j + 1, :], (NB, width))
        stacked.append(jnp.where((col == row) & (row > j), -line, 0.0))
    stacked = jnp.concatenate(stacked, axis=0)
    group_r = lax.broadcasted_iota(jnp.int32, (width, width), 0) // NB
    group_c = lax.broadcasted_iota(jnp.int32, (width, width), 1) // NB
    same = group_r == group_c
    ones = jnp.where(same, 1.0, 0.0).astype(jnp.bfloat16)
    spread = jnp.zeros(stacked.shape, jnp.float32)
    rest = stacked
    for _ in range(3):
        piece = rest.astype(jnp.bfloat16)
        rest = rest - piece.astype(jnp.float32)
        spread = spread + jnp.dot(piece, ones, preferred_element_type=jnp.float32)
    col_re = [[spread[j * NB + 8 * h : j * NB + 8 * h + 8] for h in (0, 1)] for j in range(NB)]
    base = NB * NB
    col_im = [
        [spread[base + j * NB + 8 * h : base + j * NB + 8 * h + 8] for h in (0, 1)]
        for j in range(NB)
    ]
    rows = [lax.broadcasted_iota(jnp.int32, (8, width), 0) + 8 * h for h in (0, 1)]
    lanes = lax.broadcasted_iota(jnp.int32, (8, width), 1) % NB
    inv_re = [jnp.where(rows[h] == lanes, 1.0, 0.0) for h in (0, 1)]
    inv_im = [jnp.zeros((8, width), jnp.float32) for h in (0, 1)]
    low_re = [jnp.zeros((8, width), jnp.float32) for h in (0, 1)]
    low_im = [jnp.zeros((8, width), jnp.float32) for h in (0, 1)]

    def pick(halves, i):
        return jnp.broadcast_to(halves[i // 8][i % 8 : i % 8 + 1, :], (8, width))

    pivots = [pick(col_re[j], j) + epsilon for j in range(NB)]
    scales = [jnp.zeros((8, width), jnp.float32) for h in (0, 1)]
    for p in range(NB):
        scale = inv_sqrt(pivots[p])
        inverse = scale * scale
        for h in range(p // 8, 2):
            below = rows[h] > p
            here = lanes == p
            scales[h] = jnp.where(rows[h] == p, scale, scales[h])
            col_re[p][h] = jnp.where(below, col_re[p][h], 0.0)
            col_im[p][h] = jnp.where(below, col_im[p][h], 0.0)
            diag = jnp.where(rows[h] == p, pivots[p], col_re[p][h])
            low_re[h] = jnp.where(here, diag * scale, low_re[h])
            low_im[h] = jnp.where(here, col_im[p][h] * scale, low_im[h])
        for j in range(p + 1, NB):
            a_re, a_im = pick(col_re[p], j), pick(col_im[p], j)
            u_re, u_im = a_re * inverse, a_im * inverse
            pivots[j] = pivots[j] - (a_re * u_re + a_im * u_im)
            for h in range(j // 8, 2):
                c_re, c_im = col_re[p][h], col_im[p][h]
                col_re[j][h] = col_re[j][h] - (c_re * u_re + c_im * u_im)
                col_im[j][h] = col_im[j][h] - (c_im * u_re - c_re * u_im)
        line_re = pick(inv_re, p) * inverse
        line_im = pick(inv_im, p) * inverse
        for h in range(p // 8, 2):
            c_re, c_im = col_re[p][h], col_im[p][h]
            inv_re[h] = inv_re[h] - (c_re * line_re - c_im * line_im)
            inv_im[h] = inv_im[h] - (c_re * line_im + c_im * line_re)
    inv_re = [inv_re[h] * scales[h] for h in (0, 1)]
    inv_im = [inv_im[h] * scales[h] for h in (0, 1)]

    pad = jnp.zeros((width - NB, width), jnp.float32)
    upper_re = jnp.transpose(jnp.concatenate(low_re + [pad], axis=0))
    upper_im = jnp.transpose(jnp.concatenate(low_im + [pad], axis=0))
    for f in range(local):
        factor_ref[0, f] = upper_re[f * NB : (f + 1) * NB, :NB]
        factor_ref[1, f] = -upper_im[f * NB : (f + 1) * NB, :NB]
    me = lax.axis_index("freq")
    own = own_high_ref[...], own_low_ref[...]
    other = [
        jnp.concatenate([a[...], b[...]], axis=1)
        for a, b in ((first_high_ref, last_high_ref), (first_low_ref, last_low_ref))
    ]
    part = width // 2
    lane = lax.broadcasted_iota(jnp.int32, (NB, width), 1)
    left_half = lane < part
    line = lax.broadcasted_iota(jnp.int32, (width, width), 0) % part // NB
    block = lax.broadcasted_iota(jnp.int32, (width, width), 1) % part // NB
    inv_re, inv_im = jnp.concatenate(inv_re, axis=0), jnp.concatenate(inv_im, axis=0)
    turned_re, turned_im = pltpu.roll(inv_re, part, 1), pltpu.roll(inv_im, part, 1)
    for h in range(2):
        stay = left_half if h == 0 else jnp.logical_not(left_half)
        twice_re = jnp.where(stay, inv_re, turned_re)
        twice_im = jnp.where(stay, inv_im, turned_im)
        top = jnp.where(left_half, twice_re, twice_im)
        bottom = jnp.where(left_half, -twice_im, twice_re)
        count = part // NB
        mixing = jnp.concatenate([top] * count + [bottom] * count, axis=0)
        high, low = split(jnp.where(line == block, mixing, 0.0))
        left = jnp.concatenate([high, high, low], axis=1)
        lines = [slice(r * width + h * part, r * width + (h + 1) * part) for r in range(2)]
        for place, (x_high, x_low) in ((me, own), (1 - me, other)):
            right = [x[at] for x in (x_high, x_low, x_high) for at in lines]
            out = jnp.dot(
                left, jnp.concatenate(right, axis=0), preferred_element_type=jnp.float32
            )
            cols = pl.ds(pl.multiple_of(place * share, 128), share)
            for r in range(2):
                for f in range(count):
                    at = r * part + f * NB
                    modes_ref[h * count + f, r, :, cols] = out[at : at + NB]


def finish(total, own, others, grams):
    half, share = own[0].shape
    local = half // (2 * NB)
    return pl.pallas_call(
        functools.partial(finish_kernel, total),
        out_shape=(
            jax.ShapeDtypeStruct((local, 2, NB, 2 * share), jnp.float32),
            jax.ShapeDtypeStruct((2, local, NB, NB), jnp.float32),
        ),
        compiler_params=pltpu.CompilerParams(vmem_limit_bytes=16 * MIB),
    )(*own, *others, grams)


def partner(value, axis, size, step):
    return lax.ppermute(value, axis, [(i, i ^ step) for i in range(size)])


def on_device(snapshots, weights):
    n = lax.axis_size("space")
    tm_count = lax.axis_size("tm")
    freq_count = lax.axis_size("freq")
    blocks, local_times, columns = snapshots.shape
    rows = columns // n
    share = rows // freq_count

    tables = jnp.asarray(dft_blocks(n))

    last = n - 1
    early_rows = share // 2
    targets = n * tm_count

    def send(k, skip, size):
        sent = cut(snapshots, n, k, rows, skip, size)
        return partner(sent, "space", n, k)

    halves = ((0, early_rows), (early_rows, share - early_rows))
    sends = [(last, *halves[0])]
    sends += [(k, *half) for k in range(n - 2, 0, -1) for half in halves]
    pieces = [(k, skip, send(k, skip, size)) for k, skip, size in sends]
    last_piece = send(last, *halves[1])
    before = early(tables, n, 0, 0, cut(snapshots, n, 0, rows, 0, share))
    for k, skip, piece in pieces:
        before = early(tables, n, k, skip, piece, before)
    weights = weights.reshape(1, rows)
    own, rest, other, later, gram, lent = first_part(early_rows, before, weights)
    traded = [partner(part, "freq", freq_count, 1) for part in (other, later, lent)]
    piece, (other, later, lent) = lax.optimization_barrier((last_piece, traded))
    raw = partner(piece, "freq", freq_count, 1)
    *parts, gram = last_part(
        tables, n, last, 0, rest, piece, weights, gram, lent, own, other
    )
    *last_parts, gram = last_part(tables, n, last, targets, later, raw, weights, gram)
    order = list(range(targets - 1, -1, -1))
    grams = lax.all_to_all(
        gram,
        ("space", "tm"),
        split_axis=0,
        concat_axis=0,
        axis_index_groups=[order],
        tiled=True,
    )
    total = rows * targets
    return finish(total, parts[:2], [*parts[2:], *last_parts], grams)


def solution(mesh):
    return jax.shard_map(
        on_device,
        mesh=mesh,
        in_specs=(P(None, "space", ("groups", "tm")), P(("groups", "tm", "space"))),
        out_specs=(
            P("freq", None, None, ("groups", "tm", "space")),
            P("groups", "freq", None, None),
        ),
        check_vma=False,
    )
```

```python
import functools

import numpy as np
import jax
import jax.numpy as jnp
from jax import lax
from jax.experimental import pallas as pl
from jax.experimental.pallas import tpu as pltpu
from jax.sharding import PartitionSpec as P

NB = 16
SEGMENT_FRAMES = 64
NF = 16
CUTS = 4
epsilon = 1e-05
MIB = 1024 * 1024
SMALL = pl.CostEstimate(flops=1, transcendentals=0, bytes_accessed=1)


def dft_blocks(groups):
    times = np.arange(SEGMENT_FRAMES)
    taper = 0.5 - 0.5 * np.cos(2.0 * np.pi * times / SEGMENT_FRAMES)
    taper = taper / np.sqrt(np.sum(taper * taper))
    bins = 1 + np.arange(NF)
    angles = 2.0 * np.pi * (bins[:, None] * times[None, :] % SEGMENT_FRAMES) / SEGMENT_FRAMES
    table = np.stack([np.cos(angles) * taper, -np.sin(angles) * taper])
    step = SEGMENT_FRAMES // groups
    table = table.reshape(2, 2, NF // 2, groups, step)
    spread = np.einsum("rhfgt,bc->ghrfbct", table, np.eye(NB))
    spread = spread.reshape(groups, 2 * NF * NB, NB * step).astype(np.float32)
    high = spread.astype(jnp.bfloat16)
    low = (spread - high.astype(np.float32)).astype(jnp.bfloat16)
    return np.concatenate([high, high, low], axis=2)


def split(x):
    high = x.astype(jnp.bfloat16)
    return high, (x - high.astype(jnp.float32)).astype(jnp.bfloat16)


def times_split(left, x):
    high, low = split(x)
    right = jnp.concatenate([high, low, high], axis=0)
    return jnp.dot(left, right, preferred_element_type=jnp.float32)


def rows_product(a, b):
    lines, columns = a.shape[0], b.shape[0]
    full = lax.dot_general(
        jnp.concatenate(split(a), axis=0),
        jnp.concatenate(split(b), axis=0),
        (((1,), (1,)), ((), ())),
        preferred_element_type=jnp.float32,
    )
    small = full[lines:, columns:] + full[lines:, :columns] + full[:lines, columns:]
    return small + full[:lines, :columns]


def cut_kernel(n, k, rows, skip, x_ref, o_ref, sem):
    size = o_ref.shape[2]
    to = lax.bitwise_xor(lax.axis_index("space"), k)
    share = rows // 2
    start = pl.multiple_of(to * rows + lax.axis_index("freq") * share + skip, 128)
    part = NB // CUTS
    copies = []
    for i in range(CUTS):
        blocks = pl.ds(i * part, part)
        copies.append(
            pltpu.make_async_copy(
                x_ref.at[blocks, :, pl.ds(start, size)], o_ref.at[blocks], sem.at[i]
            )
        )
    for copy in copies:
        copy.start()
    for copy in copies:
        copy.wait()


def cut(snapshots, n, k, rows, skip, size):
    blocks, local_times, _ = snapshots.shape
    if local_times % 8 == 0:
        piece = pl.pallas_call(
            functools.partial(cut_kernel, n, k, rows, skip),
            out_shape=pltpu.VMEM((blocks, local_times, size), jnp.float32),
            in_specs=[pl.BlockSpec(memory_space=pltpu.HBM)],
            out_specs=pl.BlockSpec(memory_space=pltpu.VMEM),
            scratch_shapes=[pltpu.SemaphoreType.DMA((CUTS,))],
            compiler_params=pltpu.CompilerParams(vmem_limit_bytes=4 * MIB),
            cost_estimate=SMALL,
        )(pltpu.with_memory_space_constraint(snapshots, pltpu.HBM))
    else:
        to = lax.bitwise_xor(lax.axis_index("space"), k)
        start = to * rows + lax.axis_index("freq") * (rows // 2) + skip
        piece = lax.dynamic_slice_in_dim(snapshots, start, size, axis=2)
    return piece.reshape(blocks * local_times, size)


def early_kernel(n, k, skip, t_ref, x_ref, *refs):
    src = lax.bitwise_xor(lax.axis_index("space"), k)
    part = times_split(t_ref[src], x_ref[...])
    if len(refs) == 1:
        refs[0][...] = part
        return
    before_ref, out_ref = refs
    end = skip + x_ref.shape[1]
    out_ref[:, skip:end] = before_ref[:, skip:end] + part
    if skip:
        out_ref[:, :skip] = before_ref[:, :skip]
    if end < out_ref.shape[1]:
        out_ref[:, end:] = before_ref[:, end:]


def early(tables, n, k, skip, piece, *before):
    share = before[0].shape[1] if before else piece.shape[1]
    return pl.pallas_call(
        functools.partial(early_kernel, n, k, skip),
        out_shape=jax.ShapeDtypeStruct((tables.shape[1], share), jnp.float32),
        compiler_params=pltpu.CompilerParams(vmem_limit_bytes=16 * MIB),
        cost_estimate=SMALL,
    )(tables, piece, *before)


def gram_of(z, weights):
    width = z.shape[0] // 2
    local = width // NB
    line = lax.broadcasted_iota(jnp.int32, (width, width), 0) // NB
    lane = lax.broadcasted_iota(jnp.int32, (width, width), 1) // NB
    row = lax.broadcasted_iota(jnp.int32, (NB, width), 0)
    col = lax.broadcasted_iota(jnp.int32, (NB, width), 1) % NB
    full = rows_product(z * weights, z)
    gram_re = full[:width, :width] + full[width:, width:]
    gram_im = full[:width, width:] - full[width:, :width]
    both = []
    for part in (gram_re, gram_im):
        kept = jnp.where(line == lane, part, 0.0)
        both.append(jnp.sum(kept.reshape(local, NB, width), axis=0))
    return jnp.where(row >= col, both[0], both[1])


def weights_at(w_ref, place, share, skip, size):
    return w_ref[:, pl.ds(pl.multiple_of(place * share + skip, 128), size)]


def first_part_kernel(
    sum_ref, w_ref, own_ref, rest_ref, other_ref, later_ref, gram_ref, lent_ref
):
    size = own_ref.shape[1]
    me = lax.axis_index("freq")
    spectra = sum_ref[:, :size]
    weights = weights_at(w_ref, me, sum_ref.shape[1], 0, size)
    rest = sum_ref[:, size:]
    half = spectra.shape[0] // 2
    first = me == 0
    own_ref[...] = jnp.where(first, spectra[:half], spectra[half:])
    other_ref[...] = jnp.where(first, spectra[half:], spectra[:half])
    rest_ref[...] = jnp.where(first, rest[:half], rest[half:])
    later_ref[...] = jnp.where(first, rest[half:], rest[:half])
    grams = [gram_of(z, weights) for z in (spectra[:half], spectra[half:])]
    gram_ref[...] = jnp.where(first, grams[0], grams[1])
    lent_ref[...] = jnp.where(first, grams[1], grams[0])


def first_part(size, partial_sum, weights):
    share = partial_sum.shape[1]
    half = partial_sum.shape[0] // 2
    gram = (NB, half // 2)
    shapes = [(half, size), (half, share - size), (half, size), (half, share - size), gram, gram]
    return pl.pallas_call(
        first_part_kernel,
        out_shape=[jax.ShapeDtypeStruct(shape, jnp.float32) for shape in shapes],
        compiler_params=pltpu.CompilerParams(vmem_limit_bytes=16 * MIB),
        cost_estimate=SMALL,
    )(partial_sum, weights)


def last_part_kernel(n, k, swapped, t_ref, sum_ref, x_ref, w_ref, *refs):
    half, size = sum_ref.shape
    me = lax.axis_index("freq")
    src = lax.bitwise_xor(lax.axis_index("space"), k)
    lines = pl.ds(pl.multiple_of(me * half, 128), half)
    spectra = sum_ref[...] + times_split(t_ref[src, lines], x_ref[...])
    share = w_ref.shape[1] // 2
    skip = share - size
    place = 1 - me if swapped else me
    gram = gram_of(spectra, weights_at(w_ref, place, share, skip, size))
    if swapped:
        before_ref, high_ref, low_ref, gram_ref = refs
        gram = gram + before_ref[...]
        high_ref[...], low_ref[...] = split(spectra)
        for d in range(gram_ref.shape[0]):
            gram_ref[d] = gram
        return
    gram_own_ref, gram_lent_ref, own_ref, other_ref, *refs = refs
    high_ref, low_ref, other_high_ref, other_low_ref, gram_ref = refs
    gram_ref[...] = gram + gram_own_ref[...] + gram_lent_ref[...]
    high_ref[:, :skip], low_ref[:, :skip] = split(own_ref[...])
    high_ref[:, skip:], low_ref[:, skip:] = split(spectra)
    other_high_ref[...], other_low_ref[...] = split(other_ref[...])


def last_part(tables, n, k, copies, partial_sum, piece, weights, *before):
    half, size = partial_sum.shape
    share = weights.shape[1] // 2
    gram = (NB, half // 2)
    widths = [size, size] if copies else [share, share, share - size, share - size]
    parts = [jax.ShapeDtypeStruct((half, width), jnp.bfloat16) for width in widths]
    gram = jax.ShapeDtypeStruct((copies, *gram) if copies else gram, jnp.float32)
    return pl.pallas_call(
        functools.partial(last_part_kernel, n, k, bool(copies)),
        out_shape=[*parts, gram],
        compiler_params=pltpu.CompilerParams(vmem_limit_bytes=16 * MIB),
        cost_estimate=SMALL,
    )(tables, partial_sum, piece, weights, *before)


def inv_sqrt(x):
    y = lax.rsqrt(x)
    return y * (1.5 - 0.5 * x * (y * y))


def finish_kernel(
    total,
    own_high_ref,
    own_low_ref,
    first_high_ref,
    first_low_ref,
    last_high_ref,
    last_low_ref,
    grams_ref,
    modes_ref,
    factor_ref,
):
    local = modes_ref.shape[0]
    width = local * NB
    share = modes_ref.shape[3] // 2
    gram = jnp.sum(grams_ref[...], axis=0) / total
    row = lax.broadcasted_iota(jnp.int32, (NB, width), 0)
    col = lax.broadcasted_iota(jnp.int32, (NB, width), 1) % NB
    stacked = [jnp.where(col == j, gram, 0.0) for j in range(NB)]
    for j in range(NB):
        line = jnp.broadcast_to(gram[j : j + 1, :], (NB, width))
        stacked.append(jnp.where((col == row) & (row > j), -line, 0.0))
    stacked = jnp.concatenate(stacked, axis=0)
    group_r = lax.broadcasted_iota(jnp.int32, (width, width), 0) // NB
    group_c = lax.broadcasted_iota(jnp.int32, (width, width), 1) // NB
    same = group_r == group_c
    ones = jnp.where(same, 1.0, 0.0).astype(jnp.bfloat16)
    spread = jnp.zeros(stacked.shape, jnp.float32)
    rest = stacked
    for _ in range(3):
        piece = rest.astype(jnp.bfloat16)
        rest = rest - piece.astype(jnp.float32)
        spread = spread + jnp.dot(piece, ones, preferred_element_type=jnp.float32)
    col_re = [[spread[j * NB + 8 * h : j * NB + 8 * h + 8] for h in (0, 1)] for j in range(NB)]
    base = NB * NB
    col_im = [
        [spread[base + j * NB + 8 * h : base + j * NB + 8 * h + 8] for h in (0, 1)]
        for j in range(NB)
    ]
    rows = [lax.broadcasted_iota(jnp.int32, (8, width), 0) + 8 * h for h in (0, 1)]
    lanes = lax.broadcasted_iota(jnp.int32, (8, width), 1) % NB
    inv_re = [jnp.where(rows[h] == lanes, 1.0, 0.0) for h in (0, 1)]
    inv_im = [jnp.zeros((8, width), jnp.float32) for h in (0, 1)]
    low_re = [jnp.zeros((8, width), jnp.float32) for h in (0, 1)]
    low_im = [jnp.zeros((8, width), jnp.float32) for h in (0, 1)]

    def pick(halves, i):
        return jnp.broadcast_to(halves[i // 8][i % 8 : i % 8 + 1, :], (8, width))

    pivots = [pick(col_re[j], j) + epsilon for j in range(NB)]
    scales = [jnp.zeros((8, width), jnp.float32) for h in (0, 1)]
    for p in range(NB):
        scale = inv_sqrt(pivots[p])
        inverse = scale * scale
        for h in range(p // 8, 2):
            below = rows[h] > p
            here = lanes == p
            scales[h] = jnp.where(rows[h] == p, scale, scales[h])
            col_re[p][h] = jnp.where(below, col_re[p][h], 0.0)
            col_im[p][h] = jnp.where(below, col_im[p][h], 0.0)
            diag = jnp.where(rows[h] == p, pivots[p], col_re[p][h])
            low_re[h] = jnp.where(here, diag * scale, low_re[h])
            low_im[h] = jnp.where(here, col_im[p][h] * scale, low_im[h])
        for j in range(p + 1, NB):
            a_re, a_im = pick(col_re[p], j), pick(col_im[p], j)
            u_re, u_im = a_re * inverse, a_im * inverse
            pivots[j] = pivots[j] - (a_re * u_re + a_im * u_im)
            for h in range(j // 8, 2):
                c_re, c_im = col_re[p][h], col_im[p][h]
                col_re[j][h] = col_re[j][h] - (c_re * u_re + c_im * u_im)
                col_im[j][h] = col_im[j][h] - (c_im * u_re - c_re * u_im)
        line_re = pick(inv_re, p) * inverse
        line_im = pick(inv_im, p) * inverse
        for h in range(p // 8, 2):
            c_re, c_im = col_re[p][h], col_im[p][h]
            inv_re[h] = inv_re[h] - (c_re * line_re - c_im * line_im)
            inv_im[h] = inv_im[h] - (c_re * line_im + c_im * line_re)
    inv_re = [inv_re[h] * scales[h] for h in (0, 1)]
    inv_im = [inv_im[h] * scales[h] for h in (0, 1)]

    pad = jnp.zeros((width - NB, width), jnp.float32)
    upper_re = jnp.transpose(jnp.concatenate(low_re + [pad], axis=0))
    upper_im = jnp.transpose(jnp.concatenate(low_im + [pad], axis=0))
    for f in range(local):
        factor_ref[0, f] = upper_re[f * NB : (f + 1) * NB, :NB]
        factor_ref[1, f] = -upper_im[f * NB : (f + 1) * NB, :NB]
    me = lax.axis_index("freq")
    own = own_high_ref[...], own_low_ref[...]
    other = [
        jnp.concatenate([a[...], b[...]], axis=1)
        for a, b in ((first_high_ref, last_high_ref), (first_low_ref, last_low_ref))
    ]
    part = width // 2
    lane = lax.broadcasted_iota(jnp.int32, (NB, width), 1)
    left_half = lane < part
    line = lax.broadcasted_iota(jnp.int32, (width, width), 0) % part // NB
    block = lax.broadcasted_iota(jnp.int32, (width, width), 1) % part // NB
    inv_re, inv_im = jnp.concatenate(inv_re, axis=0), jnp.concatenate(inv_im, axis=0)
    turned_re, turned_im = pltpu.roll(inv_re, part, 1), pltpu.roll(inv_im, part, 1)
    for h in range(2):
        stay = left_half if h == 0 else jnp.logical_not(left_half)
        twice_re = jnp.where(stay, inv_re, turned_re)
        twice_im = jnp.where(stay, inv_im, turned_im)
        top = jnp.where(left_half, twice_re, twice_im)
        bottom = jnp.where(left_half, -twice_im, twice_re)
        count = part // NB
        mixing = jnp.concatenate([top] * count + [bottom] * count, axis=0)
        high, low = split(jnp.where(line == block, mixing, 0.0))
        left = jnp.concatenate([high, high, low], axis=1)
        lines = [slice(r * width + h * part, r * width + (h + 1) * part) for r in range(2)]
        for place, (x_high, x_low) in ((me, own), (1 - me, other)):
            right = [x[at] for x in (x_high, x_low, x_high) for at in lines]
            out = jnp.dot(
                left, jnp.concatenate(right, axis=0), preferred_element_type=jnp.float32
            )
            cols = pl.ds(pl.multiple_of(place * share, 128), share)
            for r in range(2):
                for f in range(count):
                    at = r * part + f * NB
                    modes_ref[h * count + f, r, :, cols] = out[at : at + NB]


def finish(total, own, others, grams):
    half, share = own[0].shape
    local = half // (2 * NB)
    return pl.pallas_call(
        functools.partial(finish_kernel, total),
        out_shape=(
            jax.ShapeDtypeStruct((local, 2, NB, 2 * share), jnp.float32),
            jax.ShapeDtypeStruct((2, local, NB, NB), jnp.float32),
        ),
        compiler_params=pltpu.CompilerParams(vmem_limit_bytes=16 * MIB),
    )(*own, *others, grams)


def partner(value, axis, size, step):
    return lax.ppermute(value, axis, [(i, i ^ step) for i in range(size)])


def on_device(snapshots, weights):
    n = lax.axis_size("space")
    tm_count = lax.axis_size("tm")
    freq_count = lax.axis_size("freq")
    blocks, local_times, columns = snapshots.shape
    rows = columns // n
    share = rows // freq_count

    tables = jnp.asarray(dft_blocks(n))

    last = n - 1
    early_rows = share // 2
    targets = n * tm_count

    def send(k, skip, size):
        sent = cut(snapshots, n, k, rows, skip, size)
        return partner(sent, "space", n, k)

    halves = ((0, early_rows), (early_rows, share - early_rows))
    sends = [(last, *halves[0])]
    sends += [(k, *halves[0]) for k in range(n - 2, 0, -1)]
    sends += [(k, *halves[1]) for k in range(1, n - 1)]
    pieces = [(k, skip, send(k, skip, size)) for k, skip, size in sends]
    last_piece = send(last, *halves[1])
    before = early(tables, n, 0, 0, cut(snapshots, n, 0, rows, 0, share))
    for k, skip, piece in pieces:
        before = early(tables, n, k, skip, piece, before)
    weights = weights.reshape(1, rows)
    own, rest, other, later, gram, lent = first_part(early_rows, before, weights)
    traded = [partner(part, "freq", freq_count, 1) for part in (other, later, lent)]
    piece, (other, later, lent) = lax.optimization_barrier((last_piece, traded))
    raw = partner(piece, "freq", freq_count, 1)
    *parts, gram = last_part(
        tables, n, last, 0, rest, piece, weights, gram, lent, own, other
    )
    *last_parts, gram = last_part(tables, n, last, targets, later, raw, weights, gram)
    order = list(range(targets - 1, -1, -1))
    grams = lax.all_to_all(
        gram,
        ("space", "tm"),
        split_axis=0,
        concat_axis=0,
        axis_index_groups=[order],
        tiled=True,
    )
    total = rows * targets
    return finish(total, parts[:2], [*parts[2:], *last_parts], grams)


def solution(mesh):
    return jax.shard_map(
        on_device,
        mesh=mesh,
        in_specs=(P(None, "space", ("groups", "tm")), P(("groups", "tm", "space"))),
        out_specs=(
            P("freq", None, None, ("groups", "tm", "space")),
            P("groups", "freq", None, None),
        ),
        check_vma=False,
    )
```

```python
import functools

import numpy as np
import jax
import jax.numpy as jnp
from jax import lax
from jax.experimental import pallas as pl
from jax.experimental.pallas import tpu as pltpu
from jax.sharding import PartitionSpec as P

NB = 16
SEGMENT_FRAMES = 64
NF = 16
CUTS = 4
epsilon = 1e-05
MIB = 1024 * 1024
SMALL = pl.CostEstimate(flops=1, transcendentals=0, bytes_accessed=1)


def dft_blocks(groups):
    times = np.arange(SEGMENT_FRAMES)
    taper = 0.5 - 0.5 * np.cos(2.0 * np.pi * times / SEGMENT_FRAMES)
    taper = taper / np.sqrt(np.sum(taper * taper))
    bins = 1 + np.arange(NF)
    angles = 2.0 * np.pi * (bins[:, None] * times[None, :] % SEGMENT_FRAMES) / SEGMENT_FRAMES
    table = np.stack([np.cos(angles) * taper, -np.sin(angles) * taper])
    step = SEGMENT_FRAMES // groups
    table = table.reshape(2, 2, NF // 2, groups, step)
    spread = np.einsum("rhfgt,bc->ghrfbct", table, np.eye(NB))
    spread = spread.reshape(groups, 2 * NF * NB, NB * step).astype(np.float32)
    high = spread.astype(jnp.bfloat16)
    low = (spread - high.astype(np.float32)).astype(jnp.bfloat16)
    return np.concatenate([high, high, low], axis=2)


def split(x):
    high = x.astype(jnp.bfloat16)
    return high, (x - high.astype(jnp.float32)).astype(jnp.bfloat16)


def times_split(left, x):
    high, low = split(x)
    right = jnp.concatenate([high, low, high], axis=0)
    return jnp.dot(left, right, preferred_element_type=jnp.float32)


def rows_product(a, b):
    lines, columns = a.shape[0], b.shape[0]
    full = lax.dot_general(
        jnp.concatenate(split(a), axis=0),
        jnp.concatenate(split(b), axis=0),
        (((1,), (1,)), ((), ())),
        preferred_element_type=jnp.float32,
    )
    small = full[lines:, columns:] + full[lines:, :columns] + full[:lines, columns:]
    return small + full[:lines, :columns]


def cut_kernel(n, k, rows, skip, x_ref, o_ref, sem):
    size = o_ref.shape[2]
    to = lax.bitwise_xor(lax.axis_index("space"), k)
    share = rows // 2
    start = pl.multiple_of(to * rows + lax.axis_index("freq") * share + skip, 128)
    part = NB // CUTS
    copies = []
    for i in range(CUTS):
        blocks = pl.ds(i * part, part)
        copies.append(
            pltpu.make_async_copy(
                x_ref.at[blocks, :, pl.ds(start, size)], o_ref.at[blocks], sem.at[i]
            )
        )
    for copy in copies:
        copy.start()
    for copy in copies:
        copy.wait()


def cut(snapshots, n, k, rows, skip, size):
    blocks, local_times, _ = snapshots.shape
    if local_times % 8 == 0:
        piece = pl.pallas_call(
            functools.partial(cut_kernel, n, k, rows, skip),
            out_shape=pltpu.VMEM((blocks, local_times, size), jnp.float32),
            in_specs=[pl.BlockSpec(memory_space=pltpu.HBM)],
            out_specs=pl.BlockSpec(memory_space=pltpu.VMEM),
            scratch_shapes=[pltpu.SemaphoreType.DMA((CUTS,))],
            compiler_params=pltpu.CompilerParams(vmem_limit_bytes=4 * MIB),
            cost_estimate=SMALL,
        )(pltpu.with_memory_space_constraint(snapshots, pltpu.HBM))
    else:
        to = lax.bitwise_xor(lax.axis_index("space"), k)
        start = to * rows + lax.axis_index("freq") * (rows // 2) + skip
        piece = lax.dynamic_slice_in_dim(snapshots, start, size, axis=2)
    return piece.reshape(blocks * local_times, size)


def early_kernel(n, k, skip, t_ref, x_ref, *refs):
    src = lax.bitwise_xor(lax.axis_index("space"), k)
    part = times_split(t_ref[src], x_ref[...])
    if len(refs) == 1:
        refs[0][...] = part
        return
    before_ref, out_ref = refs
    end = skip + x_ref.shape[1]
    out_ref[:, skip:end] = before_ref[:, skip:end] + part
    if skip:
        out_ref[:, :skip] = before_ref[:, :skip]
    if end < out_ref.shape[1]:
        out_ref[:, end:] = before_ref[:, end:]


def early(tables, n, k, skip, piece, *before):
    share = before[0].shape[1] if before else piece.shape[1]
    return pl.pallas_call(
        functools.partial(early_kernel, n, k, skip),
        out_shape=jax.ShapeDtypeStruct((tables.shape[1], share), jnp.float32),
        compiler_params=pltpu.CompilerParams(vmem_limit_bytes=16 * MIB),
        cost_estimate=SMALL,
    )(tables, piece, *before)


def gram_of(z, weights):
    width = z.shape[0] // 2
    local = width // NB
    line = lax.broadcasted_iota(jnp.int32, (width, width), 0) // NB
    lane = lax.broadcasted_iota(jnp.int32, (width, width), 1) // NB
    row = lax.broadcasted_iota(jnp.int32, (NB, width), 0)
    col = lax.broadcasted_iota(jnp.int32, (NB, width), 1) % NB
    full = rows_product(z * weights, z)
    gram_re = full[:width, :width] + full[width:, width:]
    gram_im = full[:width, width:] - full[width:, :width]
    both = []
    for part in (gram_re, gram_im):
        kept = jnp.where(line == lane, part, 0.0)
        both.append(jnp.sum(kept.reshape(local, NB, width), axis=0))
    return jnp.where(row >= col, both[0], both[1])


def weights_at(w_ref, place, share, skip, size):
    return w_ref[:, pl.ds(pl.multiple_of(place * share + skip, 128), size)]


def first_part_kernel(
    sum_ref, w_ref, own_ref, rest_ref, other_ref, later_ref, gram_ref, lent_ref
):
    size = own_ref.shape[1]
    me = lax.axis_index("freq")
    spectra = sum_ref[:, :size]
    weights = weights_at(w_ref, me, sum_ref.shape[1], 0, size)
    rest = sum_ref[:, size:]
    half = spectra.shape[0] // 2
    first = me == 0
    own_ref[...] = jnp.where(first, spectra[:half], spectra[half:])
    other_ref[...] = jnp.where(first, spectra[half:], spectra[:half])
    rest_ref[...] = jnp.where(first, rest[:half], rest[half:])
    later_ref[...] = jnp.where(first, rest[half:], rest[:half])
    grams = [gram_of(z, weights) for z in (spectra[:half], spectra[half:])]
    gram_ref[...] = jnp.where(first, grams[0], grams[1])
    lent_ref[...] = jnp.where(first, grams[1], grams[0])


def first_part(size, partial_sum, weights):
    share = partial_sum.shape[1]
    half = partial_sum.shape[0] // 2
    gram = (NB, half // 2)
    shapes = [(half, size), (half, share - size), (half, size), (half, share - size), gram, gram]
    return pl.pallas_call(
        first_part_kernel,
        out_shape=[jax.ShapeDtypeStruct(shape, jnp.float32) for shape in shapes],
        compiler_params=pltpu.CompilerParams(vmem_limit_bytes=16 * MIB),
        cost_estimate=SMALL,
    )(partial_sum, weights)


def last_part_kernel(n, k, swapped, t_ref, sum_ref, x_ref, w_ref, *refs):
    half, size = sum_ref.shape
    me = lax.axis_index("freq")
    src = lax.bitwise_xor(lax.axis_index("space"), k)
    lines = pl.ds(pl.multiple_of(me * half, 128), half)
    spectra = sum_ref[...] + times_split(t_ref[src, lines], x_ref[...])
    share = w_ref.shape[1] // 2
    skip = share - size
    place = 1 - me if swapped else me
    gram = gram_of(spectra, weights_at(w_ref, place, share, skip, size))
    if swapped:
        before_ref, high_ref, low_ref, gram_ref = refs
        gram = gram + before_ref[...]
        high_ref[...], low_ref[...] = split(spectra)
        for d in range(gram_ref.shape[0]):
            gram_ref[d] = gram
        return
    gram_own_ref, gram_lent_ref, own_ref, other_ref, *refs = refs
    high_ref, low_ref, other_high_ref, other_low_ref, gram_ref = refs
    gram_ref[...] = gram + gram_own_ref[...] + gram_lent_ref[...]
    high_ref[:, :skip], low_ref[:, :skip] = split(own_ref[...])
    high_ref[:, skip:], low_ref[:, skip:] = split(spectra)
    other_high_ref[...], other_low_ref[...] = split(other_ref[...])


def last_part(tables, n, k, copies, partial_sum, piece, weights, *before):
    half, size = partial_sum.shape
    share = weights.shape[1] // 2
    gram = (NB, half // 2)
    widths = [size, size] if copies else [share, share, share - size, share - size]
    parts = [jax.ShapeDtypeStruct((half, width), jnp.bfloat16) for width in widths]
    gram = jax.ShapeDtypeStruct((copies, *gram) if copies else gram, jnp.float32)
    return pl.pallas_call(
        functools.partial(last_part_kernel, n, k, bool(copies)),
        out_shape=[*parts, gram],
        compiler_params=pltpu.CompilerParams(vmem_limit_bytes=16 * MIB),
        cost_estimate=SMALL,
    )(tables, partial_sum, piece, weights, *before)


def inv_sqrt(x):
    y = lax.rsqrt(x)
    return y * (1.5 - 0.5 * x * (y * y))


def finish_kernel(
    total,
    own_high_ref,
    own_low_ref,
    first_high_ref,
    first_low_ref,
    last_high_ref,
    last_low_ref,
    grams_ref,
    modes_ref,
    factor_ref,
):
    local = modes_ref.shape[0]
    width = local * NB
    share = modes_ref.shape[3] // 2
    gram = jnp.sum(grams_ref[...], axis=0) / total
    row = lax.broadcasted_iota(jnp.int32, (NB, width), 0)
    col = lax.broadcasted_iota(jnp.int32, (NB, width), 1) % NB
    stacked = [jnp.where(col == j, gram, 0.0) for j in range(NB)]
    for j in range(NB):
        line = jnp.broadcast_to(gram[j : j + 1, :], (NB, width))
        stacked.append(jnp.where((col == row) & (row > j), -line, 0.0))
    stacked = jnp.concatenate(stacked, axis=0)
    group_r = lax.broadcasted_iota(jnp.int32, (width, width), 0) // NB
    group_c = lax.broadcasted_iota(jnp.int32, (width, width), 1) // NB
    same = group_r == group_c
    ones = jnp.where(same, 1.0, 0.0).astype(jnp.bfloat16)
    spread = jnp.zeros(stacked.shape, jnp.float32)
    rest = stacked
    for _ in range(3):
        piece = rest.astype(jnp.bfloat16)
        rest = rest - piece.astype(jnp.float32)
        spread = spread + jnp.dot(piece, ones, preferred_element_type=jnp.float32)
    col_re = [[spread[j * NB + 8 * h : j * NB + 8 * h + 8] for h in (0, 1)] for j in range(NB)]
    base = NB * NB
    col_im = [
        [spread[base + j * NB + 8 * h : base + j * NB + 8 * h + 8] for h in (0, 1)]
        for j in range(NB)
    ]
    rows = [lax.broadcasted_iota(jnp.int32, (8, width), 0) + 8 * h for h in (0, 1)]
    lanes = lax.broadcasted_iota(jnp.int32, (8, width), 1) % NB
    inv_re = [jnp.where(rows[h] == lanes, 1.0, 0.0) for h in (0, 1)]
    inv_im = [jnp.zeros((8, width), jnp.float32) for h in (0, 1)]
    low_re = [jnp.zeros((8, width), jnp.float32) for h in (0, 1)]
    low_im = [jnp.zeros((8, width), jnp.float32) for h in (0, 1)]

    def pick(halves, i):
        return jnp.broadcast_to(halves[i // 8][i % 8 : i % 8 + 1, :], (8, width))

    pivots = [pick(col_re[j], j) + epsilon for j in range(NB)]
    scales = [jnp.zeros((8, width), jnp.float32) for h in (0, 1)]
    for p in range(NB):
        scale = inv_sqrt(pivots[p])
        inverse = scale * scale
        for h in range(p // 8, 2):
            below = rows[h] > p
            here = lanes == p
            scales[h] = jnp.where(rows[h] == p, scale, scales[h])
            col_re[p][h] = jnp.where(below, col_re[p][h], 0.0)
            col_im[p][h] = jnp.where(below, col_im[p][h], 0.0)
            diag = jnp.where(rows[h] == p, pivots[p], col_re[p][h])
            low_re[h] = jnp.where(here, diag * scale, low_re[h])
            low_im[h] = jnp.where(here, col_im[p][h] * scale, low_im[h])
        for j in range(p + 1, NB):
            a_re, a_im = pick(col_re[p], j), pick(col_im[p], j)
            u_re, u_im = a_re * inverse, a_im * inverse
            pivots[j] = pivots[j] - (a_re * u_re + a_im * u_im)
            for h in range(j // 8, 2):
                c_re, c_im = col_re[p][h], col_im[p][h]
                col_re[j][h] = col_re[j][h] - (c_re * u_re + c_im * u_im)
                col_im[j][h] = col_im[j][h] - (c_im * u_re - c_re * u_im)
        line_re = pick(inv_re, p) * inverse
        line_im = pick(inv_im, p) * inverse
        for h in range(p // 8, 2):
            c_re, c_im = col_re[p][h], col_im[p][h]
            inv_re[h] = inv_re[h] - (c_re * line_re - c_im * line_im)
            inv_im[h] = inv_im[h] - (c_re * line_im + c_im * line_re)
    inv_re = [inv_re[h] * scales[h] for h in (0, 1)]
    inv_im = [inv_im[h] * scales[h] for h in (0, 1)]

    pad = jnp.zeros((width - NB, width), jnp.float32)
    upper_re = jnp.transpose(jnp.concatenate(low_re + [pad], axis=0))
    upper_im = jnp.transpose(jnp.concatenate(low_im + [pad], axis=0))
    for f in range(local):
        factor_ref[0, f] = upper_re[f * NB : (f + 1) * NB, :NB]
        factor_ref[1, f] = -upper_im[f * NB : (f + 1) * NB, :NB]
    me = lax.axis_index("freq")
    own = own_high_ref[...], own_low_ref[...]
    other = [
        jnp.concatenate([a[...], b[...]], axis=1)
        for a, b in ((first_high_ref, last_high_ref), (first_low_ref, last_low_ref))
    ]
    part = width // 2
    lane = lax.broadcasted_iota(jnp.int32, (NB, width), 1)
    left_half = lane < part
    line = lax.broadcasted_iota(jnp.int32, (width, width), 0) % part // NB
    block = lax.broadcasted_iota(jnp.int32, (width, width), 1) % part // NB
    inv_re, inv_im = jnp.concatenate(inv_re, axis=0), jnp.concatenate(inv_im, axis=0)
    turned_re, turned_im = pltpu.roll(inv_re, part, 1), pltpu.roll(inv_im, part, 1)
    for h in range(2):
        stay = left_half if h == 0 else jnp.logical_not(left_half)
        twice_re = jnp.where(stay, inv_re, turned_re)
        twice_im = jnp.where(stay, inv_im, turned_im)
        top = jnp.where(left_half, twice_re, twice_im)
        bottom = jnp.where(left_half, -twice_im, twice_re)
        count = part // NB
        mixing = jnp.concatenate([top] * count + [bottom] * count, axis=0)
        high, low = split(jnp.where(line == block, mixing, 0.0))
        left = jnp.concatenate([high, high, low], axis=1)
        lines = [slice(r * width + h * part, r * width + (h + 1) * part) for r in range(2)]
        for place, (x_high, x_low) in ((me, own), (1 - me, other)):
            right = [x[at] for x in (x_high, x_low, x_high) for at in lines]
            out = jnp.dot(
                left, jnp.concatenate(right, axis=0), preferred_element_type=jnp.float32
            )
            cols = pl.ds(pl.multiple_of(place * share, 128), share)
            for r in range(2):
                for f in range(count):
                    at = r * part + f * NB
                    modes_ref[h * count + f, r, :, cols] = out[at : at + NB]


def finish(total, own, others, grams):
    half, share = own[0].shape
    local = half // (2 * NB)
    return pl.pallas_call(
        functools.partial(finish_kernel, total),
        out_shape=(
            jax.ShapeDtypeStruct((local, 2, NB, 2 * share), jnp.float32),
            jax.ShapeDtypeStruct((2, local, NB, NB), jnp.float32),
        ),
        compiler_params=pltpu.CompilerParams(vmem_limit_bytes=16 * MIB),
    )(*own, *others, grams)


def partner(value, axis, size, step):
    return lax.ppermute(value, axis, [(i, i ^ step) for i in range(size)])


def on_device(snapshots, weights):
    n = lax.axis_size("space")
    tm_count = lax.axis_size("tm")
    freq_count = lax.axis_size("freq")
    blocks, local_times, columns = snapshots.shape
    rows = columns // n
    share = rows // freq_count

    tables = jnp.asarray(dft_blocks(n))

    last = n - 1
    early_rows = share // 2
    targets = n * tm_count

    def send(k, skip, size):
        sent = cut(snapshots, n, k, rows, skip, size)
        return partner(sent, "space", n, k)

    halves = ((0, early_rows), (early_rows, share - early_rows))
    sends = [(last, *halves[0])]
    sends += [(k, *halves[0]) for k in range(n - 2, 0, -1)]
    sends += [(k, *halves[1]) for k in range(1, n - 1)]
    pieces = [(k, skip, send(k, skip, size)) for k, skip, size in sends]
    last_piece = send(last, *halves[1])
    before = early(tables, n, 0, 0, cut(snapshots, n, 0, rows, 0, share))
    for k, skip, piece in pieces:
        before = early(tables, n, k, skip, piece, before)
    weights = weights.reshape(1, rows)
    own, rest, other, later, gram, lent = first_part(early_rows, before, weights)
    traded = [partner(part, "freq", freq_count, 1) for part in (other, later, lent)]
    piece, (other, later, lent) = lax.optimization_barrier((last_piece, traded))
    raw = partner(piece, "freq", freq_count, 1)
    *parts, gram = last_part(
        tables, n, last, 0, rest, piece, weights, gram, lent, own, other
    )
    *last_parts, gram = last_part(tables, n, last, targets, later, raw, weights, gram)
    order = [z * tm_count + x for z in range(n - 1, -1, -1) for x in range(tm_count)]
    grams = lax.all_to_all(
        gram,
        ("space", "tm"),
        split_axis=0,
        concat_axis=0,
        axis_index_groups=[order],
        tiled=True,
    )
    total = rows * targets
    return finish(total, parts[:2], [*parts[2:], *last_parts], grams)


def solution(mesh):
    return jax.shard_map(
        on_device,
        mesh=mesh,
        in_specs=(P(None, "space", ("groups", "tm")), P(("groups", "tm", "space"))),
        out_specs=(
            P("freq", None, None, ("groups", "tm", "space")),
            P("groups", "freq", None, None),
        ),
        check_vma=False,
    )
```

```python
import functools

import numpy as np
import jax
import jax.numpy as jnp
from jax import lax
from jax.experimental import pallas as pl
from jax.experimental.pallas import tpu as pltpu
from jax.sharding import PartitionSpec as P

NB = 16
SEGMENT_FRAMES = 64
NF = 16
CUTS = 4
epsilon = 1e-05
MIB = 1024 * 1024
SMALL = pl.CostEstimate(flops=1, transcendentals=0, bytes_accessed=1)


def dft_blocks(groups):
    times = np.arange(SEGMENT_FRAMES)
    taper = 0.5 - 0.5 * np.cos(2.0 * np.pi * times / SEGMENT_FRAMES)
    taper = taper / np.sqrt(np.sum(taper * taper))
    bins = 1 + np.arange(NF)
    angles = 2.0 * np.pi * (bins[:, None] * times[None, :] % SEGMENT_FRAMES) / SEGMENT_FRAMES
    table = np.stack([np.cos(angles) * taper, -np.sin(angles) * taper])
    step = SEGMENT_FRAMES // groups
    table = table.reshape(2, 2, NF // 2, groups, step)
    spread = np.einsum("rhfgt,bc->ghrfbct", table, np.eye(NB))
    spread = spread.reshape(groups, 2 * NF * NB, NB * step).astype(np.float32)
    high = spread.astype(jnp.bfloat16)
    low = (spread - high.astype(np.float32)).astype(jnp.bfloat16)
    return np.concatenate([high, high, low], axis=2)


def split(x):
    high = x.astype(jnp.bfloat16)
    return high, (x - high.astype(jnp.float32)).astype(jnp.bfloat16)


def times_split(left, x):
    high, low = split(x)
    right = jnp.concatenate([high, low, high], axis=0)
    return jnp.dot(left, right, preferred_element_type=jnp.float32)


def rows_product(a, b):
    lines, columns = a.shape[0], b.shape[0]
    full = lax.dot_general(
        jnp.concatenate(split(a), axis=0),
        jnp.concatenate(split(b), axis=0),
        (((1,), (1,)), ((), ())),
        preferred_element_type=jnp.float32,
    )
    small = full[lines:, columns:] + full[lines:, :columns] + full[:lines, columns:]
    return small + full[:lines, :columns]


def cut_kernel(n, k, rows, skip, x_ref, o_ref, sem):
    size = o_ref.shape[2]
    to = lax.bitwise_xor(lax.axis_index("space"), k)
    share = rows // 2
    start = pl.multiple_of(to * rows + lax.axis_index("freq") * share + skip, 128)
    part = NB // CUTS
    copies = []
    for i in range(CUTS):
        blocks = pl.ds(i * part, part)
        copies.append(
            pltpu.make_async_copy(
                x_ref.at[blocks, :, pl.ds(start, size)], o_ref.at[blocks], sem.at[i]
            )
        )
    for copy in copies:
        copy.start()
    for copy in copies:
        copy.wait()


def cut(snapshots, n, k, rows, skip, size):
    blocks, local_times, _ = snapshots.shape
    if local_times % 8 == 0:
        piece = pl.pallas_call(
            functools.partial(cut_kernel, n, k, rows, skip),
            out_shape=pltpu.VMEM((blocks, local_times, size), jnp.float32),
            in_specs=[pl.BlockSpec(memory_space=pltpu.HBM)],
            out_specs=pl.BlockSpec(memory_space=pltpu.VMEM),
            scratch_shapes=[pltpu.SemaphoreType.DMA((CUTS,))],
            compiler_params=pltpu.CompilerParams(vmem_limit_bytes=4 * MIB),
            cost_estimate=SMALL,
        )(pltpu.with_memory_space_constraint(snapshots, pltpu.HBM))
    else:
        to = lax.bitwise_xor(lax.axis_index("space"), k)
        start = to * rows + lax.axis_index("freq") * (rows // 2) + skip
        piece = lax.dynamic_slice_in_dim(snapshots, start, size, axis=2)
    return piece.reshape(blocks * local_times, size)


def early_kernel(n, k, skip, t_ref, x_ref, *refs):
    src = lax.bitwise_xor(lax.axis_index("space"), k)
    part = times_split(t_ref[src], x_ref[...])
    if len(refs) == 1:
        refs[0][...] = part
        return
    before_ref, out_ref = refs
    end = skip + x_ref.shape[1]
    out_ref[:, skip:end] = before_ref[:, skip:end] + part
    if skip:
        out_ref[:, :skip] = before_ref[:, :skip]
    if end < out_ref.shape[1]:
        out_ref[:, end:] = before_ref[:, end:]


def early(tables, n, k, skip, piece, *before):
    share = before[0].shape[1] if before else piece.shape[1]
    return pl.pallas_call(
        functools.partial(early_kernel, n, k, skip),
        out_shape=jax.ShapeDtypeStruct((tables.shape[1], share), jnp.float32),
        compiler_params=pltpu.CompilerParams(vmem_limit_bytes=16 * MIB),
        cost_estimate=SMALL,
    )(tables, piece, *before)


def gram_of(z, weights):
    width = z.shape[0] // 2
    local = width // NB
    line = lax.broadcasted_iota(jnp.int32, (width, width), 0) // NB
    lane = lax.broadcasted_iota(jnp.int32, (width, width), 1) // NB
    row = lax.broadcasted_iota(jnp.int32, (NB, width), 0)
    col = lax.broadcasted_iota(jnp.int32, (NB, width), 1) % NB
    full = rows_product(z * weights, z)
    gram_re = full[:width, :width] + full[width:, width:]
    gram_im = full[:width, width:] - full[width:, :width]
    both = []
    for part in (gram_re, gram_im):
        kept = jnp.where(line == lane, part, 0.0)
        both.append(jnp.sum(kept.reshape(local, NB, width), axis=0))
    return jnp.where(row >= col, both[0], both[1])


def weights_at(w_ref, place, share, skip, size):
    return w_ref[:, pl.ds(pl.multiple_of(place * share + skip, 128), size)]


def first_part_kernel(
    sum_ref, w_ref, own_ref, rest_ref, other_ref, later_ref, gram_ref, lent_ref
):
    size = own_ref.shape[1]
    me = lax.axis_index("freq")
    spectra = sum_ref[:, :size]
    weights = weights_at(w_ref, me, sum_ref.shape[1], 0, size)
    rest = sum_ref[:, size:]
    half = spectra.shape[0] // 2
    first = me == 0
    own_ref[...] = jnp.where(first, spectra[:half], spectra[half:])
    other_ref[...] = jnp.where(first, spectra[half:], spectra[:half])
    rest_ref[...] = jnp.where(first, rest[:half], rest[half:])
    later_ref[...] = jnp.where(first, rest[half:], rest[:half])
    grams = [gram_of(z, weights) for z in (spectra[:half], spectra[half:])]
    gram_ref[...] = jnp.where(first, grams[0], grams[1])
    lent_ref[...] = jnp.where(first, grams[1], grams[0])


def first_part(size, partial_sum, weights):
    share = partial_sum.shape[1]
    half = partial_sum.shape[0] // 2
    gram = (NB, half // 2)
    shapes = [(half, size), (half, share - size), (half, size), (half, share - size), gram, gram]
    return pl.pallas_call(
        first_part_kernel,
        out_shape=[jax.ShapeDtypeStruct(shape, jnp.float32) for shape in shapes],
        compiler_params=pltpu.CompilerParams(vmem_limit_bytes=16 * MIB),
        cost_estimate=SMALL,
    )(partial_sum, weights)


def last_part_kernel(n, k, swapped, t_ref, sum_ref, x_ref, w_ref, *refs):
    half, size = sum_ref.shape
    me = lax.axis_index("freq")
    src = lax.bitwise_xor(lax.axis_index("space"), k)
    lines = pl.ds(pl.multiple_of(me * half, 128), half)
    spectra = sum_ref[...] + times_split(t_ref[src, lines], x_ref[...])
    share = w_ref.shape[1] // 2
    skip = share - size
    place = 1 - me if swapped else me
    gram = gram_of(spectra, weights_at(w_ref, place, share, skip, size))
    if swapped:
        before_ref, high_ref, low_ref, gram_ref = refs
        gram = gram + before_ref[...]
        high_ref[...], low_ref[...] = split(spectra)
        for d in range(gram_ref.shape[0]):
            gram_ref[d] = gram
        return
    gram_own_ref, gram_lent_ref, own_ref, other_ref, *refs = refs
    high_ref, low_ref, other_high_ref, other_low_ref, gram_ref = refs
    gram_ref[...] = gram + gram_own_ref[...] + gram_lent_ref[...]
    high_ref[:, :skip], low_ref[:, :skip] = split(own_ref[...])
    high_ref[:, skip:], low_ref[:, skip:] = split(spectra)
    other_high_ref[...], other_low_ref[...] = split(other_ref[...])


def last_part(tables, n, k, copies, partial_sum, piece, weights, *before):
    half, size = partial_sum.shape
    share = weights.shape[1] // 2
    gram = (NB, half // 2)
    widths = [size, size] if copies else [share, share, share - size, share - size]
    parts = [jax.ShapeDtypeStruct((half, width), jnp.bfloat16) for width in widths]
    gram = jax.ShapeDtypeStruct((copies, *gram) if copies else gram, jnp.float32)
    return pl.pallas_call(
        functools.partial(last_part_kernel, n, k, bool(copies)),
        out_shape=[*parts, gram],
        compiler_params=pltpu.CompilerParams(vmem_limit_bytes=16 * MIB),
        cost_estimate=SMALL,
    )(tables, partial_sum, piece, weights, *before)


def inv_sqrt(x):
    y = lax.rsqrt(x)
    return y * (1.5 - 0.5 * x * (y * y))


def finish_kernel(
    total,
    own_high_ref,
    own_low_ref,
    first_high_ref,
    first_low_ref,
    last_high_ref,
    last_low_ref,
    grams_ref,
    modes_ref,
    factor_ref,
):
    local = modes_ref.shape[0]
    width = local * NB
    share = modes_ref.shape[3] // 2
    gram = jnp.sum(grams_ref[...], axis=0) / total
    row = lax.broadcasted_iota(jnp.int32, (NB, width), 0)
    col = lax.broadcasted_iota(jnp.int32, (NB, width), 1) % NB
    stacked = [jnp.where(col == j, gram, 0.0) for j in range(NB)]
    for j in range(NB):
        line = jnp.broadcast_to(gram[j : j + 1, :], (NB, width))
        stacked.append(jnp.where((col == row) & (row > j), -line, 0.0))
    stacked = jnp.concatenate(stacked, axis=0)
    group_r = lax.broadcasted_iota(jnp.int32, (width, width), 0) // NB
    group_c = lax.broadcasted_iota(jnp.int32, (width, width), 1) // NB
    same = group_r == group_c
    ones = jnp.where(same, 1.0, 0.0).astype(jnp.bfloat16)
    pieces, rest = [], stacked
    for _ in range(3):
        pieces.append(rest.astype(jnp.bfloat16))
        rest = rest - pieces[-1].astype(jnp.float32)
    spread = jnp.dot(
        jnp.concatenate(pieces, axis=1),
        jnp.concatenate([ones] * 3, axis=0),
        preferred_element_type=jnp.float32,
    )
    col_re = [[spread[j * NB + 8 * h : j * NB + 8 * h + 8] for h in (0, 1)] for j in range(NB)]
    base = NB * NB
    col_im = [
        [spread[base + j * NB + 8 * h : base + j * NB + 8 * h + 8] for h in (0, 1)]
        for j in range(NB)
    ]
    rows = [lax.broadcasted_iota(jnp.int32, (8, width), 0) + 8 * h for h in (0, 1)]
    lanes = lax.broadcasted_iota(jnp.int32, (8, width), 1) % NB
    inv_re = [jnp.where(rows[h] == lanes, 1.0, 0.0) for h in (0, 1)]
    inv_im = [jnp.zeros((8, width), jnp.float32) for h in (0, 1)]
    low_re = [jnp.zeros((8, width), jnp.float32) for h in (0, 1)]
    low_im = [jnp.zeros((8, width), jnp.float32) for h in (0, 1)]

    def pick(halves, i):
        return jnp.broadcast_to(halves[i // 8][i % 8 : i % 8 + 1, :], (8, width))

    pivots = [pick(col_re[j], j) + epsilon for j in range(NB)]
    scales = [jnp.zeros((8, width), jnp.float32) for h in (0, 1)]
    for p in range(NB):
        scale = inv_sqrt(pivots[p])
        inverse = scale * scale
        for h in range(p // 8, 2):
            below = rows[h] > p
            here = lanes == p
            scales[h] = jnp.where(rows[h] == p, scale, scales[h])
            col_re[p][h] = jnp.where(below, col_re[p][h], 0.0)
            col_im[p][h] = jnp.where(below, col_im[p][h], 0.0)
            diag = jnp.where(rows[h] == p, pivots[p], col_re[p][h])
            low_re[h] = jnp.where(here, diag * scale, low_re[h])
            low_im[h] = jnp.where(here, col_im[p][h] * scale, low_im[h])
        for j in range(p + 1, NB):
            a_re, a_im = pick(col_re[p], j), pick(col_im[p], j)
            u_re, u_im = a_re * inverse, a_im * inverse
            pivots[j] = pivots[j] - (a_re * u_re + a_im * u_im)
            for h in range(j // 8, 2):
                c_re, c_im = col_re[p][h], col_im[p][h]
                col_re[j][h] = col_re[j][h] - (c_re * u_re + c_im * u_im)
                col_im[j][h] = col_im[j][h] - (c_im * u_re - c_re * u_im)
        line_re = pick(inv_re, p) * inverse
        line_im = pick(inv_im, p) * inverse
        for h in range(p // 8, 2):
            c_re, c_im = col_re[p][h], col_im[p][h]
            inv_re[h] = inv_re[h] - (c_re * line_re - c_im * line_im)
            inv_im[h] = inv_im[h] - (c_re * line_im + c_im * line_re)
    inv_re = [inv_re[h] * scales[h] for h in (0, 1)]
    inv_im = [inv_im[h] * scales[h] for h in (0, 1)]

    pad = jnp.zeros((width - NB, width), jnp.float32)
    upper_re = jnp.transpose(jnp.concatenate(low_re + [pad], axis=0))
    upper_im = jnp.transpose(jnp.concatenate(low_im + [pad], axis=0))
    for f in range(local):
        factor_ref[0, f] = upper_re[f * NB : (f + 1) * NB, :NB]
        factor_ref[1, f] = -upper_im[f * NB : (f + 1) * NB, :NB]
    me = lax.axis_index("freq")
    own = own_high_ref[...], own_low_ref[...]
    other = [
        jnp.concatenate([a[...], b[...]], axis=1)
        for a, b in ((first_high_ref, last_high_ref), (first_low_ref, last_low_ref))
    ]
    part = width // 2
    lane = lax.broadcasted_iota(jnp.int32, (NB, width), 1)
    left_half = lane < part
    line = lax.broadcasted_iota(jnp.int32, (width, width), 0) % part // NB
    block = lax.broadcasted_iota(jnp.int32, (width, width), 1) % part // NB
    inv_re, inv_im = jnp.concatenate(inv_re, axis=0), jnp.concatenate(inv_im, axis=0)
    turned_re, turned_im = pltpu.roll(inv_re, part, 1), pltpu.roll(inv_im, part, 1)
    for h in range(2):
        stay = left_half if h == 0 else jnp.logical_not(left_half)
        twice_re = jnp.where(stay, inv_re, turned_re)
        twice_im = jnp.where(stay, inv_im, turned_im)
        top = jnp.where(left_half, twice_re, twice_im)
        bottom = jnp.where(left_half, -twice_im, twice_re)
        count = part // NB
        mixing = jnp.concatenate([top] * count + [bottom] * count, axis=0)
        high, low = split(jnp.where(line == block, mixing, 0.0))
        left = jnp.concatenate([high, high, low], axis=1)
        lines = [slice(r * width + h * part, r * width + (h + 1) * part) for r in range(2)]
        for place, (x_high, x_low) in ((me, own), (1 - me, other)):
            right = [x[at] for x in (x_high, x_low, x_high) for at in lines]
            out = jnp.dot(
                left, jnp.concatenate(right, axis=0), preferred_element_type=jnp.float32
            )
            cols = pl.ds(pl.multiple_of(place * share, 128), share)
            for r in range(2):
                for f in range(count):
                    at = r * part + f * NB
                    modes_ref[h * count + f, r, :, cols] = out[at : at + NB]


def finish(total, own, others, grams):
    half, share = own[0].shape
    local = half // (2 * NB)
    return pl.pallas_call(
        functools.partial(finish_kernel, total),
        out_shape=(
            jax.ShapeDtypeStruct((local, 2, NB, 2 * share), jnp.float32),
            jax.ShapeDtypeStruct((2, local, NB, NB), jnp.float32),
        ),
        compiler_params=pltpu.CompilerParams(vmem_limit_bytes=16 * MIB),
    )(*own, *others, grams)


def partner(value, axis, size, step):
    return lax.ppermute(value, axis, [(i, i ^ step) for i in range(size)])


def on_device(snapshots, weights):
    n = lax.axis_size("space")
    tm_count = lax.axis_size("tm")
    freq_count = lax.axis_size("freq")
    blocks, local_times, columns = snapshots.shape
    rows = columns // n
    share = rows // freq_count

    tables = jnp.asarray(dft_blocks(n))

    last = n - 1
    early_rows = share // 2
    targets = n * tm_count

    def send(k, skip, size):
        sent = cut(snapshots, n, k, rows, skip, size)
        return partner(sent, "space", n, k)

    halves = ((0, early_rows), (early_rows, share - early_rows))
    sends = [(last, *halves[0])]
    sends += [(k, *halves[0]) for k in range(n - 2, 0, -1)]
    sends += [(k, *halves[1]) for k in range(1, n - 1)]
    pieces = [(k, skip, send(k, skip, size)) for k, skip, size in sends]
    last_piece = send(last, *halves[1])
    before = early(tables, n, 0, 0, cut(snapshots, n, 0, rows, 0, share))
    for k, skip, piece in pieces:
        before = early(tables, n, k, skip, piece, before)
    weights = weights.reshape(1, rows)
    own, rest, other, later, gram, lent = first_part(early_rows, before, weights)
    traded = [partner(part, "freq", freq_count, 1) for part in (other, later, lent)]
    piece, (other, later, lent) = lax.optimization_barrier((last_piece, traded))
    raw = partner(piece, "freq", freq_count, 1)
    *parts, gram = last_part(
        tables, n, last, 0, rest, piece, weights, gram, lent, own, other
    )
    *last_parts, gram = last_part(tables, n, last, targets, later, raw, weights, gram)
    order = list(range(targets - 1, -1, -1))
    grams = lax.all_to_all(
        gram,
        ("space", "tm"),
        split_axis=0,
        concat_axis=0,
        axis_index_groups=[order],
        tiled=True,
    )
    total = rows * targets
    return finish(total, parts[:2], [*parts[2:], *last_parts], grams)


def solution(mesh):
    return jax.shard_map(
        on_device,
        mesh=mesh,
        in_specs=(P(None, "space", ("groups", "tm")), P(("groups", "tm", "space"))),
        out_specs=(
            P("freq", None, None, ("groups", "tm", "space")),
            P("groups", "freq", None, None),
        ),
        check_vma=False,
    )
```
